32 devices in a mesh: ctx: 8 (over y, x, core), tp: 4 (over z).
Axes of the slice: x: 2, y: 2, z: 4, core: 2. Of those that a mesh axis runs over, the one named last changes fastest.
Arguments:
- x_gate: bfloat16 [1024, 2048], P('ctx', 'tp'), may hold values from -6 to 6
- x_post: bfloat16 [1024, 2048], P('ctx', 'tp'), may hold values from -6 to 6
- values: bfloat16 [1024, 2048], P('ctx', 'tp'), may hold values from -6 to 6
- decay: float32 [2, 2048, 16], P(None, 'tp'), may hold values from 0.00024414062 to 0.05
- residue: float32 [2, 2048, 16], P(None, 'tp'), may hold values from -4 to 4
- w_out: bfloat16 [2048, 2048], P(('tp', 'ctx')), may hold values from -0.125 to 0.125
Outputs:
- projected: bfloat16 [1024, 2048], P('ctx', 'tp')
The draws below stay inside these ranges and needn't reach their ends.
All inputs are finite; a program needn't handle non-finite values.
Results may differ from the reference program's by a relative error of at most 0.015.
Values may be sent and summed in bfloat16 or wider, within the bound.
No kernel may reach another device: no remote copies, remote signals or barrier semaphores. Data moves between devices by JAX's collectives and lax.ppermute only.
A program may use at most 128 MiB of HBM per device.

```python
import jax
import jax.numpy as jnp
from jax import lax

C = 2048
DO = 2048
K = 16
SEQ = 1024


def draw_decay(key, part):
    lowest = 1.0 / (4.0 * SEQ)
    highest = 0.05
    spread = jax.random.uniform(key, (2, C, K), jnp.float32)
    return jnp.exp(jnp.log(lowest) + spread * (jnp.log(highest) - jnp.log(lowest)))


def levels(own_key, dims, shards, low, high):
    factor_of = 1.0
    for position, parts in shards:
        draws = jax.random.uniform(jax.random.fold_in(jax.random.fold_in(own_key, 6), position), (parts,), jnp.float32, low / len(shards), high / len(shards))
        factor_of = factor_of * jnp.repeat(jnp.exp(draws), dims[position] // parts).reshape((-1,) + (1,) * (len(dims) - 1 - position))
    return factor_of


def normal_values(key, dims, scale, bound, cuts=(), kind=jnp.bfloat16):
    result = jax.random.normal(key, dims, jnp.float32) * scale
    if len(cuts) > 0:
        result = levels(key, dims, cuts, -0.22, 0.18) * result
    return jnp.clip(result, min=-bound, max=bound).astype(kind)


def setup_inputs(seed: int = 0) -> dict:
    key_of = jax.random.split(jax.random.key(seed), 7)
    return {
        "x_gate": normal_values(key_of[0], (SEQ, C), 1.0, 6.0, ((0, 8), (1, 4))),
        "x_post": normal_values(key_of[1], (SEQ, C), 1.0, 6.0, ((0, 8), (1, 4))),
        "values": normal_values(key_of[2], (SEQ, C), 1.0, 6.0, ((0, 8), (1, 4))),
        "decay": draw_decay(jax.random.fold_in(key_of[6], 71), 0),
        "residue": normal_values(key_of[4], (2, C, K), 1.0, 4.0, ((1, 4),), jnp.float32),
        "w_out": normal_values(key_of[5], (DO, C), C ** -0.5, 0.125, ((0, 32),)),
    }


def kernel(decay_rows, residue_rows):
    inner_len = min(256, SEQ)
    outer_len = SEQ // inner_len
    weight = residue_rows * jnp.sqrt(2.0 * decay_rows / K)
    coarse = jnp.exp(-decay_rows[:, :, None] * (jnp.arange(outer_len, dtype=jnp.float32) * inner_len))
    fine_part = jnp.exp(-decay_rows[:, :, None] * jnp.arange(inner_len, dtype=jnp.float32))
    filter_rows = jnp.einsum('ck,ckq,ckr->cqr', weight, coarse, fine_part, precision=lax.Precision.HIGHEST)
    return filter_rows.reshape(decay_rows.shape[0], SEQ)

def spectra(signal):
    return jnp.fft.rfft(signal, n=2 * SEQ, axis=-1)

def restore(spectrum_rows):
    return jnp.fft.irfft(spectrum_rows, n=2 * SEQ, axis=-1)[:, :SEQ]

def branch(gate_rows, post_rows, value_rows, own_spec, pair_spec):
    gate_rows = gate_rows.astype(jnp.float32)
    value_spec = spectra(value_rows.astype(jnp.float32))
    along_fwd = restore(value_spec * own_spec[0])
    along_rev = restore(value_spec * jnp.conj(pair_spec[0]))
    summed = restore(spectra(gate_rows * along_fwd) * own_spec[1] + spectra(gate_rows * along_rev) * jnp.conj(pair_spec[1]))
    return (post_rows.astype(jnp.float32) * summed).astype(jnp.bfloat16)

def block_pair(block):
    gate_lo, post_lo, value_lo, gate_hi, post_hi, value_hi, rate_lo, res_lo, rate_hi, res_hi = block
    spec_lo = [spectra(kernel(rate_lo[filter_index], res_lo[filter_index])) for filter_index in range(2)]
    spec_hi = [spectra(kernel(rate_hi[filter_index], res_hi[filter_index])) for filter_index in range(2)]
    return (branch(gate_lo, post_lo, value_lo, spec_lo, spec_hi), branch(gate_hi, post_hi, value_hi, spec_hi, spec_lo))

def reference(x_gate, x_post, values, decay, residue, w_out):
    half_count = C // 2
    block_rows = 16
    blocks = half_count // block_rows

    def lower_rows(source):
        return source.T[:half_count].reshape(blocks, block_rows, SEQ)

    def upper_rows(source):
        return source.T[::-1][:half_count].reshape(blocks, block_rows, SEQ)

    def params_low(source):
        return jnp.transpose(source[:, :half_count].reshape(2, blocks, block_rows, K), (1, 0, 2, 3))

    def params_high(source):
        return jnp.transpose(source[:, ::-1][:, :half_count].reshape(2, blocks, block_rows, K), (1, 0, 2, 3))
    low_out, high_out = lax.map(block_pair, (lower_rows(x_gate), lower_rows(x_post), lower_rows(values), upper_rows(x_gate), upper_rows(x_post), upper_rows(values), params_low(decay), params_low(residue), params_high(decay), params_high(residue)))
    mixed = jnp.concatenate([low_out.reshape(half_count, SEQ), high_out.reshape(half_count, SEQ)[::-1]], axis=0).T
    return jnp.dot(mixed, w_out.T, preferred_element_type=jnp.float32).astype(jnp.bfloat16)
```

```python
import functools
import math

import jax
import jax.numpy as jnp
import ml_dtypes
import numpy as np
from jax import lax
from jax.experimental import pallas as pl
from jax.experimental.pallas import tpu as pltpu
from jax.sharding import PartitionSpec as P

HIGHEST = lax.Precision.HIGHEST


def partner(value, axis, bit):
    mask = 2**bit
    pairs = [(source, source ^ mask) for source in range(lax.axis_size(axis))]
    return lax.ppermute(value, axis, pairs)


def radices(length_all):
    last_radix = min(128, length_all // 4)
    first_radix = min(32, length_all // last_radix)
    return (first_radix, length_all // (first_radix * last_radix), last_radix)


def rotation(row_count, col_count, modulus):
    product = (
        lax.broadcasted_iota(jnp.int32, (row_count, col_count), 0)
        * lax.broadcasted_iota(jnp.int32, (row_count, col_count), 1)
        % modulus
    )
    angle = product.astype(jnp.float32) * (2.0 * math.pi / modulus)
    return (jnp.cos(angle), -jnp.sin(angle))


def tables(radix_sizes):
    first_radix, mid_radix, last_radix = radix_sizes
    length_all = first_radix * mid_radix * last_radix
    outer_real, outer_imag = rotation(first_radix, first_radix, first_radix)
    mid_real, mid_imag = rotation(mid_radix, mid_radix, mid_radix)
    last_real, last_imag = rotation(last_radix, last_radix, last_radix)
    twist_real, twist_imag = rotation(first_radix, mid_radix * last_radix, length_all)
    twist_real = twist_real.reshape(first_radix, mid_radix, last_radix)
    twist_imag = twist_imag.reshape(first_radix, mid_radix, last_radix)
    inner_real, inner_imag = rotation(mid_radix, last_radix, mid_radix * last_radix)
    return (
        outer_real,
        outer_imag,
        mid_real,
        mid_imag,
        last_real,
        last_imag,
        twist_real,
        twist_imag,
        inner_real,
        inner_imag,
    )


def apply_matrix(pattern, real_part, imag_part, matrix_real, matrix_imag):
    out_real = jnp.einsum(pattern, real_part, matrix_real, precision=HIGHEST) - jnp.einsum(
        pattern, imag_part, matrix_imag, precision=HIGHEST
    )
    out_imag = jnp.einsum(pattern, real_part, matrix_imag, precision=HIGHEST) + jnp.einsum(
        pattern, imag_part, matrix_real, precision=HIGHEST
    )
    return (out_real, out_imag)


def complex_times(left_real, left_imag, right_real, right_imag):
    return (
        left_real * right_real - left_imag * right_imag,
        left_real * right_imag + left_imag * right_real,
    )


def forward(real_part, imag_part, table_set, radix_sizes):
    first_radix, mid_radix, last_radix = radix_sizes
    half_first = first_radix // 2
    batch_rows = real_part.shape[0]
    (
        outer_real,
        outer_imag,
        mid_real,
        mid_imag,
        last_real,
        last_imag,
        twist_real,
        twist_imag,
        inner_real,
        inner_imag,
    ) = table_set
    real_part = real_part.reshape(batch_rows, half_first, mid_radix, last_radix)
    imag_part = imag_part.reshape(batch_rows, half_first, mid_radix, last_radix)
    real_part, imag_part = apply_matrix(
        "banm,ak->bknm", real_part, imag_part, outer_real[:half_first], outer_imag[:half_first]
    )
    real_part, imag_part = complex_times(real_part, imag_part, twist_real, twist_imag)
    real_part, imag_part = apply_matrix("bknm,nj->bkjm", real_part, imag_part, mid_real, mid_imag)
    real_part, imag_part = complex_times(real_part, imag_part, inner_real, inner_imag)
    return apply_matrix("bkjm,mq->bkjq", real_part, imag_part, last_real, last_imag)


def inverse(real_part, imag_part, table_set, radix_sizes):
    first_radix, mid_radix, last_radix = radix_sizes
    half_first = first_radix // 2
    batch_rows = real_part.shape[0]
    (
        outer_real,
        outer_imag,
        mid_real,
        mid_imag,
        last_real,
        last_imag,
        twist_real,
        twist_imag,
        inner_real,
        inner_imag,
    ) = table_set
    real_part, imag_part = apply_matrix(
        "bkjq,mq->bkjm", real_part, imag_part, last_real / last_radix, -last_imag / last_radix
    )
    real_part, imag_part = complex_times(real_part, imag_part, inner_real, -inner_imag)
    real_part, imag_part = apply_matrix(
        "bkjm,nj->bknm", real_part, imag_part, mid_real / mid_radix, -mid_imag / mid_radix
    )
    real_part, imag_part = complex_times(real_part, imag_part, twist_real, -twist_imag)
    matrix_real = outer_real[:half_first] / first_radix
    matrix_imag = -outer_imag[:half_first] / first_radix
    out_real, out_imag = apply_matrix(
        "bknm,ak->banm", real_part, imag_part, matrix_real, matrix_imag
    )
    return (out_real.reshape(batch_rows, -1), out_imag.reshape(batch_rows, -1))


def spectrum(decay_rows, residue_rows, radix_sizes, seq_length):
    first_radix, mid_radix, last_radix = radix_sizes
    length_all = first_radix * mid_radix * last_radix
    poles = decay_rows.shape[1]
    shape_all = (first_radix, mid_radix, last_radix)
    frequency = (
        lax.broadcasted_iota(jnp.int32, shape_all, 0)
        + first_radix * lax.broadcasted_iota(jnp.int32, shape_all, 1)
        + first_radix * mid_radix * lax.broadcasted_iota(jnp.int32, shape_all, 2)
    )
    half_angle = frequency.astype(jnp.float32) * (math.pi / length_all)
    sin_half = jnp.sin(half_angle)
    sin_full = jnp.sin(2.0 * half_angle)
    parity_sign = (1 - 2 * (frequency % 2)).astype(jnp.float32)

    def add_pole(pole_index, running):
        run_real, run_imag = running
        rate_col = lax.dynamic_slice_in_dim(decay_rows, pole_index, 1, 1).reshape(-1, 1, 1, 1)
        weight = lax.dynamic_slice_in_dim(residue_rows, pole_index, 1, 1).reshape(
            -1, 1, 1, 1
        ) * jnp.sqrt(2.0 * rate_col / poles)
        retained = jnp.exp(-rate_col)
        den_real = -jnp.expm1(-rate_col) + 2.0 * retained * sin_half * sin_half
        den_imag = retained * sin_full
        pole_scale = (
            weight
            * (1.0 - jnp.exp(-rate_col * seq_length) * parity_sign)
            / (den_real * den_real + den_imag * den_imag)
        )
        return (run_real + pole_scale * den_real, run_imag - pole_scale * den_imag)

    zeros_all = jnp.zeros((decay_rows.shape[0],) + shape_all, jnp.float32)
    return lax.fori_loop(0, poles, add_pole, (zeros_all, zeros_all))


def general(x_gate, x_post, values, decay, residue, w_out):
    tok_rows, block_width = x_gate.shape
    ctx_count = lax.axis_size("ctx")
    tp_count = lax.axis_size("tp")
    chan_group = block_width // ctx_count
    seq_length = tok_rows * ctx_count
    radix_sizes = radices(2 * seq_length)
    table_set = tables(radix_sizes)
    first_row = lax.axis_index("ctx") * chan_group
    own_rate = lax.dynamic_slice_in_dim(decay, first_row, chan_group, 1)
    own_residue = lax.dynamic_slice_in_dim(residue, first_row, chan_group, 1)
    own_spec = [
        spectrum(own_rate[filter_index], own_residue[filter_index], radix_sizes, seq_length)
        for filter_index in range(2)
    ]
    forward_rows = [x_gate, values] + [x_post]
    row_count = len(forward_rows)
    base_rows = jnp.stack(forward_rows)
    copied = base_rows
    for bit_index in range(tp_count.bit_length() - 1):
        copied = partner(copied, "tp", bit_index)
    sent_rows = jnp.concatenate([base_rows, copied[:, :, ::-1]], axis=0)
    received = lax.all_to_all(
        jnp.swapaxes(sent_rows, 1, 2), "ctx", split_axis=1, concat_axis=2, tiled=True
    )
    gate_fwd = received[0].astype(jnp.float32)
    value_fwd = received[1].astype(jnp.float32)
    mirrored = received[row_count:, :, ::-1].astype(jnp.float32)
    spec_real, spec_imag = forward(value_fwd, mirrored[1], table_set, radix_sizes)
    spec_real, spec_imag = complex_times(spec_real, spec_imag, own_spec[0][0], own_spec[0][1])
    along_fwd, along_rev = inverse(spec_real, spec_imag, table_set, radix_sizes)
    spec_real, spec_imag = forward(
        gate_fwd * along_fwd, mirrored[0] * along_rev, table_set, radix_sizes
    )
    spec_real, spec_imag = complex_times(spec_real, spec_imag, own_spec[1][0], own_spec[1][1])
    sum_fwd, sum_rev = inverse(spec_real, spec_imag, table_set, radix_sizes)
    sum_fwd = received[2].astype(jnp.float32) * sum_fwd
    sum_rev = mirrored[2] * sum_rev
    results = jnp.stack([sum_fwd, sum_rev[:, ::-1]])
    returned = lax.all_to_all(
        results.astype(jnp.bfloat16), "ctx", split_axis=2, concat_axis=1, tiled=True
    ).astype(results.dtype)
    flipped = returned[1, ::-1, :]
    for bit_index in range(tp_count.bit_length() - 1):
        flipped = partner(flipped.astype(jnp.bfloat16), "tp", bit_index).astype(flipped.dtype)
    total_rows = returned[0] + flipped
    total_rows = total_rows.T
    mixed_rows = total_rows.astype(jnp.bfloat16)
    whole_rows = lax.all_gather(mixed_rows, "tp", axis=1, tiled=True)
    projected = lax.dot_general(
        whole_rows,
        lax.all_gather(w_out, "ctx", axis=0, tiled=True),
        (((1,), (1,)), ((), ())),
        preferred_element_type=jnp.float32,
    )
    return projected.astype(jnp.bfloat16)


def block_tables(block):
    angle = np.pi * np.outer(np.arange(block), np.arange(block) + 0.5) / block
    to_freq = np.concatenate([np.cos(angle), -np.sin(angle)], axis=1)
    result = []
    for table in (to_freq, to_freq.T / block):
        high = table.astype(ml_dtypes.bfloat16)
        low = (table - high.astype(np.float64)).astype(ml_dtypes.bfloat16)
        result += [jnp.asarray(high), jnp.asarray(low)]
    return result


def halves(value):
    high = value.astype(jnp.bfloat16)
    return high, (value - high.astype(jnp.float32)).astype(jnp.bfloat16)


def mul(left, right):
    return jnp.dot(left, right, preferred_element_type=jnp.float32)


def mul3(left_high, left_low, right_high, right_low):
    return mul(left_high, right_high) + (mul(left_low, right_high) + mul(left_high, right_low))


def pack_kernel(gate_ref, value_ref, post_ref, out_ref):
    ctx_count, _, group, tok = out_ref.shape
    width = gate_ref.shape[1]
    for position, ref in enumerate((gate_ref, value_ref, post_ref)):
        for first in range(0, width, tok):
            turned = ref[:, first : first + tok].T
            for part in range(tok // group):
                out_ref[first // group + part, position] = turned[part * group : (part + 1) * group]


def filter_kernel(poles, par_ref, fh_ref, fl_ref, out_ref, time_ref):
    blocks, group, twice = out_ref.shape[2:]
    block = twice // 2
    lanes = 128
    turned = par_ref[...].T
    ramp = lax.broadcasted_iota(jnp.int32, (8, lanes), 1).astype(jnp.float32)
    for index in range(2):
        for side in range(2):
            for row in range(0, group, 8):
                rows = slice(side * group + row, side * group + row + 8)
                rate = turned[rows, index * poles : (index + 1) * poles]
                scale = turned[rows, (2 + index) * poles : (3 + index) * poles] * jnp.sqrt(rate * (2.0 / poles))
                jump = jnp.exp(rate * -lanes)
                sums = [None] * (blocks * block // lanes)
                for pole in range(poles):
                    term = scale[:, pole : pole + 1] * jnp.exp(-rate[:, pole : pole + 1] * ramp)
                    step = jnp.broadcast_to(jump[:, pole : pole + 1], (8, lanes))
                    for place in range(len(sums)):
                        sums[place] = term if pole == 0 else sums[place] + term
                        if place + 1 < len(sums):
                            term = term * step
                for place, total in enumerate(sums):
                    lag, lane = divmod(place * lanes, block)
                    first = ((index * 2 + side) * blocks + lag) * group + row
                    time_ref[first : first + 8, lane : lane + lanes] = total
    sign = (1 - 2 * (lax.broadcasted_iota(jnp.int32, (group, block), 1) % 2)).astype(jnp.float32)
    for index in range(2):
        for side in range(2):
            first = (index * 2 + side) * blocks * group
            high, low = halves(time_ref[first : first + blocks * group])
            spec = mul3(high, low, fh_ref[...], fl_ref[...])
            for lag in range(blocks):
                real = spec[lag * group : (lag + 1) * group, :block]
                imag = spec[lag * group : (lag + 1) * group, block:]
                if lag > 0:
                    real = real - sign * spec[(lag - 1) * group : lag * group, block:]
                    imag = imag + sign * spec[(lag - 1) * group : lag * group, :block]
                out_ref[index, side, lag, :, :block] = real
                out_ref[index, side, lag, :, block:] = imag


def conv_kernel(x_ref, h_ref, fh_ref, fl_ref, gh_ref, gl_ref, out_ref, spec_ref, high_ref, low_ref):
    blocks, group, twice = h_ref.shape[2:]
    block = twice // 2
    rows_all = blocks * group
    tall, wide = 16, 128
    pieces = x_ref.shape[0] // blocks

    def rows_of(position):
        return jnp.concatenate(
            [
                jnp.concatenate([x_ref[m * pieces + s, position] for s in range(pieces)], axis=1)
                for m in range(blocks)
            ],
            axis=0,
        )

    def times(index, side, source, row, lane):
        data = []
        for m in range(blocks):
            rows = slice(source + m * group + row, source + m * group + row + tall)
            data.append((spec_ref[rows, lane : lane + wide], spec_ref[rows, block + lane : block + lane + wide]))
        sums = [None] * blocks
        for lag in range(blocks):
            f_re = h_ref[index, side, lag, row : row + tall, lane : lane + wide]
            f_im = h_ref[index, side, lag, row : row + tall, block + lane : block + lane + wide]
            for m in range(blocks - lag):
                target, (d_re, d_im) = (m + lag, data[m]) if side == 0 else (m, data[m + lag])
                if side == 0:
                    real, imag = f_re * d_re - f_im * d_im, f_re * d_im + f_im * d_re
                else:
                    real, imag = f_re * d_re + f_im * d_im, f_re * d_im - f_im * d_re
                if sums[target] is not None:
                    real, imag = sums[target][0] + real, sums[target][1] + imag
                sums[target] = (real, imag)
        return sums

    def keep(target, row, lane, sums):
        for m in range(blocks):
            rows = slice(target + m * group + row, target + m * group + row + tall)
            for part in range(2):
                cols = slice(part * block + lane, part * block + lane + wide)
                high_ref[rows, cols], low_ref[rows, cols] = halves(sums[m][part])

    chunks = [(row, lane) for row in range(0, group, tall) for lane in range(0, block, wide)]

    value = rows_of(1)
    spec_ref[:rows_all] = mul(value, fh_ref[...]) + mul(value, fl_ref[...])
    for row, lane in chunks:
        for side in range(2):
            keep(side * rows_all, row, lane, times(0, side, 0, row, lane))
    along = mul3(high_ref[...], low_ref[...], gh_ref[...], gl_ref[...])
    gate = rows_of(0).astype(jnp.float32)
    high, low = halves(jnp.concatenate([gate, gate], axis=0) * along)
    spec_ref[...] = mul3(high, low, fh_ref[...], fl_ref[...])
    for row, lane in chunks:
        ahead, back = times(1, 0, 0, row, lane), times(1, 1, rows_all, row, lane)
        keep(0, row, lane, [(a[0] + b[0], a[1] + b[1]) for a, b in zip(ahead, back)])
    summed = mul3(high_ref[:rows_all], low_ref[:rows_all], gh_ref[...], gl_ref[...])
    mixed = (rows_of(2).astype(jnp.float32) * summed).astype(jnp.bfloat16)
    tok = block // pieces
    for m in range(blocks):
        for s in range(pieces):
            out_ref[m * pieces + s] = mixed[m * group : (m + 1) * group, s * tok : (s + 1) * tok]


def project_kernel(w_ref, mixed_ref, out_ref):
    out_ref[...] = mul(w_ref[...], mixed_ref[...]).T.astype(jnp.bfloat16)


def whole_call(kernel, out_shape, scratch, flops, nbytes, *operands):
    return pl.pallas_call(
        kernel,
        out_shape=out_shape,
        in_specs=[pl.BlockSpec(memory_space=pltpu.VMEM)] * len(operands),
        out_specs=pl.BlockSpec(memory_space=pltpu.VMEM),
        scratch_shapes=scratch,
        cost_estimate=pl.CostEstimate(flops=flops, bytes_accessed=nbytes, transcendentals=0),
        compiler_params=pltpu.CompilerParams(vmem_limit_bytes=32 * 2**20),
    )(*operands)


def blocked(x_gate, x_post, values, decay, residue, w_out):
    tok, width = x_gate.shape
    ctx_count = lax.axis_size("ctx")
    tp_count = lax.axis_size("tp")
    group = width // ctx_count
    poles = decay.shape[2]
    block = 2 * tok
    blocks = tok * ctx_count // block
    position = lax.axis_index("ctx")
    tables = block_tables(block)
    gathered_w = lax.all_gather(w_out, "ctx", axis=0, tiled=True)

    packed = whole_call(
        pack_kernel,
        jax.ShapeDtypeStruct((ctx_count, 3, group, tok), jnp.bfloat16),
        [],
        0,
        6 * tok * width * 2,
        x_gate,
        values,
        x_post,
    )
    received = lax.all_to_all(packed, "ctx", split_axis=0, concat_axis=0, tiled=True)

    params = jnp.swapaxes(jnp.concatenate([decay, residue], axis=0), 1, 2).reshape(4 * poles, width)
    own = lax.dynamic_slice_in_dim(params, position * group, group, 1)
    mirrored = lax.dynamic_slice_in_dim(params, (ctx_count - 1 - position) * group, group, 1)[:, ::-1]
    paired = lax.ppermute(mirrored, "tp", [(z, tp_count - 1 - z) for z in range(tp_count)])
    both = jnp.concatenate([own, paired], axis=1)
    spectra = whole_call(
        functools.partial(filter_kernel, poles),
        jax.ShapeDtypeStruct((2, 2, blocks, group, 2 * block), jnp.float32),
        [pltpu.VMEM((4 * blocks * group, block), jnp.float32)],
        2 * 4 * blocks * group * block * 2 * block * 3,
        4 * blocks * group * 2 * block * 4,
        both,
        tables[0],
        tables[1],
    )
    mixed = whole_call(
        conv_kernel,
        jax.ShapeDtypeStruct((ctx_count, group, tok), jnp.bfloat16),
        [
            pltpu.VMEM((2 * blocks * group, 2 * block), jnp.float32),
            pltpu.VMEM((2 * blocks * group, 2 * block), jnp.bfloat16),
            pltpu.VMEM((2 * blocks * group, 2 * block), jnp.bfloat16),
        ],
        2 * 6 * blocks * group * block * 2 * block * 3,
        4 * blocks * group * 2 * block * 4,
        received,
        spectra,
        *tables,
    )
    mine = lax.all_to_all(mixed, "ctx", split_axis=0, concat_axis=0, tiled=True)
    every = lax.all_gather(mine.reshape(width, tok), "tp", axis=0, tiled=True)
    features, channels = gathered_w.shape
    tile = 128
    return pl.pallas_call(
        project_kernel,
        out_shape=jax.ShapeDtypeStruct((tok, features), jnp.bfloat16),
        grid=(features // tile,),
        in_specs=[
            pl.BlockSpec((tile, channels), lambda f: (f, 0)),
            pl.BlockSpec((channels, tok), lambda f: (0, 0)),
        ],
        out_specs=pl.BlockSpec((tok, tile), lambda f: (0, f)),
        cost_estimate=pl.CostEstimate(
            flops=2 * tok * features * channels, bytes_accessed=2 * features * channels, transcendentals=0
        ),
    )(gathered_w, every)


def local(x_gate, x_post, values, decay, residue, w_out):
    tok, width = x_gate.shape
    ctx_count = lax.axis_size("ctx")
    if tok == 128 and width == 64 * ctx_count and ctx_count <= 16:
        return blocked(x_gate, x_post, values, decay, residue, w_out)
    return general(x_gate, x_post, values, decay, residue, w_out)


def solution(mesh):
    in_specs = (
        P("ctx", "tp"),
        P("ctx", "tp"),
        P("ctx", "tp"),
        P(None, "tp", None),
        P(None, "tp", None),
        P(("tp", "ctx"), None),
    )
    out_specs = P("ctx", "tp")
    return jax.shard_map(local, mesh=mesh, in_specs=in_specs, out_specs=out_specs, check_vma=False)
```

```python
import functools
import math

import jax
import jax.numpy as jnp
import ml_dtypes
import numpy as np
from jax import lax
from jax.experimental import pallas as pl
from jax.experimental.pallas import tpu as pltpu
from jax.sharding import PartitionSpec as P

HIGHEST = lax.Precision.HIGHEST


def partner(value, axis, bit):
    mask = 2**bit
    pairs = [(source, source ^ mask) for source in range(lax.axis_size(axis))]
    return lax.ppermute(value, axis, pairs)


def radices(length_all):
    last_radix = min(128, length_all // 4)
    first_radix = min(32, length_all // last_radix)
    return (first_radix, length_all // (first_radix * last_radix), last_radix)


def rotation(row_count, col_count, modulus):
    product = (
        lax.broadcasted_iota(jnp.int32, (row_count, col_count), 0)
        * lax.broadcasted_iota(jnp.int32, (row_count, col_count), 1)
        % modulus
    )
    angle = product.astype(jnp.float32) * (2.0 * math.pi / modulus)
    return (jnp.cos(angle), -jnp.sin(angle))


def tables(radix_sizes):
    first_radix, mid_radix, last_radix = radix_sizes
    length_all = first_radix * mid_radix * last_radix
    outer_real, outer_imag = rotation(first_radix, first_radix, first_radix)
    mid_real, mid_imag = rotation(mid_radix, mid_radix, mid_radix)
    last_real, last_imag = rotation(last_radix, last_radix, last_radix)
    twist_real, twist_imag = rotation(first_radix, mid_radix * last_radix, length_all)
    twist_real = twist_real.reshape(first_radix, mid_radix, last_radix)
    twist_imag = twist_imag.reshape(first_radix, mid_radix, last_radix)
    inner_real, inner_imag = rotation(mid_radix, last_radix, mid_radix * last_radix)
    return (
        outer_real,
        outer_imag,
        mid_real,
        mid_imag,
        last_real,
        last_imag,
        twist_real,
        twist_imag,
        inner_real,
        inner_imag,
    )


def apply_matrix(pattern, real_part, imag_part, matrix_real, matrix_imag):
    out_real = jnp.einsum(pattern, real_part, matrix_real, precision=HIGHEST) - jnp.einsum(
        pattern, imag_part, matrix_imag, precision=HIGHEST
    )
    out_imag = jnp.einsum(pattern, real_part, matrix_imag, precision=HIGHEST) + jnp.einsum(
        pattern, imag_part, matrix_real, precision=HIGHEST
    )
    return (out_real, out_imag)


def complex_times(left_real, left_imag, right_real, right_imag):
    return (
        left_real * right_real - left_imag * right_imag,
        left_real * right_imag + left_imag * right_real,
    )


def forward(real_part, imag_part, table_set, radix_sizes):
    first_radix, mid_radix, last_radix = radix_sizes
    half_first = first_radix // 2
    batch_rows = real_part.shape[0]
    (
        outer_real,
        outer_imag,
        mid_real,
        mid_imag,
        last_real,
        last_imag,
        twist_real,
        twist_imag,
        inner_real,
        inner_imag,
    ) = table_set
    real_part = real_part.reshape(batch_rows, half_first, mid_radix, last_radix)
    imag_part = imag_part.reshape(batch_rows, half_first, mid_radix, last_radix)
    real_part, imag_part = apply_matrix(
        "banm,ak->bknm", real_part, imag_part, outer_real[:half_first], outer_imag[:half_first]
    )
    real_part, imag_part = complex_times(real_part, imag_part, twist_real, twist_imag)
    real_part, imag_part = apply_matrix("bknm,nj->bkjm", real_part, imag_part, mid_real, mid_imag)
    real_part, imag_part = complex_times(real_part, imag_part, inner_real, inner_imag)
    return apply_matrix("bkjm,mq->bkjq", real_part, imag_part, last_real, last_imag)


def inverse(real_part, imag_part, table_set, radix_sizes):
    first_radix, mid_radix, last_radix = radix_sizes
    half_first = first_radix // 2
    batch_rows = real_part.shape[0]
    (
        outer_real,
        outer_imag,
        mid_real,
        mid_imag,
        last_real,
        last_imag,
        twist_real,
        twist_imag,
        inner_real,
        inner_imag,
    ) = table_set
    real_part, imag_part = apply_matrix(
        "bkjq,mq->bkjm", real_part, imag_part, last_real / last_radix, -last_imag / last_radix
    )
    real_part, imag_part = complex_times(real_part, imag_part, inner_real, -inner_imag)
    real_part, imag_part = apply_matrix(
        "bkjm,nj->bknm", real_part, imag_part, mid_real / mid_radix, -mid_imag / mid_radix
    )
    real_part, imag_part = complex_times(real_part, imag_part, twist_real, -twist_imag)
    matrix_real = outer_real[:half_first] / first_radix
    matrix_imag = -outer_imag[:half_first] / first_radix
    out_real, out_imag = apply_matrix(
        "bknm,ak->banm", real_part, imag_part, matrix_real, matrix_imag
    )
    return (out_real.reshape(batch_rows, -1), out_imag.reshape(batch_rows, -1))


def spectrum(decay_rows, residue_rows, radix_sizes, seq_length):
    first_radix, mid_radix, last_radix = radix_sizes
    length_all = first_radix * mid_radix * last_radix
    poles = decay_rows.shape[1]
    shape_all = (first_radix, mid_radix, last_radix)
    frequency = (
        lax.broadcasted_iota(jnp.int32, shape_all, 0)
        + first_radix * lax.broadcasted_iota(jnp.int32, shape_all, 1)
        + first_radix * mid_radix * lax.broadcasted_iota(jnp.int32, shape_all, 2)
    )
    half_angle = frequency.astype(jnp.float32) * (math.pi / length_all)
    sin_half = jnp.sin(half_angle)
    sin_full = jnp.sin(2.0 * half_angle)
    parity_sign = (1 - 2 * (frequency % 2)).astype(jnp.float32)

    def add_pole(pole_index, running):
        run_real, run_imag = running
        rate_col = lax.dynamic_slice_in_dim(decay_rows, pole_index, 1, 1).reshape(-1, 1, 1, 1)
        weight = lax.dynamic_slice_in_dim(residue_rows, pole_index, 1, 1).reshape(
            -1, 1, 1, 1
        ) * jnp.sqrt(2.0 * rate_col / poles)
        retained = jnp.exp(-rate_col)
        den_real = -jnp.expm1(-rate_col) + 2.0 * retained * sin_half * sin_half
        den_imag = retained * sin_full
        pole_scale = (
            weight
            * (1.0 - jnp.exp(-rate_col * seq_length) * parity_sign)
            / (den_real * den_real + den_imag * den_imag)
        )
        return (run_real + pole_scale * den_real, run_imag - pole_scale * den_imag)

    zeros_all = jnp.zeros((decay_rows.shape[0],) + shape_all, jnp.float32)
    return lax.fori_loop(0, poles, add_pole, (zeros_all, zeros_all))


def general(x_gate, x_post, values, decay, residue, w_out):
    tok_rows, block_width = x_gate.shape
    ctx_count = lax.axis_size("ctx")
    tp_count = lax.axis_size("tp")
    chan_group = block_width // ctx_count
    seq_length = tok_rows * ctx_count
    radix_sizes = radices(2 * seq_length)
    table_set = tables(radix_sizes)
    first_row = lax.axis_index("ctx") * chan_group
    own_rate = lax.dynamic_slice_in_dim(decay, first_row, chan_group, 1)
    own_residue = lax.dynamic_slice_in_dim(residue, first_row, chan_group, 1)
    own_spec = [
        spectrum(own_rate[filter_index], own_residue[filter_index], radix_sizes, seq_length)
        for filter_index in range(2)
    ]
    forward_rows = [x_gate, values] + [x_post]
    row_count = len(forward_rows)
    base_rows = jnp.stack(forward_rows)
    copied = base_rows
    for bit_index in range(tp_count.bit_length() - 1):
        copied = partner(copied, "tp", bit_index)
    sent_rows = jnp.concatenate([base_rows, copied[:, :, ::-1]], axis=0)
    received = lax.all_to_all(
        jnp.swapaxes(sent_rows, 1, 2), "ctx", split_axis=1, concat_axis=2, tiled=True
    )
    gate_fwd = received[0].astype(jnp.float32)
    value_fwd = received[1].astype(jnp.float32)
    mirrored = received[row_count:, :, ::-1].astype(jnp.float32)
    spec_real, spec_imag = forward(value_fwd, mirrored[1], table_set, radix_sizes)
    spec_real, spec_imag = complex_times(spec_real, spec_imag, own_spec[0][0], own_spec[0][1])
    along_fwd, along_rev = inverse(spec_real, spec_imag, table_set, radix_sizes)
    spec_real, spec_imag = forward(
        gate_fwd * along_fwd, mirrored[0] * along_rev, table_set, radix_sizes
    )
    spec_real, spec_imag = complex_times(spec_real, spec_imag, own_spec[1][0], own_spec[1][1])
    sum_fwd, sum_rev = inverse(spec_real, spec_imag, table_set, radix_sizes)
    sum_fwd = received[2].astype(jnp.float32) * sum_fwd
    sum_rev = mirrored[2] * sum_rev
    results = jnp.stack([sum_fwd, sum_rev[:, ::-1]])
    returned = lax.all_to_all(
        results.astype(jnp.bfloat16), "ctx", split_axis=2, concat_axis=1, tiled=True
    ).astype(results.dtype)
    flipped = returned[1, ::-1, :]
    for bit_index in range(tp_count.bit_length() - 1):
        flipped = partner(flipped.astype(jnp.bfloat16), "tp", bit_index).astype(flipped.dtype)
    total_rows = returned[0] + flipped
    total_rows = total_rows.T
    mixed_rows = total_rows.astype(jnp.bfloat16)
    whole_rows = lax.all_gather(mixed_rows, "tp", axis=1, tiled=True)
    projected = lax.dot_general(
        whole_rows,
        lax.all_gather(w_out, "ctx", axis=0, tiled=True),
        (((1,), (1,)), ((), ())),
        preferred_element_type=jnp.float32,
    )
    return projected.astype(jnp.bfloat16)


def block_tables(block):
    angle = np.pi * np.outer(np.arange(block), np.arange(block) + 0.5) / block
    to_freq = np.concatenate([np.cos(angle), -np.sin(angle)], axis=1)
    result = []
    for table in (to_freq, to_freq.T / block):
        high = table.astype(ml_dtypes.bfloat16)
        low = (table - high.astype(np.float64)).astype(ml_dtypes.bfloat16)
        result += [jnp.asarray(high), jnp.asarray(low)]
    return result


def halves(value):
    high = value.astype(jnp.bfloat16)
    return high, (value - high.astype(jnp.float32)).astype(jnp.bfloat16)


def mul(left, right):
    return jnp.dot(left, right, preferred_element_type=jnp.float32)


def mul3(left_high, left_low, right_high, right_low):
    return mul(left_high, right_high) + (mul(left_low, right_high) + mul(left_high, right_low))


def pack_kernel(gate_hbm, value_hbm, post_hbm, out_ref, held_ref, sems):
    ctx_count, _, group, tok = out_ref.shape
    width = gate_hbm.shape[1]
    copies = [
        pltpu.make_async_copy(source, held_ref.at[position], sems.at[position])
        for position, source in enumerate((gate_hbm, value_hbm, post_hbm))
    ]
    for copy in copies:
        copy.start()
    for position, copy in enumerate(copies):
        copy.wait()
        for first in range(0, width, tok):
            turned = held_ref[position, :, first : first + tok].T
            for part in range(tok // group):
                out_ref[first // group + part, position] = turned[part * group : (part + 1) * group]


def filter_kernel(poles, par_ref, fh_ref, fl_ref, out_ref, time_ref):
    blocks, group, twice = out_ref.shape[2:]
    block = twice // 2
    lanes = 128
    turned = par_ref[...].T
    ramp = lax.broadcasted_iota(jnp.int32, (8, lanes), 1).astype(jnp.float32)
    for index in range(2):
        for side in range(2):
            for row in range(0, group, 8):
                rows = slice(side * group + row, side * group + row + 8)
                rate = turned[rows, index * poles : (index + 1) * poles]
                scale = turned[rows, (2 + index) * poles : (3 + index) * poles] * jnp.sqrt(rate * (2.0 / poles))
                jump = jnp.exp(rate * -lanes)
                sums = [None] * (blocks * block // lanes)
                for pole in range(poles):
                    term = scale[:, pole : pole + 1] * jnp.exp(-rate[:, pole : pole + 1] * ramp)
                    step = jnp.broadcast_to(jump[:, pole : pole + 1], (8, lanes))
                    for place in range(len(sums)):
                        sums[place] = term if pole == 0 else sums[place] + term
                        if place + 1 < len(sums):
                            term = term * step
                for place, total in enumerate(sums):
                    lag, lane = divmod(place * lanes, block)
                    first = ((index * 2 + side) * blocks + lag) * group + row
                    time_ref[first : first + 8, lane : lane + lanes] = total
    sign = (1 - 2 * (lax.broadcasted_iota(jnp.int32, (group, block), 1) % 2)).astype(jnp.float32)
    for index in range(2):
        for side in range(2):
            first = (index * 2 + side) * blocks * group
            high, low = halves(time_ref[first : first + blocks * group])
            spec = mul3(high, low, fh_ref[...], fl_ref[...])
            for lag in range(blocks):
                real = spec[lag * group : (lag + 1) * group, :block]
                imag = spec[lag * group : (lag + 1) * group, block:]
                if lag > 0:
                    real = real - sign * spec[(lag - 1) * group : lag * group, block:]
                    imag = imag + sign * spec[(lag - 1) * group : lag * group, :block]
                out_ref[index, side, lag, :, :block] = real
                out_ref[index, side, lag, :, block:] = imag


def conv_kernel(x_ref, h_ref, fh_ref, fl_ref, gh_ref, gl_ref, out_ref, spec_ref, high_ref, low_ref):
    blocks, group, twice = h_ref.shape[2:]
    block = twice // 2
    rows_all = blocks * group
    tall, wide = 16, 128
    pieces = x_ref.shape[0] // blocks

    def rows_of(position):
        return jnp.concatenate(
            [
                jnp.concatenate([x_ref[m * pieces + s, position] for s in range(pieces)], axis=1)
                for m in range(blocks)
            ],
            axis=0,
        )

    def times(index, side, source, row, lane):
        data = []
        for m in range(blocks):
            rows = slice(source + m * group + row, source + m * group + row + tall)
            data.append((spec_ref[rows, lane : lane + wide], spec_ref[rows, block + lane : block + lane + wide]))
        sums = [None] * blocks
        for lag in range(blocks):
            f_re = h_ref[index, side, lag, row : row + tall, lane : lane + wide]
            f_im = h_ref[index, side, lag, row : row + tall, block + lane : block + lane + wide]
            for m in range(blocks - lag):
                target, (d_re, d_im) = (m + lag, data[m]) if side == 0 else (m, data[m + lag])
                if side == 0:
                    real, imag = f_re * d_re - f_im * d_im, f_re * d_im + f_im * d_re
                else:
                    real, imag = f_re * d_re + f_im * d_im, f_re * d_im - f_im * d_re
                if sums[target] is not None:
                    real, imag = sums[target][0] + real, sums[target][1] + imag
                sums[target] = (real, imag)
        return sums

    def keep(target, row, lane, sums):
        for m in range(blocks):
            rows = slice(target + m * group + row, target + m * group + row + tall)
            for part in range(2):
                cols = slice(part * block + lane, part * block + lane + wide)
                high_ref[rows, cols], low_ref[rows, cols] = halves(sums[m][part])

    chunks = [(row, lane) for row in range(0, group, tall) for lane in range(0, block, wide)]

    value = rows_of(1)
    spec_ref[:rows_all] = mul(value, fh_ref[...]) + mul(value, fl_ref[...])
    for row, lane in chunks:
        for side in range(2):
            keep(side * rows_all, row, lane, times(0, side, 0, row, lane))
    along = mul3(high_ref[...], low_ref[...], gh_ref[...], gl_ref[...])
    gate = rows_of(0).astype(jnp.float32)
    high, low = halves(jnp.concatenate([gate, gate], axis=0) * along)
    spec_ref[...] = mul3(high, low, fh_ref[...], fl_ref[...])
    for row, lane in chunks:
        ahead, back = times(1, 0, 0, row, lane), times(1, 1, rows_all, row, lane)
        keep(0, row, lane, [(a[0] + b[0], a[1] + b[1]) for a, b in zip(ahead, back)])
    summed = mul3(high_ref[:rows_all], low_ref[:rows_all], gh_ref[...], gl_ref[...])
    mixed = (rows_of(2).astype(jnp.float32) * summed).astype(jnp.bfloat16)
    tok = block // pieces
    for m in range(blocks):
        for s in range(pieces):
            out_ref[m * pieces + s] = mixed[m * group : (m + 1) * group, s * tok : (s + 1) * tok]


def project_kernel(w_hbm, *refs):
    parts, (out_ref, held_ref, sems) = refs[:-3], refs[-3:]
    width = parts[0].shape[0]
    me = lax.axis_index("tp")
    copies = []
    for place in range(len(parts)):
        columns = pl.ds(pl.multiple_of((me ^ place) * width, width), width)
        copies.append(pltpu.make_async_copy(w_hbm.at[:, columns], held_ref.at[place], sems.at[place]))
        copies[-1].start()
    total = None
    for place, copy in enumerate(copies):
        copy.wait()
        term = mul(held_ref[place], parts[place][...])
        total = term if total is None else total + term
    out_ref[...] = total.T.astype(jnp.bfloat16)


def whole_call(kernel, out_shape, scratch, flops, nbytes, *operands, in_hbm=0):
    return pl.pallas_call(
        kernel,
        out_shape=out_shape,
        in_specs=[
            pl.BlockSpec(memory_space=pltpu.HBM if place < in_hbm else pltpu.VMEM) for place in range(len(operands))
        ],
        out_specs=pl.BlockSpec(memory_space=pltpu.VMEM),
        scratch_shapes=scratch,
        cost_estimate=pl.CostEstimate(flops=flops, bytes_accessed=nbytes, transcendentals=0),
        compiler_params=pltpu.CompilerParams(vmem_limit_bytes=None if in_hbm else 32 * 2**20),
    )(*operands)


def blocked(x_gate, x_post, values, decay, residue, w_out):
    tok, width = x_gate.shape
    ctx_count = lax.axis_size("ctx")
    tp_count = lax.axis_size("tp")
    group = width // ctx_count
    poles = decay.shape[2]
    block = 2 * tok
    blocks = tok * ctx_count // block
    position = lax.axis_index("ctx")
    tables = block_tables(block)
    gathered_w = lax.all_gather(w_out, "ctx", axis=0, tiled=True)

    params = jnp.swapaxes(jnp.concatenate([decay, residue], axis=0), 1, 2).reshape(4 * poles, width)
    own = lax.dynamic_slice_in_dim(params, position * group, group, 1)
    mirrored = lax.dynamic_slice_in_dim(params, (ctx_count - 1 - position) * group, group, 1)[:, ::-1]
    paired = lax.ppermute(mirrored, "tp", [(z, tp_count - 1 - z) for z in range(tp_count)])
    packed = whole_call(
        pack_kernel,
        jax.ShapeDtypeStruct((ctx_count, 3, group, tok), jnp.bfloat16),
        [pltpu.VMEM((3, tok, width), jnp.bfloat16), pltpu.SemaphoreType.DMA((3,))],
        0,
        6 * tok * width * 2,
        x_gate,
        values,
        x_post,
        in_hbm=3,
    )
    received = lax.all_to_all(packed, "ctx", split_axis=0, concat_axis=0, tiled=True)
    both = jnp.concatenate([own, paired], axis=1)
    spectra = whole_call(
        functools.partial(filter_kernel, poles),
        jax.ShapeDtypeStruct((2, 2, blocks, group, 2 * block), jnp.float32),
        [pltpu.VMEM((4 * blocks * group, block), jnp.float32)],
        2 * 4 * blocks * group * block * 2 * block * 3,
        4 * blocks * group * 2 * block * 4,
        both,
        tables[0],
        tables[1],
    )
    mixed = whole_call(
        conv_kernel,
        jax.ShapeDtypeStruct((ctx_count, group, tok), jnp.bfloat16),
        [
            pltpu.VMEM((2 * blocks * group, 2 * block), jnp.float32),
            pltpu.VMEM((2 * blocks * group, 2 * block), jnp.bfloat16),
            pltpu.VMEM((2 * blocks * group, 2 * block), jnp.bfloat16),
        ],
        2 * 6 * blocks * group * block * 2 * block * 3,
        4 * blocks * group * 2 * block * 4,
        received,
        spectra,
        *tables,
    )
    mine = lax.all_to_all(mixed, "ctx", split_axis=0, concat_axis=0, tiled=True)
    mine = mine.reshape(width, tok)
    far = partner(mine, "tp", 1)
    near = partner(mine, "tp", 0)
    last = partner(far, "tp", 0)
    features, channels = gathered_w.shape
    return whole_call(
        project_kernel,
        jax.ShapeDtypeStruct((tok, features), jnp.bfloat16),
        [pltpu.VMEM((tp_count, features, width), jnp.bfloat16), pltpu.SemaphoreType.DMA((tp_count,))],
        2 * tok * features * channels,
        2 * features * channels,
        gathered_w,
        mine,
        near,
        far,
        last,
        in_hbm=1,
    )


def local(x_gate, x_post, values, decay, residue, w_out):
    tok, width = x_gate.shape
    ctx_count = lax.axis_size("ctx")
    if tok == 128 and width == 64 * ctx_count and ctx_count <= 16 and lax.axis_size("tp") == 4:
        return blocked(x_gate, x_post, values, decay, residue, w_out)
    return general(x_gate, x_post, values, decay, residue, w_out)


def solution(mesh):
    in_specs = (
        P("ctx", "tp"),
        P("ctx", "tp"),
        P("ctx", "tp"),
        P(None, "tp", None),
        P(None, "tp", None),
        P(("tp", "ctx"), None),
    )
    out_specs = P("ctx", "tp")
    return jax.shard_map(local, mesh=mesh, in_specs=in_specs, out_specs=out_specs, check_vma=False)
```

```python
import functools
import math

import jax
import jax.numpy as jnp
import ml_dtypes
import numpy as np
from jax import lax
from jax.experimental import pallas as pl
from jax.experimental.pallas import tpu as pltpu
from jax.sharding import PartitionSpec as P

HIGHEST = lax.Precision.HIGHEST


def partner(value, axis, bit):
    mask = 2**bit
    pairs = [(source, source ^ mask) for source in range(lax.axis_size(axis))]
    return lax.ppermute(value, axis, pairs)


def radices(length_all):
    last_radix = min(128, length_all // 4)
    first_radix = min(32, length_all // last_radix)
    return (first_radix, length_all // (first_radix * last_radix), last_radix)


def rotation(row_count, col_count, modulus):
    product = (
        lax.broadcasted_iota(jnp.int32, (row_count, col_count), 0)
        * lax.broadcasted_iota(jnp.int32, (row_count, col_count), 1)
        % modulus
    )
    angle = product.astype(jnp.float32) * (2.0 * math.pi / modulus)
    return (jnp.cos(angle), -jnp.sin(angle))


def tables(radix_sizes):
    first_radix, mid_radix, last_radix = radix_sizes
    length_all = first_radix * mid_radix * last_radix
    outer_real, outer_imag = rotation(first_radix, first_radix, first_radix)
    mid_real, mid_imag = rotation(mid_radix, mid_radix, mid_radix)
    last_real, last_imag = rotation(last_radix, last_radix, last_radix)
    twist_real, twist_imag = rotation(first_radix, mid_radix * last_radix, length_all)
    twist_real = twist_real.reshape(first_radix, mid_radix, last_radix)
    twist_imag = twist_imag.reshape(first_radix, mid_radix, last_radix)
    inner_real, inner_imag = rotation(mid_radix, last_radix, mid_radix * last_radix)
    return (
        outer_real,
        outer_imag,
        mid_real,
        mid_imag,
        last_real,
        last_imag,
        twist_real,
        twist_imag,
        inner_real,
        inner_imag,
    )


def apply_matrix(pattern, real_part, imag_part, matrix_real, matrix_imag):
    out_real = jnp.einsum(pattern, real_part, matrix_real, precision=HIGHEST) - jnp.einsum(
        pattern, imag_part, matrix_imag, precision=HIGHEST
    )
    out_imag = jnp.einsum(pattern, real_part, matrix_imag, precision=HIGHEST) + jnp.einsum(
        pattern, imag_part, matrix_real, precision=HIGHEST
    )
    return (out_real, out_imag)


def complex_times(left_real, left_imag, right_real, right_imag):
    return (
        left_real * right_real - left_imag * right_imag,
        left_real * right_imag + left_imag * right_real,
    )


def forward(real_part, imag_part, table_set, radix_sizes):
    first_radix, mid_radix, last_radix = radix_sizes
    half_first = first_radix // 2
    batch_rows = real_part.shape[0]
    (
        outer_real,
        outer_imag,
        mid_real,
        mid_imag,
        last_real,
        last_imag,
        twist_real,
        twist_imag,
        inner_real,
        inner_imag,
    ) = table_set
    real_part = real_part.reshape(batch_rows, half_first, mid_radix, last_radix)
    imag_part = imag_part.reshape(batch_rows, half_first, mid_radix, last_radix)
    real_part, imag_part = apply_matrix(
        "banm,ak->bknm", real_part, imag_part, outer_real[:half_first], outer_imag[:half_first]
    )
    real_part, imag_part = complex_times(real_part, imag_part, twist_real, twist_imag)
    real_part, imag_part = apply_matrix("bknm,nj->bkjm", real_part, imag_part, mid_real, mid_imag)
    real_part, imag_part = complex_times(real_part, imag_part, inner_real, inner_imag)
    return apply_matrix("bkjm,mq->bkjq", real_part, imag_part, last_real, last_imag)


def inverse(real_part, imag_part, table_set, radix_sizes):
    first_radix, mid_radix, last_radix = radix_sizes
    half_first = first_radix // 2
    batch_rows = real_part.shape[0]
    (
        outer_real,
        outer_imag,
        mid_real,
        mid_imag,
        last_real,
        last_imag,
        twist_real,
        twist_imag,
        inner_real,
        inner_imag,
    ) = table_set
    real_part, imag_part = apply_matrix(
        "bkjq,mq->bkjm", real_part, imag_part, last_real / last_radix, -last_imag / last_radix
    )
    real_part, imag_part = complex_times(real_part, imag_part, inner_real, -inner_imag)
    real_part, imag_part = apply_matrix(
        "bkjm,nj->bknm", real_part, imag_part, mid_real / mid_radix, -mid_imag / mid_radix
    )
    real_part, imag_part = complex_times(real_part, imag_part, twist_real, -twist_imag)
    matrix_real = outer_real[:half_first] / first_radix
    matrix_imag = -outer_imag[:half_first] / first_radix
    out_real, out_imag = apply_matrix(
        "bknm,ak->banm", real_part, imag_part, matrix_real, matrix_imag
    )
    return (out_real.reshape(batch_rows, -1), out_imag.reshape(batch_rows, -1))


def spectrum(decay_rows, residue_rows, radix_sizes, seq_length):
    first_radix, mid_radix, last_radix = radix_sizes
    length_all = first_radix * mid_radix * last_radix
    poles = decay_rows.shape[1]
    shape_all = (first_radix, mid_radix, last_radix)
    frequency = (
        lax.broadcasted_iota(jnp.int32, shape_all, 0)
        + first_radix * lax.broadcasted_iota(jnp.int32, shape_all, 1)
        + first_radix * mid_radix * lax.broadcasted_iota(jnp.int32, shape_all, 2)
    )
    half_angle = frequency.astype(jnp.float32) * (math.pi / length_all)
    sin_half = jnp.sin(half_angle)
    sin_full = jnp.sin(2.0 * half_angle)
    parity_sign = (1 - 2 * (frequency % 2)).astype(jnp.float32)

    def add_pole(pole_index, running):
        run_real, run_imag = running
        rate_col = lax.dynamic_slice_in_dim(decay_rows, pole_index, 1, 1).reshape(-1, 1, 1, 1)
        weight = lax.dynamic_slice_in_dim(residue_rows, pole_index, 1, 1).reshape(
            -1, 1, 1, 1
        ) * jnp.sqrt(2.0 * rate_col / poles)
        retained = jnp.exp(-rate_col)
        den_real = -jnp.expm1(-rate_col) + 2.0 * retained * sin_half * sin_half
        den_imag = retained * sin_full
        pole_scale = (
            weight
            * (1.0 - jnp.exp(-rate_col * seq_length) * parity_sign)
            / (den_real * den_real + den_imag * den_imag)
        )
        return (run_real + pole_scale * den_real, run_imag - pole_scale * den_imag)

    zeros_all = jnp.zeros((decay_rows.shape[0],) + shape_all, jnp.float32)
    return lax.fori_loop(0, poles, add_pole, (zeros_all, zeros_all))


def general(x_gate, x_post, values, decay, residue, w_out):
    tok_rows, block_width = x_gate.shape
    ctx_count = lax.axis_size("ctx")
    tp_count = lax.axis_size("tp")
    chan_group = block_width // ctx_count
    seq_length = tok_rows * ctx_count
    radix_sizes = radices(2 * seq_length)
    table_set = tables(radix_sizes)
    first_row = lax.axis_index("ctx") * chan_group
    own_rate = lax.dynamic_slice_in_dim(decay, first_row, chan_group, 1)
    own_residue = lax.dynamic_slice_in_dim(residue, first_row, chan_group, 1)
    own_spec = [
        spectrum(own_rate[filter_index], own_residue[filter_index], radix_sizes, seq_length)
        for filter_index in range(2)
    ]
    forward_rows = [x_gate, values] + [x_post]
    row_count = len(forward_rows)
    base_rows = jnp.stack(forward_rows)
    copied = base_rows
    for bit_index in range(tp_count.bit_length() - 1):
        copied = partner(copied, "tp", bit_index)
    sent_rows = jnp.concatenate([base_rows, copied[:, :, ::-1]], axis=0)
    received = lax.all_to_all(
        jnp.swapaxes(sent_rows, 1, 2), "ctx", split_axis=1, concat_axis=2, tiled=True
    )
    gate_fwd = received[0].astype(jnp.float32)
    value_fwd = received[1].astype(jnp.float32)
    mirrored = received[row_count:, :, ::-1].astype(jnp.float32)
    spec_real, spec_imag = forward(value_fwd, mirrored[1], table_set, radix_sizes)
    spec_real, spec_imag = complex_times(spec_real, spec_imag, own_spec[0][0], own_spec[0][1])
    along_fwd, along_rev = inverse(spec_real, spec_imag, table_set, radix_sizes)
    spec_real, spec_imag = forward(
        gate_fwd * along_fwd, mirrored[0] * along_rev, table_set, radix_sizes
    )
    spec_real, spec_imag = complex_times(spec_real, spec_imag, own_spec[1][0], own_spec[1][1])
    sum_fwd, sum_rev = inverse(spec_real, spec_imag, table_set, radix_sizes)
    sum_fwd = received[2].astype(jnp.float32) * sum_fwd
    sum_rev = mirrored[2] * sum_rev
    results = jnp.stack([sum_fwd, sum_rev[:, ::-1]])
    returned = lax.all_to_all(
        results.astype(jnp.bfloat16), "ctx", split_axis=2, concat_axis=1, tiled=True
    ).astype(results.dtype)
    flipped = returned[1, ::-1, :]
    for bit_index in range(tp_count.bit_length() - 1):
        flipped = partner(flipped.astype(jnp.bfloat16), "tp", bit_index).astype(flipped.dtype)
    total_rows = returned[0] + flipped
    total_rows = total_rows.T
    mixed_rows = total_rows.astype(jnp.bfloat16)
    whole_rows = lax.all_gather(mixed_rows, "tp", axis=1, tiled=True)
    projected = lax.dot_general(
        whole_rows,
        lax.all_gather(w_out, "ctx", axis=0, tiled=True),
        (((1,), (1,)), ((), ())),
        preferred_element_type=jnp.float32,
    )
    return projected.astype(jnp.bfloat16)


def block_tables(block):
    angle = np.pi * np.outer(np.arange(block), np.arange(block) + 0.5) / block
    to_freq = np.concatenate([np.cos(angle), -np.sin(angle)], axis=1)
    result = []
    for table in (to_freq, to_freq.T / block):
        high = table.astype(ml_dtypes.bfloat16)
        low = (table - high.astype(np.float64)).astype(ml_dtypes.bfloat16)
        result += [jnp.asarray(high), jnp.asarray(low)]
    return result


def halves(value):
    high = value.astype(jnp.bfloat16)
    return high, (value - high.astype(jnp.float32)).astype(jnp.bfloat16)


def mul(left, right):
    return jnp.dot(left, right, preferred_element_type=jnp.float32)


def mul3(left_high, left_low, right_high, right_low):
    return mul(left_high, right_high) + (mul(left_low, right_high) + mul(left_high, right_low))


def pack_kernel(gate_hbm, value_hbm, post_hbm, decay_hbm, residue_hbm, out_ref, own_ref, sent_ref, held_ref, par_ref, sems):
    ctx_count, _, group, tok = out_ref.shape
    width = gate_hbm.shape[1]
    half = decay_hbm.shape[0]
    position = lax.axis_index("ctx")
    pairs = [(decay_hbm, par_ref.at[:half]), (residue_hbm, par_ref.at[half:])]
    pairs += [(source, held_ref.at[place]) for place, source in enumerate((gate_hbm, value_hbm, post_hbm))]
    copies = [pltpu.make_async_copy(*pair, sems.at[place]) for place, pair in enumerate(pairs)]
    for copy in copies:
        copy.start()
    copies[0].wait()
    copies[1].wait()
    odd = position % 2 == 1
    lane = lax.broadcasted_iota(jnp.int32, own_ref.shape, 1)

    def tile_of(index):
        return par_ref[:, pl.ds(pl.multiple_of(index // 2 * tok, tok), tok)]

    def to_front(value):
        return jnp.where(odd, pltpu.roll(value, group, 1), value)

    own_ref[...] = to_front(tile_of(position))
    turned = tile_of(ctx_count - 1 - position)
    shift = 1
    while shift < tok:
        turned = jnp.where(lane & shift == 0, pltpu.roll(turned, tok - shift, 1), pltpu.roll(turned, shift, 1))
        shift *= 2
    sent_ref[...] = to_front(turned)
    for place in range(3):
        copies[2 + place].wait()
        for first in range(0, width, tok):
            turned = held_ref[place, :, first : first + tok].T
            for part in range(tok // group):
                out_ref[first // group + part, place] = turned[part * group : (part + 1) * group]


def filter_kernel(poles, par_ref, fh_ref, fl_ref, out_ref, time_ref):
    blocks, group, twice = out_ref.shape[1:]
    block = twice // 2
    lanes = 128
    turned = par_ref[...].T
    ramp = lax.broadcasted_iota(jnp.int32, (8, lanes), 1).astype(jnp.float32)
    for index in range(2):
        for row in range(0, group, 8):
            rows = slice(row, row + 8)
            rate = turned[rows, index * poles : (index + 1) * poles]
            scale = turned[rows, (2 + index) * poles : (3 + index) * poles] * jnp.sqrt(rate * (2.0 / poles))
            jump = jnp.exp(rate * -lanes)
            sums = [None] * (blocks * block // lanes)
            for pole in range(poles):
                term = scale[:, pole : pole + 1] * jnp.exp(-rate[:, pole : pole + 1] * ramp)
                step = jnp.broadcast_to(jump[:, pole : pole + 1], (8, lanes))
                for place in range(len(sums)):
                    sums[place] = term if pole == 0 else sums[place] + term
                    if place + 1 < len(sums):
                        term = term * step
            for place, total in enumerate(sums):
                lag, lane = divmod(place * lanes, block)
                first = (index * blocks + lag) * group + row
                time_ref[first : first + 8, lane : lane + lanes] = total
    sign = (1 - 2 * (lax.broadcasted_iota(jnp.int32, (group, block), 1) % 2)).astype(jnp.float32)
    for index in range(2):
        first = index * blocks * group
        high, low = halves(time_ref[first : first + blocks * group])
        spec = mul3(high, low, fh_ref[...], fl_ref[...])
        for lag in range(blocks):
            real = spec[lag * group : (lag + 1) * group, :block]
            imag = spec[lag * group : (lag + 1) * group, block:]
            if lag > 0:
                real = real - sign * spec[(lag - 1) * group : lag * group, block:]
                imag = imag + sign * spec[(lag - 1) * group : lag * group, :block]
            out_ref[index, lag, :, :block] = real
            out_ref[index, lag, :, block:] = imag


def conv_kernel(x_ref, own_ref, paired_ref, fh_ref, fl_ref, gh_ref, gl_ref, *refs):
    out_refs, (spec_ref, high_ref, low_ref, mixed_ref) = refs[:-4], refs[-4:]
    blocks, group, twice = own_ref.shape[1:]
    block = twice // 2
    rows_all = blocks * group
    tall, wide = 16, 128
    pieces = x_ref.shape[0] // blocks

    def rows_of(position):
        return jnp.concatenate(
            [
                jnp.concatenate([x_ref[m * pieces + s, position] for s in range(pieces)], axis=1)
                for m in range(blocks)
            ],
            axis=0,
        )

    def times(index, side, source, row, lane):
        data = []
        for m in range(blocks):
            rows = slice(source + m * group + row, source + m * group + row + tall)
            data.append((spec_ref[rows, lane : lane + wide], spec_ref[rows, block + lane : block + lane + wide]))
        sums = [None] * blocks
        for lag in range(blocks):
            h_ref = (own_ref, paired_ref)[side]
            f_re = h_ref[index, lag, row : row + tall, lane : lane + wide]
            f_im = h_ref[index, lag, row : row + tall, block + lane : block + lane + wide]
            for m in range(blocks - lag):
                target, (d_re, d_im) = (m + lag, data[m]) if side == 0 else (m, data[m + lag])
                if side == 0:
                    real, imag = f_re * d_re - f_im * d_im, f_re * d_im + f_im * d_re
                else:
                    real, imag = f_re * d_re + f_im * d_im, f_re * d_im - f_im * d_re
                if sums[target] is not None:
                    real, imag = sums[target][0] + real, sums[target][1] + imag
                sums[target] = (real, imag)
        return sums

    def keep(target, row, lane, sums):
        for m in range(blocks):
            rows = slice(target + m * group + row, target + m * group + row + tall)
            for part in range(2):
                cols = slice(part * block + lane, part * block + lane + wide)
                high_ref[rows, cols], low_ref[rows, cols] = halves(sums[m][part])

    chunks = [(row, lane) for row in range(0, group, tall) for lane in range(0, block, wide)]

    value = rows_of(1)
    spec_ref[:rows_all] = mul(value, fh_ref[...]) + mul(value, fl_ref[...])
    for row, lane in chunks:
        for side in range(2):
            keep(side * rows_all, row, lane, times(0, side, 0, row, lane))
    along = mul3(high_ref[...], low_ref[...], gh_ref[...], gl_ref[...])
    gate = rows_of(0).astype(jnp.float32)
    high, low = halves(jnp.concatenate([gate, gate], axis=0) * along)
    spec_ref[...] = mul3(high, low, fh_ref[...], fl_ref[...])
    for row, lane in chunks:
        ahead, back = times(1, 0, 0, row, lane), times(1, 1, rows_all, row, lane)
        keep(0, row, lane, [(a[0] + b[0], a[1] + b[1]) for a, b in zip(ahead, back)])
    summed = mul3(high_ref[:rows_all], low_ref[:rows_all], gh_ref[...], gl_ref[...])
    mixed = (rows_of(2).astype(jnp.float32) * summed).astype(jnp.bfloat16)
    tok = block // pieces
    for m in range(blocks):
        for s in range(pieces):
            mixed_ref[m * pieces + s] = mixed[m * group : (m + 1) * group, s * tok : (s + 1) * tok]
    position = lax.axis_index("ctx")
    for mask, out_ref in enumerate(out_refs):
        out_ref[...] = mixed_ref[position ^ mask]


def order_kernel(*refs):
    pieces, out_ref = refs[:-1], refs[-1]
    position = lax.axis_index("ctx")
    for mask, piece in enumerate(pieces):
        out_ref[position ^ mask] = piece[...]


def project_kernel(ctx_count, *refs):
    w_refs, parts, (out_ref, held_ref) = refs[:ctx_count], refs[ctx_count:-2], refs[-2:]
    rows = w_refs[0].shape[0]
    width = parts[0].shape[0]
    me = lax.axis_index("tp")
    position = lax.axis_index("ctx")
    total = None
    for place, part in enumerate(parts):
        columns = pl.ds(pl.multiple_of((me ^ place) * width, width), width)
        term = mul(jnp.concatenate([w_ref[:, columns] for w_ref in w_refs], axis=0), part[...])
        total = term if total is None else total + term
    for mask in range(ctx_count):
        first = pl.multiple_of((position ^ mask) * rows, rows)
        held_ref[pl.ds(first, rows)] = total[mask * rows : (mask + 1) * rows]
    out_ref[...] = held_ref[...].T.astype(jnp.bfloat16)


def whole_call(kernel, out_shape, scratch, flops, nbytes, *operands, in_hbm=0):
    return pl.pallas_call(
        kernel,
        out_shape=out_shape,
        in_specs=[
            pl.BlockSpec(memory_space=pltpu.HBM if place < in_hbm else pltpu.VMEM) for place in range(len(operands))
        ],
        out_specs=jax.tree.map(lambda _: pl.BlockSpec(memory_space=pltpu.VMEM), out_shape),
        scratch_shapes=scratch,
        cost_estimate=pl.CostEstimate(flops=flops, bytes_accessed=nbytes, transcendentals=0),
        compiler_params=pltpu.CompilerParams(vmem_limit_bytes=None if in_hbm else 32 * 2**20),
    )(*operands)


def blocked(x_gate, x_post, values, decay, residue, w_out):
    tok, width = x_gate.shape
    ctx_count = lax.axis_size("ctx")
    tp_count = lax.axis_size("tp")
    group = width // ctx_count
    poles = decay.shape[2]
    block = 2 * tok
    blocks = tok * ctx_count // block
    rows, channels = w_out.shape
    tables = block_tables(block)
    half = 2 * poles

    packed, own, mirrored = whole_call(
        pack_kernel,
        (
            jax.ShapeDtypeStruct((ctx_count, 3, group, tok), jnp.bfloat16),
            jax.ShapeDtypeStruct((2 * half, tok), jnp.float32),
            jax.ShapeDtypeStruct((2 * half, tok), jnp.float32),
        ),
        [
            pltpu.VMEM((3, tok, width), jnp.bfloat16),
            pltpu.VMEM((2 * half, width), jnp.float32),
            pltpu.SemaphoreType.DMA((5,)),
        ],
        0,
        6 * tok * width * 2,
        x_gate,
        values,
        x_post,
        jnp.swapaxes(decay, 1, 2).reshape(half, width),
        jnp.swapaxes(residue, 1, 2).reshape(half, width),
        in_hbm=5,
    )
    paired = lax.ppermute(mirrored, "tp", [(z, tp_count - 1 - z) for z in range(tp_count)])
    received = lax.all_to_all(packed, "ctx", split_axis=0, concat_axis=0, tiled=True)

    w_blocks = {0: w_out}
    w_blocks[2] = partner(w_out, "ctx", 1)
    w_blocks[4] = partner(w_out, "ctx", 2)
    w_blocks[6] = partner(w_blocks[2], "ctx", 2)
    for mask in range(0, ctx_count, 2):
        w_blocks[mask + 1] = partner(w_blocks[mask], "ctx", 0)

    def spectra(params):
        return whole_call(
            functools.partial(filter_kernel, poles),
            jax.ShapeDtypeStruct((2, blocks, group, 2 * block), jnp.float32),
            [pltpu.VMEM((2 * blocks * group, block), jnp.float32)],
            2 * 2 * blocks * group * block * 2 * block * 3,
            2 * blocks * group * 2 * block * 4,
            params,
            tables[0],
            tables[1],
        )

    pieces = whole_call(
        conv_kernel,
        (jax.ShapeDtypeStruct((group, tok), jnp.bfloat16),) * ctx_count,
        [
            pltpu.VMEM((2 * blocks * group, 2 * block), jnp.float32),
            pltpu.VMEM((2 * blocks * group, 2 * block), jnp.bfloat16),
            pltpu.VMEM((2 * blocks * group, 2 * block), jnp.bfloat16),
            pltpu.VMEM((ctx_count, group, tok), jnp.bfloat16),
        ],
        2 * 6 * blocks * group * block * 2 * block * 3,
        4 * blocks * group * 2 * block * 4,
        received,
        spectra(own),
        spectra(paired),
        *tables,
    )
    arrived = [pieces[0]]
    for mask in range(1, ctx_count):
        arrived.append(lax.ppermute(pieces[mask], "ctx", [(i, i ^ mask) for i in range(ctx_count)]))
    mine = whole_call(
        order_kernel,
        jax.ShapeDtypeStruct((ctx_count, group, tok), jnp.bfloat16),
        [],
        0,
        2 * ctx_count * group * tok * 2,
        *arrived,
    ).reshape(width, tok)
    far = partner(mine, "tp", 1)
    near = partner(mine, "tp", 0)
    last = partner(far, "tp", 0)
    return whole_call(
        functools.partial(project_kernel, ctx_count),
        jax.ShapeDtypeStruct((tok, rows * ctx_count), jnp.bfloat16),
        [pltpu.VMEM((rows * ctx_count, tok), jnp.float32)],
        2 * tok * rows * ctx_count * channels,
        2 * rows * ctx_count * channels,
        *[w_blocks[mask] for mask in range(ctx_count)],
        mine,
        near,
        far,
        last,
    )


def local(x_gate, x_post, values, decay, residue, w_out):
    tok, width = x_gate.shape
    ctx_count = lax.axis_size("ctx")
    if tok == 128 and width == 512 and ctx_count == 8 and lax.axis_size("tp") == 4:
        return blocked(x_gate, x_post, values, decay, residue, w_out)
    return general(x_gate, x_post, values, decay, residue, w_out)


def solution(mesh):
    in_specs = (
        P("ctx", "tp"),
        P("ctx", "tp"),
        P("ctx", "tp"),
        P(None, "tp", None),
        P(None, "tp", None),
        P(("tp", "ctx"), None),
    )
    out_specs = P("ctx", "tp")
    return jax.shard_map(local, mesh=mesh, in_specs=in_specs, out_specs=out_specs, check_vma=False)
```

```python
import functools
import math

import jax
import jax.numpy as jnp
import ml_dtypes
import numpy as np
from jax import lax
from jax.experimental import pallas as pl
from jax.experimental.pallas import tpu as pltpu
from jax.sharding import PartitionSpec as P

HIGHEST = lax.Precision.HIGHEST


def partner(value, axis, bit):
    mask = 2**bit
    pairs = [(source, source ^ mask) for source in range(lax.axis_size(axis))]
    return lax.ppermute(value, axis, pairs)


def radices(length_all):
    last_radix = min(128, length_all // 4)
    first_radix = min(32, length_all // last_radix)
    return (first_radix, length_all // (first_radix * last_radix), last_radix)


def rotation(row_count, col_count, modulus):
    product = (
        lax.broadcasted_iota(jnp.int32, (row_count, col_count), 0)
        * lax.broadcasted_iota(jnp.int32, (row_count, col_count), 1)
        % modulus
    )
    angle = product.astype(jnp.float32) * (2.0 * math.pi / modulus)
    return (jnp.cos(angle), -jnp.sin(angle))


def tables(radix_sizes):
    first_radix, mid_radix, last_radix = radix_sizes
    length_all = first_radix * mid_radix * last_radix
    outer_real, outer_imag = rotation(first_radix, first_radix, first_radix)
    mid_real, mid_imag = rotation(mid_radix, mid_radix, mid_radix)
    last_real, last_imag = rotation(last_radix, last_radix, last_radix)
    twist_real, twist_imag = rotation(first_radix, mid_radix * last_radix, length_all)
    twist_real = twist_real.reshape(first_radix, mid_radix, last_radix)
    twist_imag = twist_imag.reshape(first_radix, mid_radix, last_radix)
    inner_real, inner_imag = rotation(mid_radix, last_radix, mid_radix * last_radix)
    return (
        outer_real,
        outer_imag,
        mid_real,
        mid_imag,
        last_real,
        last_imag,
        twist_real,
        twist_imag,
        inner_real,
        inner_imag,
    )


def apply_matrix(pattern, real_part, imag_part, matrix_real, matrix_imag):
    out_real = jnp.einsum(pattern, real_part, matrix_real, precision=HIGHEST) - jnp.einsum(
        pattern, imag_part, matrix_imag, precision=HIGHEST
    )
    out_imag = jnp.einsum(pattern, real_part, matrix_imag, precision=HIGHEST) + jnp.einsum(
        pattern, imag_part, matrix_real, precision=HIGHEST
    )
    return (out_real, out_imag)


def complex_times(left_real, left_imag, right_real, right_imag):
    return (
        left_real * right_real - left_imag * right_imag,
        left_real * right_imag + left_imag * right_real,
    )


def forward(real_part, imag_part, table_set, radix_sizes):
    first_radix, mid_radix, last_radix = radix_sizes
    half_first = first_radix // 2
    batch_rows = real_part.shape[0]
    (
        outer_real,
        outer_imag,
        mid_real,
        mid_imag,
        last_real,
        last_imag,
        twist_real,
        twist_imag,
        inner_real,
        inner_imag,
    ) = table_set
    real_part = real_part.reshape(batch_rows, half_first, mid_radix, last_radix)
    imag_part = imag_part.reshape(batch_rows, half_first, mid_radix, last_radix)
    real_part, imag_part = apply_matrix(
        "banm,ak->bknm", real_part, imag_part, outer_real[:half_first], outer_imag[:half_first]
    )
    real_part, imag_part = complex_times(real_part, imag_part, twist_real, twist_imag)
    real_part, imag_part = apply_matrix("bknm,nj->bkjm", real_part, imag_part, mid_real, mid_imag)
    real_part, imag_part = complex_times(real_part, imag_part, inner_real, inner_imag)
    return apply_matrix("bkjm,mq->bkjq", real_part, imag_part, last_real, last_imag)


def inverse(real_part, imag_part, table_set, radix_sizes):
    first_radix, mid_radix, last_radix = radix_sizes
    half_first = first_radix // 2
    batch_rows = real_part.shape[0]
    (
        outer_real,
        outer_imag,
        mid_real,
        mid_imag,
        last_real,
        last_imag,
        twist_real,
        twist_imag,
        inner_real,
        inner_imag,
    ) = table_set
    real_part, imag_part = apply_matrix(
        "bkjq,mq->bkjm", real_part, imag_part, last_real / last_radix, -last_imag / last_radix
    )
    real_part, imag_part = complex_times(real_part, imag_part, inner_real, -inner_imag)
    real_part, imag_part = apply_matrix(
        "bkjm,nj->bknm", real_part, imag_part, mid_real / mid_radix, -mid_imag / mid_radix
    )
    real_part, imag_part = complex_times(real_part, imag_part, twist_real, -twist_imag)
    matrix_real = outer_real[:half_first] / first_radix
    matrix_imag = -outer_imag[:half_first] / first_radix
    out_real, out_imag = apply_matrix(
        "bknm,ak->banm", real_part, imag_part, matrix_real, matrix_imag
    )
    return (out_real.reshape(batch_rows, -1), out_imag.reshape(batch_rows, -1))


def spectrum(decay_rows, residue_rows, radix_sizes, seq_length):
    first_radix, mid_radix, last_radix = radix_sizes
    length_all = first_radix * mid_radix * last_radix
    poles = decay_rows.shape[1]
    shape_all = (first_radix, mid_radix, last_radix)
    frequency = (
        lax.broadcasted_iota(jnp.int32, shape_all, 0)
        + first_radix * lax.broadcasted_iota(jnp.int32, shape_all, 1)
        + first_radix * mid_radix * lax.broadcasted_iota(jnp.int32, shape_all, 2)
    )
    half_angle = frequency.astype(jnp.float32) * (math.pi / length_all)
    sin_half = jnp.sin(half_angle)
    sin_full = jnp.sin(2.0 * half_angle)
    parity_sign = (1 - 2 * (frequency % 2)).astype(jnp.float32)

    def add_pole(pole_index, running):
        run_real, run_imag = running
        rate_col = lax.dynamic_slice_in_dim(decay_rows, pole_index, 1, 1).reshape(-1, 1, 1, 1)
        weight = lax.dynamic_slice_in_dim(residue_rows, pole_index, 1, 1).reshape(
            -1, 1, 1, 1
        ) * jnp.sqrt(2.0 * rate_col / poles)
        retained = jnp.exp(-rate_col)
        den_real = -jnp.expm1(-rate_col) + 2.0 * retained * sin_half * sin_half
        den_imag = retained * sin_full
        pole_scale = (
            weight
            * (1.0 - jnp.exp(-rate_col * seq_length) * parity_sign)
            / (den_real * den_real + den_imag * den_imag)
        )
        return (run_real + pole_scale * den_real, run_imag - pole_scale * den_imag)

    zeros_all = jnp.zeros((decay_rows.shape[0],) + shape_all, jnp.float32)
    return lax.fori_loop(0, poles, add_pole, (zeros_all, zeros_all))


def general(x_gate, x_post, values, decay, residue, w_out):
    tok_rows, block_width = x_gate.shape
    ctx_count = lax.axis_size("ctx")
    tp_count = lax.axis_size("tp")
    chan_group = block_width // ctx_count
    seq_length = tok_rows * ctx_count
    radix_sizes = radices(2 * seq_length)
    table_set = tables(radix_sizes)
    first_row = lax.axis_index("ctx") * chan_group
    own_rate = lax.dynamic_slice_in_dim(decay, first_row, chan_group, 1)
    own_residue = lax.dynamic_slice_in_dim(residue, first_row, chan_group, 1)
    own_spec = [
        spectrum(own_rate[filter_index], own_residue[filter_index], radix_sizes, seq_length)
        for filter_index in range(2)
    ]
    forward_rows = [x_gate, values] + [x_post]
    row_count = len(forward_rows)
    base_rows = jnp.stack(forward_rows)
    copied = base_rows
    for bit_index in range(tp_count.bit_length() - 1):
        copied = partner(copied, "tp", bit_index)
    sent_rows = jnp.concatenate([base_rows, copied[:, :, ::-1]], axis=0)
    received = lax.all_to_all(
        jnp.swapaxes(sent_rows, 1, 2), "ctx", split_axis=1, concat_axis=2, tiled=True
    )
    gate_fwd = received[0].astype(jnp.float32)
    value_fwd = received[1].astype(jnp.float32)
    mirrored = received[row_count:, :, ::-1].astype(jnp.float32)
    spec_real, spec_imag = forward(value_fwd, mirrored[1], table_set, radix_sizes)
    spec_real, spec_imag = complex_times(spec_real, spec_imag, own_spec[0][0], own_spec[0][1])
    along_fwd, along_rev = inverse(spec_real, spec_imag, table_set, radix_sizes)
    spec_real, spec_imag = forward(
        gate_fwd * along_fwd, mirrored[0] * along_rev, table_set, radix_sizes
    )
    spec_real, spec_imag = complex_times(spec_real, spec_imag, own_spec[1][0], own_spec[1][1])
    sum_fwd, sum_rev = inverse(spec_real, spec_imag, table_set, radix_sizes)
    sum_fwd = received[2].astype(jnp.float32) * sum_fwd
    sum_rev = mirrored[2] * sum_rev
    results = jnp.stack([sum_fwd, sum_rev[:, ::-1]])
    returned = lax.all_to_all(
        results.astype(jnp.bfloat16), "ctx", split_axis=2, concat_axis=1, tiled=True
    ).astype(results.dtype)
    flipped = returned[1, ::-1, :]
    for bit_index in range(tp_count.bit_length() - 1):
        flipped = partner(flipped.astype(jnp.bfloat16), "tp", bit_index).astype(flipped.dtype)
    total_rows = returned[0] + flipped
    total_rows = total_rows.T
    mixed_rows = total_rows.astype(jnp.bfloat16)
    whole_rows = lax.all_gather(mixed_rows, "tp", axis=1, tiled=True)
    projected = lax.dot_general(
        whole_rows,
        lax.all_gather(w_out, "ctx", axis=0, tiled=True),
        (((1,), (1,)), ((), ())),
        preferred_element_type=jnp.float32,
    )
    return projected.astype(jnp.bfloat16)


def block_table(block):
    angle = np.pi * np.outer(np.arange(block), np.arange(block) + 0.5) / block
    table = np.concatenate([np.cos(angle), -np.sin(angle)], axis=1)
    high = table.astype(ml_dtypes.bfloat16)
    low = (table - high.astype(np.float64)).astype(ml_dtypes.bfloat16)
    return jnp.asarray(np.stack([high, low]))


def halves(value):
    high = value.astype(jnp.bfloat16)
    return high, (value - high.astype(jnp.float32)).astype(jnp.bfloat16)


def mul(left, right):
    return jnp.dot(left, right, preferred_element_type=jnp.float32)


def mul_back(left, right):
    return lax.dot_general(left, right, (((1,), (1,)), ((), ())), preferred_element_type=jnp.float32)


def to_freq(high, low, table_ref):
    return mul(high, table_ref[0]) + (mul(low, table_ref[0]) + mul(high, table_ref[1]))


def to_time(high, low, table_ref):
    return mul_back(high, table_ref[0]) + (mul_back(low, table_ref[0]) + mul_back(high, table_ref[1]))


def pack_kernel(
    gate_hbm, value_hbm, post_hbm, decay_hbm, residue_hbm, table_hbm,
    out_ref, own_ref, sent_ref, table_ref, held_ref, par_ref, sems,
):
    ctx_count, _, group, tok = out_ref.shape
    width = gate_hbm.shape[1]
    half = decay_hbm.shape[0]
    position = lax.axis_index("ctx")
    pairs = [(decay_hbm, par_ref.at[:half]), (residue_hbm, par_ref.at[half:])]
    pairs += [(source, held_ref.at[place]) for place, source in enumerate((gate_hbm, value_hbm, post_hbm))]
    pairs += [(table_hbm, table_ref)]
    copies = [pltpu.make_async_copy(*pair, sems.at[place]) for place, pair in enumerate(pairs)]
    for copy in copies:
        copy.start()
    copies[0].wait()
    copies[1].wait()
    odd = position % 2 == 1
    lane = lax.broadcasted_iota(jnp.int32, own_ref.shape, 1)

    def tile_of(index):
        return par_ref[:, pl.ds(pl.multiple_of(index // 2 * tok, tok), tok)]

    def to_front(value):
        return jnp.where(odd, pltpu.roll(value, group, 1), value)

    own_ref[...] = to_front(tile_of(position))
    turned = tile_of(ctx_count - 1 - position)
    shift = 1
    while shift < tok:
        turned = jnp.where(lane & shift == 0, pltpu.roll(turned, tok - shift, 1), pltpu.roll(turned, shift, 1))
        shift *= 2
    sent_ref[...] = to_front(turned)
    for place in range(3):
        copies[2 + place].wait()
        for first in range(0, width, tok):
            turned = held_ref[place, :, first : first + tok].T
            for part in range(tok // group):
                out_ref[first // group + part, place] = turned[part * group : (part + 1) * group]
    copies[5].wait()


def filter_kernel(poles, par_ref, table_ref, out_ref, time_ref):
    blocks, group, twice = out_ref.shape[1:]
    block = twice // 2
    lanes = 128
    turned = par_ref[...].T
    ramp = lax.broadcasted_iota(jnp.int32, (8, lanes), 1).astype(jnp.float32)
    for index in range(2):
        for row in range(0, group, 8):
            rows = slice(row, row + 8)
            rate = turned[rows, index * poles : (index + 1) * poles]
            scale = turned[rows, (2 + index) * poles : (3 + index) * poles] * (jnp.sqrt(rate * (2.0 / poles)) / block)
            jump = jnp.exp(rate * -lanes)
            sums = [None] * (blocks * block // lanes)
            for pole in range(poles):
                term = scale[:, pole : pole + 1] * jnp.exp(-rate[:, pole : pole + 1] * ramp)
                step = jnp.broadcast_to(jump[:, pole : pole + 1], (8, lanes))
                for place in range(len(sums)):
                    sums[place] = term if pole == 0 else sums[place] + term
                    if place + 1 < len(sums):
                        term = term * step
            for place, total in enumerate(sums):
                lag, lane = divmod(place * lanes, block)
                first = (index * blocks + lag) * group + row
                time_ref[first : first + 8, lane : lane + lanes] = total
    sign = (1 - 2 * (lax.broadcasted_iota(jnp.int32, (group, block), 1) % 2)).astype(jnp.float32)
    for index in range(2):
        first = index * blocks * group
        high, low = halves(time_ref[first : first + blocks * group])
        spec = to_freq(high, low, table_ref)
        for lag in range(blocks):
            real = spec[lag * group : (lag + 1) * group, :block]
            imag = spec[lag * group : (lag + 1) * group, block:]
            if lag > 0:
                real = real - sign * spec[(lag - 1) * group : lag * group, block:]
                imag = imag + sign * spec[(lag - 1) * group : lag * group, :block]
            out_ref[index, lag, :, :block] = real
            out_ref[index, lag, :, block:] = imag


def conv_kernel(x_ref, own_ref, paired_ref, table_ref, out_ref, spec_ref, high_ref, low_ref):
    blocks, group, twice = own_ref.shape[1:]
    block = twice // 2
    rows_all = blocks * group
    tall, wide = 16, 128
    pieces = x_ref.shape[0] // blocks

    def rows_of(position):
        return jnp.concatenate(
            [
                jnp.concatenate([x_ref[m * pieces + s, position] for s in range(pieces)], axis=1)
                for m in range(blocks)
            ],
            axis=0,
        )

    def times(index, side, source, row, lane):
        data = []
        for m in range(blocks):
            rows = slice(source + m * group + row, source + m * group + row + tall)
            data.append((spec_ref[rows, lane : lane + wide], spec_ref[rows, block + lane : block + lane + wide]))
        sums = [None] * blocks
        for lag in range(blocks):
            h_ref = (own_ref, paired_ref)[side]
            f_re = h_ref[index, lag, row : row + tall, lane : lane + wide]
            f_im = h_ref[index, lag, row : row + tall, block + lane : block + lane + wide]
            for m in range(blocks - lag):
                target, (d_re, d_im) = (m + lag, data[m]) if side == 0 else (m, data[m + lag])
                if side == 0:
                    real, imag = f_re * d_re - f_im * d_im, f_re * d_im + f_im * d_re
                else:
                    real, imag = f_re * d_re + f_im * d_im, f_re * d_im - f_im * d_re
                if sums[target] is not None:
                    real, imag = sums[target][0] + real, sums[target][1] + imag
                sums[target] = (real, imag)
        return sums

    def keep(target, row, lane, sums):
        for m in range(blocks):
            rows = slice(target + m * group + row, target + m * group + row + tall)
            for part in range(2):
                cols = slice(part * block + lane, part * block + lane + wide)
                high_ref[rows, cols], low_ref[rows, cols] = halves(sums[m][part])

    chunks = [(row, lane) for row in range(0, group, tall) for lane in range(0, block, wide)]

    value = rows_of(1)
    spec_ref[:rows_all] = mul(value, table_ref[0]) + mul(value, table_ref[1])
    for row, lane in chunks:
        for side in range(2):
            keep(side * rows_all, row, lane, times(0, side, 0, row, lane))
    along = to_time(high_ref[...], low_ref[...], table_ref)
    gate = rows_of(0).astype(jnp.float32)
    high, low = halves(jnp.concatenate([gate, gate], axis=0) * along)
    spec_ref[...] = to_freq(high, low, table_ref)
    for row, lane in chunks:
        ahead, back = times(1, 0, 0, row, lane), times(1, 1, rows_all, row, lane)
        keep(0, row, lane, [(a[0] + b[0], a[1] + b[1]) for a, b in zip(ahead, back)])
    summed = to_time(high_ref[:rows_all], low_ref[:rows_all], table_ref)
    mixed = (rows_of(2).astype(jnp.float32) * summed).astype(jnp.bfloat16)
    tok = block // pieces
    for m in range(blocks):
        for s in range(pieces):
            piece = mixed[m * group : (m + 1) * group, s * tok : (s + 1) * tok]
            for copy in range(out_ref.shape[0]):
                out_ref[copy, m * pieces + s] = piece


def project_kernel(mixed_ref, *refs):
    w_refs, (out_ref, held_ref) = refs[:-2], refs[-2:]
    rows = w_refs[0].shape[0]
    position = lax.axis_index("ctx")
    total = mul(jnp.concatenate([w_ref[...] for w_ref in w_refs], axis=0), mixed_ref[...])
    for mask in range(len(w_refs)):
        first = pl.multiple_of((position ^ mask) * rows, rows)
        held_ref[pl.ds(first, rows)] = total[mask * rows : (mask + 1) * rows]
    out_ref[...] = held_ref[...].T.astype(jnp.bfloat16)


def whole_call(kernel, out_shape, scratch, flops, nbytes, *operands, in_hbm=0):
    return pl.pallas_call(
        kernel,
        out_shape=out_shape,
        in_specs=[
            pl.BlockSpec(memory_space=pltpu.HBM if place < in_hbm else pltpu.VMEM) for place in range(len(operands))
        ],
        out_specs=jax.tree.map(lambda _: pl.BlockSpec(memory_space=pltpu.VMEM), out_shape),
        scratch_shapes=scratch,
        cost_estimate=pl.CostEstimate(flops=flops, bytes_accessed=nbytes, transcendentals=0),
        compiler_params=pltpu.CompilerParams(vmem_limit_bytes=None if in_hbm else 32 * 2**20),
    )(*operands)


def blocked(x_gate, x_post, values, decay, residue, w_out):
    tok, width = x_gate.shape
    ctx_count = lax.axis_size("ctx")
    tp_count = lax.axis_size("tp")
    group = width // ctx_count
    poles = decay.shape[2]
    block = 2 * tok
    blocks = tok * ctx_count // block
    rows, channels = w_out.shape
    half = 2 * poles

    packed, own, mirrored, table = whole_call(
        pack_kernel,
        (
            jax.ShapeDtypeStruct((ctx_count, 3, group, tok), jnp.bfloat16),
            jax.ShapeDtypeStruct((2 * half, tok), jnp.float32),
            jax.ShapeDtypeStruct((2 * half, tok), jnp.float32),
            jax.ShapeDtypeStruct((2, block, 2 * block), jnp.bfloat16),
        ),
        [
            pltpu.VMEM((3, tok, width), jnp.bfloat16),
            pltpu.VMEM((2 * half, width), jnp.float32),
            pltpu.SemaphoreType.DMA((6,)),
        ],
        0,
        6 * tok * width * 2,
        x_gate,
        values,
        x_post,
        jnp.swapaxes(decay, 1, 2).reshape(half, width),
        jnp.swapaxes(residue, 1, 2).reshape(half, width),
        block_table(block),
        in_hbm=6,
    )
    paired = lax.ppermute(mirrored, "tp", [(z, tp_count - 1 - z) for z in range(tp_count)])
    received = lax.all_to_all(packed, "ctx", split_axis=0, concat_axis=0, tiled=True)

    def spectra(params):
        return whole_call(
            functools.partial(filter_kernel, poles),
            jax.ShapeDtypeStruct((2, blocks, group, 2 * block), jnp.float32),
            [pltpu.VMEM((2 * blocks * group, block), jnp.float32)],
            2 * 2 * blocks * group * block * 2 * block * 3,
            2 * blocks * group * 2 * block * 4,
            params,
            table,
        )

    own_spectra, paired_spectra = spectra(own), spectra(paired)
    w_late, paired_spectra = lax.optimization_barrier((w_out, paired_spectra))
    w_blocks = {0: w_out}
    for mask in range(2, ctx_count, 2):
        w_blocks[mask] = lax.ppermute(w_late, "ctx", [(i, i ^ mask) for i in range(ctx_count)])
    for mask in range(0, ctx_count, 2):
        w_blocks[mask + 1] = partner(w_blocks[mask], "ctx", 0)
    mixed = whole_call(
        conv_kernel,
        jax.ShapeDtypeStruct((tp_count, ctx_count, group, tok), jnp.bfloat16),
        [
            pltpu.VMEM((2 * blocks * group, 2 * block), jnp.float32),
            pltpu.VMEM((2 * blocks * group, 2 * block), jnp.bfloat16),
            pltpu.VMEM((2 * blocks * group, 2 * block), jnp.bfloat16),
        ],
        2 * 6 * blocks * group * block * 2 * block * 3,
        4 * blocks * group * 2 * block * 4,
        received,
        own_spectra,
        paired_spectra,
        table,
    )
    every = lax.all_to_all(
        mixed.reshape(tp_count * ctx_count, group, tok), ("tp", "ctx"), split_axis=0, concat_axis=0, tiled=True
    ).reshape(channels, tok)
    return whole_call(
        project_kernel,
        jax.ShapeDtypeStruct((tok, rows * ctx_count), jnp.bfloat16),
        [pltpu.VMEM((rows * ctx_count, tok), jnp.float32)],
        2 * tok * rows * ctx_count * channels,
        2 * rows * ctx_count * channels,
        every,
        *[w_blocks[mask] for mask in range(ctx_count)],
    )


def local(x_gate, x_post, values, decay, residue, w_out):
    tok, width = x_gate.shape
    ctx_count = lax.axis_size("ctx")
    if tok == 128 and width == 512 and ctx_count == 8 and lax.axis_size("tp") == 4:
        return blocked(x_gate, x_post, values, decay, residue, w_out)
    return general(x_gate, x_post, values, decay, residue, w_out)


def solution(mesh):
    in_specs = (
        P("ctx", "tp"),
        P("ctx", "tp"),
        P("ctx", "tp"),
        P(None, "tp", None),
        P(None, "tp", None),
        P(("tp", "ctx"), None),
    )
    out_specs = P("ctx", "tp")
    return jax.shard_map(local, mesh=mesh, in_specs=in_specs, out_specs=out_specs, check_vma=False)
```

```python
import functools
import math

import jax
import jax.numpy as jnp
import ml_dtypes
import numpy as np
from jax import lax
from jax.experimental import pallas as pl
from jax.experimental.pallas import tpu as pltpu
from jax.sharding import PartitionSpec as P

HIGHEST = lax.Precision.HIGHEST


def partner(value, axis, bit):
    mask = 2**bit
    pairs = [(source, source ^ mask) for source in range(lax.axis_size(axis))]
    return lax.ppermute(value, axis, pairs)


def radices(length_all):
    last_radix = min(128, length_all // 4)
    first_radix = min(32, length_all // last_radix)
    return (first_radix, length_all // (first_radix * last_radix), last_radix)


def rotation(row_count, col_count, modulus):
    product = (
        lax.broadcasted_iota(jnp.int32, (row_count, col_count), 0)
        * lax.broadcasted_iota(jnp.int32, (row_count, col_count), 1)
        % modulus
    )
    angle = product.astype(jnp.float32) * (2.0 * math.pi / modulus)
    return (jnp.cos(angle), -jnp.sin(angle))


def tables(radix_sizes):
    first_radix, mid_radix, last_radix = radix_sizes
    length_all = first_radix * mid_radix * last_radix
    outer_real, outer_imag = rotation(first_radix, first_radix, first_radix)
    mid_real, mid_imag = rotation(mid_radix, mid_radix, mid_radix)
    last_real, last_imag = rotation(last_radix, last_radix, last_radix)
    twist_real, twist_imag = rotation(first_radix, mid_radix * last_radix, length_all)
    twist_real = twist_real.reshape(first_radix, mid_radix, last_radix)
    twist_imag = twist_imag.reshape(first_radix, mid_radix, last_radix)
    inner_real, inner_imag = rotation(mid_radix, last_radix, mid_radix * last_radix)
    return (
        outer_real,
        outer_imag,
        mid_real,
        mid_imag,
        last_real,
        last_imag,
        twist_real,
        twist_imag,
        inner_real,
        inner_imag,
    )


def apply_matrix(pattern, real_part, imag_part, matrix_real, matrix_imag):
    out_real = jnp.einsum(pattern, real_part, matrix_real, precision=HIGHEST) - jnp.einsum(
        pattern, imag_part, matrix_imag, precision=HIGHEST
    )
    out_imag = jnp.einsum(pattern, real_part, matrix_imag, precision=HIGHEST) + jnp.einsum(
        pattern, imag_part, matrix_real, precision=HIGHEST
    )
    return (out_real, out_imag)


def complex_times(left_real, left_imag, right_real, right_imag):
    return (
        left_real * right_real - left_imag * right_imag,
        left_real * right_imag + left_imag * right_real,
    )


def forward(real_part, imag_part, table_set, radix_sizes):
    first_radix, mid_radix, last_radix = radix_sizes
    half_first = first_radix // 2
    batch_rows = real_part.shape[0]
    (
        outer_real,
        outer_imag,
        mid_real,
        mid_imag,
        last_real,
        last_imag,
        twist_real,
        twist_imag,
        inner_real,
        inner_imag,
    ) = table_set
    real_part = real_part.reshape(batch_rows, half_first, mid_radix, last_radix)
    imag_part = imag_part.reshape(batch_rows, half_first, mid_radix, last_radix)
    real_part, imag_part = apply_matrix(
        "banm,ak->bknm", real_part, imag_part, outer_real[:half_first], outer_imag[:half_first]
    )
    real_part, imag_part = complex_times(real_part, imag_part, twist_real, twist_imag)
    real_part, imag_part = apply_matrix("bknm,nj->bkjm", real_part, imag_part, mid_real, mid_imag)
    real_part, imag_part = complex_times(real_part, imag_part, inner_real, inner_imag)
    return apply_matrix("bkjm,mq->bkjq", real_part, imag_part, last_real, last_imag)


def inverse(real_part, imag_part, table_set, radix_sizes):
    first_radix, mid_radix, last_radix = radix_sizes
    half_first = first_radix // 2
    batch_rows = real_part.shape[0]
    (
        outer_real,
        outer_imag,
        mid_real,
        mid_imag,
        last_real,
        last_imag,
        twist_real,
        twist_imag,
        inner_real,
        inner_imag,
    ) = table_set
    real_part, imag_part = apply_matrix(
        "bkjq,mq->bkjm", real_part, imag_part, last_real / last_radix, -last_imag / last_radix
    )
    real_part, imag_part = complex_times(real_part, imag_part, inner_real, -inner_imag)
    real_part, imag_part = apply_matrix(
        "bkjm,nj->bknm", real_part, imag_part, mid_real / mid_radix, -mid_imag / mid_radix
    )
    real_part, imag_part = complex_times(real_part, imag_part, twist_real, -twist_imag)
    matrix_real = outer_real[:half_first] / first_radix
    matrix_imag = -outer_imag[:half_first] / first_radix
    out_real, out_imag = apply_matrix(
        "bknm,ak->banm", real_part, imag_part, matrix_real, matrix_imag
    )
    return (out_real.reshape(batch_rows, -1), out_imag.reshape(batch_rows, -1))


def spectrum(decay_rows, residue_rows, radix_sizes, seq_length):
    first_radix, mid_radix, last_radix = radix_sizes
    length_all = first_radix * mid_radix * last_radix
    poles = decay_rows.shape[1]
    shape_all = (first_radix, mid_radix, last_radix)
    frequency = (
        lax.broadcasted_iota(jnp.int32, shape_all, 0)
        + first_radix * lax.broadcasted_iota(jnp.int32, shape_all, 1)
        + first_radix * mid_radix * lax.broadcasted_iota(jnp.int32, shape_all, 2)
    )
    half_angle = frequency.astype(jnp.float32) * (math.pi / length_all)
    sin_half = jnp.sin(half_angle)
    sin_full = jnp.sin(2.0 * half_angle)
    parity_sign = (1 - 2 * (frequency % 2)).astype(jnp.float32)

    def add_pole(pole_index, running):
        run_real, run_imag = running
        rate_col = lax.dynamic_slice_in_dim(decay_rows, pole_index, 1, 1).reshape(-1, 1, 1, 1)
        weight = lax.dynamic_slice_in_dim(residue_rows, pole_index, 1, 1).reshape(
            -1, 1, 1, 1
        ) * jnp.sqrt(2.0 * rate_col / poles)
        retained = jnp.exp(-rate_col)
        den_real = -jnp.expm1(-rate_col) + 2.0 * retained * sin_half * sin_half
        den_imag = retained * sin_full
        pole_scale = (
            weight
            * (1.0 - jnp.exp(-rate_col * seq_length) * parity_sign)
            / (den_real * den_real + den_imag * den_imag)
        )
        return (run_real + pole_scale * den_real, run_imag - pole_scale * den_imag)

    zeros_all = jnp.zeros((decay_rows.shape[0],) + shape_all, jnp.float32)
    return lax.fori_loop(0, poles, add_pole, (zeros_all, zeros_all))


def general(x_gate, x_post, values, decay, residue, w_out):
    tok_rows, block_width = x_gate.shape
    ctx_count = lax.axis_size("ctx")
    tp_count = lax.axis_size("tp")
    chan_group = block_width // ctx_count
    seq_length = tok_rows * ctx_count
    radix_sizes = radices(2 * seq_length)
    table_set = tables(radix_sizes)
    first_row = lax.axis_index("ctx") * chan_group
    own_rate = lax.dynamic_slice_in_dim(decay, first_row, chan_group, 1)
    own_residue = lax.dynamic_slice_in_dim(residue, first_row, chan_group, 1)
    own_spec = [
        spectrum(own_rate[filter_index], own_residue[filter_index], radix_sizes, seq_length)
        for filter_index in range(2)
    ]
    forward_rows = [x_gate, values] + [x_post]
    row_count = len(forward_rows)
    base_rows = jnp.stack(forward_rows)
    copied = base_rows
    for bit_index in range(tp_count.bit_length() - 1):
        copied = partner(copied, "tp", bit_index)
    sent_rows = jnp.concatenate([base_rows, copied[:, :, ::-1]], axis=0)
    received = lax.all_to_all(
        jnp.swapaxes(sent_rows, 1, 2), "ctx", split_axis=1, concat_axis=2, tiled=True
    )
    gate_fwd = received[0].astype(jnp.float32)
    value_fwd = received[1].astype(jnp.float32)
    mirrored = received[row_count:, :, ::-1].astype(jnp.float32)
    spec_real, spec_imag = forward(value_fwd, mirrored[1], table_set, radix_sizes)
    spec_real, spec_imag = complex_times(spec_real, spec_imag, own_spec[0][0], own_spec[0][1])
    along_fwd, along_rev = inverse(spec_real, spec_imag, table_set, radix_sizes)
    spec_real, spec_imag = forward(
        gate_fwd * along_fwd, mirrored[0] * along_rev, table_set, radix_sizes
    )
    spec_real, spec_imag = complex_times(spec_real, spec_imag, own_spec[1][0], own_spec[1][1])
    sum_fwd, sum_rev = inverse(spec_real, spec_imag, table_set, radix_sizes)
    sum_fwd = received[2].astype(jnp.float32) * sum_fwd
    sum_rev = mirrored[2] * sum_rev
    results = jnp.stack([sum_fwd, sum_rev[:, ::-1]])
    returned = lax.all_to_all(
        results.astype(jnp.bfloat16), "ctx", split_axis=2, concat_axis=1, tiled=True
    ).astype(results.dtype)
    flipped = returned[1, ::-1, :]
    for bit_index in range(tp_count.bit_length() - 1):
        flipped = partner(flipped.astype(jnp.bfloat16), "tp", bit_index).astype(flipped.dtype)
    total_rows = returned[0] + flipped
    total_rows = total_rows.T
    mixed_rows = total_rows.astype(jnp.bfloat16)
    whole_rows = lax.all_gather(mixed_rows, "tp", axis=1, tiled=True)
    projected = lax.dot_general(
        whole_rows,
        lax.all_gather(w_out, "ctx", axis=0, tiled=True),
        (((1,), (1,)), ((), ())),
        preferred_element_type=jnp.float32,
    )
    return projected.astype(jnp.bfloat16)


def block_tables(block):
    angle = np.pi * np.outer(np.arange(block), np.arange(block) + 0.5) / block
    table = np.concatenate([np.cos(angle), -np.sin(angle)], axis=1)
    high = table.astype(ml_dtypes.bfloat16)
    low = (table - high.astype(np.float64)).astype(ml_dtypes.bfloat16)
    return jnp.asarray(np.stack([high, low])), jnp.asarray(np.stack([high.T, low.T]))


def halves(value):
    high = value.astype(jnp.bfloat16)
    return high, (value - high.astype(jnp.float32)).astype(jnp.bfloat16)


def mul(left, right):
    return jnp.dot(left, right, preferred_element_type=jnp.float32)


def mul3(high, low, table_ref):
    return mul(high, table_ref[0]) + (mul(low, table_ref[0]) + mul(high, table_ref[1]))


def pack_kernel(
    gate_hbm, value_hbm, post_hbm, decay_hbm, residue_hbm, table_hbm, back_hbm,
    out_ref, own_ref, sent_ref, table_ref, back_ref, held_ref, par_ref, sems,
):
    ctx_count, _, group, tok = out_ref.shape
    width = gate_hbm.shape[1]
    half = decay_hbm.shape[0]
    position = lax.axis_index("ctx")
    pairs = [(decay_hbm, par_ref.at[:half]), (residue_hbm, par_ref.at[half:])]
    pairs += [(source, held_ref.at[place]) for place, source in enumerate((gate_hbm, value_hbm, post_hbm))]
    pairs += [(table_hbm, table_ref), (back_hbm, back_ref)]
    copies = [pltpu.make_async_copy(*pair, sems.at[place]) for place, pair in enumerate(pairs)]
    for copy in copies:
        copy.start()
    copies[0].wait()
    copies[1].wait()
    odd = position % 2 == 1
    lane = lax.broadcasted_iota(jnp.int32, own_ref.shape, 1)

    def tile_of(index):
        return par_ref[:, pl.ds(pl.multiple_of(index // 2 * tok, tok), tok)]

    def to_front(value):
        return jnp.where(odd, pltpu.roll(value, group, 1), value)

    own_ref[...] = to_front(tile_of(position))
    turned = tile_of(ctx_count - 1 - position)
    shift = 1
    while shift < tok:
        turned = jnp.where(lane & shift == 0, pltpu.roll(turned, tok - shift, 1), pltpu.roll(turned, shift, 1))
        shift *= 2
    sent_ref[...] = to_front(turned)
    for place in range(3):
        copies[2 + place].wait()
        for first in range(0, width, tok):
            turned = held_ref[place, :, first : first + tok].T
            for part in range(tok // group):
                out_ref[first // group + part, place] = turned[part * group : (part + 1) * group]
    copies[5].wait()
    copies[6].wait()


def filter_kernel(poles, par_ref, table_ref, out_ref, time_ref):
    blocks, group, twice = out_ref.shape[1:]
    block = twice // 2
    lanes = 128
    turned = par_ref[...].T
    ramp = lax.broadcasted_iota(jnp.int32, (8, lanes), 1).astype(jnp.float32)
    for index in range(2):
        for row in range(0, group, 8):
            rows = slice(row, row + 8)
            rate = turned[rows, index * poles : (index + 1) * poles]
            scale = turned[rows, (2 + index) * poles : (3 + index) * poles] * (jnp.sqrt(rate * (2.0 / poles)) / block)
            jump = jnp.exp(rate * -lanes)
            sums = [None] * (blocks * block // lanes)
            for pole in range(poles):
                term = scale[:, pole : pole + 1] * jnp.exp(-rate[:, pole : pole + 1] * ramp)
                step = jnp.broadcast_to(jump[:, pole : pole + 1], (8, lanes))
                for place in range(len(sums)):
                    sums[place] = term if pole == 0 else sums[place] + term
                    if place + 1 < len(sums):
                        term = term * step
            for place, total in enumerate(sums):
                lag, lane = divmod(place * lanes, block)
                first = (index * blocks + lag) * group + row
                time_ref[first : first + 8, lane : lane + lanes] = total
    sign = (1 - 2 * (lax.broadcasted_iota(jnp.int32, (group, block), 1) % 2)).astype(jnp.float32)
    for index in range(2):
        first = index * blocks * group
        high, low = halves(time_ref[first : first + blocks * group])
        spec = mul3(high, low, table_ref)
        for lag in range(blocks):
            real = spec[lag * group : (lag + 1) * group, :block]
            imag = spec[lag * group : (lag + 1) * group, block:]
            if lag > 0:
                real = real - sign * spec[(lag - 1) * group : lag * group, block:]
                imag = imag + sign * spec[(lag - 1) * group : lag * group, :block]
            out_ref[index, lag, :, :block] = real
            out_ref[index, lag, :, block:] = imag


def conv_kernel(x_ref, own_ref, paired_ref, table_ref, back_ref, out_ref, spec_ref, high_ref, low_ref):
    blocks, group, twice = own_ref.shape[1:]
    block = twice // 2
    rows_all = blocks * group
    tall, wide = 16, 128
    pieces = x_ref.shape[0] // blocks

    def rows_of(position):
        return jnp.concatenate(
            [
                jnp.concatenate([x_ref[m * pieces + s, position] for s in range(pieces)], axis=1)
                for m in range(blocks)
            ],
            axis=0,
        )

    def times(index, side, source, row, lane):
        data = []
        for m in range(blocks):
            rows = slice(source + m * group + row, source + m * group + row + tall)
            data.append((spec_ref[rows, lane : lane + wide], spec_ref[rows, block + lane : block + lane + wide]))
        sums = [None] * blocks
        for lag in range(blocks):
            h_ref = (own_ref, paired_ref)[side]
            f_re = h_ref[index, lag, row : row + tall, lane : lane + wide]
            f_im = h_ref[index, lag, row : row + tall, block + lane : block + lane + wide]
            for m in range(blocks - lag):
                target, (d_re, d_im) = (m + lag, data[m]) if side == 0 else (m, data[m + lag])
                if side == 0:
                    real, imag = f_re * d_re - f_im * d_im, f_re * d_im + f_im * d_re
                else:
                    real, imag = f_re * d_re + f_im * d_im, f_re * d_im - f_im * d_re
                if sums[target] is not None:
                    real, imag = sums[target][0] + real, sums[target][1] + imag
                sums[target] = (real, imag)
        return sums

    def keep(target, row, lane, sums):
        for m in range(blocks):
            rows = slice(target + m * group + row, target + m * group + row + tall)
            for part in range(2):
                cols = slice(part * block + lane, part * block + lane + wide)
                high_ref[rows, cols], low_ref[rows, cols] = halves(sums[m][part])

    chunks = [(row, lane) for row in range(0, group, tall) for lane in range(0, block, wide)]

    value = rows_of(1)
    spec_ref[:rows_all] = mul(value, table_ref[0]) + mul(value, table_ref[1])
    for row, lane in chunks:
        for side in range(2):
            keep(side * rows_all, row, lane, times(0, side, 0, row, lane))
    along = mul3(high_ref[...], low_ref[...], back_ref)
    gate = rows_of(0).astype(jnp.float32)
    high, low = halves(jnp.concatenate([gate, gate], axis=0) * along)
    spec_ref[...] = mul3(high, low, table_ref)
    for row, lane in chunks:
        ahead, back = times(1, 0, 0, row, lane), times(1, 1, rows_all, row, lane)
        keep(0, row, lane, [(a[0] + b[0], a[1] + b[1]) for a, b in zip(ahead, back)])
    summed = mul3(high_ref[:rows_all], low_ref[:rows_all], back_ref)
    mixed = (rows_of(2).astype(jnp.float32) * summed).astype(jnp.bfloat16)
    tok = block // pieces
    for m in range(blocks):
        for s in range(pieces):
            piece = mixed[m * group : (m + 1) * group, s * tok : (s + 1) * tok]
            for copy in range(out_ref.shape[0]):
                out_ref[copy, m * pieces + s] = piece


def project_kernel(mixed_ref, *refs):
    w_refs, (out_ref, held_ref) = refs[:-2], refs[-2:]
    rows = w_refs[0].shape[0]
    position = lax.axis_index("ctx")
    total = mul(jnp.concatenate([w_ref[...] for w_ref in w_refs], axis=0), mixed_ref[...])
    for mask in range(len(w_refs)):
        first = pl.multiple_of((position ^ mask) * rows, rows)
        held_ref[pl.ds(first, rows)] = total[mask * rows : (mask + 1) * rows]
    out_ref[...] = held_ref[...].T.astype(jnp.bfloat16)


def whole_call(kernel, out_shape, scratch, flops, nbytes, *operands, in_hbm=0):
    return pl.pallas_call(
        kernel,
        out_shape=out_shape,
        in_specs=[
            pl.BlockSpec(memory_space=pltpu.HBM if place < in_hbm else pltpu.VMEM) for place in range(len(operands))
        ],
        out_specs=jax.tree.map(lambda _: pl.BlockSpec(memory_space=pltpu.VMEM), out_shape),
        scratch_shapes=scratch,
        cost_estimate=pl.CostEstimate(flops=flops, bytes_accessed=nbytes, transcendentals=0),
        compiler_params=pltpu.CompilerParams(vmem_limit_bytes=None if in_hbm else 32 * 2**20),
    )(*operands)


def blocked(x_gate, x_post, values, decay, residue, w_out):
    tok, width = x_gate.shape
    ctx_count = lax.axis_size("ctx")
    tp_count = lax.axis_size("tp")
    group = width // ctx_count
    poles = decay.shape[2]
    block = 2 * tok
    blocks = tok * ctx_count // block
    rows, channels = w_out.shape
    half = 2 * poles

    packed, own, mirrored, table, back_table = whole_call(
        pack_kernel,
        (
            jax.ShapeDtypeStruct((ctx_count, 3, group, tok), jnp.bfloat16),
            jax.ShapeDtypeStruct((2 * half, tok), jnp.float32),
            jax.ShapeDtypeStruct((2 * half, tok), jnp.float32),
            jax.ShapeDtypeStruct((2, block, 2 * block), jnp.bfloat16),
            jax.ShapeDtypeStruct((2, 2 * block, block), jnp.bfloat16),
        ),
        [
            pltpu.VMEM((3, tok, width), jnp.bfloat16),
            pltpu.VMEM((2 * half, width), jnp.float32),
            pltpu.SemaphoreType.DMA((7,)),
        ],
        0,
        6 * tok * width * 2,
        x_gate,
        values,
        x_post,
        jnp.swapaxes(decay, 1, 2).reshape(half, width),
        jnp.swapaxes(residue, 1, 2).reshape(half, width),
        *block_tables(block),
        in_hbm=7,
    )
    paired = lax.ppermute(mirrored, "tp", [(z, tp_count - 1 - z) for z in range(tp_count)])
    received = lax.all_to_all(packed, "ctx", split_axis=0, concat_axis=0, tiled=True)

    def spectra(params):
        return whole_call(
            functools.partial(filter_kernel, poles),
            jax.ShapeDtypeStruct((2, blocks, group, 2 * block), jnp.float32),
            [pltpu.VMEM((2 * blocks * group, block), jnp.float32)],
            2 * 2 * blocks * group * block * 2 * block * 3,
            2 * blocks * group * 2 * block * 4,
            params,
            table,
        )

    own_spectra, paired_spectra = spectra(own), spectra(paired)
    w_late, paired_spectra = lax.optimization_barrier((w_out, paired_spectra))
    w_blocks = {0: w_out, 2: partner(w_out, "ctx", 1), 4: partner(w_out, "ctx", 2)}
    w_blocks[6] = lax.ppermute(w_late, "ctx", [(i, i ^ 6) for i in range(ctx_count)])
    w_blocks[1] = partner(w_late, "ctx", 0)
    for mask in (2, 4, 6):
        w_blocks[mask + 1] = partner(w_blocks[mask], "ctx", 0)
    mixed = whole_call(
        conv_kernel,
        jax.ShapeDtypeStruct((tp_count, ctx_count, group, tok), jnp.bfloat16),
        [
            pltpu.VMEM((2 * blocks * group, 2 * block), jnp.float32),
            pltpu.VMEM((2 * blocks * group, 2 * block), jnp.bfloat16),
            pltpu.VMEM((2 * blocks * group, 2 * block), jnp.bfloat16),
        ],
        2 * 6 * blocks * group * block * 2 * block * 3,
        4 * blocks * group * 2 * block * 4,
        received,
        own_spectra,
        paired_spectra,
        table,
        back_table,
    )
    every = lax.all_to_all(
        mixed.reshape(tp_count * ctx_count, group, tok), ("tp", "ctx"), split_axis=0, concat_axis=0, tiled=True
    ).reshape(channels, tok)
    return whole_call(
        project_kernel,
        jax.ShapeDtypeStruct((tok, rows * ctx_count), jnp.bfloat16),
        [pltpu.VMEM((rows * ctx_count, tok), jnp.float32)],
        2 * tok * rows * ctx_count * channels,
        2 * rows * ctx_count * channels,
        every,
        *[w_blocks[mask] for mask in range(ctx_count)],
    )


def local(x_gate, x_post, values, decay, residue, w_out):
    tok, width = x_gate.shape
    ctx_count = lax.axis_size("ctx")
    if tok == 128 and width == 512 and ctx_count == 8 and lax.axis_size("tp") == 4:
        return blocked(x_gate, x_post, values, decay, residue, w_out)
    return general(x_gate, x_post, values, decay, residue, w_out)


def solution(mesh):
    in_specs = (
        P("ctx", "tp"),
        P("ctx", "tp"),
        P("ctx", "tp"),
        P(None, "tp", None),
        P(None, "tp", None),
        P(("tp", "ctx"), None),
    )
    out_specs = P("ctx", "tp")
    return jax.shard_map(local, mesh=mesh, in_specs=in_specs, out_specs=out_specs, check_vma=False)
```

```python
import functools
import math

import jax
import jax.numpy as jnp
import ml_dtypes
import numpy as np
from jax import lax
from jax.experimental import pallas as pl
from jax.experimental.pallas import tpu as pltpu
from jax.sharding import PartitionSpec as P

HIGHEST = lax.Precision.HIGHEST


def partner(value, axis, bit):
    mask = 2**bit
    pairs = [(source, source ^ mask) for source in range(lax.axis_size(axis))]
    return lax.ppermute(value, axis, pairs)


def radices(length_all):
    last_radix = min(128, length_all // 4)
    first_radix = min(32, length_all // last_radix)
    return (first_radix, length_all // (first_radix * last_radix), last_radix)


def rotation(row_count, col_count, modulus):
    product = (
        lax.broadcasted_iota(jnp.int32, (row_count, col_count), 0)
        * lax.broadcasted_iota(jnp.int32, (row_count, col_count), 1)
        % modulus
    )
    angle = product.astype(jnp.float32) * (2.0 * math.pi / modulus)
    return (jnp.cos(angle), -jnp.sin(angle))


def tables(radix_sizes):
    first_radix, mid_radix, last_radix = radix_sizes
    length_all = first_radix * mid_radix * last_radix
    outer_real, outer_imag = rotation(first_radix, first_radix, first_radix)
    mid_real, mid_imag = rotation(mid_radix, mid_radix, mid_radix)
    last_real, last_imag = rotation(last_radix, last_radix, last_radix)
    twist_real, twist_imag = rotation(first_radix, mid_radix * last_radix, length_all)
    twist_real = twist_real.reshape(first_radix, mid_radix, last_radix)
    twist_imag = twist_imag.reshape(first_radix, mid_radix, last_radix)
    inner_real, inner_imag = rotation(mid_radix, last_radix, mid_radix * last_radix)
    return (
        outer_real,
        outer_imag,
        mid_real,
        mid_imag,
        last_real,
        last_imag,
        twist_real,
        twist_imag,
        inner_real,
        inner_imag,
    )


def apply_matrix(pattern, real_part, imag_part, matrix_real, matrix_imag):
    out_real = jnp.einsum(pattern, real_part, matrix_real, precision=HIGHEST) - jnp.einsum(
        pattern, imag_part, matrix_imag, precision=HIGHEST
    )
    out_imag = jnp.einsum(pattern, real_part, matrix_imag, precision=HIGHEST) + jnp.einsum(
        pattern, imag_part, matrix_real, precision=HIGHEST
    )
    return (out_real, out_imag)


def complex_times(left_real, left_imag, right_real, right_imag):
    return (
        left_real * right_real - left_imag * right_imag,
        left_real * right_imag + left_imag * right_real,
    )


def forward(real_part, imag_part, table_set, radix_sizes):
    first_radix, mid_radix, last_radix = radix_sizes
    half_first = first_radix // 2
    batch_rows = real_part.shape[0]
    (
        outer_real,
        outer_imag,
        mid_real,
        mid_imag,
        last_real,
        last_imag,
        twist_real,
        twist_imag,
        inner_real,
        inner_imag,
    ) = table_set
    real_part = real_part.reshape(batch_rows, half_first, mid_radix, last_radix)
    imag_part = imag_part.reshape(batch_rows, half_first, mid_radix, last_radix)
    real_part, imag_part = apply_matrix(
        "banm,ak->bknm", real_part, imag_part, outer_real[:half_first], outer_imag[:half_first]
    )
    real_part, imag_part = complex_times(real_part, imag_part, twist_real, twist_imag)
    real_part, imag_part = apply_matrix("bknm,nj->bkjm", real_part, imag_part, mid_real, mid_imag)
    real_part, imag_part = complex_times(real_part, imag_part, inner_real, inner_imag)
    return apply_matrix("bkjm,mq->bkjq", real_part, imag_part, last_real, last_imag)


def inverse(real_part, imag_part, table_set, radix_sizes):
    first_radix, mid_radix, last_radix = radix_sizes
    half_first = first_radix // 2
    batch_rows = real_part.shape[0]
    (
        outer_real,
        outer_imag,
        mid_real,
        mid_imag,
        last_real,
        last_imag,
        twist_real,
        twist_imag,
        inner_real,
        inner_imag,
    ) = table_set
    real_part, imag_part = apply_matrix(
        "bkjq,mq->bkjm", real_part, imag_part, last_real / last_radix, -last_imag / last_radix
    )
    real_part, imag_part = complex_times(real_part, imag_part, inner_real, -inner_imag)
    real_part, imag_part = apply_matrix(
        "bkjm,nj->bknm", real_part, imag_part, mid_real / mid_radix, -mid_imag / mid_radix
    )
    real_part, imag_part = complex_times(real_part, imag_part, twist_real, -twist_imag)
    matrix_real = outer_real[:half_first] / first_radix
    matrix_imag = -outer_imag[:half_first] / first_radix
    out_real, out_imag = apply_matrix(
        "bknm,ak->banm", real_part, imag_part, matrix_real, matrix_imag
    )
    return (out_real.reshape(batch_rows, -1), out_imag.reshape(batch_rows, -1))


def spectrum(decay_rows, residue_rows, radix_sizes, seq_length):
    first_radix, mid_radix, last_radix = radix_sizes
    length_all = first_radix * mid_radix * last_radix
    poles = decay_rows.shape[1]
    shape_all = (first_radix, mid_radix, last_radix)
    frequency = (
        lax.broadcasted_iota(jnp.int32, shape_all, 0)
        + first_radix * lax.broadcasted_iota(jnp.int32, shape_all, 1)
        + first_radix * mid_radix * lax.broadcasted_iota(jnp.int32, shape_all, 2)
    )
    half_angle = frequency.astype(jnp.float32) * (math.pi / length_all)
    sin_half = jnp.sin(half_angle)
    sin_full = jnp.sin(2.0 * half_angle)
    parity_sign = (1 - 2 * (frequency % 2)).astype(jnp.float32)

    def add_pole(pole_index, running):
        run_real, run_imag = running
        rate_col = lax.dynamic_slice_in_dim(decay_rows, pole_index, 1, 1).reshape(-1, 1, 1, 1)
        weight = lax.dynamic_slice_in_dim(residue_rows, pole_index, 1, 1).reshape(
            -1, 1, 1, 1
        ) * jnp.sqrt(2.0 * rate_col / poles)
        retained = jnp.exp(-rate_col)
        den_real = -jnp.expm1(-rate_col) + 2.0 * retained * sin_half * sin_half
        den_imag = retained * sin_full
        pole_scale = (
            weight
            * (1.0 - jnp.exp(-rate_col * seq_length) * parity_sign)
            / (den_real * den_real + den_imag * den_imag)
        )
        return (run_real + pole_scale * den_real, run_imag - pole_scale * den_imag)

    zeros_all = jnp.zeros((decay_rows.shape[0],) + shape_all, jnp.float32)
    return lax.fori_loop(0, poles, add_pole, (zeros_all, zeros_all))


def general(x_gate, x_post, values, decay, residue, w_out):
    tok_rows, block_width = x_gate.shape
    ctx_count = lax.axis_size("ctx")
    tp_count = lax.axis_size("tp")
    chan_group = block_width // ctx_count
    seq_length = tok_rows * ctx_count
    radix_sizes = radices(2 * seq_length)
    table_set = tables(radix_sizes)
    first_row = lax.axis_index("ctx") * chan_group
    own_rate = lax.dynamic_slice_in_dim(decay, first_row, chan_group, 1)
    own_residue = lax.dynamic_slice_in_dim(residue, first_row, chan_group, 1)
    own_spec = [
        spectrum(own_rate[filter_index], own_residue[filter_index], radix_sizes, seq_length)
        for filter_index in range(2)
    ]
    forward_rows = [x_gate, values] + [x_post]
    row_count = len(forward_rows)
    base_rows = jnp.stack(forward_rows)
    copied = base_rows
    for bit_index in range(tp_count.bit_length() - 1):
        copied = partner(copied, "tp", bit_index)
    sent_rows = jnp.concatenate([base_rows, copied[:, :, ::-1]], axis=0)
    received = lax.all_to_all(
        jnp.swapaxes(sent_rows, 1, 2), "ctx", split_axis=1, concat_axis=2, tiled=True
    )
    gate_fwd = received[0].astype(jnp.float32)
    value_fwd = received[1].astype(jnp.float32)
    mirrored = received[row_count:, :, ::-1].astype(jnp.float32)
    spec_real, spec_imag = forward(value_fwd, mirrored[1], table_set, radix_sizes)
    spec_real, spec_imag = complex_times(spec_real, spec_imag, own_spec[0][0], own_spec[0][1])
    along_fwd, along_rev = inverse(spec_real, spec_imag, table_set, radix_sizes)
    spec_real, spec_imag = forward(
        gate_fwd * along_fwd, mirrored[0] * along_rev, table_set, radix_sizes
    )
    spec_real, spec_imag = complex_times(spec_real, spec_imag, own_spec[1][0], own_spec[1][1])
    sum_fwd, sum_rev = inverse(spec_real, spec_imag, table_set, radix_sizes)
    sum_fwd = received[2].astype(jnp.float32) * sum_fwd
    sum_rev = mirrored[2] * sum_rev
    results = jnp.stack([sum_fwd, sum_rev[:, ::-1]])
    returned = lax.all_to_all(
        results.astype(jnp.bfloat16), "ctx", split_axis=2, concat_axis=1, tiled=True
    ).astype(results.dtype)
    flipped = returned[1, ::-1, :]
    for bit_index in range(tp_count.bit_length() - 1):
        flipped = partner(flipped.astype(jnp.bfloat16), "tp", bit_index).astype(flipped.dtype)
    total_rows = returned[0] + flipped
    total_rows = total_rows.T
    mixed_rows = total_rows.astype(jnp.bfloat16)
    whole_rows = lax.all_gather(mixed_rows, "tp", axis=1, tiled=True)
    projected = lax.dot_general(
        whole_rows,
        lax.all_gather(w_out, "ctx", axis=0, tiled=True),
        (((1,), (1,)), ((), ())),
        preferred_element_type=jnp.float32,
    )
    return projected.astype(jnp.bfloat16)


def block_tables(block):
    angle = np.pi * np.outer(np.arange(block), np.arange(block) + 0.5) / block
    table = np.concatenate([np.cos(angle), -np.sin(angle)], axis=1)
    high = table.astype(ml_dtypes.bfloat16)
    low = (table - high.astype(np.float64)).astype(ml_dtypes.bfloat16)
    return jnp.asarray(np.stack([high, low])), jnp.asarray(np.stack([high.T, low.T]))


def halves(value):
    high = value.astype(jnp.bfloat16)
    return high, (value - high.astype(jnp.float32)).astype(jnp.bfloat16)


def mul(left, right):
    return jnp.dot(left, right, preferred_element_type=jnp.float32)


def mul3(high, low, table_ref):
    return mul(high, table_ref[0]) + (mul(low, table_ref[0]) + mul(high, table_ref[1]))


def pack_kernel(
    gate_hbm, value_hbm, post_hbm, decay_hbm, residue_hbm, table_hbm, back_hbm,
    out_hbm, own_ref, sent_ref, table_out, back_out, held_ref, par_ref, ready_ref, sems, out_sems,
):
    ctx_count, _, group, tok = out_hbm.shape
    width = gate_hbm.shape[1]
    half = decay_hbm.shape[0]
    position = lax.axis_index("ctx")
    pairs = [(source, held_ref.at[place]) for place, source in enumerate((value_hbm, gate_hbm, post_hbm))]
    pairs += [(decay_hbm, par_ref.at[:half]), (residue_hbm, par_ref.at[half:])]
    pairs += [(table_hbm, table_out), (back_hbm, back_out)]
    copies = [pltpu.make_async_copy(*pair, sems.at[place]) for place, pair in enumerate(pairs)]
    for copy in copies:
        copy.start()
    sends = []
    for place, copy in enumerate(copies[:3]):
        copy.wait()
        for first in range(0, width, tok):
            turned = held_ref[place, :, first : first + tok].T
            for part in range(tok // group):
                ready_ref[first // group + part, place] = turned[part * group : (part + 1) * group]
        sends.append(pltpu.make_async_copy(ready_ref.at[:, place], out_hbm.at[:, place], out_sems.at[place]))
        sends[-1].start()
    copies[3].wait()
    copies[4].wait()
    odd = position % 2 == 1
    lane = lax.broadcasted_iota(jnp.int32, own_ref.shape, 1)

    def tile_of(index):
        return par_ref[:, pl.ds(pl.multiple_of(index // 2 * tok, tok), tok)]

    def to_front(value):
        return jnp.where(odd, pltpu.roll(value, group, 1), value)

    own_ref[...] = to_front(tile_of(position))
    turned = tile_of(ctx_count - 1 - position)
    shift = 1
    while shift < tok:
        turned = jnp.where(lane & shift == 0, pltpu.roll(turned, tok - shift, 1), pltpu.roll(turned, shift, 1))
        shift *= 2
    sent_ref[...] = to_front(turned)
    for copy in copies[5:] + sends:
        copy.wait()


def filter_kernel(poles, par_ref, table_ref, out_ref, time_ref):
    blocks, group, twice = out_ref.shape[1:]
    block = twice // 2
    lanes = 128
    turned = par_ref[...].T
    ramp = lax.broadcasted_iota(jnp.int32, (8, lanes), 1).astype(jnp.float32)
    for index in range(2):
        for row in range(0, group, 8):
            rows = slice(row, row + 8)
            rate = turned[rows, index * poles : (index + 1) * poles]
            scale = turned[rows, (2 + index) * poles : (3 + index) * poles] * (jnp.sqrt(rate * (2.0 / poles)) / block)
            jump = jnp.exp(rate * -lanes)
            sums = [None] * (blocks * block // lanes)
            for pole in range(poles):
                term = scale[:, pole : pole + 1] * jnp.exp(-rate[:, pole : pole + 1] * ramp)
                step = jnp.broadcast_to(jump[:, pole : pole + 1], (8, lanes))
                for place in range(len(sums)):
                    sums[place] = term if pole == 0 else sums[place] + term
                    if place + 1 < len(sums):
                        term = term * step
            for place, total in enumerate(sums):
                lag, lane = divmod(place * lanes, block)
                first = (index * blocks + lag) * group + row
                time_ref[first : first + 8, lane : lane + lanes] = total
    sign = (1 - 2 * (lax.broadcasted_iota(jnp.int32, (group, block), 1) % 2)).astype(jnp.float32)
    for index in range(2):
        first = index * blocks * group
        high, low = halves(time_ref[first : first + blocks * group])
        spec = mul3(high, low, table_ref)
        for lag in range(blocks):
            real = spec[lag * group : (lag + 1) * group, :block]
            imag = spec[lag * group : (lag + 1) * group, block:]
            if lag > 0:
                real = real - sign * spec[(lag - 1) * group : lag * group, block:]
                imag = imag + sign * spec[(lag - 1) * group : lag * group, :block]
            out_ref[index, lag, :, :block] = real
            out_ref[index, lag, :, block:] = imag


def conv_kernel(x_ref, own_ref, paired_ref, table_ref, back_ref, out_hbm, spec_ref, high_ref, low_ref, ready_ref, sems):
    blocks, group, twice = own_ref.shape[1:]
    block = twice // 2
    rows_all = blocks * group
    tall, wide = 16, 128
    pieces = x_ref.shape[0] // blocks

    def rows_of(position):
        return jnp.concatenate(
            [
                jnp.concatenate([x_ref[m * pieces + s, position] for s in range(pieces)], axis=1)
                for m in range(blocks)
            ],
            axis=0,
        )

    def times(index, side, source, row, lane):
        data = []
        for m in range(blocks):
            rows = slice(source + m * group + row, source + m * group + row + tall)
            data.append((spec_ref[rows, lane : lane + wide], spec_ref[rows, block + lane : block + lane + wide]))
        sums = [None] * blocks
        for lag in range(blocks):
            h_ref = (own_ref, paired_ref)[side]
            f_re = h_ref[index, lag, row : row + tall, lane : lane + wide]
            f_im = h_ref[index, lag, row : row + tall, block + lane : block + lane + wide]
            for m in range(blocks - lag):
                target, (d_re, d_im) = (m + lag, data[m]) if side == 0 else (m, data[m + lag])
                if side == 0:
                    real, imag = f_re * d_re - f_im * d_im, f_re * d_im + f_im * d_re
                else:
                    real, imag = f_re * d_re + f_im * d_im, f_re * d_im - f_im * d_re
                if sums[target] is not None:
                    real, imag = sums[target][0] + real, sums[target][1] + imag
                sums[target] = (real, imag)
        return sums

    def keep(target, row, lane, sums):
        for m in range(blocks):
            rows = slice(target + m * group + row, target + m * group + row + tall)
            for part in range(2):
                cols = slice(part * block + lane, part * block + lane + wide)
                high_ref[rows, cols], low_ref[rows, cols] = halves(sums[m][part])

    chunks = [(row, lane) for row in range(0, group, tall) for lane in range(0, block, wide)]

    value = rows_of(0)
    spec_ref[:rows_all] = mul(value, table_ref[0]) + mul(value, table_ref[1])
    for row, lane in chunks:
        for side in range(2):
            keep(side * rows_all, row, lane, times(0, side, 0, row, lane))
    along = mul3(high_ref[...], low_ref[...], back_ref)
    gate = rows_of(1).astype(jnp.float32)
    high, low = halves(jnp.concatenate([gate, gate], axis=0) * along)
    spec_ref[...] = mul3(high, low, table_ref)
    for row, lane in chunks:
        ahead, back = times(1, 0, 0, row, lane), times(1, 1, rows_all, row, lane)
        keep(0, row, lane, [(a[0] + b[0], a[1] + b[1]) for a, b in zip(ahead, back)])
    post = rows_of(2)
    tok = block // pieces
    sends = []
    for part in range(2):
        rows = slice(part * rows_all // 2, (part + 1) * rows_all // 2)
        summed = mul3(high_ref[rows], low_ref[rows], back_ref)
        mixed = (post[rows].astype(jnp.float32) * summed).astype(jnp.bfloat16)
        first = part * blocks // 2 * pieces
        for m in range(blocks // 2):
            for s in range(pieces):
                ready_ref[first + m * pieces + s] = mixed[m * group : (m + 1) * group, s * tok : (s + 1) * tok]
        span = pl.ds(first, blocks // 2 * pieces)
        for copy in range(out_hbm.shape[0]):
            sends.append(pltpu.make_async_copy(ready_ref.at[span], out_hbm.at[copy, span], sems.at[part, copy]))
            sends[-1].start()
    for send in sends:
        send.wait()


def project_kernel(mixed_ref, *refs):
    w_refs, (out_ref, held_ref) = refs[:-2], refs[-2:]
    rows = w_refs[0].shape[0]
    position = lax.axis_index("ctx")
    total = mul(jnp.concatenate([w_ref[...] for w_ref in w_refs], axis=0), mixed_ref[...])
    for mask in range(len(w_refs)):
        first = pl.multiple_of((position ^ mask) * rows, rows)
        held_ref[pl.ds(first, rows)] = total[mask * rows : (mask + 1) * rows]
    out_ref[...] = held_ref[...].T.astype(jnp.bfloat16)


def whole_call(kernel, out_shape, scratch, flops, nbytes, *operands, in_hbm=0, out_hbm=()):
    results = pl.pallas_call(
        kernel,
        out_shape=out_shape,
        in_specs=[
            pl.BlockSpec(memory_space=pltpu.HBM if place < in_hbm else pltpu.VMEM) for place in range(len(operands))
        ],
        out_specs=[
            pl.BlockSpec(memory_space=pltpu.HBM if place in out_hbm else pltpu.VMEM) for place in range(len(out_shape))
        ],
        scratch_shapes=scratch,
        cost_estimate=pl.CostEstimate(flops=flops, bytes_accessed=nbytes, transcendentals=0),
        compiler_params=pltpu.CompilerParams(vmem_limit_bytes=None if in_hbm else 32 * 2**20),
    )(*operands)
    return results if len(out_shape) > 1 else results[0]


def blocked(x_gate, x_post, values, decay, residue, w_out):
    tok, width = x_gate.shape
    ctx_count = lax.axis_size("ctx")
    tp_count = lax.axis_size("tp")
    group = width // ctx_count
    poles = decay.shape[2]
    block = 2 * tok
    blocks = tok * ctx_count // block
    rows, channels = w_out.shape
    half = 2 * poles

    packed, own, mirrored, table, back_table = whole_call(
        pack_kernel,
        (
            jax.ShapeDtypeStruct((ctx_count, 3, group, tok), jnp.bfloat16),
            jax.ShapeDtypeStruct((2 * half, tok), jnp.float32),
            jax.ShapeDtypeStruct((2 * half, tok), jnp.float32),
            jax.ShapeDtypeStruct((2, block, 2 * block), jnp.bfloat16),
            jax.ShapeDtypeStruct((2, 2 * block, block), jnp.bfloat16),
        ),
        [
            pltpu.VMEM((3, tok, width), jnp.bfloat16),
            pltpu.VMEM((2 * half, width), jnp.float32),
            pltpu.VMEM((ctx_count, 3, group, tok), jnp.bfloat16),
            pltpu.SemaphoreType.DMA((7,)),
            pltpu.SemaphoreType.DMA((3,)),
        ],
        0,
        6 * tok * width * 2,
        x_gate,
        values,
        x_post,
        jnp.swapaxes(decay, 1, 2).reshape(half, width),
        jnp.swapaxes(residue, 1, 2).reshape(half, width),
        *block_tables(block),
        in_hbm=7,
        out_hbm=(0, 3, 4),
    )
    paired = lax.ppermute(mirrored, "tp", [(z, tp_count - 1 - z) for z in range(tp_count)])
    received = lax.all_to_all(packed, "ctx", split_axis=0, concat_axis=0, tiled=True)

    def spectra(params):
        return whole_call(
            functools.partial(filter_kernel, poles),
            (jax.ShapeDtypeStruct((2, blocks, group, 2 * block), jnp.float32),),
            [pltpu.VMEM((2 * blocks * group, block), jnp.float32)],
            2 * 2 * blocks * group * block * 2 * block * 3,
            2 * blocks * group * 2 * block * 4,
            params,
            table,
        )

    own_spectra, paired_spectra = spectra(own), spectra(paired)
    w_x, w_y = partner(w_out, "ctx", 1), partner(w_out, "ctx", 2)
    w_late, w_x, w_y, paired_spectra = lax.optimization_barrier((w_out, w_x, w_y, paired_spectra))
    w_blocks = {0: w_out, 2: w_x, 4: w_y, 6: lax.ppermute(w_late, "ctx", [(i, i ^ 6) for i in range(ctx_count)])}
    w_blocks[1] = partner(w_late, "ctx", 0)
    for mask in (2, 4, 6):
        w_blocks[mask + 1] = partner(w_blocks[mask], "ctx", 0)
    mixed = whole_call(
        conv_kernel,
        (jax.ShapeDtypeStruct((tp_count, ctx_count, group, tok), jnp.bfloat16),),
        [
            pltpu.VMEM((2 * blocks * group, 2 * block), jnp.float32),
            pltpu.VMEM((2 * blocks * group, 2 * block), jnp.bfloat16),
            pltpu.VMEM((2 * blocks * group, 2 * block), jnp.bfloat16),
            pltpu.VMEM((ctx_count, group, tok), jnp.bfloat16),
            pltpu.SemaphoreType.DMA((2, tp_count)),
        ],
        2 * 6 * blocks * group * block * 2 * block * 3,
        4 * blocks * group * 2 * block * 4,
        received,
        own_spectra,
        paired_spectra,
        table,
        back_table,
        out_hbm=(0,),
    )
    every = lax.all_to_all(
        mixed.reshape(tp_count * ctx_count, group, tok), ("tp", "ctx"), split_axis=0, concat_axis=0, tiled=True
    ).reshape(channels, tok)
    return whole_call(
        project_kernel,
        (jax.ShapeDtypeStruct((tok, rows * ctx_count), jnp.bfloat16),),
        [pltpu.VMEM((rows * ctx_count, tok), jnp.float32)],
        2 * tok * rows * ctx_count * channels,
        2 * rows * ctx_count * channels,
        every,
        *[w_blocks[mask] for mask in range(ctx_count)],
    )


def local(x_gate, x_post, values, decay, residue, w_out):
    tok, width = x_gate.shape
    ctx_count = lax.axis_size("ctx")
    if tok == 128 and width == 512 and ctx_count == 8 and lax.axis_size("tp") == 4:
        return blocked(x_gate, x_post, values, decay, residue, w_out)
    return general(x_gate, x_post, values, decay, residue, w_out)


def solution(mesh):
    in_specs = (
        P("ctx", "tp"),
        P("ctx", "tp"),
        P("ctx", "tp"),
        P(None, "tp", None),
        P(None, "tp", None),
        P(("tp", "ctx"), None),
    )
    out_specs = P("ctx", "tp")
    return jax.shard_map(local, mesh=mesh, in_specs=in_specs, out_specs=out_specs, check_vma=False)
```

```python
import functools
import math

import jax
import jax.numpy as jnp
import ml_dtypes
import numpy as np
from jax import lax
from jax.experimental import pallas as pl
from jax.experimental.pallas import tpu as pltpu
from jax.sharding import PartitionSpec as P

HIGHEST = lax.Precision.HIGHEST


def partner(value, axis, bit):
    mask = 2**bit
    pairs = [(source, source ^ mask) for source in range(lax.axis_size(axis))]
    return lax.ppermute(value, axis, pairs)


def radices(length_all):
    last_radix = min(128, length_all // 4)
    first_radix = min(32, length_all // last_radix)
    return (first_radix, length_all // (first_radix * last_radix), last_radix)


def rotation(row_count, col_count, modulus):
    product = (
        lax.broadcasted_iota(jnp.int32, (row_count, col_count), 0)
        * lax.broadcasted_iota(jnp.int32, (row_count, col_count), 1)
        % modulus
    )
    angle = product.astype(jnp.float32) * (2.0 * math.pi / modulus)
    return (jnp.cos(angle), -jnp.sin(angle))


def tables(radix_sizes):
    first_radix, mid_radix, last_radix = radix_sizes
    length_all = first_radix * mid_radix * last_radix
    outer_real, outer_imag = rotation(first_radix, first_radix, first_radix)
    mid_real, mid_imag = rotation(mid_radix, mid_radix, mid_radix)
    last_real, last_imag = rotation(last_radix, last_radix, last_radix)
    twist_real, twist_imag = rotation(first_radix, mid_radix * last_radix, length_all)
    twist_real = twist_real.reshape(first_radix, mid_radix, last_radix)
    twist_imag = twist_imag.reshape(first_radix, mid_radix, last_radix)
    inner_real, inner_imag = rotation(mid_radix, last_radix, mid_radix * last_radix)
    return (
        outer_real,
        outer_imag,
        mid_real,
        mid_imag,
        last_real,
        last_imag,
        twist_real,
        twist_imag,
        inner_real,
        inner_imag,
    )


def apply_matrix(pattern, real_part, imag_part, matrix_real, matrix_imag):
    out_real = jnp.einsum(pattern, real_part, matrix_real, precision=HIGHEST) - jnp.einsum(
        pattern, imag_part, matrix_imag, precision=HIGHEST
    )
    out_imag = jnp.einsum(pattern, real_part, matrix_imag, precision=HIGHEST) + jnp.einsum(
        pattern, imag_part, matrix_real, precision=HIGHEST
    )
    return (out_real, out_imag)


def complex_times(left_real, left_imag, right_real, right_imag):
    return (
        left_real * right_real - left_imag * right_imag,
        left_real * right_imag + left_imag * right_real,
    )


def forward(real_part, imag_part, table_set, radix_sizes):
    first_radix, mid_radix, last_radix = radix_sizes
    half_first = first_radix // 2
    batch_rows = real_part.shape[0]
    (
        outer_real,
        outer_imag,
        mid_real,
        mid_imag,
        last_real,
        last_imag,
        twist_real,
        twist_imag,
        inner_real,
        inner_imag,
    ) = table_set
    real_part = real_part.reshape(batch_rows, half_first, mid_radix, last_radix)
    imag_part = imag_part.reshape(batch_rows, half_first, mid_radix, last_radix)
    real_part, imag_part = apply_matrix(
        "banm,ak->bknm", real_part, imag_part, outer_real[:half_first], outer_imag[:half_first]
    )
    real_part, imag_part = complex_times(real_part, imag_part, twist_real, twist_imag)
    real_part, imag_part = apply_matrix("bknm,nj->bkjm", real_part, imag_part, mid_real, mid_imag)
    real_part, imag_part = complex_times(real_part, imag_part, inner_real, inner_imag)
    return apply_matrix("bkjm,mq->bkjq", real_part, imag_part, last_real, last_imag)


def inverse(real_part, imag_part, table_set, radix_sizes):
    first_radix, mid_radix, last_radix = radix_sizes
    half_first = first_radix // 2
    batch_rows = real_part.shape[0]
    (
        outer_real,
        outer_imag,
        mid_real,
        mid_imag,
        last_real,
        last_imag,
        twist_real,
        twist_imag,
        inner_real,
        inner_imag,
    ) = table_set
    real_part, imag_part = apply_matrix(
        "bkjq,mq->bkjm", real_part, imag_part, last_real / last_radix, -last_imag / last_radix
    )
    real_part, imag_part = complex_times(real_part, imag_part, inner_real, -inner_imag)
    real_part, imag_part = apply_matrix(
        "bkjm,nj->bknm", real_part, imag_part, mid_real / mid_radix, -mid_imag / mid_radix
    )
    real_part, imag_part = complex_times(real_part, imag_part, twist_real, -twist_imag)
    matrix_real = outer_real[:half_first] / first_radix
    matrix_imag = -outer_imag[:half_first] / first_radix
    out_real, out_imag = apply_matrix(
        "bknm,ak->banm", real_part, imag_part, matrix_real, matrix_imag
    )
    return (out_real.reshape(batch_rows, -1), out_imag.reshape(batch_rows, -1))


def spectrum(decay_rows, residue_rows, radix_sizes, seq_length):
    first_radix, mid_radix, last_radix = radix_sizes
    length_all = first_radix * mid_radix * last_radix
    poles = decay_rows.shape[1]
    shape_all = (first_radix, mid_radix, last_radix)
    frequency = (
        lax.broadcasted_iota(jnp.int32, shape_all, 0)
        + first_radix * lax.broadcasted_iota(jnp.int32, shape_all, 1)
        + first_radix * mid_radix * lax.broadcasted_iota(jnp.int32, shape_all, 2)
    )
    half_angle = frequency.astype(jnp.float32) * (math.pi / length_all)
    sin_half = jnp.sin(half_angle)
    sin_full = jnp.sin(2.0 * half_angle)
    parity_sign = (1 - 2 * (frequency % 2)).astype(jnp.float32)

    def add_pole(pole_index, running):
        run_real, run_imag = running
        rate_col = lax.dynamic_slice_in_dim(decay_rows, pole_index, 1, 1).reshape(-1, 1, 1, 1)
        weight = lax.dynamic_slice_in_dim(residue_rows, pole_index, 1, 1).reshape(
            -1, 1, 1, 1
        ) * jnp.sqrt(2.0 * rate_col / poles)
        retained = jnp.exp(-rate_col)
        den_real = -jnp.expm1(-rate_col) + 2.0 * retained * sin_half * sin_half
        den_imag = retained * sin_full
        pole_scale = (
            weight
            * (1.0 - jnp.exp(-rate_col * seq_length) * parity_sign)
            / (den_real * den_real + den_imag * den_imag)
        )
        return (run_real + pole_scale * den_real, run_imag - pole_scale * den_imag)

    zeros_all = jnp.zeros((decay_rows.shape[0],) + shape_all, jnp.float32)
    return lax.fori_loop(0, poles, add_pole, (zeros_all, zeros_all))


def general(x_gate, x_post, values, decay, residue, w_out):
    tok_rows, block_width = x_gate.shape
    ctx_count = lax.axis_size("ctx")
    tp_count = lax.axis_size("tp")
    chan_group = block_width // ctx_count
    seq_length = tok_rows * ctx_count
    radix_sizes = radices(2 * seq_length)
    table_set = tables(radix_sizes)
    first_row = lax.axis_index("ctx") * chan_group
    own_rate = lax.dynamic_slice_in_dim(decay, first_row, chan_group, 1)
    own_residue = lax.dynamic_slice_in_dim(residue, first_row, chan_group, 1)
    own_spec = [
        spectrum(own_rate[filter_index], own_residue[filter_index], radix_sizes, seq_length)
        for filter_index in range(2)
    ]
    forward_rows = [x_gate, values] + [x_post]
    row_count = len(forward_rows)
    base_rows = jnp.stack(forward_rows)
    copied = base_rows
    for bit_index in range(tp_count.bit_length() - 1):
        copied = partner(copied, "tp", bit_index)
    sent_rows = jnp.concatenate([base_rows, copied[:, :, ::-1]], axis=0)
    received = lax.all_to_all(
        jnp.swapaxes(sent_rows, 1, 2), "ctx", split_axis=1, concat_axis=2, tiled=True
    )
    gate_fwd = received[0].astype(jnp.float32)
    value_fwd = received[1].astype(jnp.float32)
    mirrored = received[row_count:, :, ::-1].astype(jnp.float32)
    spec_real, spec_imag = forward(value_fwd, mirrored[1], table_set, radix_sizes)
    spec_real, spec_imag = complex_times(spec_real, spec_imag, own_spec[0][0], own_spec[0][1])
    along_fwd, along_rev = inverse(spec_real, spec_imag, table_set, radix_sizes)
    spec_real, spec_imag = forward(
        gate_fwd * along_fwd, mirrored[0] * along_rev, table_set, radix_sizes
    )
    spec_real, spec_imag = complex_times(spec_real, spec_imag, own_spec[1][0], own_spec[1][1])
    sum_fwd, sum_rev = inverse(spec_real, spec_imag, table_set, radix_sizes)
    sum_fwd = received[2].astype(jnp.float32) * sum_fwd
    sum_rev = mirrored[2] * sum_rev
    results = jnp.stack([sum_fwd, sum_rev[:, ::-1]])
    returned = lax.all_to_all(
        results.astype(jnp.bfloat16), "ctx", split_axis=2, concat_axis=1, tiled=True
    ).astype(results.dtype)
    flipped = returned[1, ::-1, :]
    for bit_index in range(tp_count.bit_length() - 1):
        flipped = partner(flipped.astype(jnp.bfloat16), "tp", bit_index).astype(flipped.dtype)
    total_rows = returned[0] + flipped
    total_rows = total_rows.T
    mixed_rows = total_rows.astype(jnp.bfloat16)
    whole_rows = lax.all_gather(mixed_rows, "tp", axis=1, tiled=True)
    projected = lax.dot_general(
        whole_rows,
        lax.all_gather(w_out, "ctx", axis=0, tiled=True),
        (((1,), (1,)), ((), ())),
        preferred_element_type=jnp.float32,
    )
    return projected.astype(jnp.bfloat16)


def cycle(row_factor, col_factor, modulus):
    angle = (row_factor * col_factor % modulus).astype(jnp.float32) * (2.0 * math.pi / modulus)
    return jnp.cos(angle), jnp.sin(angle)


def make_tables(table_ref, back_ref):
    block = table_ref.shape[1]
    modulus = 4 * block
    coarse = 16
    rows = lax.broadcasted_iota(jnp.int32, (coarse, block), 0)
    cols = lax.broadcasted_iota(jnp.int32, (coarse, block), 1)

    def fill(ref, big, small, put):
        for place in range(block // coarse):
            big_cos, big_sin = (part[place : place + 1] for part in big)
            put(ref, place, big_cos * small[0] - big_sin * small[1], -(big_sin * small[0] + big_cos * small[1]))

    def put_freq(ref, place, cos, sin):
        span = slice(place * coarse, (place + 1) * coarse)
        ref[0, span, :block], ref[1, span, :block] = halves(cos)
        ref[0, span, block:], ref[1, span, block:] = halves(sin)

    def put_time(ref, place, cos, sin):
        span = slice(place * coarse, (place + 1) * coarse)
        ref[0, span], ref[1, span] = halves(cos)
        span = slice(block + place * coarse, block + (place + 1) * coarse)
        ref[0, span], ref[1, span] = halves(sin)

    fill(table_ref, cycle(coarse * rows, 2 * cols + 1, modulus), cycle(rows, 2 * cols + 1, modulus), put_freq)
    fill(back_ref, cycle(2 * coarse * rows, cols, modulus), cycle(2 * rows + 1, cols, modulus), put_time)


def halves(value):
    high = value.astype(jnp.bfloat16)
    return high, (value - high.astype(jnp.float32)).astype(jnp.bfloat16)


def mul(left, right):
    return jnp.dot(left, right, preferred_element_type=jnp.float32)


def mul3(high, low, table_ref):
    return mul(high, table_ref[0]) + (mul(low, table_ref[0]) + mul(high, table_ref[1]))


def pack_kernel(
    gate_hbm, value_hbm, post_hbm, decay_hbm, residue_hbm,
    out_hbm, own_ref, sent_ref, held_ref, par_ref, ready_ref, sems, out_sems,
):
    ctx_count, _, group, tok = out_hbm.shape
    width = gate_hbm.shape[1]
    half = decay_hbm.shape[0]
    position = lax.axis_index("ctx")
    pairs = [(source, held_ref.at[place]) for place, source in enumerate((value_hbm, gate_hbm, post_hbm))]
    pairs += [(decay_hbm, par_ref.at[:half]), (residue_hbm, par_ref.at[half:])]
    copies = [pltpu.make_async_copy(*pair, sems.at[place]) for place, pair in enumerate(pairs)]
    for copy in copies:
        copy.start()
    sends = []
    for place, copy in enumerate(copies[:3]):
        copy.wait()
        for first in range(0, width, tok):
            turned = held_ref[place, :, first : first + tok].T
            for part in range(tok // group):
                ready_ref[first // group + part, place] = turned[part * group : (part + 1) * group]
        sends.append(pltpu.make_async_copy(ready_ref.at[:, place], out_hbm.at[:, place], out_sems.at[place]))
        sends[-1].start()
    copies[3].wait()
    copies[4].wait()
    odd = position % 2 == 1
    lane = lax.broadcasted_iota(jnp.int32, own_ref.shape, 1)

    def tile_of(index):
        return par_ref[:, pl.ds(pl.multiple_of(index // 2 * tok, tok), tok)]

    def to_front(value):
        return jnp.where(odd, pltpu.roll(value, group, 1), value)

    own_ref[...] = to_front(tile_of(position))
    turned = tile_of(ctx_count - 1 - position)
    shift = 1
    while shift < tok:
        turned = jnp.where(lane & shift == 0, pltpu.roll(turned, tok - shift, 1), pltpu.roll(turned, shift, 1))
        shift *= 2
    sent_ref[...] = to_front(turned)
    for copy in sends:
        copy.wait()


def own_filter_kernel(poles, par_ref, out_ref, table_ref, back_ref, time_ref):
    make_tables(table_ref, back_ref)
    filter_kernel(poles, par_ref, table_ref, out_ref, time_ref)


def filter_kernel(poles, par_ref, table_ref, out_ref, time_ref):
    blocks, group, twice = out_ref.shape[1:]
    block = twice // 2
    lanes = 128
    turned = par_ref[...].T
    ramp = lax.broadcasted_iota(jnp.int32, (8, lanes), 1).astype(jnp.float32)
    for index in range(2):
        for row in range(0, group, 8):
            rows = slice(row, row + 8)
            rate = turned[rows, index * poles : (index + 1) * poles]
            scale = turned[rows, (2 + index) * poles : (3 + index) * poles] * (jnp.sqrt(rate * (2.0 / poles)) / block)
            jump = jnp.exp(rate * -lanes)
            sums = [None] * (blocks * block // lanes)
            for pole in range(poles):
                term = scale[:, pole : pole + 1] * jnp.exp(-rate[:, pole : pole + 1] * ramp)
                step = jnp.broadcast_to(jump[:, pole : pole + 1], (8, lanes))
                for place in range(len(sums)):
                    sums[place] = term if pole == 0 else sums[place] + term
                    if place + 1 < len(sums):
                        term = term * step
            for place, total in enumerate(sums):
                lag, lane = divmod(place * lanes, block)
                first = (index * blocks + lag) * group + row
                time_ref[first : first + 8, lane : lane + lanes] = total
    sign = (1 - 2 * (lax.broadcasted_iota(jnp.int32, (group, block), 1) % 2)).astype(jnp.float32)
    for index in range(2):
        first = index * blocks * group
        high, low = halves(time_ref[first : first + blocks * group])
        spec = mul3(high, low, table_ref)
        for lag in range(blocks):
            real = spec[lag * group : (lag + 1) * group, :block]
            imag = spec[lag * group : (lag + 1) * group, block:]
            if lag > 0:
                real = real - sign * spec[(lag - 1) * group : lag * group, block:]
                imag = imag + sign * spec[(lag - 1) * group : lag * group, :block]
            out_ref[index, lag, :, :block] = real
            out_ref[index, lag, :, block:] = imag


def conv_kernel(x_ref, own_ref, paired_ref, table_ref, back_ref, out_hbm, spec_ref, high_ref, low_ref, ready_ref, sems):
    blocks, group, twice = own_ref.shape[1:]
    block = twice // 2
    rows_all = blocks * group
    tall, wide = 16, 128
    pieces = x_ref.shape[0] // blocks

    def rows_of(position):
        return jnp.concatenate(
            [
                jnp.concatenate([x_ref[m * pieces + s, position] for s in range(pieces)], axis=1)
                for m in range(blocks)
            ],
            axis=0,
        )

    def times(index, side, source, row, lane):
        data = []
        for m in range(blocks):
            rows = slice(source + m * group + row, source + m * group + row + tall)
            data.append((spec_ref[rows, lane : lane + wide], spec_ref[rows, block + lane : block + lane + wide]))
        sums = [None] * blocks
        for lag in range(blocks):
            h_ref = (own_ref, paired_ref)[side]
            f_re = h_ref[index, lag, row : row + tall, lane : lane + wide]
            f_im = h_ref[index, lag, row : row + tall, block + lane : block + lane + wide]
            for m in range(blocks - lag):
                target, (d_re, d_im) = (m + lag, data[m]) if side == 0 else (m, data[m + lag])
                if side == 0:
                    real, imag = f_re * d_re - f_im * d_im, f_re * d_im + f_im * d_re
                else:
                    real, imag = f_re * d_re + f_im * d_im, f_re * d_im - f_im * d_re
                if sums[target] is not None:
                    real, imag = sums[target][0] + real, sums[target][1] + imag
                sums[target] = (real, imag)
        return sums

    def keep(target, row, lane, sums):
        for m in range(blocks):
            rows = slice(target + m * group + row, target + m * group + row + tall)
            for part in range(2):
                cols = slice(part * block + lane, part * block + lane + wide)
                high_ref[rows, cols], low_ref[rows, cols] = halves(sums[m][part])

    chunks = [(row, lane) for row in range(0, group, tall) for lane in range(0, block, wide)]

    value = rows_of(0)
    spec_ref[:rows_all] = mul(value, table_ref[0]) + mul(value, table_ref[1])
    for row, lane in chunks:
        for side in range(2):
            keep(side * rows_all, row, lane, times(0, side, 0, row, lane))
    along = mul3(high_ref[...], low_ref[...], back_ref)
    gate = rows_of(1).astype(jnp.float32)
    high, low = halves(jnp.concatenate([gate, gate], axis=0) * along)
    spec_ref[...] = mul3(high, low, table_ref)
    for row, lane in chunks:
        ahead, back = times(1, 0, 0, row, lane), times(1, 1, rows_all, row, lane)
        keep(0, row, lane, [(a[0] + b[0], a[1] + b[1]) for a, b in zip(ahead, back)])
    post = rows_of(2)
    tok = block // pieces
    sends = []
    for part in range(2):
        rows = slice(part * rows_all // 2, (part + 1) * rows_all // 2)
        summed = mul3(high_ref[rows], low_ref[rows], back_ref)
        mixed = (post[rows].astype(jnp.float32) * summed).astype(jnp.bfloat16)
        first = part * blocks // 2 * pieces
        for m in range(blocks // 2):
            for s in range(pieces):
                ready_ref[first + m * pieces + s] = mixed[m * group : (m + 1) * group, s * tok : (s + 1) * tok]
        span = pl.ds(first, blocks // 2 * pieces)
        for copy in range(out_hbm.shape[0]):
            sends.append(pltpu.make_async_copy(ready_ref.at[span], out_hbm.at[copy, span], sems.at[part, copy]))
            sends[-1].start()
    for send in sends:
        send.wait()


def project_kernel(mixed_ref, *refs):
    w_refs, (out_ref, held_ref) = refs[:-2], refs[-2:]
    rows = w_refs[0].shape[0]
    position = lax.axis_index("ctx")
    total = mul(jnp.concatenate([w_ref[...] for w_ref in w_refs], axis=0), mixed_ref[...])
    for mask in range(len(w_refs)):
        first = pl.multiple_of((position ^ mask) * rows, rows)
        held_ref[pl.ds(first, rows)] = total[mask * rows : (mask + 1) * rows]
    out_ref[...] = held_ref[...].T.astype(jnp.bfloat16)


def whole_call(kernel, out_shape, scratch, flops, nbytes, *operands, in_hbm=0, out_hbm=()):
    results = pl.pallas_call(
        kernel,
        out_shape=out_shape,
        in_specs=[
            pl.BlockSpec(memory_space=pltpu.HBM if place < in_hbm else pltpu.VMEM) for place in range(len(operands))
        ],
        out_specs=[
            pl.BlockSpec(memory_space=pltpu.HBM if place in out_hbm else pltpu.VMEM) for place in range(len(out_shape))
        ],
        scratch_shapes=scratch,
        cost_estimate=pl.CostEstimate(flops=flops, bytes_accessed=nbytes, transcendentals=0),
        compiler_params=pltpu.CompilerParams(vmem_limit_bytes=None if in_hbm else 32 * 2**20),
    )(*operands)
    return results if len(out_shape) > 1 else results[0]


def blocked(x_gate, x_post, values, decay, residue, w_out):
    tok, width = x_gate.shape
    ctx_count = lax.axis_size("ctx")
    tp_count = lax.axis_size("tp")
    group = width // ctx_count
    poles = decay.shape[2]
    block = 2 * tok
    blocks = tok * ctx_count // block
    rows, channels = w_out.shape
    half = 2 * poles

    packed, own, mirrored = whole_call(
        pack_kernel,
        (
            jax.ShapeDtypeStruct((ctx_count, 3, group, tok), jnp.bfloat16),
            jax.ShapeDtypeStruct((2 * half, tok), jnp.float32),
            jax.ShapeDtypeStruct((2 * half, tok), jnp.float32),
        ),
        [
            pltpu.VMEM((3, tok, width), jnp.bfloat16),
            pltpu.VMEM((2 * half, width), jnp.float32),
            pltpu.VMEM((ctx_count, 3, group, tok), jnp.bfloat16),
            pltpu.SemaphoreType.DMA((5,)),
            pltpu.SemaphoreType.DMA((3,)),
        ],
        0,
        6 * tok * width * 2,
        x_gate,
        values,
        x_post,
        jnp.swapaxes(decay, 1, 2).reshape(half, width),
        jnp.swapaxes(residue, 1, 2).reshape(half, width),
        in_hbm=5,
        out_hbm=(0,),
    )
    paired = lax.ppermute(mirrored, "tp", [(z, tp_count - 1 - z) for z in range(tp_count)])
    received = lax.all_to_all(packed, "ctx", split_axis=0, concat_axis=0, tiled=True)

    w_x, w_y = partner(w_out, "ctx", 1), partner(w_out, "ctx", 2)
    w_late, w_x, w_y, own = lax.optimization_barrier((w_out, w_x, w_y, own))
    w_far = lax.ppermute(w_late, "ctx", [(i, i ^ 6) for i in range(ctx_count)])

    spectra_shape = jax.ShapeDtypeStruct((2, blocks, group, 2 * block), jnp.float32)
    spectra_cost = (2 * 2 * blocks * group * block * 2 * block * 3, 2 * blocks * group * 2 * block * 4)
    own_spectra, table, back_table = whole_call(
        functools.partial(own_filter_kernel, poles),
        (
            spectra_shape,
            jax.ShapeDtypeStruct((2, block, 2 * block), jnp.bfloat16),
            jax.ShapeDtypeStruct((2, 2 * block, block), jnp.bfloat16),
        ),
        [pltpu.VMEM((2 * blocks * group, block), jnp.float32)],
        *spectra_cost,
        own,
    )
    paired_spectra = whole_call(
        functools.partial(filter_kernel, poles),
        (spectra_shape,),
        [pltpu.VMEM((2 * blocks * group, block), jnp.float32)],
        *spectra_cost,
        paired,
        table,
    )
    mixed = whole_call(
        conv_kernel,
        (jax.ShapeDtypeStruct((tp_count, ctx_count, group, tok), jnp.bfloat16),),
        [
            pltpu.VMEM((2 * blocks * group, 2 * block), jnp.float32),
            pltpu.VMEM((2 * blocks * group, 2 * block), jnp.bfloat16),
            pltpu.VMEM((2 * blocks * group, 2 * block), jnp.bfloat16),
            pltpu.VMEM((ctx_count, group, tok), jnp.bfloat16),
            pltpu.SemaphoreType.DMA((2, tp_count)),
        ],
        2 * 6 * blocks * group * block * 2 * block * 3,
        4 * blocks * group * 2 * block * 4,
        received,
        own_spectra,
        paired_spectra,
        table,
        back_table,
        out_hbm=(0,),
    )
    mixed, w_far = lax.optimization_barrier((mixed, w_far))
    w_blocks = {0: w_late, 2: w_x, 4: w_y, 6: w_far}
    for mask in range(0, ctx_count, 2):
        w_blocks[mask + 1] = partner(w_blocks[mask], "ctx", 0)
    every = lax.all_to_all(
        mixed.reshape(tp_count * ctx_count, group, tok), ("tp", "ctx"), split_axis=0, concat_axis=0, tiled=True
    ).reshape(channels, tok)
    return whole_call(
        project_kernel,
        (jax.ShapeDtypeStruct((tok, rows * ctx_count), jnp.bfloat16),),
        [pltpu.VMEM((rows * ctx_count, tok), jnp.float32)],
        2 * tok * rows * ctx_count * channels,
        2 * rows * ctx_count * channels,
        every,
        *[w_blocks[mask] for mask in range(ctx_count)],
    )


def local(x_gate, x_post, values, decay, residue, w_out):
    tok, width = x_gate.shape
    ctx_count = lax.axis_size("ctx")
    if tok == 128 and width == 512 and ctx_count == 8 and lax.axis_size("tp") == 4:
        return blocked(x_gate, x_post, values, decay, residue, w_out)
    return general(x_gate, x_post, values, decay, residue, w_out)


def solution(mesh):
    in_specs = (
        P("ctx", "tp"),
        P("ctx", "tp"),
        P("ctx", "tp"),
        P(None, "tp", None),
        P(None, "tp", None),
        P(("tp", "ctx"), None),
    )
    out_specs = P("ctx", "tp")
    return jax.shard_map(local, mesh=mesh, in_specs=in_specs, out_specs=out_specs, check_vma=False)
```

```python
import functools
import math

import jax
import jax.numpy as jnp
from jax import lax
from jax.experimental import pallas as pl
from jax.experimental.pallas import tpu as pltpu
from jax.sharding import PartitionSpec as P

HIGHEST = lax.Precision.HIGHEST


def partner(value, axis, bit):
    mask = 2**bit
    pairs = [(source, source ^ mask) for source in range(lax.axis_size(axis))]
    return lax.ppermute(value, axis, pairs)


def radices(length_all):
    last_radix = min(128, length_all // 4)
    first_radix = min(32, length_all // last_radix)
    return (first_radix, length_all // (first_radix * last_radix), last_radix)


def rotation(row_count, col_count, modulus):
    product = (
        lax.broadcasted_iota(jnp.int32, (row_count, col_count), 0)
        * lax.broadcasted_iota(jnp.int32, (row_count, col_count), 1)
        % modulus
    )
    angle = product.astype(jnp.float32) * (2.0 * math.pi / modulus)
    return (jnp.cos(angle), -jnp.sin(angle))


def tables(radix_sizes):
    first_radix, mid_radix, last_radix = radix_sizes
    length_all = first_radix * mid_radix * last_radix
    outer_real, outer_imag = rotation(first_radix, first_radix, first_radix)
    mid_real, mid_imag = rotation(mid_radix, mid_radix, mid_radix)
    last_real, last_imag = rotation(last_radix, last_radix, last_radix)
    twist_real, twist_imag = rotation(first_radix, mid_radix * last_radix, length_all)
    twist_real = twist_real.reshape(first_radix, mid_radix, last_radix)
    twist_imag = twist_imag.reshape(first_radix, mid_radix, last_radix)
    inner_real, inner_imag = rotation(mid_radix, last_radix, mid_radix * last_radix)
    return (
        outer_real,
        outer_imag,
        mid_real,
        mid_imag,
        last_real,
        last_imag,
        twist_real,
        twist_imag,
        inner_real,
        inner_imag,
    )


def apply_matrix(pattern, real_part, imag_part, matrix_real, matrix_imag):
    out_real = jnp.einsum(pattern, real_part, matrix_real, precision=HIGHEST) - jnp.einsum(
        pattern, imag_part, matrix_imag, precision=HIGHEST
    )
    out_imag = jnp.einsum(pattern, real_part, matrix_imag, precision=HIGHEST) + jnp.einsum(
        pattern, imag_part, matrix_real, precision=HIGHEST
    )
    return (out_real, out_imag)


def complex_times(left_real, left_imag, right_real, right_imag):
    return (
        left_real * right_real - left_imag * right_imag,
        left_real * right_imag + left_imag * right_real,
    )


def forward(real_part, imag_part, table_set, radix_sizes):
    first_radix, mid_radix, last_radix = radix_sizes
    half_first = first_radix // 2
    batch_rows = real_part.shape[0]
    (
        outer_real,
        outer_imag,
        mid_real,
        mid_imag,
        last_real,
        last_imag,
        twist_real,
        twist_imag,
        inner_real,
        inner_imag,
    ) = table_set
    real_part = real_part.reshape(batch_rows, half_first, mid_radix, last_radix)
    imag_part = imag_part.reshape(batch_rows, half_first, mid_radix, last_radix)
    real_part, imag_part = apply_matrix(
        "banm,ak->bknm", real_part, imag_part, outer_real[:half_first], outer_imag[:half_first]
    )
    real_part, imag_part = complex_times(real_part, imag_part, twist_real, twist_imag)
    real_part, imag_part = apply_matrix("bknm,nj->bkjm", real_part, imag_part, mid_real, mid_imag)
    real_part, imag_part = complex_times(real_part, imag_part, inner_real, inner_imag)
    return apply_matrix("bkjm,mq->bkjq", real_part, imag_part, last_real, last_imag)


def inverse(real_part, imag_part, table_set, radix_sizes):
    first_radix, mid_radix, last_radix = radix_sizes
    half_first = first_radix // 2
    batch_rows = real_part.shape[0]
    (
        outer_real,
        outer_imag,
        mid_real,
        mid_imag,
        last_real,
        last_imag,
        twist_real,
        twist_imag,
        inner_real,
        inner_imag,
    ) = table_set
    real_part, imag_part = apply_matrix(
        "bkjq,mq->bkjm", real_part, imag_part, last_real / last_radix, -last_imag / last_radix
    )
    real_part, imag_part = complex_times(real_part, imag_part, inner_real, -inner_imag)
    real_part, imag_part = apply_matrix(
        "bkjm,nj->bknm", real_part, imag_part, mid_real / mid_radix, -mid_imag / mid_radix
    )
    real_part, imag_part = complex_times(real_part, imag_part, twist_real, -twist_imag)
    matrix_real = outer_real[:half_first] / first_radix
    matrix_imag = -outer_imag[:half_first] / first_radix
    out_real, out_imag = apply_matrix(
        "bknm,ak->banm", real_part, imag_part, matrix_real, matrix_imag
    )
    return (out_real.reshape(batch_rows, -1), out_imag.reshape(batch_rows, -1))


def spectrum(decay_rows, residue_rows, radix_sizes, seq_length):
    first_radix, mid_radix, last_radix = radix_sizes
    length_all = first_radix * mid_radix * last_radix
    poles = decay_rows.shape[1]
    shape_all = (first_radix, mid_radix, last_radix)
    frequency = (
        lax.broadcasted_iota(jnp.int32, shape_all, 0)
        + first_radix * lax.broadcasted_iota(jnp.int32, shape_all, 1)
        + first_radix * mid_radix * lax.broadcasted_iota(jnp.int32, shape_all, 2)
    )
    half_angle = frequency.astype(jnp.float32) * (math.pi / length_all)
    sin_half = jnp.sin(half_angle)
    sin_full = jnp.sin(2.0 * half_angle)
    parity_sign = (1 - 2 * (frequency % 2)).astype(jnp.float32)

    def add_pole(pole_index, running):
        run_real, run_imag = running
        rate_col = lax.dynamic_slice_in_dim(decay_rows, pole_index, 1, 1).reshape(-1, 1, 1, 1)
        weight = lax.dynamic_slice_in_dim(residue_rows, pole_index, 1, 1).reshape(
            -1, 1, 1, 1
        ) * jnp.sqrt(2.0 * rate_col / poles)
        retained = jnp.exp(-rate_col)
        den_real = -jnp.expm1(-rate_col) + 2.0 * retained * sin_half * sin_half
        den_imag = retained * sin_full
        pole_scale = (
            weight
            * (1.0 - jnp.exp(-rate_col * seq_length) * parity_sign)
            / (den_real * den_real + den_imag * den_imag)
        )
        return (run_real + pole_scale * den_real, run_imag - pole_scale * den_imag)

    zeros_all = jnp.zeros((decay_rows.shape[0],) + shape_all, jnp.float32)
    return lax.fori_loop(0, poles, add_pole, (zeros_all, zeros_all))


def general(x_gate, x_post, values, decay, residue, w_out):
    tok_rows, block_width = x_gate.shape
    ctx_count = lax.axis_size("ctx")
    tp_count = lax.axis_size("tp")
    chan_group = block_width // ctx_count
    seq_length = tok_rows * ctx_count
    radix_sizes = radices(2 * seq_length)
    table_set = tables(radix_sizes)
    first_row = lax.axis_index("ctx") * chan_group
    own_rate = lax.dynamic_slice_in_dim(decay, first_row, chan_group, 1)
    own_residue = lax.dynamic_slice_in_dim(residue, first_row, chan_group, 1)
    own_spec = [
        spectrum(own_rate[filter_index], own_residue[filter_index], radix_sizes, seq_length)
        for filter_index in range(2)
    ]
    forward_rows = [x_gate, values] + [x_post]
    row_count = len(forward_rows)
    base_rows = jnp.stack(forward_rows)
    copied = base_rows
    for bit_index in range(tp_count.bit_length() - 1):
        copied = partner(copied, "tp", bit_index)
    sent_rows = jnp.concatenate([base_rows, copied[:, :, ::-1]], axis=0)
    received = lax.all_to_all(
        jnp.swapaxes(sent_rows, 1, 2), "ctx", split_axis=1, concat_axis=2, tiled=True
    )
    gate_fwd = received[0].astype(jnp.float32)
    value_fwd = received[1].astype(jnp.float32)
    mirrored = received[row_count:, :, ::-1].astype(jnp.float32)
    spec_real, spec_imag = forward(value_fwd, mirrored[1], table_set, radix_sizes)
    spec_real, spec_imag = complex_times(spec_real, spec_imag, own_spec[0][0], own_spec[0][1])
    along_fwd, along_rev = inverse(spec_real, spec_imag, table_set, radix_sizes)
    spec_real, spec_imag = forward(
        gate_fwd * along_fwd, mirrored[0] * along_rev, table_set, radix_sizes
    )
    spec_real, spec_imag = complex_times(spec_real, spec_imag, own_spec[1][0], own_spec[1][1])
    sum_fwd, sum_rev = inverse(spec_real, spec_imag, table_set, radix_sizes)
    sum_fwd = received[2].astype(jnp.float32) * sum_fwd
    sum_rev = mirrored[2] * sum_rev
    results = jnp.stack([sum_fwd, sum_rev[:, ::-1]])
    returned = lax.all_to_all(
        results.astype(jnp.bfloat16), "ctx", split_axis=2, concat_axis=1, tiled=True
    ).astype(results.dtype)
    flipped = returned[1, ::-1, :]
    for bit_index in range(tp_count.bit_length() - 1):
        flipped = partner(flipped.astype(jnp.bfloat16), "tp", bit_index).astype(flipped.dtype)
    total_rows = returned[0] + flipped
    total_rows = total_rows.T
    mixed_rows = total_rows.astype(jnp.bfloat16)
    whole_rows = lax.all_gather(mixed_rows, "tp", axis=1, tiled=True)
    projected = lax.dot_general(
        whole_rows,
        lax.all_gather(w_out, "ctx", axis=0, tiled=True),
        (((1,), (1,)), ((), ())),
        preferred_element_type=jnp.float32,
    )
    return projected.astype(jnp.bfloat16)


def cycle(row_factor, col_factor, modulus):
    angle = (row_factor * col_factor % modulus).astype(jnp.float32) * (2.0 * math.pi / modulus)
    return jnp.cos(angle), jnp.sin(angle)


def put_tables(table_ref, back_ref=None):
    block = table_ref.shape[1]
    modulus = 4 * block
    coarse = 16
    rows = lax.broadcasted_iota(jnp.int32, (coarse, block), 0)
    cols = lax.broadcasted_iota(jnp.int32, (coarse, block), 1)

    def parts(big, small):
        for place in range(block // coarse):
            big_cos, big_sin = (part[place : place + 1] for part in big)
            span = slice(place * coarse, (place + 1) * coarse)
            below = slice(block + place * coarse, block + (place + 1) * coarse)
            cos = halves(big_cos * small[0] - big_sin * small[1])
            sin = halves(-(big_sin * small[0] + big_cos * small[1]))
            yield span, below, cos, sin

    frequency = 2 * cols + 1
    for span, _, cos, sin in parts(cycle(coarse * rows, frequency, modulus), cycle(rows, frequency, modulus)):
        table_ref[0, span, :block], table_ref[1, span, :block] = cos
        table_ref[0, span, block:], table_ref[1, span, block:] = sin
    if back_ref is not None:
        for span, below, cos, sin in parts(cycle(2 * coarse * rows, cols, modulus), cycle(2 * rows + 1, cols, modulus)):
            back_ref[0, span], back_ref[1, span] = cos
            back_ref[0, below], back_ref[1, below] = sin


def halves(value):
    high = value.astype(jnp.bfloat16)
    return high, (value - high.astype(jnp.float32)).astype(jnp.bfloat16)


def mul(left, right):
    return jnp.dot(left, right, preferred_element_type=jnp.float32)


def mul3(high, low, table_ref):
    return mul(high, table_ref[0]) + (mul(low, table_ref[0]) + mul(high, table_ref[1]))


def pack_kernel(
    gate_hbm, value_hbm, post_hbm, decay_hbm, residue_hbm,
    out_hbm, own_ref, sent_ref, held_ref, par_ref, ready_ref, sems, out_sems,
):
    ctx_count, _, group, tok = out_hbm.shape
    width = gate_hbm.shape[1]
    half = decay_hbm.shape[0]
    position = lax.axis_index("ctx")
    pairs = [(source, held_ref.at[place]) for place, source in enumerate((value_hbm, gate_hbm, post_hbm))]
    pairs += [(decay_hbm, par_ref.at[:half]), (residue_hbm, par_ref.at[half:])]
    copies = [pltpu.make_async_copy(*pair, sems.at[place]) for place, pair in enumerate(pairs)]
    for copy in copies:
        copy.start()
    sends = []
    for place, copy in enumerate(copies[:3]):
        copy.wait()
        for first in range(0, width, tok):
            turned = held_ref[place, :, first : first + tok].T
            for part in range(tok // group):
                ready_ref[first // group + part, place] = turned[part * group : (part + 1) * group]
        sends.append(pltpu.make_async_copy(ready_ref.at[:, place], out_hbm.at[:, place], out_sems.at[place]))
        sends[-1].start()
    copies[3].wait()
    copies[4].wait()
    odd = position % 2 == 1
    lane = lax.broadcasted_iota(jnp.int32, own_ref.shape, 1)

    def tile_of(index):
        return par_ref[:, pl.ds(pl.multiple_of(index // 2 * tok, tok), tok)]

    def to_front(value):
        return jnp.where(odd, pltpu.roll(value, group, 1), value)

    own_ref[...] = to_front(tile_of(position))
    turned = tile_of(ctx_count - 1 - position)
    shift = 1
    while shift < tok:
        turned = jnp.where(lane & shift == 0, pltpu.roll(turned, tok - shift, 1), pltpu.roll(turned, shift, 1))
        shift *= 2
    sent_ref[...] = to_front(turned)
    for copy in sends:
        copy.wait()


def filter_kernel(poles, par_ref, out_ref, time_ref, table_ref):
    blocks, group, twice = out_ref.shape[1:]
    block = twice // 2
    lanes = 128
    put_tables(table_ref)
    turned = par_ref[...].T
    ramp = lax.broadcasted_iota(jnp.int32, (8, lanes), 1).astype(jnp.float32)
    sign = (1 - 2 * (lax.broadcasted_iota(jnp.int32, (group, block), 1) % 2)).astype(jnp.float32)
    for index in range(2):
        for row in range(0, group, 8):
            rows = slice(row, row + 8)
            rate = turned[rows, index * poles : (index + 1) * poles]
            scale = turned[rows, (2 + index) * poles : (3 + index) * poles] * (jnp.sqrt(rate * (2.0 / poles)) / block)
            jump = jnp.exp(rate * -lanes)
            sums = [None] * (blocks * block // lanes)
            for pole in range(poles):
                term = scale[:, pole : pole + 1] * jnp.exp(-rate[:, pole : pole + 1] * ramp)
                step = jnp.broadcast_to(jump[:, pole : pole + 1], (8, lanes))
                for place in range(len(sums)):
                    sums[place] = term if pole == 0 else sums[place] + term
                    if place + 1 < len(sums):
                        term = term * step
            for place, total in enumerate(sums):
                lag, lane = divmod(place * lanes, block)
                first = (index * blocks + lag) * group + row
                time_ref[first : first + 8, lane : lane + lanes] = total
        first = index * blocks * group
        high, low = halves(time_ref[first : first + blocks * group])
        spec = mul3(high, low, table_ref)
        for lag in range(blocks):
            real = spec[lag * group : (lag + 1) * group, :block]
            imag = spec[lag * group : (lag + 1) * group, block:]
            if lag > 0:
                real = real - sign * spec[(lag - 1) * group : lag * group, block:]
                imag = imag + sign * spec[(lag - 1) * group : lag * group, :block]
            out_ref[index, lag, :, :block] = real
            out_ref[index, lag, :, block:] = imag


def conv_kernel(x_ref, own_ref, paired_ref, out_hbm, table_ref, back_ref, spec_ref, high_ref, low_ref, ready_ref, sems):
    put_tables(table_ref, back_ref)
    blocks, group, twice = own_ref.shape[1:]
    block = twice // 2
    rows_all = blocks * group
    tall, wide = 16, 128
    pieces = x_ref.shape[0] // blocks

    def rows_of(position):
        return jnp.concatenate(
            [
                jnp.concatenate([x_ref[m * pieces + s, position] for s in range(pieces)], axis=1)
                for m in range(blocks)
            ],
            axis=0,
        )

    def times(index, side, source, row, lane):
        data = []
        for m in range(blocks):
            rows = slice(source + m * group + row, source + m * group + row + tall)
            data.append((spec_ref[rows, lane : lane + wide], spec_ref[rows, block + lane : block + lane + wide]))
        sums = [None] * blocks
        for lag in range(blocks):
            h_ref = (own_ref, paired_ref)[side]
            f_re = h_ref[index, lag, row : row + tall, lane : lane + wide]
            f_im = h_ref[index, lag, row : row + tall, block + lane : block + lane + wide]
            for m in range(blocks - lag):
                target, (d_re, d_im) = (m + lag, data[m]) if side == 0 else (m, data[m + lag])
                if side == 0:
                    real, imag = f_re * d_re - f_im * d_im, f_re * d_im + f_im * d_re
                else:
                    real, imag = f_re * d_re + f_im * d_im, f_re * d_im - f_im * d_re
                if sums[target] is not None:
                    real, imag = sums[target][0] + real, sums[target][1] + imag
                sums[target] = (real, imag)
        return sums

    def keep(target, row, lane, sums):
        for m in range(blocks):
            rows = slice(target + m * group + row, target + m * group + row + tall)
            for part in range(2):
                cols = slice(part * block + lane, part * block + lane + wide)
                high_ref[rows, cols], low_ref[rows, cols] = halves(sums[m][part])

    chunks = [(row, lane) for row in range(0, group, tall) for lane in range(0, block, wide)]

    value = rows_of(0)
    gate = rows_of(1).astype(jnp.float32)
    spec_ref[:rows_all] = mul(value, table_ref[0]) + mul(value, table_ref[1])
    sides = [slice(side * rows_all, (side + 1) * rows_all) for side in range(2)]
    gated = []
    for side in range(2):
        for row, lane in chunks:
            keep(side * rows_all, row, lane, times(0, side, 0, row, lane))
        gated.append(halves(gate * mul3(high_ref[sides[side]], low_ref[sides[side]], back_ref)))
    for side in range(2):
        spec_ref[sides[side]] = mul3(*gated[side], table_ref)
    for row, lane in chunks:
        ahead, back = times(1, 0, 0, row, lane), times(1, 1, rows_all, row, lane)
        keep(0, row, lane, [(a[0] + b[0], a[1] + b[1]) for a, b in zip(ahead, back)])
    post = rows_of(2)
    tok = block // pieces
    sends = []
    for part in range(2):
        rows = slice(part * rows_all // 2, (part + 1) * rows_all // 2)
        summed = mul3(high_ref[rows], low_ref[rows], back_ref)
        mixed = (post[rows].astype(jnp.float32) * summed).astype(jnp.bfloat16)
        first = part * blocks // 2 * pieces
        for m in range(blocks // 2):
            for s in range(pieces):
                ready_ref[first + m * pieces + s] = mixed[m * group : (m + 1) * group, s * tok : (s + 1) * tok]
        span = pl.ds(first, blocks // 2 * pieces)
        for copy in range(out_hbm.shape[0]):
            sends.append(pltpu.make_async_copy(ready_ref.at[span], out_hbm.at[copy, span], sems.at[part, copy]))
            sends[-1].start()
    for send in sends:
        send.wait()


def project_kernel(mixed_ref, *refs):
    w_refs, (out_ref, held_ref) = refs[:-2], refs[-2:]
    rows = w_refs[0].shape[0]
    position = lax.axis_index("ctx")
    total = mul(jnp.concatenate([w_ref[...] for w_ref in w_refs], axis=0), mixed_ref[...])
    for mask in range(len(w_refs)):
        first = pl.multiple_of((position ^ mask) * rows, rows)
        held_ref[pl.ds(first, rows)] = total[mask * rows : (mask + 1) * rows]
    out_ref[...] = held_ref[...].T.astype(jnp.bfloat16)


def whole_call(kernel, out_shape, scratch, flops, nbytes, *operands, in_hbm=0, out_hbm=()):
    results = pl.pallas_call(
        kernel,
        out_shape=out_shape,
        in_specs=[
            pl.BlockSpec(memory_space=pltpu.HBM if place < in_hbm else pltpu.VMEM) for place in range(len(operands))
        ],
        out_specs=[
            pl.BlockSpec(memory_space=pltpu.HBM if place in out_hbm else pltpu.VMEM) for place in range(len(out_shape))
        ],
        scratch_shapes=scratch,
        cost_estimate=pl.CostEstimate(flops=flops, bytes_accessed=nbytes, transcendentals=0),
        compiler_params=pltpu.CompilerParams(vmem_limit_bytes=None if in_hbm else 32 * 2**20),
    )(*operands)
    return results if len(out_shape) > 1 else results[0]


def blocked(x_gate, x_post, values, decay, residue, w_out):
    tok, width = x_gate.shape
    ctx_count = lax.axis_size("ctx")
    tp_count = lax.axis_size("tp")
    group = width // ctx_count
    poles = decay.shape[2]
    block = 2 * tok
    blocks = tok * ctx_count // block
    rows, channels = w_out.shape
    half = 2 * poles

    packed, own, mirrored = whole_call(
        pack_kernel,
        (
            jax.ShapeDtypeStruct((ctx_count, 3, group, tok), jnp.bfloat16),
            jax.ShapeDtypeStruct((2 * half, tok), jnp.float32),
            jax.ShapeDtypeStruct((2 * half, tok), jnp.float32),
        ),
        [
            pltpu.VMEM((3, tok, width), jnp.bfloat16),
            pltpu.VMEM((2 * half, width), jnp.float32),
            pltpu.VMEM((ctx_count, 3, group, tok), jnp.bfloat16),
            pltpu.SemaphoreType.DMA((5,)),
            pltpu.SemaphoreType.DMA((3,)),
        ],
        0,
        6 * tok * width * 2,
        x_gate,
        values,
        x_post,
        jnp.swapaxes(decay, 1, 2).reshape(half, width),
        jnp.swapaxes(residue, 1, 2).reshape(half, width),
        in_hbm=5,
        out_hbm=(0,),
    )
    paired = lax.ppermute(mirrored, "tp", [(z, tp_count - 1 - z) for z in range(tp_count)])
    received = lax.all_to_all(packed, "ctx", split_axis=0, concat_axis=0, tiled=True)

    w_x, w_y = partner(w_out, "ctx", 1), partner(w_out, "ctx", 2)
    w_x, w_y, own = lax.optimization_barrier((w_x, w_y, own))

    def spectra(params):
        return whole_call(
            functools.partial(filter_kernel, poles),
            (jax.ShapeDtypeStruct((2, blocks, group, 2 * block), jnp.float32),),
            [
                pltpu.VMEM((2 * blocks * group, block), jnp.float32),
                pltpu.VMEM((2, block, 2 * block), jnp.bfloat16),
            ],
            2 * 2 * blocks * group * block * 2 * block * 3,
            2 * blocks * group * 2 * block * 4,
            params,
        )

    own_spectra = spectra(own)
    w_late, own_spectra = lax.optimization_barrier((w_x, own_spectra))
    w_far = partner(w_late, "ctx", 2)
    paired_spectra = spectra(paired)
    mixed = whole_call(
        conv_kernel,
        (jax.ShapeDtypeStruct((tp_count, ctx_count, group, tok), jnp.bfloat16),),
        [
            pltpu.VMEM((2, block, 2 * block), jnp.bfloat16),
            pltpu.VMEM((2, 2 * block, block), jnp.bfloat16),
            pltpu.VMEM((2 * blocks * group, 2 * block), jnp.float32),
            pltpu.VMEM((2 * blocks * group, 2 * block), jnp.bfloat16),
            pltpu.VMEM((2 * blocks * group, 2 * block), jnp.bfloat16),
            pltpu.VMEM((ctx_count, group, tok), jnp.bfloat16),
            pltpu.SemaphoreType.DMA((2, tp_count)),
        ],
        2 * 6 * blocks * group * block * 2 * block * 3,
        4 * blocks * group * 2 * block * 4,
        received,
        own_spectra,
        paired_spectra,
        out_hbm=(0,),
    )
    mixed, w_far, w_own = lax.optimization_barrier((mixed, w_far, w_out))
    w_blocks = {0: w_own, 2: w_x, 4: w_y, 6: w_far}
    for mask in range(0, ctx_count, 2):
        w_blocks[mask + 1] = partner(w_blocks[mask], "ctx", 0)
    every = lax.all_to_all(
        mixed.reshape(tp_count * ctx_count, group, tok), ("tp", "ctx"), split_axis=0, concat_axis=0, tiled=True
    ).reshape(channels, tok)
    return whole_call(
        project_kernel,
        (jax.ShapeDtypeStruct((tok, rows * ctx_count), jnp.bfloat16),),
        [pltpu.VMEM((rows * ctx_count, tok), jnp.float32)],
        2 * tok * rows * ctx_count * channels,
        2 * rows * ctx_count * channels,
        every,
        *[w_blocks[mask] for mask in range(ctx_count)],
    )


def local(x_gate, x_post, values, decay, residue, w_out):
    tok, width = x_gate.shape
    ctx_count = lax.axis_size("ctx")
    if tok == 128 and width == 512 and ctx_count == 8 and lax.axis_size("tp") == 4:
        return blocked(x_gate, x_post, values, decay, residue, w_out)
    return general(x_gate, x_post, values, decay, residue, w_out)


def solution(mesh):
    in_specs = (
        P("ctx", "tp"),
        P("ctx", "tp"),
        P("ctx", "tp"),
        P(None, "tp", None),
        P(None, "tp", None),
        P(("tp", "ctx"), None),
    )
    out_specs = P("ctx", "tp")
    return jax.shard_map(local, mesh=mesh, in_specs=in_specs, out_specs=out_specs, check_vma=False)
```

```python
import functools
import math

import jax
import jax.numpy as jnp
from jax import lax
from jax.experimental import pallas as pl
from jax.experimental.pallas import tpu as pltpu
from jax.sharding import PartitionSpec as P

HIGHEST = lax.Precision.HIGHEST


def partner(value, axis, bit):
    mask = 2**bit
    pairs = [(source, source ^ mask) for source in range(lax.axis_size(axis))]
    return lax.ppermute(value, axis, pairs)


def radices(length_all):
    last_radix = min(128, length_all // 4)
    first_radix = min(32, length_all // last_radix)
    return (first_radix, length_all // (first_radix * last_radix), last_radix)


def rotation(row_count, col_count, modulus):
    product = (
        lax.broadcasted_iota(jnp.int32, (row_count, col_count), 0)
        * lax.broadcasted_iota(jnp.int32, (row_count, col_count), 1)
        % modulus
    )
    angle = product.astype(jnp.float32) * (2.0 * math.pi / modulus)
    return (jnp.cos(angle), -jnp.sin(angle))


def tables(radix_sizes):
    first_radix, mid_radix, last_radix = radix_sizes
    length_all = first_radix * mid_radix * last_radix
    outer_real, outer_imag = rotation(first_radix, first_radix, first_radix)
    mid_real, mid_imag = rotation(mid_radix, mid_radix, mid_radix)
    last_real, last_imag = rotation(last_radix, last_radix, last_radix)
    twist_real, twist_imag = rotation(first_radix, mid_radix * last_radix, length_all)
    twist_real = twist_real.reshape(first_radix, mid_radix, last_radix)
    twist_imag = twist_imag.reshape(first_radix, mid_radix, last_radix)
    inner_real, inner_imag = rotation(mid_radix, last_radix, mid_radix * last_radix)
    return (
        outer_real,
        outer_imag,
        mid_real,
        mid_imag,
        last_real,
        last_imag,
        twist_real,
        twist_imag,
        inner_real,
        inner_imag,
    )


def apply_matrix(pattern, real_part, imag_part, matrix_real, matrix_imag):
    out_real = jnp.einsum(pattern, real_part, matrix_real, precision=HIGHEST) - jnp.einsum(
        pattern, imag_part, matrix_imag, precision=HIGHEST
    )
    out_imag = jnp.einsum(pattern, real_part, matrix_imag, precision=HIGHEST) + jnp.einsum(
        pattern, imag_part, matrix_real, precision=HIGHEST
    )
    return (out_real, out_imag)


def complex_times(left_real, left_imag, right_real, right_imag):
    return (
        left_real * right_real - left_imag * right_imag,
        left_real * right_imag + left_imag * right_real,
    )


def forward(real_part, imag_part, table_set, radix_sizes):
    first_radix, mid_radix, last_radix = radix_sizes
    half_first = first_radix // 2
    batch_rows = real_part.shape[0]
    (
        outer_real,
        outer_imag,
        mid_real,
        mid_imag,
        last_real,
        last_imag,
        twist_real,
        twist_imag,
        inner_real,
        inner_imag,
    ) = table_set
    real_part = real_part.reshape(batch_rows, half_first, mid_radix, last_radix)
    imag_part = imag_part.reshape(batch_rows, half_first, mid_radix, last_radix)
    real_part, imag_part = apply_matrix(
        "banm,ak->bknm", real_part, imag_part, outer_real[:half_first], outer_imag[:half_first]
    )
    real_part, imag_part = complex_times(real_part, imag_part, twist_real, twist_imag)
    real_part, imag_part = apply_matrix("bknm,nj->bkjm", real_part, imag_part, mid_real, mid_imag)
    real_part, imag_part = complex_times(real_part, imag_part, inner_real, inner_imag)
    return apply_matrix("bkjm,mq->bkjq", real_part, imag_part, last_real, last_imag)


def inverse(real_part, imag_part, table_set, radix_sizes):
    first_radix, mid_radix, last_radix = radix_sizes
    half_first = first_radix // 2
    batch_rows = real_part.shape[0]
    (
        outer_real,
        outer_imag,
        mid_real,
        mid_imag,
        last_real,
        last_imag,
        twist_real,
        twist_imag,
        inner_real,
        inner_imag,
    ) = table_set
    real_part, imag_part = apply_matrix(
        "bkjq,mq->bkjm", real_part, imag_part, last_real / last_radix, -last_imag / last_radix
    )
    real_part, imag_part = complex_times(real_part, imag_part, inner_real, -inner_imag)
    real_part, imag_part = apply_matrix(
        "bkjm,nj->bknm", real_part, imag_part, mid_real / mid_radix, -mid_imag / mid_radix
    )
    real_part, imag_part = complex_times(real_part, imag_part, twist_real, -twist_imag)
    matrix_real = outer_real[:half_first] / first_radix
    matrix_imag = -outer_imag[:half_first] / first_radix
    out_real, out_imag = apply_matrix(
        "bknm,ak->banm", real_part, imag_part, matrix_real, matrix_imag
    )
    return (out_real.reshape(batch_rows, -1), out_imag.reshape(batch_rows, -1))


def spectrum(decay_rows, residue_rows, radix_sizes, seq_length):
    first_radix, mid_radix, last_radix = radix_sizes
    length_all = first_radix * mid_radix * last_radix
    poles = decay_rows.shape[1]
    shape_all = (first_radix, mid_radix, last_radix)
    frequency = (
        lax.broadcasted_iota(jnp.int32, shape_all, 0)
        + first_radix * lax.broadcasted_iota(jnp.int32, shape_all, 1)
        + first_radix * mid_radix * lax.broadcasted_iota(jnp.int32, shape_all, 2)
    )
    half_angle = frequency.astype(jnp.float32) * (math.pi / length_all)
    sin_half = jnp.sin(half_angle)
    sin_full = jnp.sin(2.0 * half_angle)
    parity_sign = (1 - 2 * (frequency % 2)).astype(jnp.float32)

    def add_pole(pole_index, running):
        run_real, run_imag = running
        rate_col = lax.dynamic_slice_in_dim(decay_rows, pole_index, 1, 1).reshape(-1, 1, 1, 1)
        weight = lax.dynamic_slice_in_dim(residue_rows, pole_index, 1, 1).reshape(
            -1, 1, 1, 1
        ) * jnp.sqrt(2.0 * rate_col / poles)
        retained = jnp.exp(-rate_col)
        den_real = -jnp.expm1(-rate_col) + 2.0 * retained * sin_half * sin_half
        den_imag = retained * sin_full
        pole_scale = (
            weight
            * (1.0 - jnp.exp(-rate_col * seq_length) * parity_sign)
            / (den_real * den_real + den_imag * den_imag)
        )
        return (run_real + pole_scale * den_real, run_imag - pole_scale * den_imag)

    zeros_all = jnp.zeros((decay_rows.shape[0],) + shape_all, jnp.float32)
    return lax.fori_loop(0, poles, add_pole, (zeros_all, zeros_all))


def general(x_gate, x_post, values, decay, residue, w_out):
    tok_rows, block_width = x_gate.shape
    ctx_count = lax.axis_size("ctx")
    tp_count = lax.axis_size("tp")
    chan_group = block_width // ctx_count
    seq_length = tok_rows * ctx_count
    radix_sizes = radices(2 * seq_length)
    table_set = tables(radix_sizes)
    first_row = lax.axis_index("ctx") * chan_group
    own_rate = lax.dynamic_slice_in_dim(decay, first_row, chan_group, 1)
    own_residue = lax.dynamic_slice_in_dim(residue, first_row, chan_group, 1)
    own_spec = [
        spectrum(own_rate[filter_index], own_residue[filter_index], radix_sizes, seq_length)
        for filter_index in range(2)
    ]
    forward_rows = [x_gate, values] + [x_post]
    row_count = len(forward_rows)
    base_rows = jnp.stack(forward_rows)
    copied = base_rows
    for bit_index in range(tp_count.bit_length() - 1):
        copied = partner(copied, "tp", bit_index)
    sent_rows = jnp.concatenate([base_rows, copied[:, :, ::-1]], axis=0)
    received = lax.all_to_all(
        jnp.swapaxes(sent_rows, 1, 2), "ctx", split_axis=1, concat_axis=2, tiled=True
    )
    gate_fwd = received[0].astype(jnp.float32)
    value_fwd = received[1].astype(jnp.float32)
    mirrored = received[row_count:, :, ::-1].astype(jnp.float32)
    spec_real, spec_imag = forward(value_fwd, mirrored[1], table_set, radix_sizes)
    spec_real, spec_imag = complex_times(spec_real, spec_imag, own_spec[0][0], own_spec[0][1])
    along_fwd, along_rev = inverse(spec_real, spec_imag, table_set, radix_sizes)
    spec_real, spec_imag = forward(
        gate_fwd * along_fwd, mirrored[0] * along_rev, table_set, radix_sizes
    )
    spec_real, spec_imag = complex_times(spec_real, spec_imag, own_spec[1][0], own_spec[1][1])
    sum_fwd, sum_rev = inverse(spec_real, spec_imag, table_set, radix_sizes)
    sum_fwd = received[2].astype(jnp.float32) * sum_fwd
    sum_rev = mirrored[2] * sum_rev
    results = jnp.stack([sum_fwd, sum_rev[:, ::-1]])
    returned = lax.all_to_all(
        results.astype(jnp.bfloat16), "ctx", split_axis=2, concat_axis=1, tiled=True
    ).astype(results.dtype)
    flipped = returned[1, ::-1, :]
    for bit_index in range(tp_count.bit_length() - 1):
        flipped = partner(flipped.astype(jnp.bfloat16), "tp", bit_index).astype(flipped.dtype)
    total_rows = returned[0] + flipped
    total_rows = total_rows.T
    mixed_rows = total_rows.astype(jnp.bfloat16)
    whole_rows = lax.all_gather(mixed_rows, "tp", axis=1, tiled=True)
    projected = lax.dot_general(
        whole_rows,
        lax.all_gather(w_out, "ctx", axis=0, tiled=True),
        (((1,), (1,)), ((), ())),
        preferred_element_type=jnp.float32,
    )
    return projected.astype(jnp.bfloat16)


def cycle(row_factor, col_factor, modulus):
    angle = (row_factor * col_factor % modulus).astype(jnp.float32) * (2.0 * math.pi / modulus)
    return jnp.cos(angle), jnp.sin(angle)


def put_tables(table_ref, back_ref=None):
    block = table_ref.shape[1]
    modulus = 4 * block
    coarse = 16
    rows = lax.broadcasted_iota(jnp.int32, (coarse, block), 0)
    cols = lax.broadcasted_iota(jnp.int32, (coarse, block), 1)

    def parts(big, small):
        for place in range(block // coarse):
            big_cos, big_sin = (part[place : place + 1] for part in big)
            span = slice(place * coarse, (place + 1) * coarse)
            below = slice(block + place * coarse, block + (place + 1) * coarse)
            cos = halves(big_cos * small[0] - big_sin * small[1])
            sin = halves(-(big_sin * small[0] + big_cos * small[1]))
            yield span, below, cos, sin

    frequency = 2 * cols + 1
    for span, _, cos, sin in parts(cycle(coarse * rows, frequency, modulus), cycle(rows, frequency, modulus)):
        table_ref[0, span, :block], table_ref[1, span, :block] = cos
        table_ref[0, span, block:], table_ref[1, span, block:] = sin
    if back_ref is not None:
        for span, below, cos, sin in parts(cycle(2 * coarse * rows, cols, modulus), cycle(2 * rows + 1, cols, modulus)):
            back_ref[0, span], back_ref[1, span] = cos
            back_ref[0, below], back_ref[1, below] = sin


def halves(value):
    high = value.astype(jnp.bfloat16)
    return high, (value - high.astype(jnp.float32)).astype(jnp.bfloat16)


def mul(left, right):
    return jnp.dot(left, right, preferred_element_type=jnp.float32)


def mul3(high, low, table_ref):
    return mul(high, table_ref[0]) + (mul(low, table_ref[0]) + mul(high, table_ref[1]))


def pack_kernel(gate_hbm, value_hbm, post_hbm, out_hbm, held_ref, ready_ref, sems, out_sems):
    _, _, group, tok = out_hbm.shape
    width = gate_hbm.shape[1]
    copies = [
        pltpu.make_async_copy(source, held_ref.at[place], sems.at[place])
        for place, source in enumerate((value_hbm, gate_hbm, post_hbm))
    ]
    for copy in copies:
        copy.start()
    sends = []
    for place, copy in enumerate(copies):
        copy.wait()
        for first in range(0, width, tok):
            turned = held_ref[place, :, first : first + tok].T
            for part in range(tok // group):
                ready_ref[first // group + part, place] = turned[part * group : (part + 1) * group]
        sends.append(pltpu.make_async_copy(ready_ref.at[:, place], out_hbm.at[:, place], out_sems.at[place]))
        sends[-1].start()
    for send in sends:
        send.wait()


def filter_kernel(poles, par_ref, out_ref, time_ref, table_ref):
    blocks, group, twice = out_ref.shape[2:]
    block = twice // 2
    lanes = 128
    put_tables(table_ref)
    turned = par_ref[...].T
    ramp = lax.broadcasted_iota(jnp.int32, (8, lanes), 1).astype(jnp.float32)
    sign = (1 - 2 * (lax.broadcasted_iota(jnp.int32, (group, block), 1) % 2)).astype(jnp.float32)
    for index, side in ((0, 0), (0, 1), (1, 0), (1, 1)):
        base = (index * 2 + side) * blocks * group
        for row in range(0, group, 8):
            rows = slice(side * group + row, side * group + row + 8)
            rate = turned[rows, index * poles : (index + 1) * poles]
            scale = turned[rows, (2 + index) * poles : (3 + index) * poles] * (jnp.sqrt(rate * (2.0 / poles)) / block)
            jump = jnp.exp(rate * -lanes)
            sums = [None] * (blocks * block // lanes)
            for pole in range(poles):
                term = scale[:, pole : pole + 1] * jnp.exp(-rate[:, pole : pole + 1] * ramp)
                step = jnp.broadcast_to(jump[:, pole : pole + 1], (8, lanes))
                for place in range(len(sums)):
                    sums[place] = term if pole == 0 else sums[place] + term
                    if place + 1 < len(sums):
                        term = term * step
            for place, total in enumerate(sums):
                lag, lane = divmod(place * lanes, block)
                first = base + lag * group + row
                time_ref[first : first + 8, lane : lane + lanes] = total
        high, low = halves(time_ref[base : base + blocks * group])
        spec = mul3(high, low, table_ref)
        for lag in range(blocks):
            real = spec[lag * group : (lag + 1) * group, :block]
            imag = spec[lag * group : (lag + 1) * group, block:]
            if lag > 0:
                real = real - sign * spec[(lag - 1) * group : lag * group, block:]
                imag = imag + sign * spec[(lag - 1) * group : lag * group, :block]
            out_ref[index, side, lag, :, :block] = real
            out_ref[index, side, lag, :, block:] = imag


def conv_kernel(x_ref, h_ref, out_hbm, table_ref, back_ref, spec_ref, high_ref, low_ref, ready_ref, sems):
    put_tables(table_ref, back_ref)
    blocks, group, twice = h_ref.shape[2:]
    block = twice // 2
    rows_all = blocks * group
    tall, wide = 16, 128
    pieces = x_ref.shape[0] // blocks

    def rows_of(position):
        return jnp.concatenate(
            [
                jnp.concatenate([x_ref[m * pieces + s, position] for s in range(pieces)], axis=1)
                for m in range(blocks)
            ],
            axis=0,
        )

    def times(index, side, source, row, lane):
        data = []
        for m in range(blocks):
            rows = slice(source + m * group + row, source + m * group + row + tall)
            data.append((spec_ref[rows, lane : lane + wide], spec_ref[rows, block + lane : block + lane + wide]))
        sums = [None] * blocks
        for lag in range(blocks):
            f_re = h_ref[index, side, lag, row : row + tall, lane : lane + wide]
            f_im = h_ref[index, side, lag, row : row + tall, block + lane : block + lane + wide]
            for m in range(blocks - lag):
                target, (d_re, d_im) = (m + lag, data[m]) if side == 0 else (m, data[m + lag])
                if side == 0:
                    real, imag = f_re * d_re - f_im * d_im, f_re * d_im + f_im * d_re
                else:
                    real, imag = f_re * d_re + f_im * d_im, f_re * d_im - f_im * d_re
                if sums[target] is not None:
                    real, imag = sums[target][0] + real, sums[target][1] + imag
                sums[target] = (real, imag)
        return sums

    def keep(target, row, lane, sums):
        for m in range(blocks):
            rows = slice(target + m * group + row, target + m * group + row + tall)
            for part in range(2):
                cols = slice(part * block + lane, part * block + lane + wide)
                high_ref[rows, cols], low_ref[rows, cols] = halves(sums[m][part])

    chunks = [(row, lane) for row in range(0, group, tall) for lane in range(0, block, wide)]

    value = rows_of(0)
    gate = rows_of(1).astype(jnp.float32)
    spec_ref[:rows_all] = mul(value, table_ref[0]) + mul(value, table_ref[1])
    sides = [slice(side * rows_all, (side + 1) * rows_all) for side in range(2)]
    gated = []
    for side in range(2):
        for row, lane in chunks:
            keep(side * rows_all, row, lane, times(0, side, 0, row, lane))
        gated.append(halves(gate * mul3(high_ref[sides[side]], low_ref[sides[side]], back_ref)))
    for side in range(2):
        spec_ref[sides[side]] = mul3(*gated[side], table_ref)
    for row, lane in chunks:
        ahead, back = times(1, 0, 0, row, lane), times(1, 1, rows_all, row, lane)
        keep(0, row, lane, [(a[0] + b[0], a[1] + b[1]) for a, b in zip(ahead, back)])
    post = rows_of(2)
    tok = block // pieces
    sends = []
    for part in range(2):
        rows = slice(part * rows_all // 2, (part + 1) * rows_all // 2)
        summed = mul3(high_ref[rows], low_ref[rows], back_ref)
        mixed = (post[rows].astype(jnp.float32) * summed).astype(jnp.bfloat16)
        first = part * blocks // 2 * pieces
        for m in range(blocks // 2):
            for s in range(pieces):
                ready_ref[first + m * pieces + s] = mixed[m * group : (m + 1) * group, s * tok : (s + 1) * tok]
        span = pl.ds(first, blocks // 2 * pieces)
        for copy in range(out_hbm.shape[0]):
            sends.append(pltpu.make_async_copy(ready_ref.at[span], out_hbm.at[copy, span], sems.at[part, copy]))
            sends[-1].start()
    for send in sends:
        send.wait()


def project_kernel(mixed_ref, *refs):
    w_refs, (out_ref, held_ref) = refs[:-2], refs[-2:]
    rows = w_refs[0].shape[0]
    position = lax.axis_index("ctx")
    total = mul(jnp.concatenate([w_ref[...] for w_ref in w_refs], axis=0), mixed_ref[...])
    for mask in range(len(w_refs)):
        first = pl.multiple_of((position ^ mask) * rows, rows)
        held_ref[pl.ds(first, rows)] = total[mask * rows : (mask + 1) * rows]
    out_ref[...] = held_ref[...].T.astype(jnp.bfloat16)


def whole_call(kernel, out_shape, scratch, flops, nbytes, *operands, in_hbm=0, out_hbm=()):
    results = pl.pallas_call(
        kernel,
        out_shape=out_shape,
        in_specs=[
            pl.BlockSpec(memory_space=pltpu.HBM if place < in_hbm else pltpu.VMEM) for place in range(len(operands))
        ],
        out_specs=[
            pl.BlockSpec(memory_space=pltpu.HBM if place in out_hbm else pltpu.VMEM) for place in range(len(out_shape))
        ],
        scratch_shapes=scratch,
        cost_estimate=pl.CostEstimate(flops=flops, bytes_accessed=nbytes, transcendentals=0),
        compiler_params=pltpu.CompilerParams(vmem_limit_bytes=None if in_hbm else 32 * 2**20),
    )(*operands)
    return results if len(out_shape) > 1 else results[0]


def blocked(x_gate, x_post, values, decay, residue, w_out):
    tok, width = x_gate.shape
    ctx_count = lax.axis_size("ctx")
    tp_count = lax.axis_size("tp")
    group = width // ctx_count
    poles = decay.shape[2]
    block = 2 * tok
    blocks = tok * ctx_count // block
    rows, channels = w_out.shape
    position = lax.axis_index("ctx")

    params = jnp.swapaxes(jnp.concatenate([decay, residue], axis=0), 1, 2).reshape(4 * poles, width)
    own = lax.dynamic_slice_in_dim(params, position * group, group, 1)
    mirrored = lax.dynamic_slice_in_dim(params, (ctx_count - 1 - position) * group, group, 1)[:, ::-1]
    paired = lax.ppermute(mirrored, "tp", [(z, tp_count - 1 - z) for z in range(tp_count)])
    w_x, w_y = partner(w_out, "ctx", 1), partner(w_out, "ctx", 2)
    x_gate, paired = lax.optimization_barrier((x_gate, paired))
    packed = whole_call(
        pack_kernel,
        (jax.ShapeDtypeStruct((ctx_count, 3, group, tok), jnp.bfloat16),),
        [
            pltpu.VMEM((3, tok, width), jnp.bfloat16),
            pltpu.VMEM((ctx_count, 3, group, tok), jnp.bfloat16),
            pltpu.SemaphoreType.DMA((3,)),
            pltpu.SemaphoreType.DMA((3,)),
        ],
        0,
        6 * tok * width * 2,
        x_gate,
        values,
        x_post,
        in_hbm=3,
        out_hbm=(0,),
    )
    received = lax.all_to_all(packed, "ctx", split_axis=0, concat_axis=0, tiled=True)
    w_x, w_y, both = lax.optimization_barrier((w_x, w_y, jnp.concatenate([own, paired], axis=1)))
    spectra = whole_call(
        functools.partial(filter_kernel, poles),
        (jax.ShapeDtypeStruct((2, 2, blocks, group, 2 * block), jnp.float32),),
        [
            pltpu.VMEM((4 * blocks * group, block), jnp.float32),
            pltpu.VMEM((2, block, 2 * block), jnp.bfloat16),
        ],
        2 * 4 * blocks * group * block * 2 * block * 3,
        4 * blocks * group * 2 * block * 4,
        both,
    )
    w_late, received, spectra = lax.optimization_barrier((w_x, received, spectra))
    w_far = partner(w_late, "ctx", 2)
    mixed = whole_call(
        conv_kernel,
        (jax.ShapeDtypeStruct((tp_count, ctx_count, group, tok), jnp.bfloat16),),
        [
            pltpu.VMEM((2, block, 2 * block), jnp.bfloat16),
            pltpu.VMEM((2, 2 * block, block), jnp.bfloat16),
            pltpu.VMEM((2 * blocks * group, 2 * block), jnp.float32),
            pltpu.VMEM((2 * blocks * group, 2 * block), jnp.bfloat16),
            pltpu.VMEM((2 * blocks * group, 2 * block), jnp.bfloat16),
            pltpu.VMEM((ctx_count, group, tok), jnp.bfloat16),
            pltpu.SemaphoreType.DMA((2, tp_count)),
        ],
        2 * 6 * blocks * group * block * 2 * block * 3,
        4 * blocks * group * 2 * block * 4,
        received,
        spectra,
        out_hbm=(0,),
    )
    mixed, w_own, w_x, w_y = lax.optimization_barrier((mixed, w_out, w_x, w_y))
    w_blocks = {0: w_own, 2: w_x, 4: w_y, 6: w_far}
    for mask in range(0, ctx_count, 2):
        w_blocks[mask + 1] = partner(w_blocks[mask], "ctx", 0)
    every = lax.all_to_all(
        mixed.reshape(tp_count * ctx_count, group, tok), ("tp", "ctx"), split_axis=0, concat_axis=0, tiled=True
    ).reshape(channels, tok)
    return whole_call(
        project_kernel,
        (jax.ShapeDtypeStruct((tok, rows * ctx_count), jnp.bfloat16),),
        [pltpu.VMEM((rows * ctx_count, tok), jnp.float32)],
        2 * tok * rows * ctx_count * channels,
        2 * rows * ctx_count * channels,
        every,
        *[w_blocks[mask] for mask in range(ctx_count)],
    )


def local(x_gate, x_post, values, decay, residue, w_out):
    tok, width = x_gate.shape
    ctx_count = lax.axis_size("ctx")
    if tok == 128 and width == 512 and ctx_count == 8 and lax.axis_size("tp") == 4:
        return blocked(x_gate, x_post, values, decay, residue, w_out)
    return general(x_gate, x_post, values, decay, residue, w_out)


def solution(mesh):
    in_specs = (
        P("ctx", "tp"),
        P("ctx", "tp"),
        P("ctx", "tp"),
        P(None, "tp", None),
        P(None, "tp", None),
        P(("tp", "ctx"), None),
    )
    out_specs = P("ctx", "tp")
    return jax.shard_map(local, mesh=mesh, in_specs=in_specs, out_specs=out_specs, check_vma=False)
```

```python
import functools
import math

import jax
import jax.numpy as jnp
from jax import lax
from jax.experimental import pallas as pl
from jax.experimental.pallas import tpu as pltpu
from jax.sharding import PartitionSpec as P

HIGHEST = lax.Precision.HIGHEST


def partner(value, axis, bit):
    mask = 2**bit
    pairs = [(source, source ^ mask) for source in range(lax.axis_size(axis))]
    return lax.ppermute(value, axis, pairs)


def radices(length_all):
    last_radix = min(128, length_all // 4)
    first_radix = min(32, length_all // last_radix)
    return (first_radix, length_all // (first_radix * last_radix), last_radix)


def rotation(row_count, col_count, modulus):
    product = (
        lax.broadcasted_iota(jnp.int32, (row_count, col_count), 0)
        * lax.broadcasted_iota(jnp.int32, (row_count, col_count), 1)
        % modulus
    )
    angle = product.astype(jnp.float32) * (2.0 * math.pi / modulus)
    return (jnp.cos(angle), -jnp.sin(angle))


def tables(radix_sizes):
    first_radix, mid_radix, last_radix = radix_sizes
    length_all = first_radix * mid_radix * last_radix
    outer_real, outer_imag = rotation(first_radix, first_radix, first_radix)
    mid_real, mid_imag = rotation(mid_radix, mid_radix, mid_radix)
    last_real, last_imag = rotation(last_radix, last_radix, last_radix)
    twist_real, twist_imag = rotation(first_radix, mid_radix * last_radix, length_all)
    twist_real = twist_real.reshape(first_radix, mid_radix, last_radix)
    twist_imag = twist_imag.reshape(first_radix, mid_radix, last_radix)
    inner_real, inner_imag = rotation(mid_radix, last_radix, mid_radix * last_radix)
    return (
        outer_real,
        outer_imag,
        mid_real,
        mid_imag,
        last_real,
        last_imag,
        twist_real,
        twist_imag,
        inner_real,
        inner_imag,
    )


def apply_matrix(pattern, real_part, imag_part, matrix_real, matrix_imag):
    out_real = jnp.einsum(pattern, real_part, matrix_real, precision=HIGHEST) - jnp.einsum(
        pattern, imag_part, matrix_imag, precision=HIGHEST
    )
    out_imag = jnp.einsum(pattern, real_part, matrix_imag, precision=HIGHEST) + jnp.einsum(
        pattern, imag_part, matrix_real, precision=HIGHEST
    )
    return (out_real, out_imag)


def complex_times(left_real, left_imag, right_real, right_imag):
    return (
        left_real * right_real - left_imag * right_imag,
        left_real * right_imag + left_imag * right_real,
    )


def forward(real_part, imag_part, table_set, radix_sizes):
    first_radix, mid_radix, last_radix = radix_sizes
    half_first = first_radix // 2
    batch_rows = real_part.shape[0]
    (
        outer_real,
        outer_imag,
        mid_real,
        mid_imag,
        last_real,
        last_imag,
        twist_real,
        twist_imag,
        inner_real,
        inner_imag,
    ) = table_set
    real_part = real_part.reshape(batch_rows, half_first, mid_radix, last_radix)
    imag_part = imag_part.reshape(batch_rows, half_first, mid_radix, last_radix)
    real_part, imag_part = apply_matrix(
        "banm,ak->bknm", real_part, imag_part, outer_real[:half_first], outer_imag[:half_first]
    )
    real_part, imag_part = complex_times(real_part, imag_part, twist_real, twist_imag)
    real_part, imag_part = apply_matrix("bknm,nj->bkjm", real_part, imag_part, mid_real, mid_imag)
    real_part, imag_part = complex_times(real_part, imag_part, inner_real, inner_imag)
    return apply_matrix("bkjm,mq->bkjq", real_part, imag_part, last_real, last_imag)


def inverse(real_part, imag_part, table_set, radix_sizes):
    first_radix, mid_radix, last_radix = radix_sizes
    half_first = first_radix // 2
    batch_rows = real_part.shape[0]
    (
        outer_real,
        outer_imag,
        mid_real,
        mid_imag,
        last_real,
        last_imag,
        twist_real,
        twist_imag,
        inner_real,
        inner_imag,
    ) = table_set
    real_part, imag_part = apply_matrix(
        "bkjq,mq->bkjm", real_part, imag_part, last_real / last_radix, -last_imag / last_radix
    )
    real_part, imag_part = complex_times(real_part, imag_part, inner_real, -inner_imag)
    real_part, imag_part = apply_matrix(
        "bkjm,nj->bknm", real_part, imag_part, mid_real / mid_radix, -mid_imag / mid_radix
    )
    real_part, imag_part = complex_times(real_part, imag_part, twist_real, -twist_imag)
    matrix_real = outer_real[:half_first] / first_radix
    matrix_imag = -outer_imag[:half_first] / first_radix
    out_real, out_imag = apply_matrix(
        "bknm,ak->banm", real_part, imag_part, matrix_real, matrix_imag
    )
    return (out_real.reshape(batch_rows, -1), out_imag.reshape(batch_rows, -1))


def spectrum(decay_rows, residue_rows, radix_sizes, seq_length):
    first_radix, mid_radix, last_radix = radix_sizes
    length_all = first_radix * mid_radix * last_radix
    poles = decay_rows.shape[1]
    shape_all = (first_radix, mid_radix, last_radix)
    frequency = (
        lax.broadcasted_iota(jnp.int32, shape_all, 0)
        + first_radix * lax.broadcasted_iota(jnp.int32, shape_all, 1)
        + first_radix * mid_radix * lax.broadcasted_iota(jnp.int32, shape_all, 2)
    )
    half_angle = frequency.astype(jnp.float32) * (math.pi / length_all)
    sin_half = jnp.sin(half_angle)
    sin_full = jnp.sin(2.0 * half_angle)
    parity_sign = (1 - 2 * (frequency % 2)).astype(jnp.float32)

    def add_pole(pole_index, running):
        run_real, run_imag = running
        rate_col = lax.dynamic_slice_in_dim(decay_rows, pole_index, 1, 1).reshape(-1, 1, 1, 1)
        weight = lax.dynamic_slice_in_dim(residue_rows, pole_index, 1, 1).reshape(
            -1, 1, 1, 1
        ) * jnp.sqrt(2.0 * rate_col / poles)
        retained = jnp.exp(-rate_col)
        den_real = -jnp.expm1(-rate_col) + 2.0 * retained * sin_half * sin_half
        den_imag = retained * sin_full
        pole_scale = (
            weight
            * (1.0 - jnp.exp(-rate_col * seq_length) * parity_sign)
            / (den_real * den_real + den_imag * den_imag)
        )
        return (run_real + pole_scale * den_real, run_imag - pole_scale * den_imag)

    zeros_all = jnp.zeros((decay_rows.shape[0],) + shape_all, jnp.float32)
    return lax.fori_loop(0, poles, add_pole, (zeros_all, zeros_all))


def general(x_gate, x_post, values, decay, residue, w_out):
    tok_rows, block_width = x_gate.shape
    ctx_count = lax.axis_size("ctx")
    tp_count = lax.axis_size("tp")
    chan_group = block_width // ctx_count
    seq_length = tok_rows * ctx_count
    radix_sizes = radices(2 * seq_length)
    table_set = tables(radix_sizes)
    first_row = lax.axis_index("ctx") * chan_group
    own_rate = lax.dynamic_slice_in_dim(decay, first_row, chan_group, 1)
    own_residue = lax.dynamic_slice_in_dim(residue, first_row, chan_group, 1)
    own_spec = [
        spectrum(own_rate[filter_index], own_residue[filter_index], radix_sizes, seq_length)
        for filter_index in range(2)
    ]
    forward_rows = [x_gate, values] + [x_post]
    row_count = len(forward_rows)
    base_rows = jnp.stack(forward_rows)
    copied = base_rows
    for bit_index in range(tp_count.bit_length() - 1):
        copied = partner(copied, "tp", bit_index)
    sent_rows = jnp.concatenate([base_rows, copied[:, :, ::-1]], axis=0)
    received = lax.all_to_all(
        jnp.swapaxes(sent_rows, 1, 2), "ctx", split_axis=1, concat_axis=2, tiled=True
    )
    gate_fwd = received[0].astype(jnp.float32)
    value_fwd = received[1].astype(jnp.float32)
    mirrored = received[row_count:, :, ::-1].astype(jnp.float32)
    spec_real, spec_imag = forward(value_fwd, mirrored[1], table_set, radix_sizes)
    spec_real, spec_imag = complex_times(spec_real, spec_imag, own_spec[0][0], own_spec[0][1])
    along_fwd, along_rev = inverse(spec_real, spec_imag, table_set, radix_sizes)
    spec_real, spec_imag = forward(
        gate_fwd * along_fwd, mirrored[0] * along_rev, table_set, radix_sizes
    )
    spec_real, spec_imag = complex_times(spec_real, spec_imag, own_spec[1][0], own_spec[1][1])
    sum_fwd, sum_rev = inverse(spec_real, spec_imag, table_set, radix_sizes)
    sum_fwd = received[2].astype(jnp.float32) * sum_fwd
    sum_rev = mirrored[2] * sum_rev
    results = jnp.stack([sum_fwd, sum_rev[:, ::-1]])
    returned = lax.all_to_all(
        results.astype(jnp.bfloat16), "ctx", split_axis=2, concat_axis=1, tiled=True
    ).astype(results.dtype)
    flipped = returned[1, ::-1, :]
    for bit_index in range(tp_count.bit_length() - 1):
        flipped = partner(flipped.astype(jnp.bfloat16), "tp", bit_index).astype(flipped.dtype)
    total_rows = returned[0] + flipped
    total_rows = total_rows.T
    mixed_rows = total_rows.astype(jnp.bfloat16)
    whole_rows = lax.all_gather(mixed_rows, "tp", axis=1, tiled=True)
    projected = lax.dot_general(
        whole_rows,
        lax.all_gather(w_out, "ctx", axis=0, tiled=True),
        (((1,), (1,)), ((), ())),
        preferred_element_type=jnp.float32,
    )
    return projected.astype(jnp.bfloat16)


def cycle(row_factor, col_factor, modulus):
    angle = (row_factor * col_factor % modulus).astype(jnp.float32) * (2.0 * math.pi / modulus)
    return jnp.cos(angle), jnp.sin(angle)


def put_tables(table_ref, back_ref=None):
    block = table_ref.shape[1]
    modulus = 4 * block
    coarse = 16
    rows = lax.broadcasted_iota(jnp.int32, (coarse, block), 0)
    cols = lax.broadcasted_iota(jnp.int32, (coarse, block), 1)

    def parts(big, small):
        for place in range(block // coarse):
            big_cos, big_sin = (part[place : place + 1] for part in big)
            span = slice(place * coarse, (place + 1) * coarse)
            below = slice(block + place * coarse, block + (place + 1) * coarse)
            cos = halves(big_cos * small[0] - big_sin * small[1])
            sin = halves(-(big_sin * small[0] + big_cos * small[1]))
            yield span, below, cos, sin

    frequency = 2 * cols + 1
    for span, _, cos, sin in parts(cycle(coarse * rows, frequency, modulus), cycle(rows, frequency, modulus)):
        table_ref[0, span, :block], table_ref[1, span, :block] = cos
        table_ref[0, span, block:], table_ref[1, span, block:] = sin
    if back_ref is not None:
        for span, below, cos, sin in parts(cycle(2 * coarse * rows, cols, modulus), cycle(2 * rows + 1, cols, modulus)):
            back_ref[0, span], back_ref[1, span] = cos
            back_ref[0, below], back_ref[1, below] = sin


def halves(value):
    high = value.astype(jnp.bfloat16)
    return high, (value - high.astype(jnp.float32)).astype(jnp.bfloat16)


def mul(left, right):
    return jnp.dot(left, right, preferred_element_type=jnp.float32)


def mul3(high, low, table_ref):
    return mul(high, table_ref[0]) + (mul(low, table_ref[0]) + mul(high, table_ref[1]))


def pack_kernel(
    gate_hbm, value_hbm, post_hbm, decay_hbm, residue_hbm,
    out_hbm, own_ref, sent_ref, held_ref, par_ref, ready_ref, sems, out_sems,
):
    ctx_count, _, group, tok = out_hbm.shape
    width = gate_hbm.shape[1]
    half = decay_hbm.shape[0]
    position = lax.axis_index("ctx")
    pairs = [(source, held_ref.at[place]) for place, source in enumerate((value_hbm, gate_hbm, post_hbm))]
    pairs += [(decay_hbm, par_ref.at[:half]), (residue_hbm, par_ref.at[half:])]
    copies = [pltpu.make_async_copy(*pair, sems.at[place]) for place, pair in enumerate(pairs)]
    for copy in copies:
        copy.start()
    sends = []
    for place, copy in enumerate(copies[:3]):
        copy.wait()
        for first in range(0, width, tok):
            turned = held_ref[place, :, first : first + tok].T
            for part in range(tok // group):
                ready_ref[first // group + part, place] = turned[part * group : (part + 1) * group]
        sends.append(pltpu.make_async_copy(ready_ref.at[:, place], out_hbm.at[:, place], out_sems.at[place]))
        sends[-1].start()
    copies[3].wait()
    copies[4].wait()
    odd = position % 2 == 1
    lane = lax.broadcasted_iota(jnp.int32, own_ref.shape, 1)

    def tile_of(index):
        return par_ref[:, pl.ds(pl.multiple_of(index // 2 * tok, tok), tok)]

    def to_front(value):
        return jnp.where(odd, pltpu.roll(value, group, 1), value)

    own_ref[...] = to_front(tile_of(position))
    turned = tile_of(ctx_count - 1 - position)
    shift = 1
    while shift < tok:
        turned = jnp.where(lane & shift == 0, pltpu.roll(turned, tok - shift, 1), pltpu.roll(turned, shift, 1))
        shift *= 2
    sent_ref[...] = to_front(turned)
    for copy in sends:
        copy.wait()


def put_spectra(poles, index, turned, out_ref, time_ref, table_ref):
    blocks, group, twice = out_ref.shape
    block = twice // 2
    lanes = 128
    ramp = lax.broadcasted_iota(jnp.int32, (8, lanes), 1).astype(jnp.float32)
    sign = (1 - 2 * (lax.broadcasted_iota(jnp.int32, (group, block), 1) % 2)).astype(jnp.float32)
    for row in range(0, group, 8):
        rows = slice(row, row + 8)
        rate = turned[rows, index * poles : (index + 1) * poles]
        scale = turned[rows, (2 + index) * poles : (3 + index) * poles] * (jnp.sqrt(rate * (2.0 / poles)) / block)
        jump = jnp.exp(rate * -lanes)
        sums = [None] * (blocks * block // lanes)
        for pole in range(poles):
            term = scale[:, pole : pole + 1] * jnp.exp(-rate[:, pole : pole + 1] * ramp)
            step = jnp.broadcast_to(jump[:, pole : pole + 1], (8, lanes))
            for place in range(len(sums)):
                sums[place] = term if pole == 0 else sums[place] + term
                if place + 1 < len(sums):
                    term = term * step
        for place, total in enumerate(sums):
            lag, lane = divmod(place * lanes, block)
            time_ref[lag * group + row : lag * group + row + 8, lane : lane + lanes] = total
    spec = mul3(*halves(time_ref[...]), table_ref)
    for lag in range(blocks):
        real = spec[lag * group : (lag + 1) * group, :block]
        imag = spec[lag * group : (lag + 1) * group, block:]
        if lag > 0:
            real = real - sign * spec[(lag - 1) * group : lag * group, block:]
            imag = imag + sign * spec[(lag - 1) * group : lag * group, :block]
        out_ref[lag, :, :block] = real
        out_ref[lag, :, block:] = imag


def filter_kernel(poles, par_ref, out_ref, time_ref, table_ref):
    put_tables(table_ref)
    turned = par_ref[...].T
    for index in range(2):
        put_spectra(poles, index, turned, out_ref.at[index], time_ref.at[index], table_ref)


def conv_kernel(
    poles, x_ref, own_ref, par_ref, out_hbm,
    paired_ref, time_ref, table_ref, back_ref, spec_ref, high_ref, low_ref, ready_ref, sems,
):
    put_tables(table_ref, back_ref)
    turned = par_ref[...].T
    blocks, group, twice = own_ref.shape[1:]
    block = twice // 2
    rows_all = blocks * group
    tall, wide = 16, 128
    pieces = x_ref.shape[0] // blocks

    def rows_of(position):
        return jnp.concatenate(
            [
                jnp.concatenate([x_ref[m * pieces + s, position] for s in range(pieces)], axis=1)
                for m in range(blocks)
            ],
            axis=0,
        )

    def times(index, side, source, row, lane):
        data = []
        for m in range(blocks):
            rows = slice(source + m * group + row, source + m * group + row + tall)
            data.append((spec_ref[rows, lane : lane + wide], spec_ref[rows, block + lane : block + lane + wide]))
        sums = [None] * blocks
        for lag in range(blocks):
            h_ref = (own_ref, paired_ref)[side]
            f_re = h_ref[index, lag, row : row + tall, lane : lane + wide]
            f_im = h_ref[index, lag, row : row + tall, block + lane : block + lane + wide]
            for m in range(blocks - lag):
                target, (d_re, d_im) = (m + lag, data[m]) if side == 0 else (m, data[m + lag])
                if side == 0:
                    real, imag = f_re * d_re - f_im * d_im, f_re * d_im + f_im * d_re
                else:
                    real, imag = f_re * d_re + f_im * d_im, f_re * d_im - f_im * d_re
                if sums[target] is not None:
                    real, imag = sums[target][0] + real, sums[target][1] + imag
                sums[target] = (real, imag)
        return sums

    def keep(target, row, lane, sums):
        for m in range(blocks):
            rows = slice(target + m * group + row, target + m * group + row + tall)
            for part in range(2):
                cols = slice(part * block + lane, part * block + lane + wide)
                high_ref[rows, cols], low_ref[rows, cols] = halves(sums[m][part])

    chunks = [(row, lane) for row in range(0, group, tall) for lane in range(0, block, wide)]

    value = rows_of(0)
    gate = rows_of(1).astype(jnp.float32)
    spec_ref[:rows_all] = mul(value, table_ref[0]) + mul(value, table_ref[1])
    sides = [slice(side * rows_all, (side + 1) * rows_all) for side in range(2)]
    gated = []
    put_spectra(poles, 0, turned, paired_ref.at[0], time_ref.at[0], table_ref)
    for side in range(2):
        for row, lane in chunks:
            keep(side * rows_all, row, lane, times(0, side, 0, row, lane))
        gated.append(halves(gate * mul3(high_ref[sides[side]], low_ref[sides[side]], back_ref)))
    put_spectra(poles, 1, turned, paired_ref.at[1], time_ref.at[1], table_ref)
    for side in range(2):
        spec_ref[sides[side]] = mul3(*gated[side], table_ref)
    for row, lane in chunks:
        ahead, back = times(1, 0, 0, row, lane), times(1, 1, rows_all, row, lane)
        keep(0, row, lane, [(a[0] + b[0], a[1] + b[1]) for a, b in zip(ahead, back)])
    post = rows_of(2)
    tok = block // pieces
    sends = []
    for part in range(2):
        rows = slice(part * rows_all // 2, (part + 1) * rows_all // 2)
        summed = mul3(high_ref[rows], low_ref[rows], back_ref)
        mixed = (post[rows].astype(jnp.float32) * summed).astype(jnp.bfloat16)
        first = part * blocks // 2 * pieces
        for m in range(blocks // 2):
            for s in range(pieces):
                ready_ref[first + m * pieces + s] = mixed[m * group : (m + 1) * group, s * tok : (s + 1) * tok]
        span = pl.ds(first, blocks // 2 * pieces)
        for copy in range(out_hbm.shape[0]):
            sends.append(pltpu.make_async_copy(ready_ref.at[span], out_hbm.at[copy, span], sems.at[part, copy]))
            sends[-1].start()
    for send in sends:
        send.wait()


def project_kernel(mixed_ref, *refs):
    w_refs, (out_ref, held_ref) = refs[:-2], refs[-2:]
    rows = w_refs[0].shape[0]
    position = lax.axis_index("ctx")
    total = mul(jnp.concatenate([w_ref[...] for w_ref in w_refs], axis=0), mixed_ref[...])
    for mask in range(len(w_refs)):
        first = pl.multiple_of((position ^ mask) * rows, rows)
        held_ref[pl.ds(first, rows)] = total[mask * rows : (mask + 1) * rows]
    out_ref[...] = held_ref[...].T.astype(jnp.bfloat16)


def whole_call(kernel, out_shape, scratch, flops, nbytes, *operands, in_hbm=0, out_hbm=()):
    results = pl.pallas_call(
        kernel,
        out_shape=out_shape,
        in_specs=[
            pl.BlockSpec(memory_space=pltpu.HBM if place < in_hbm else pltpu.VMEM) for place in range(len(operands))
        ],
        out_specs=[
            pl.BlockSpec(memory_space=pltpu.HBM if place in out_hbm else pltpu.VMEM) for place in range(len(out_shape))
        ],
        scratch_shapes=scratch,
        cost_estimate=pl.CostEstimate(flops=flops, bytes_accessed=nbytes, transcendentals=0),
        compiler_params=pltpu.CompilerParams(vmem_limit_bytes=None if in_hbm else 32 * 2**20),
    )(*operands)
    return results if len(out_shape) > 1 else results[0]


def blocked(x_gate, x_post, values, decay, residue, w_out):
    tok, width = x_gate.shape
    ctx_count = lax.axis_size("ctx")
    tp_count = lax.axis_size("tp")
    group = width // ctx_count
    poles = decay.shape[2]
    block = 2 * tok
    blocks = tok * ctx_count // block
    rows, channels = w_out.shape
    half = 2 * poles

    packed, own, mirrored = whole_call(
        pack_kernel,
        (
            jax.ShapeDtypeStruct((ctx_count, 3, group, tok), jnp.bfloat16),
            jax.ShapeDtypeStruct((2 * half, tok), jnp.float32),
            jax.ShapeDtypeStruct((2 * half, tok), jnp.float32),
        ),
        [
            pltpu.VMEM((3, tok, width), jnp.bfloat16),
            pltpu.VMEM((2 * half, width), jnp.float32),
            pltpu.VMEM((ctx_count, 3, group, tok), jnp.bfloat16),
            pltpu.SemaphoreType.DMA((5,)),
            pltpu.SemaphoreType.DMA((3,)),
        ],
        0,
        6 * tok * width * 2,
        x_gate,
        values,
        x_post,
        jnp.swapaxes(decay, 1, 2).reshape(half, width),
        jnp.swapaxes(residue, 1, 2).reshape(half, width),
        in_hbm=5,
        out_hbm=(0,),
    )
    paired = lax.ppermute(mirrored, "tp", [(z, tp_count - 1 - z) for z in range(tp_count)])
    received = lax.all_to_all(packed, "ctx", split_axis=0, concat_axis=0, tiled=True)

    w_x, w_y = partner(w_out, "ctx", 1), partner(w_out, "ctx", 2)
    w_x, w_y, own = lax.optimization_barrier((w_x, w_y, own))
    w_far = partner(w_x, "ctx", 2)
    own_spectra = whole_call(
        functools.partial(filter_kernel, poles),
        (jax.ShapeDtypeStruct((2, blocks, group, 2 * block), jnp.float32),),
        [
            pltpu.VMEM((2, blocks * group, block), jnp.float32),
            pltpu.VMEM((2, block, 2 * block), jnp.bfloat16),
        ],
        2 * 2 * blocks * group * block * 2 * block * 3,
        2 * blocks * group * 2 * block * 4,
        own,
    )
    mixed = whole_call(
        functools.partial(conv_kernel, poles),
        (jax.ShapeDtypeStruct((tp_count, ctx_count, group, tok), jnp.bfloat16),),
        [
            pltpu.VMEM((2, blocks, group, 2 * block), jnp.float32),
            pltpu.VMEM((2, blocks * group, block), jnp.float32),
            pltpu.VMEM((2, block, 2 * block), jnp.bfloat16),
            pltpu.VMEM((2, 2 * block, block), jnp.bfloat16),
            pltpu.VMEM((2 * blocks * group, 2 * block), jnp.float32),
            pltpu.VMEM((2 * blocks * group, 2 * block), jnp.bfloat16),
            pltpu.VMEM((2 * blocks * group, 2 * block), jnp.bfloat16),
            pltpu.VMEM((ctx_count, group, tok), jnp.bfloat16),
            pltpu.SemaphoreType.DMA((2, tp_count)),
        ],
        2 * 8 * blocks * group * block * 2 * block * 3,
        4 * blocks * group * 2 * block * 4,
        received,
        own_spectra,
        paired,
        out_hbm=(0,),
    )
    mixed, w_far, w_x, w_y, w_own = lax.optimization_barrier((mixed, w_far, w_x, w_y, w_out))
    w_blocks = {0: w_own, 2: w_x, 4: w_y, 6: w_far}
    for mask in range(0, ctx_count, 2):
        w_blocks[mask + 1] = partner(w_blocks[mask], "ctx", 0)
    every = lax.all_to_all(
        mixed.reshape(tp_count * ctx_count, group, tok), ("tp", "ctx"), split_axis=0, concat_axis=0, tiled=True
    ).reshape(channels, tok)
    return whole_call(
        project_kernel,
        (jax.ShapeDtypeStruct((tok, rows * ctx_count), jnp.bfloat16),),
        [pltpu.VMEM((rows * ctx_count, tok), jnp.float32)],
        2 * tok * rows * ctx_count * channels,
        2 * rows * ctx_count * channels,
        every,
        *[w_blocks[mask] for mask in range(ctx_count)],
    )


def local(x_gate, x_post, values, decay, residue, w_out):
    tok, width = x_gate.shape
    ctx_count = lax.axis_size("ctx")
    if tok == 128 and width == 512 and ctx_count == 8 and lax.axis_size("tp") == 4:
        return blocked(x_gate, x_post, values, decay, residue, w_out)
    return general(x_gate, x_post, values, decay, residue, w_out)


def solution(mesh):
    in_specs = (
        P("ctx", "tp"),
        P("ctx", "tp"),
        P("ctx", "tp"),
        P(None, "tp", None),
        P(None, "tp", None),
        P(("tp", "ctx"), None),
    )
    out_specs = P("ctx", "tp")
    return jax.shard_map(local, mesh=mesh, in_specs=in_specs, out_specs=out_specs, check_vma=False)
```

```python
import functools
import math

import jax
import jax.numpy as jnp
from jax import lax
from jax.experimental import pallas as pl
from jax.experimental.pallas import tpu as pltpu
from jax.sharding import PartitionSpec as P

HIGHEST = lax.Precision.HIGHEST


def partner(value, axis, bit):
    mask = 2**bit
    pairs = [(source, source ^ mask) for source in range(lax.axis_size(axis))]
    return lax.ppermute(value, axis, pairs)


def radices(length_all):
    last_radix = min(128, length_all // 4)
    first_radix = min(32, length_all // last_radix)
    return (first_radix, length_all // (first_radix * last_radix), last_radix)


def rotation(row_count, col_count, modulus):
    product = (
        lax.broadcasted_iota(jnp.int32, (row_count, col_count), 0)
        * lax.broadcasted_iota(jnp.int32, (row_count, col_count), 1)
        % modulus
    )
    angle = product.astype(jnp.float32) * (2.0 * math.pi / modulus)
    return (jnp.cos(angle), -jnp.sin(angle))


def tables(radix_sizes):
    first_radix, mid_radix, last_radix = radix_sizes
    length_all = first_radix * mid_radix * last_radix
    outer_real, outer_imag = rotation(first_radix, first_radix, first_radix)
    mid_real, mid_imag = rotation(mid_radix, mid_radix, mid_radix)
    last_real, last_imag = rotation(last_radix, last_radix, last_radix)
    twist_real, twist_imag = rotation(first_radix, mid_radix * last_radix, length_all)
    twist_real = twist_real.reshape(first_radix, mid_radix, last_radix)
    twist_imag = twist_imag.reshape(first_radix, mid_radix, last_radix)
    inner_real, inner_imag = rotation(mid_radix, last_radix, mid_radix * last_radix)
    return (
        outer_real,
        outer_imag,
        mid_real,
        mid_imag,
        last_real,
        last_imag,
        twist_real,
        twist_imag,
        inner_real,
        inner_imag,
    )


def apply_matrix(pattern, real_part, imag_part, matrix_real, matrix_imag):
    out_real = jnp.einsum(pattern, real_part, matrix_real, precision=HIGHEST) - jnp.einsum(
        pattern, imag_part, matrix_imag, precision=HIGHEST
    )
    out_imag = jnp.einsum(pattern, real_part, matrix_imag, precision=HIGHEST) + jnp.einsum(
        pattern, imag_part, matrix_real, precision=HIGHEST
    )
    return (out_real, out_imag)


def complex_times(left_real, left_imag, right_real, right_imag):
    return (
        left_real * right_real - left_imag * right_imag,
        left_real * right_imag + left_imag * right_real,
    )


def forward(real_part, imag_part, table_set, radix_sizes):
    first_radix, mid_radix, last_radix = radix_sizes
    half_first = first_radix // 2
    batch_rows = real_part.shape[0]
    (
        outer_real,
        outer_imag,
        mid_real,
        mid_imag,
        last_real,
        last_imag,
        twist_real,
        twist_imag,
        inner_real,
        inner_imag,
    ) = table_set
    real_part = real_part.reshape(batch_rows, half_first, mid_radix, last_radix)
    imag_part = imag_part.reshape(batch_rows, half_first, mid_radix, last_radix)
    real_part, imag_part = apply_matrix(
        "banm,ak->bknm", real_part, imag_part, outer_real[:half_first], outer_imag[:half_first]
    )
    real_part, imag_part = complex_times(real_part, imag_part, twist_real, twist_imag)
    real_part, imag_part = apply_matrix("bknm,nj->bkjm", real_part, imag_part, mid_real, mid_imag)
    real_part, imag_part = complex_times(real_part, imag_part, inner_real, inner_imag)
    return apply_matrix("bkjm,mq->bkjq", real_part, imag_part, last_real, last_imag)


def inverse(real_part, imag_part, table_set, radix_sizes):
    first_radix, mid_radix, last_radix = radix_sizes
    half_first = first_radix // 2
    batch_rows = real_part.shape[0]
    (
        outer_real,
        outer_imag,
        mid_real,
        mid_imag,
        last_real,
        last_imag,
        twist_real,
        twist_imag,
        inner_real,
        inner_imag,
    ) = table_set
    real_part, imag_part = apply_matrix(
        "bkjq,mq->bkjm", real_part, imag_part, last_real / last_radix, -last_imag / last_radix
    )
    real_part, imag_part = complex_times(real_part, imag_part, inner_real, -inner_imag)
    real_part, imag_part = apply_matrix(
        "bkjm,nj->bknm", real_part, imag_part, mid_real / mid_radix, -mid_imag / mid_radix
    )
    real_part, imag_part = complex_times(real_part, imag_part, twist_real, -twist_imag)
    matrix_real = outer_real[:half_first] / first_radix
    matrix_imag = -outer_imag[:half_first] / first_radix
    out_real, out_imag = apply_matrix(
        "bknm,ak->banm", real_part, imag_part, matrix_real, matrix_imag
    )
    return (out_real.reshape(batch_rows, -1), out_imag.reshape(batch_rows, -1))


def spectrum(decay_rows, residue_rows, radix_sizes, seq_length):
    first_radix, mid_radix, last_radix = radix_sizes
    length_all = first_radix * mid_radix * last_radix
    poles = decay_rows.shape[1]
    shape_all = (first_radix, mid_radix, last_radix)
    frequency = (
        lax.broadcasted_iota(jnp.int32, shape_all, 0)
        + first_radix * lax.broadcasted_iota(jnp.int32, shape_all, 1)
        + first_radix * mid_radix * lax.broadcasted_iota(jnp.int32, shape_all, 2)
    )
    half_angle = frequency.astype(jnp.float32) * (math.pi / length_all)
    sin_half = jnp.sin(half_angle)
    sin_full = jnp.sin(2.0 * half_angle)
    parity_sign = (1 - 2 * (frequency % 2)).astype(jnp.float32)

    def add_pole(pole_index, running):
        run_real, run_imag = running
        rate_col = lax.dynamic_slice_in_dim(decay_rows, pole_index, 1, 1).reshape(-1, 1, 1, 1)
        weight = lax.dynamic_slice_in_dim(residue_rows, pole_index, 1, 1).reshape(
            -1, 1, 1, 1
        ) * jnp.sqrt(2.0 * rate_col / poles)
        retained = jnp.exp(-rate_col)
        den_real = -jnp.expm1(-rate_col) + 2.0 * retained * sin_half * sin_half
        den_imag = retained * sin_full
        pole_scale = (
            weight
            * (1.0 - jnp.exp(-rate_col * seq_length) * parity_sign)
            / (den_real * den_real + den_imag * den_imag)
        )
        return (run_real + pole_scale * den_real, run_imag - pole_scale * den_imag)

    zeros_all = jnp.zeros((decay_rows.shape[0],) + shape_all, jnp.float32)
    return lax.fori_loop(0, poles, add_pole, (zeros_all, zeros_all))


def general(x_gate, x_post, values, decay, residue, w_out):
    tok_rows, block_width = x_gate.shape
    ctx_count = lax.axis_size("ctx")
    tp_count = lax.axis_size("tp")
    chan_group = block_width // ctx_count
    seq_length = tok_rows * ctx_count
    radix_sizes = radices(2 * seq_length)
    table_set = tables(radix_sizes)
    first_row = lax.axis_index("ctx") * chan_group
    own_rate = lax.dynamic_slice_in_dim(decay, first_row, chan_group, 1)
    own_residue = lax.dynamic_slice_in_dim(residue, first_row, chan_group, 1)
    own_spec = [
        spectrum(own_rate[filter_index], own_residue[filter_index], radix_sizes, seq_length)
        for filter_index in range(2)
    ]
    forward_rows = [x_gate, values] + [x_post]
    row_count = len(forward_rows)
    base_rows = jnp.stack(forward_rows)
    copied = base_rows
    for bit_index in range(tp_count.bit_length() - 1):
        copied = partner(copied, "tp", bit_index)
    sent_rows = jnp.concatenate([base_rows, copied[:, :, ::-1]], axis=0)
    received = lax.all_to_all(
        jnp.swapaxes(sent_rows, 1, 2), "ctx", split_axis=1, concat_axis=2, tiled=True
    )
    gate_fwd = received[0].astype(jnp.float32)
    value_fwd = received[1].astype(jnp.float32)
    mirrored = received[row_count:, :, ::-1].astype(jnp.float32)
    spec_real, spec_imag = forward(value_fwd, mirrored[1], table_set, radix_sizes)
    spec_real, spec_imag = complex_times(spec_real, spec_imag, own_spec[0][0], own_spec[0][1])
    along_fwd, along_rev = inverse(spec_real, spec_imag, table_set, radix_sizes)
    spec_real, spec_imag = forward(
        gate_fwd * along_fwd, mirrored[0] * along_rev, table_set, radix_sizes
    )
    spec_real, spec_imag = complex_times(spec_real, spec_imag, own_spec[1][0], own_spec[1][1])
    sum_fwd, sum_rev = inverse(spec_real, spec_imag, table_set, radix_sizes)
    sum_fwd = received[2].astype(jnp.float32) * sum_fwd
    sum_rev = mirrored[2] * sum_rev
    results = jnp.stack([sum_fwd, sum_rev[:, ::-1]])
    returned = lax.all_to_all(
        results.astype(jnp.bfloat16), "ctx", split_axis=2, concat_axis=1, tiled=True
    ).astype(results.dtype)
    flipped = returned[1, ::-1, :]
    for bit_index in range(tp_count.bit_length() - 1):
        flipped = partner(flipped.astype(jnp.bfloat16), "tp", bit_index).astype(flipped.dtype)
    total_rows = returned[0] + flipped
    total_rows = total_rows.T
    mixed_rows = total_rows.astype(jnp.bfloat16)
    whole_rows = lax.all_gather(mixed_rows, "tp", axis=1, tiled=True)
    projected = lax.dot_general(
        whole_rows,
        lax.all_gather(w_out, "ctx", axis=0, tiled=True),
        (((1,), (1,)), ((), ())),
        preferred_element_type=jnp.float32,
    )
    return projected.astype(jnp.bfloat16)


def cycle(row_factor, col_factor, modulus):
    angle = (row_factor * col_factor % modulus).astype(jnp.float32) * (2.0 * math.pi / modulus)
    return jnp.cos(angle), jnp.sin(angle)


def put_tables(table_ref, back_ref=None):
    block = table_ref.shape[1]
    modulus = 4 * block
    coarse = 16
    rows = lax.broadcasted_iota(jnp.int32, (coarse, block), 0)
    cols = lax.broadcasted_iota(jnp.int32, (coarse, block), 1)

    def parts(big, small):
        for place in range(block // coarse):
            big_cos, big_sin = (part[place : place + 1] for part in big)
            span = slice(place * coarse, (place + 1) * coarse)
            below = slice(block + place * coarse, block + (place + 1) * coarse)
            cos = halves(big_cos * small[0] - big_sin * small[1])
            sin = halves(-(big_sin * small[0] + big_cos * small[1]))
            yield span, below, cos, sin

    frequency = 2 * cols + 1
    for span, _, cos, sin in parts(cycle(coarse * rows, frequency, modulus), cycle(rows, frequency, modulus)):
        table_ref[0, span, :block], table_ref[1, span, :block] = cos
        table_ref[0, span, block:], table_ref[1, span, block:] = sin
    if back_ref is not None:
        for span, below, cos, sin in parts(cycle(2 * coarse * rows, cols, modulus), cycle(2 * rows + 1, cols, modulus)):
            back_ref[0, span], back_ref[1, span] = cos
            back_ref[0, below], back_ref[1, below] = sin


def halves(value):
    high = value.astype(jnp.bfloat16)
    return high, (value - high.astype(jnp.float32)).astype(jnp.bfloat16)


def mul(left, right):
    return jnp.dot(left, right, preferred_element_type=jnp.float32)


def mul3(high, low, table_ref):
    return mul(high, table_ref[0]) + (mul(low, table_ref[0]) + mul(high, table_ref[1]))


def pack_kernel(
    gate_hbm, value_hbm, post_hbm, decay_hbm, residue_hbm,
    out_hbm, own_hbm, sent_hbm, held_ref, par_ref, cut_ref, ready_ref, sems, out_sems,
):
    ctx_count, _, group, tok = out_hbm.shape
    width = gate_hbm.shape[1]
    half = decay_hbm.shape[0]
    position = lax.axis_index("ctx")
    pairs = [(decay_hbm, par_ref.at[:half]), (residue_hbm, par_ref.at[half:])]
    pairs += [(source, held_ref.at[place]) for place, source in enumerate((value_hbm, gate_hbm, post_hbm))]
    copies = [pltpu.make_async_copy(*pair, sems.at[place]) for place, pair in enumerate(pairs)]
    for copy in copies:
        copy.start()
    copies[0].wait()
    copies[1].wait()
    odd = position % 2 == 1
    lane = lax.broadcasted_iota(jnp.int32, (2 * half, tok), 1)

    def tile_of(index):
        return par_ref[:, pl.ds(pl.multiple_of(index // 2 * tok, tok), tok)]

    def to_front(value):
        return jnp.where(odd, pltpu.roll(value, group, 1), value)

    turned = tile_of(ctx_count - 1 - position)
    shift = 1
    while shift < tok:
        turned = jnp.where(lane & shift == 0, pltpu.roll(turned, tok - shift, 1), pltpu.roll(turned, shift, 1))
        shift *= 2
    cut_ref[0] = to_front(turned)
    cut_ref[1] = to_front(tile_of(position))
    sends = [
        pltpu.make_async_copy(cut_ref.at[place], target, out_sems.at[3 + place])
        for place, target in enumerate((sent_hbm, own_hbm))
    ]
    for send in sends:
        send.start()
    for place, copy in enumerate(copies[2:]):
        copy.wait()
        for first in range(0, width, tok):
            turned = held_ref[place, :, first : first + tok].T
            for part in range(tok // group):
                ready_ref[first // group + part, place] = turned[part * group : (part + 1) * group]
        sends.append(pltpu.make_async_copy(ready_ref.at[:, place], out_hbm.at[:, place], out_sems.at[place]))
        sends[-1].start()
    for send in sends:
        send.wait()


def put_spectra(poles, index, turned, out_ref, time_ref, table_ref):
    blocks, group, twice = out_ref.shape
    block = twice // 2
    lanes = 128
    ramp = lax.broadcasted_iota(jnp.int32, (8, lanes), 1).astype(jnp.float32)
    sign = (1 - 2 * (lax.broadcasted_iota(jnp.int32, (group, block), 1) % 2)).astype(jnp.float32)
    for row in range(0, group, 8):
        rows = slice(row, row + 8)
        rate = turned[rows, index * poles : (index + 1) * poles]
        scale = turned[rows, (2 + index) * poles : (3 + index) * poles] * (jnp.sqrt(rate * (2.0 / poles)) / block)
        jump = jnp.exp(rate * -lanes)
        sums = [None] * (blocks * block // lanes)
        for pole in range(poles):
            term = scale[:, pole : pole + 1] * jnp.exp(-rate[:, pole : pole + 1] * ramp)
            step = jnp.broadcast_to(jump[:, pole : pole + 1], (8, lanes))
            for place in range(len(sums)):
                sums[place] = term if pole == 0 else sums[place] + term
                if place + 1 < len(sums):
                    term = term * step
        for place, total in enumerate(sums):
            lag, lane = divmod(place * lanes, block)
            time_ref[lag * group + row : lag * group + row + 8, lane : lane + lanes] = total
    spec = mul3(*halves(time_ref[...]), table_ref)
    for lag in range(blocks):
        real = spec[lag * group : (lag + 1) * group, :block]
        imag = spec[lag * group : (lag + 1) * group, block:]
        if lag > 0:
            real = real - sign * spec[(lag - 1) * group : lag * group, block:]
            imag = imag + sign * spec[(lag - 1) * group : lag * group, :block]
        out_ref[lag, :, :block] = real
        out_ref[lag, :, block:] = imag


def filter_kernel(poles, par_ref, out_ref, time_ref, table_ref):
    put_tables(table_ref)
    turned = par_ref[...].T
    for index in range(2):
        put_spectra(poles, index, turned, out_ref.at[index], time_ref.at[index], table_ref)


def conv_kernel(
    poles, x_ref, own_ref, par_ref, out_hbm,
    paired_ref, time_ref, table_ref, back_ref, spec_ref, high_ref, low_ref, ready_ref, sems,
):
    put_tables(table_ref, back_ref)
    turned = par_ref[...].T
    blocks, group, twice = own_ref.shape[1:]
    block = twice // 2
    rows_all = blocks * group
    tall, wide = 16, 128
    pieces = x_ref.shape[0] // blocks

    def rows_of(position):
        return jnp.concatenate(
            [
                jnp.concatenate([x_ref[m * pieces + s, position] for s in range(pieces)], axis=1)
                for m in range(blocks)
            ],
            axis=0,
        )

    def times(index, side, source, row, lane):
        data = []
        for m in range(blocks):
            rows = slice(source + m * group + row, source + m * group + row + tall)
            data.append((spec_ref[rows, lane : lane + wide], spec_ref[rows, block + lane : block + lane + wide]))
        sums = [None] * blocks
        for lag in range(blocks):
            h_ref = (own_ref, paired_ref)[side]
            f_re = h_ref[index, lag, row : row + tall, lane : lane + wide]
            f_im = h_ref[index, lag, row : row + tall, block + lane : block + lane + wide]
            for m in range(blocks - lag):
                target, (d_re, d_im) = (m + lag, data[m]) if side == 0 else (m, data[m + lag])
                if side == 0:
                    real, imag = f_re * d_re - f_im * d_im, f_re * d_im + f_im * d_re
                else:
                    real, imag = f_re * d_re + f_im * d_im, f_re * d_im - f_im * d_re
                if sums[target] is not None:
                    real, imag = sums[target][0] + real, sums[target][1] + imag
                sums[target] = (real, imag)
        return sums

    def keep(target, row, lane, sums):
        for m in range(blocks):
            rows = slice(target + m * group + row, target + m * group + row + tall)
            for part in range(2):
                cols = slice(part * block + lane, part * block + lane + wide)
                high_ref[rows, cols], low_ref[rows, cols] = halves(sums[m][part])

    chunks = [(row, lane) for row in range(0, group, tall) for lane in range(0, block, wide)]

    value = rows_of(0)
    gate = rows_of(1).astype(jnp.float32)
    spec_ref[:rows_all] = mul(value, table_ref[0]) + mul(value, table_ref[1])
    sides = [slice(side * rows_all, (side + 1) * rows_all) for side in range(2)]
    gated = []
    put_spectra(poles, 0, turned, paired_ref.at[0], time_ref.at[0], table_ref)
    for side in range(2):
        for row, lane in chunks:
            keep(side * rows_all, row, lane, times(0, side, 0, row, lane))
        gated.append(halves(gate * mul3(high_ref[sides[side]], low_ref[sides[side]], back_ref)))
    put_spectra(poles, 1, turned, paired_ref.at[1], time_ref.at[1], table_ref)
    for side in range(2):
        spec_ref[sides[side]] = mul3(*gated[side], table_ref)
    for row, lane in chunks:
        ahead, back = times(1, 0, 0, row, lane), times(1, 1, rows_all, row, lane)
        keep(0, row, lane, [(a[0] + b[0], a[1] + b[1]) for a, b in zip(ahead, back)])
    post = rows_of(2)
    tok = block // pieces
    sends = []
    for part in range(2):
        rows = slice(part * rows_all // 2, (part + 1) * rows_all // 2)
        summed = mul3(high_ref[rows], low_ref[rows], back_ref)
        mixed = (post[rows].astype(jnp.float32) * summed).astype(jnp.bfloat16)
        first = part * blocks // 2 * pieces
        for m in range(blocks // 2):
            for s in range(pieces):
                ready_ref[first + m * pieces + s] = mixed[m * group : (m + 1) * group, s * tok : (s + 1) * tok]
        span = pl.ds(first, blocks // 2 * pieces)
        for copy in range(out_hbm.shape[0]):
            sends.append(pltpu.make_async_copy(ready_ref.at[span], out_hbm.at[copy, span], sems.at[part, copy]))
            sends[-1].start()
    for send in sends:
        send.wait()


def project_kernel(mixed_ref, *refs):
    w_refs, (out_ref, held_ref) = refs[:-2], refs[-2:]
    rows = w_refs[0].shape[0]
    position = lax.axis_index("ctx")
    total = mul(jnp.concatenate([w_ref[...] for w_ref in w_refs], axis=0), mixed_ref[...])
    for mask in range(len(w_refs)):
        first = pl.multiple_of((position ^ mask) * rows, rows)
        held_ref[pl.ds(first, rows)] = total[mask * rows : (mask + 1) * rows]
    out_ref[...] = held_ref[...].T.astype(jnp.bfloat16)


def whole_call(kernel, out_shape, scratch, flops, nbytes, *operands, in_hbm=0, out_hbm=()):
    results = pl.pallas_call(
        kernel,
        out_shape=out_shape,
        in_specs=[
            pl.BlockSpec(memory_space=pltpu.HBM if place < in_hbm else pltpu.VMEM) for place in range(len(operands))
        ],
        out_specs=[
            pl.BlockSpec(memory_space=pltpu.HBM if place in out_hbm else pltpu.VMEM) for place in range(len(out_shape))
        ],
        scratch_shapes=scratch,
        cost_estimate=pl.CostEstimate(flops=flops, bytes_accessed=nbytes, transcendentals=0),
        compiler_params=pltpu.CompilerParams(vmem_limit_bytes=None if in_hbm else 32 * 2**20),
    )(*operands)
    return results if len(out_shape) > 1 else results[0]


def blocked(x_gate, x_post, values, decay, residue, w_out):
    tok, width = x_gate.shape
    ctx_count = lax.axis_size("ctx")
    tp_count = lax.axis_size("tp")
    group = width // ctx_count
    poles = decay.shape[2]
    block = 2 * tok
    blocks = tok * ctx_count // block
    rows, channels = w_out.shape
    half = 2 * poles

    packed, own, mirrored = whole_call(
        pack_kernel,
        (
            jax.ShapeDtypeStruct((ctx_count, 3, group, tok), jnp.bfloat16),
            jax.ShapeDtypeStruct((2 * half, tok), jnp.float32),
            jax.ShapeDtypeStruct((2 * half, tok), jnp.float32),
        ),
        [
            pltpu.VMEM((3, tok, width), jnp.bfloat16),
            pltpu.VMEM((2 * half, width), jnp.float32),
            pltpu.VMEM((2, 2 * half, tok), jnp.float32),
            pltpu.VMEM((ctx_count, 3, group, tok), jnp.bfloat16),
            pltpu.SemaphoreType.DMA((5,)),
            pltpu.SemaphoreType.DMA((5,)),
        ],
        0,
        6 * tok * width * 2,
        x_gate,
        values,
        x_post,
        jnp.swapaxes(decay, 1, 2).reshape(half, width),
        jnp.swapaxes(residue, 1, 2).reshape(half, width),
        in_hbm=5,
        out_hbm=(0, 1, 2),
    )
    paired = lax.ppermute(mirrored, "tp", [(z, tp_count - 1 - z) for z in range(tp_count)])
    received = lax.all_to_all(packed, "ctx", split_axis=0, concat_axis=0, tiled=True)

    w_late, mirrored = lax.optimization_barrier((w_out, mirrored))
    w_x, w_y = partner(w_late, "ctx", 1), partner(w_late, "ctx", 2)
    own_spectra = whole_call(
        functools.partial(filter_kernel, poles),
        (jax.ShapeDtypeStruct((2, blocks, group, 2 * block), jnp.float32),),
        [
            pltpu.VMEM((2, blocks * group, block), jnp.float32),
            pltpu.VMEM((2, block, 2 * block), jnp.bfloat16),
        ],
        2 * 2 * blocks * group * block * 2 * block * 3,
        2 * blocks * group * 2 * block * 4,
        own,
    )
    mixed = whole_call(
        functools.partial(conv_kernel, poles),
        (jax.ShapeDtypeStruct((tp_count, ctx_count, group, tok), jnp.bfloat16),),
        [
            pltpu.VMEM((2, blocks, group, 2 * block), jnp.float32),
            pltpu.VMEM((2, blocks * group, block), jnp.float32),
            pltpu.VMEM((2, block, 2 * block), jnp.bfloat16),
            pltpu.VMEM((2, 2 * block, block), jnp.bfloat16),
            pltpu.VMEM((2 * blocks * group, 2 * block), jnp.float32),
            pltpu.VMEM((2 * blocks * group, 2 * block), jnp.bfloat16),
            pltpu.VMEM((2 * blocks * group, 2 * block), jnp.bfloat16),
            pltpu.VMEM((ctx_count, group, tok), jnp.bfloat16),
            pltpu.SemaphoreType.DMA((2, tp_count)),
        ],
        2 * 8 * blocks * group * block * 2 * block * 3,
        4 * blocks * group * 2 * block * 4,
        received,
        own_spectra,
        paired,
        out_hbm=(0,),
    )
    mixed, w_x, w_y, w_own = lax.optimization_barrier((mixed, w_x, w_y, w_out))
    w_far = partner(w_x, "ctx", 2)
    w_blocks = {0: w_own, 2: w_x, 4: w_y, 6: w_far}
    for mask in range(0, ctx_count, 2):
        w_blocks[mask + 1] = partner(w_blocks[mask], "ctx", 0)
    every = lax.all_to_all(
        mixed.reshape(tp_count * ctx_count, group, tok), ("tp", "ctx"), split_axis=0, concat_axis=0, tiled=True
    ).reshape(channels, tok)
    return whole_call(
        project_kernel,
        (jax.ShapeDtypeStruct((tok, rows * ctx_count), jnp.bfloat16),),
        [pltpu.VMEM((rows * ctx_count, tok), jnp.float32)],
        2 * tok * rows * ctx_count * channels,
        2 * rows * ctx_count * channels,
        every,
        *[w_blocks[mask] for mask in range(ctx_count)],
    )


def local(x_gate, x_post, values, decay, residue, w_out):
    tok, width = x_gate.shape
    ctx_count = lax.axis_size("ctx")
    if tok == 128 and width == 512 and ctx_count == 8 and lax.axis_size("tp") == 4:
        return blocked(x_gate, x_post, values, decay, residue, w_out)
    return general(x_gate, x_post, values, decay, residue, w_out)


def solution(mesh):
    in_specs = (
        P("ctx", "tp"),
        P("ctx", "tp"),
        P("ctx", "tp"),
        P(None, "tp", None),
        P(None, "tp", None),
        P(("tp", "ctx"), None),
    )
    out_specs = P("ctx", "tp")
    return jax.shard_map(local, mesh=mesh, in_specs=in_specs, out_specs=out_specs, check_vma=False)
```

```python
import functools
import math

import jax
import jax.numpy as jnp
from jax import lax
from jax.experimental import pallas as pl
from jax.experimental.pallas import tpu as pltpu
from jax.sharding import PartitionSpec as P

HIGHEST = lax.Precision.HIGHEST


def partner(value, axis, bit):
    mask = 2**bit
    pairs = [(source, source ^ mask) for source in range(lax.axis_size(axis))]
    return lax.ppermute(value, axis, pairs)


def radices(length_all):
    last_radix = min(128, length_all // 4)
    first_radix = min(32, length_all // last_radix)
    return (first_radix, length_all // (first_radix * last_radix), last_radix)


def rotation(row_count, col_count, modulus):
    product = (
        lax.broadcasted_iota(jnp.int32, (row_count, col_count), 0)
        * lax.broadcasted_iota(jnp.int32, (row_count, col_count), 1)
        % modulus
    )
    angle = product.astype(jnp.float32) * (2.0 * math.pi / modulus)
    return (jnp.cos(angle), -jnp.sin(angle))


def tables(radix_sizes):
    first_radix, mid_radix, last_radix = radix_sizes
    length_all = first_radix * mid_radix * last_radix
    outer_real, outer_imag = rotation(first_radix, first_radix, first_radix)
    mid_real, mid_imag = rotation(mid_radix, mid_radix, mid_radix)
    last_real, last_imag = rotation(last_radix, last_radix, last_radix)
    twist_real, twist_imag = rotation(first_radix, mid_radix * last_radix, length_all)
    twist_real = twist_real.reshape(first_radix, mid_radix, last_radix)
    twist_imag = twist_imag.reshape(first_radix, mid_radix, last_radix)
    inner_real, inner_imag = rotation(mid_radix, last_radix, mid_radix * last_radix)
    return (
        outer_real,
        outer_imag,
        mid_real,
        mid_imag,
        last_real,
        last_imag,
        twist_real,
        twist_imag,
        inner_real,
        inner_imag,
    )


def apply_matrix(pattern, real_part, imag_part, matrix_real, matrix_imag):
    out_real = jnp.einsum(pattern, real_part, matrix_real, precision=HIGHEST) - jnp.einsum(
        pattern, imag_part, matrix_imag, precision=HIGHEST
    )
    out_imag = jnp.einsum(pattern, real_part, matrix_imag, precision=HIGHEST) + jnp.einsum(
        pattern, imag_part, matrix_real, precision=HIGHEST
    )
    return (out_real, out_imag)


def complex_times(left_real, left_imag, right_real, right_imag):
    return (
        left_real * right_real - left_imag * right_imag,
        left_real * right_imag + left_imag * right_real,
    )


def forward(real_part, imag_part, table_set, radix_sizes):
    first_radix, mid_radix, last_radix = radix_sizes
    half_first = first_radix // 2
    batch_rows = real_part.shape[0]
    (
        outer_real,
        outer_imag,
        mid_real,
        mid_imag,
        last_real,
        last_imag,
        twist_real,
        twist_imag,
        inner_real,
        inner_imag,
    ) = table_set
    real_part = real_part.reshape(batch_rows, half_first, mid_radix, last_radix)
    imag_part = imag_part.reshape(batch_rows, half_first, mid_radix, last_radix)
    real_part, imag_part = apply_matrix(
        "banm,ak->bknm", real_part, imag_part, outer_real[:half_first], outer_imag[:half_first]
    )
    real_part, imag_part = complex_times(real_part, imag_part, twist_real, twist_imag)
    real_part, imag_part = apply_matrix("bknm,nj->bkjm", real_part, imag_part, mid_real, mid_imag)
    real_part, imag_part = complex_times(real_part, imag_part, inner_real, inner_imag)
    return apply_matrix("bkjm,mq->bkjq", real_part, imag_part, last_real, last_imag)


def inverse(real_part, imag_part, table_set, radix_sizes):
    first_radix, mid_radix, last_radix = radix_sizes
    half_first = first_radix // 2
    batch_rows = real_part.shape[0]
    (
        outer_real,
        outer_imag,
        mid_real,
        mid_imag,
        last_real,
        last_imag,
        twist_real,
        twist_imag,
        inner_real,
        inner_imag,
    ) = table_set
    real_part, imag_part = apply_matrix(
        "bkjq,mq->bkjm", real_part, imag_part, last_real / last_radix, -last_imag / last_radix
    )
    real_part, imag_part = complex_times(real_part, imag_part, inner_real, -inner_imag)
    real_part, imag_part = apply_matrix(
        "bkjm,nj->bknm", real_part, imag_part, mid_real / mid_radix, -mid_imag / mid_radix
    )
    real_part, imag_part = complex_times(real_part, imag_part, twist_real, -twist_imag)
    matrix_real = outer_real[:half_first] / first_radix
    matrix_imag = -outer_imag[:half_first] / first_radix
    out_real, out_imag = apply_matrix(
        "bknm,ak->banm", real_part, imag_part, matrix_real, matrix_imag
    )
    return (out_real.reshape(batch_rows, -1), out_imag.reshape(batch_rows, -1))


def spectrum(decay_rows, residue_rows, radix_sizes, seq_length):
    first_radix, mid_radix, last_radix = radix_sizes
    length_all = first_radix * mid_radix * last_radix
    poles = decay_rows.shape[1]
    shape_all = (first_radix, mid_radix, last_radix)
    frequency = (
        lax.broadcasted_iota(jnp.int32, shape_all, 0)
        + first_radix * lax.broadcasted_iota(jnp.int32, shape_all, 1)
        + first_radix * mid_radix * lax.broadcasted_iota(jnp.int32, shape_all, 2)
    )
    half_angle = frequency.astype(jnp.float32) * (math.pi / length_all)
    sin_half = jnp.sin(half_angle)
    sin_full = jnp.sin(2.0 * half_angle)
    parity_sign = (1 - 2 * (frequency % 2)).astype(jnp.float32)

    def add_pole(pole_index, running):
        run_real, run_imag = running
        rate_col = lax.dynamic_slice_in_dim(decay_rows, pole_index, 1, 1).reshape(-1, 1, 1, 1)
        weight = lax.dynamic_slice_in_dim(residue_rows, pole_index, 1, 1).reshape(
            -1, 1, 1, 1
        ) * jnp.sqrt(2.0 * rate_col / poles)
        retained = jnp.exp(-rate_col)
        den_real = -jnp.expm1(-rate_col) + 2.0 * retained * sin_half * sin_half
        den_imag = retained * sin_full
        pole_scale = (
            weight
            * (1.0 - jnp.exp(-rate_col * seq_length) * parity_sign)
            / (den_real * den_real + den_imag * den_imag)
        )
        return (run_real + pole_scale * den_real, run_imag - pole_scale * den_imag)

    zeros_all = jnp.zeros((decay_rows.shape[0],) + shape_all, jnp.float32)
    return lax.fori_loop(0, poles, add_pole, (zeros_all, zeros_all))


def general(x_gate, x_post, values, decay, residue, w_out):
    tok_rows, block_width = x_gate.shape
    ctx_count = lax.axis_size("ctx")
    tp_count = lax.axis_size("tp")
    chan_group = block_width // ctx_count
    seq_length = tok_rows * ctx_count
    radix_sizes = radices(2 * seq_length)
    table_set = tables(radix_sizes)
    first_row = lax.axis_index("ctx") * chan_group
    own_rate = lax.dynamic_slice_in_dim(decay, first_row, chan_group, 1)
    own_residue = lax.dynamic_slice_in_dim(residue, first_row, chan_group, 1)
    own_spec = [
        spectrum(own_rate[filter_index], own_residue[filter_index], radix_sizes, seq_length)
        for filter_index in range(2)
    ]
    forward_rows = [x_gate, values] + [x_post]
    row_count = len(forward_rows)
    base_rows = jnp.stack(forward_rows)
    copied = base_rows
    for bit_index in range(tp_count.bit_length() - 1):
        copied = partner(copied, "tp", bit_index)
    sent_rows = jnp.concatenate([base_rows, copied[:, :, ::-1]], axis=0)
    received = lax.all_to_all(
        jnp.swapaxes(sent_rows, 1, 2), "ctx", split_axis=1, concat_axis=2, tiled=True
    )
    gate_fwd = received[0].astype(jnp.float32)
    value_fwd = received[1].astype(jnp.float32)
    mirrored = received[row_count:, :, ::-1].astype(jnp.float32)
    spec_real, spec_imag = forward(value_fwd, mirrored[1], table_set, radix_sizes)
    spec_real, spec_imag = complex_times(spec_real, spec_imag, own_spec[0][0], own_spec[0][1])
    along_fwd, along_rev = inverse(spec_real, spec_imag, table_set, radix_sizes)
    spec_real, spec_imag = forward(
        gate_fwd * along_fwd, mirrored[0] * along_rev, table_set, radix_sizes
    )
    spec_real, spec_imag = complex_times(spec_real, spec_imag, own_spec[1][0], own_spec[1][1])
    sum_fwd, sum_rev = inverse(spec_real, spec_imag, table_set, radix_sizes)
    sum_fwd = received[2].astype(jnp.float32) * sum_fwd
    sum_rev = mirrored[2] * sum_rev
    results = jnp.stack([sum_fwd, sum_rev[:, ::-1]])
    returned = lax.all_to_all(
        results.astype(jnp.bfloat16), "ctx", split_axis=2, concat_axis=1, tiled=True
    ).astype(results.dtype)
    flipped = returned[1, ::-1, :]
    for bit_index in range(tp_count.bit_length() - 1):
        flipped = partner(flipped.astype(jnp.bfloat16), "tp", bit_index).astype(flipped.dtype)
    total_rows = returned[0] + flipped
    total_rows = total_rows.T
    mixed_rows = total_rows.astype(jnp.bfloat16)
    whole_rows = lax.all_gather(mixed_rows, "tp", axis=1, tiled=True)
    projected = lax.dot_general(
        whole_rows,
        lax.all_gather(w_out, "ctx", axis=0, tiled=True),
        (((1,), (1,)), ((), ())),
        preferred_element_type=jnp.float32,
    )
    return projected.astype(jnp.bfloat16)


def cycle(row_factor, col_factor, modulus):
    angle = (row_factor * col_factor % modulus).astype(jnp.float32) * (2.0 * math.pi / modulus)
    return jnp.cos(angle), jnp.sin(angle)


def put_tables(table_ref, back_ref=None):
    block = table_ref.shape[1]
    modulus = 4 * block
    coarse = 16
    rows = lax.broadcasted_iota(jnp.int32, (coarse, block), 0)
    cols = lax.broadcasted_iota(jnp.int32, (coarse, block), 1)

    def parts(big, small):
        for place in range(block // coarse):
            big_cos, big_sin = (part[place : place + 1] for part in big)
            span = slice(place * coarse, (place + 1) * coarse)
            below = slice(block + place * coarse, block + (place + 1) * coarse)
            cos = halves(big_cos * small[0] - big_sin * small[1])
            sin = halves(-(big_sin * small[0] + big_cos * small[1]))
            yield span, below, cos, sin

    frequency = 2 * cols + 1
    for span, _, cos, sin in parts(cycle(coarse * rows, frequency, modulus), cycle(rows, frequency, modulus)):
        table_ref[0, span, :block], table_ref[1, span, :block] = cos
        table_ref[0, span, block:], table_ref[1, span, block:] = sin
    if back_ref is not None:
        for span, below, cos, sin in parts(cycle(2 * coarse * rows, cols, modulus), cycle(2 * rows + 1, cols, modulus)):
            back_ref[0, span], back_ref[1, span] = cos
            back_ref[0, below], back_ref[1, below] = sin


def halves(value):
    high = value.astype(jnp.bfloat16)
    return high, (value - high.astype(jnp.float32)).astype(jnp.bfloat16)


def mul(left, right):
    return jnp.dot(left, right, preferred_element_type=jnp.float32)


def mul3(high, low, table_ref):
    return mul(high, table_ref[0]) + (mul(low, table_ref[0]) + mul(high, table_ref[1]))


def pack_kernel(
    gate_hbm, value_hbm, post_hbm, decay_hbm, residue_hbm,
    out_hbm, own_hbm, sent_hbm, held_ref, cut_ref, ready_ref, sems, out_sems,
):
    ctx_count, _, group, tok = out_hbm.shape
    width = gate_hbm.shape[1]
    half = decay_hbm.shape[0]
    position = lax.axis_index("ctx")
    pairs = []
    for place, index in enumerate((position, ctx_count - 1 - position)):
        columns = pl.ds(pl.multiple_of(index * group // tok * tok, tok), tok)
        pairs += [(decay_hbm.at[:, columns], cut_ref.at[place, :half]), (residue_hbm.at[:, columns], cut_ref.at[place, half:])]
    pairs += [(source, held_ref.at[place]) for place, source in enumerate((value_hbm, gate_hbm, post_hbm))]
    copies = [pltpu.make_async_copy(*pair, sems.at[place]) for place, pair in enumerate(pairs)]
    for copy in copies:
        copy.start()
    sends = []
    for place, target in enumerate((own_hbm, sent_hbm)):
        copies[2 * place].wait()
        copies[2 * place + 1].wait()
        sends.append(pltpu.make_async_copy(cut_ref.at[place], target, out_sems.at[3 + place]))
        sends[-1].start()
    for place, copy in enumerate(copies[4:]):
        copy.wait()
        for first in range(0, width, tok):
            turned = held_ref[place, :, first : first + tok].T
            for part in range(tok // group):
                ready_ref[first // group + part, place] = turned[part * group : (part + 1) * group]
        sends.append(pltpu.make_async_copy(ready_ref.at[:, place], out_hbm.at[:, place], out_sems.at[place]))
        sends[-1].start()
    for send in sends:
        send.wait()


def mirror_rows(value):
    row = lax.broadcasted_iota(jnp.int32, (8, value.shape[1]), 0)
    result = []
    for first in range(value.shape[0] - 8, -1, -8):
        part = value[first : first + 8]
        for shift in (1, 2, 4):
            part = jnp.where(row & shift == 0, pltpu.roll(part, 8 - shift, 0), pltpu.roll(part, shift, 0))
        result.append(part)
    return jnp.concatenate(result, axis=0)


def put_spectra(poles, index, turned, out_ref, time_ref, table_ref):
    blocks, group, twice = out_ref.shape
    block = twice // 2
    lanes = 128
    ramp = lax.broadcasted_iota(jnp.int32, (8, lanes), 1).astype(jnp.float32)
    sign = (1 - 2 * (lax.broadcasted_iota(jnp.int32, (group, block), 1) % 2)).astype(jnp.float32)
    for row in range(0, group, 8):
        rows = slice(row, row + 8)
        rate = turned[rows, index * poles : (index + 1) * poles]
        scale = turned[rows, (2 + index) * poles : (3 + index) * poles] * (jnp.sqrt(rate * (2.0 / poles)) / block)
        jump = jnp.exp(rate * -lanes)
        sums = [None] * (blocks * block // lanes)
        for pole in range(poles):
            term = scale[:, pole : pole + 1] * jnp.exp(-rate[:, pole : pole + 1] * ramp)
            step = jnp.broadcast_to(jump[:, pole : pole + 1], (8, lanes))
            for place in range(len(sums)):
                sums[place] = term if pole == 0 else sums[place] + term
                if place + 1 < len(sums):
                    term = term * step
        for place, total in enumerate(sums):
            lag, lane = divmod(place * lanes, block)
            time_ref[lag * group + row : lag * group + row + 8, lane : lane + lanes] = total
    spec = mul3(*halves(time_ref[...]), table_ref)
    for lag in range(blocks):
        real = spec[lag * group : (lag + 1) * group, :block]
        imag = spec[lag * group : (lag + 1) * group, block:]
        if lag > 0:
            real = real - sign * spec[(lag - 1) * group : lag * group, block:]
            imag = imag + sign * spec[(lag - 1) * group : lag * group, :block]
        out_ref[lag, :, :block] = real
        out_ref[lag, :, block:] = imag


def filter_kernel(poles, par_ref, out_ref, time_ref, table_ref, turned_ref):
    group = out_ref.shape[2]
    put_tables(table_ref)
    turned_ref[...] = par_ref[...].T
    turned = turned_ref[pl.ds(pl.multiple_of(lax.axis_index("ctx") * group % turned_ref.shape[0], group), group)]
    for index in range(2):
        put_spectra(poles, index, turned, out_ref.at[index], time_ref.at[index], table_ref)


def conv_kernel(
    poles, x_ref, own_ref, par_ref, out_hbm,
    paired_ref, time_ref, table_ref, back_ref, turned_ref, spec_ref, high_ref, ready_ref, sems,
):
    put_tables(table_ref, back_ref)
    turned_ref[...] = par_ref[...].T
    blocks, group, twice = own_ref.shape[1:]
    block = twice // 2
    rows_all = blocks * group
    tall, wide = 16, 128
    pieces = x_ref.shape[0] // blocks
    first = (x_ref.shape[0] - 1 - lax.axis_index("ctx")) * group % turned_ref.shape[0]
    turned = mirror_rows(turned_ref[pl.ds(pl.multiple_of(first, group), group)])

    def rows_of(position):
        return jnp.concatenate(
            [
                jnp.concatenate([x_ref[m * pieces + s, position] for s in range(pieces)], axis=1)
                for m in range(blocks)
            ],
            axis=0,
        )

    def times(index, side, source, row, lane):
        data = []
        for m in range(blocks):
            rows = slice(source + m * group + row, source + m * group + row + tall)
            data.append((spec_ref[rows, lane : lane + wide], spec_ref[rows, block + lane : block + lane + wide]))
        sums = [None] * blocks
        for lag in range(blocks):
            h_ref = (own_ref, paired_ref)[side]
            f_re = h_ref[index, lag, row : row + tall, lane : lane + wide]
            f_im = h_ref[index, lag, row : row + tall, block + lane : block + lane + wide]
            for m in range(blocks - lag):
                target, (d_re, d_im) = (m + lag, data[m]) if side == 0 else (m, data[m + lag])
                if side == 0:
                    real, imag = f_re * d_re - f_im * d_im, f_re * d_im + f_im * d_re
                else:
                    real, imag = f_re * d_re + f_im * d_im, f_re * d_im - f_im * d_re
                if sums[target] is not None:
                    real, imag = sums[target][0] + real, sums[target][1] + imag
                sums[target] = (real, imag)
        return sums

    def to_time(rows):
        return mul(high_ref[rows], back_ref[0]) + mul(high_ref[rows], back_ref[1])

    def keep(target, row, lane, sums):
        for m in range(blocks):
            rows = slice(target + m * group + row, target + m * group + row + tall)
            for part in range(2):
                cols = slice(part * block + lane, part * block + lane + wide)
                high_ref[rows, cols] = sums[m][part].astype(jnp.bfloat16)

    chunks = [(row, lane) for row in range(0, group, tall) for lane in range(0, block, wide)]

    value = rows_of(0)
    gate = rows_of(1).astype(jnp.float32)
    spec_ref[:rows_all] = mul(value, table_ref[0]) + mul(value, table_ref[1])
    sides = [slice(side * rows_all, (side + 1) * rows_all) for side in range(2)]
    gated = []
    put_spectra(poles, 0, turned, paired_ref.at[0], time_ref.at[0], table_ref)
    for side in range(2):
        for row, lane in chunks:
            keep(side * rows_all, row, lane, times(0, side, 0, row, lane))
        gated.append(halves(gate * to_time(sides[side])))
    put_spectra(poles, 1, turned, paired_ref.at[1], time_ref.at[1], table_ref)
    for side in range(2):
        spec_ref[sides[side]] = mul3(*gated[side], table_ref)
    for row, lane in chunks:
        ahead, back = times(1, 0, 0, row, lane), times(1, 1, rows_all, row, lane)
        keep(0, row, lane, [(a[0] + b[0], a[1] + b[1]) for a, b in zip(ahead, back)])
    post = rows_of(2)
    tok = block // pieces
    sends = []
    for part in range(2):
        rows = slice(part * rows_all // 2, (part + 1) * rows_all // 2)
        summed = to_time(rows)
        mixed = (post[rows].astype(jnp.float32) * summed).astype(jnp.bfloat16)
        first = part * blocks // 2 * pieces
        for m in range(blocks // 2):
            for s in range(pieces):
                ready_ref[first + m * pieces + s] = mixed[m * group : (m + 1) * group, s * tok : (s + 1) * tok]
        span = pl.ds(first, blocks // 2 * pieces)
        for copy in range(out_hbm.shape[0]):
            sends.append(pltpu.make_async_copy(ready_ref.at[span], out_hbm.at[copy, span], sems.at[part, copy]))
            sends[-1].start()
    for send in sends:
        send.wait()


def project_kernel(mixed_ref, *refs):
    w_refs, (out_hbm, held_ref, ready_ref, sems) = refs[:-4], refs[-4:]
    rows = w_refs[0].shape[0]
    tile = 2 * rows
    position = lax.axis_index("ctx")
    even = pl.multiple_of(position % 2 * rows, rows)
    odd = pl.multiple_of((1 - position % 2) * rows, rows)
    sends = []
    for part in range(0, len(w_refs), 4):
        total = mul(jnp.concatenate([w_ref[...] for w_ref in w_refs[part : part + 4]], axis=0), mixed_ref[...])
        for pair in range(2):
            place = part // 2 + pair
            held_ref[place, pl.ds(even, rows)] = total[pair * tile : pair * tile + rows]
            held_ref[place, pl.ds(odd, rows)] = total[pair * tile + rows : (pair + 1) * tile]
            ready_ref[place] = held_ref[place].T.astype(jnp.bfloat16)
            columns = pl.ds(pl.multiple_of((position // 2 ^ place) * tile, tile), tile)
            sends.append(pltpu.make_async_copy(ready_ref.at[place], out_hbm.at[:, columns], sems.at[place]))
            sends[-1].start()
    for send in sends:
        send.wait()


def whole_call(kernel, out_shape, scratch, flops, nbytes, *operands, in_hbm=0, out_hbm=()):
    results = pl.pallas_call(
        kernel,
        out_shape=out_shape,
        in_specs=[
            pl.BlockSpec(memory_space=pltpu.HBM if place < in_hbm else pltpu.VMEM) for place in range(len(operands))
        ],
        out_specs=[
            pl.BlockSpec(memory_space=pltpu.HBM if place in out_hbm else pltpu.VMEM) for place in range(len(out_shape))
        ],
        scratch_shapes=scratch,
        cost_estimate=pl.CostEstimate(flops=flops, bytes_accessed=nbytes, transcendentals=0),
        compiler_params=pltpu.CompilerParams(vmem_limit_bytes=None if in_hbm else 32 * 2**20),
    )(*operands)
    return results if len(out_shape) > 1 else results[0]


def blocked(x_gate, x_post, values, decay, residue, w_out):
    tok, width = x_gate.shape
    ctx_count = lax.axis_size("ctx")
    tp_count = lax.axis_size("tp")
    group = width // ctx_count
    poles = decay.shape[2]
    block = 2 * tok
    blocks = tok * ctx_count // block
    rows, channels = w_out.shape
    half = 2 * poles

    packed, own, mirrored = whole_call(
        pack_kernel,
        (
            jax.ShapeDtypeStruct((ctx_count, 3, group, tok), jnp.bfloat16),
            jax.ShapeDtypeStruct((2 * half, tok), jnp.float32),
            jax.ShapeDtypeStruct((2 * half, tok), jnp.float32),
        ),
        [
            pltpu.VMEM((3, tok, width), jnp.bfloat16),
            pltpu.VMEM((2, 2 * half, tok), jnp.float32),
            pltpu.VMEM((ctx_count, 3, group, tok), jnp.bfloat16),
            pltpu.SemaphoreType.DMA((7,)),
            pltpu.SemaphoreType.DMA((5,)),
        ],
        0,
        6 * tok * width * 2,
        x_gate,
        values,
        x_post,
        jnp.swapaxes(decay, 1, 2).reshape(half, width),
        jnp.swapaxes(residue, 1, 2).reshape(half, width),
        in_hbm=5,
        out_hbm=(0, 1, 2),
    )
    paired = lax.ppermute(mirrored, "tp", [(z, tp_count - 1 - z) for z in range(tp_count)])
    received = lax.all_to_all(packed, "ctx", split_axis=0, concat_axis=0, tiled=True)

    w_late, mirrored = lax.optimization_barrier((w_out, mirrored))
    w_x, w_y = partner(w_late, "ctx", 1), partner(w_late, "ctx", 2)
    own_spectra = whole_call(
        functools.partial(filter_kernel, poles),
        (jax.ShapeDtypeStruct((2, blocks, group, 2 * block), jnp.float32),),
        [
            pltpu.VMEM((2, blocks * group, block), jnp.float32),
            pltpu.VMEM((2, block, 2 * block), jnp.bfloat16),
            pltpu.VMEM((tok, 2 * half), jnp.float32),
        ],
        2 * 2 * blocks * group * block * 2 * block * 3,
        2 * blocks * group * 2 * block * 4,
        own,
    )
    mixed = whole_call(
        functools.partial(conv_kernel, poles),
        (jax.ShapeDtypeStruct((tp_count, ctx_count, group, tok), jnp.bfloat16),),
        [
            pltpu.VMEM((2, blocks, group, 2 * block), jnp.float32),
            pltpu.VMEM((2, blocks * group, block), jnp.float32),
            pltpu.VMEM((2, block, 2 * block), jnp.bfloat16),
            pltpu.VMEM((2, 2 * block, block), jnp.bfloat16),
            pltpu.VMEM((tok, 2 * half), jnp.float32),
            pltpu.VMEM((2 * blocks * group, 2 * block), jnp.float32),
            pltpu.VMEM((2 * blocks * group, 2 * block), jnp.bfloat16),
            pltpu.VMEM((ctx_count, group, tok), jnp.bfloat16),
            pltpu.SemaphoreType.DMA((2, tp_count)),
        ],
        2 * 8 * blocks * group * block * 2 * block * 3,
        4 * blocks * group * 2 * block * 4,
        received,
        own_spectra,
        paired,
        out_hbm=(0,),
    )
    mixed, w_x, w_y, w_own = lax.optimization_barrier((mixed, w_x, w_y, w_out))
    w_far = partner(w_x, "ctx", 2)
    w_blocks = {0: w_own, 2: w_x, 4: w_y, 6: w_far}
    for mask in range(0, ctx_count, 2):
        w_blocks[mask + 1] = partner(w_blocks[mask], "ctx", 0)
    every = lax.all_to_all(
        mixed.reshape(tp_count * ctx_count, group, tok), ("tp", "ctx"), split_axis=0, concat_axis=0, tiled=True
    ).reshape(channels, tok)
    return whole_call(
        project_kernel,
        (jax.ShapeDtypeStruct((tok, rows * ctx_count), jnp.bfloat16),),
        [
            pltpu.VMEM((ctx_count // 2, 2 * rows, tok), jnp.float32),
            pltpu.VMEM((ctx_count // 2, tok, 2 * rows), jnp.bfloat16),
            pltpu.SemaphoreType.DMA((ctx_count // 2,)),
        ],
        2 * tok * rows * ctx_count * channels,
        2 * rows * ctx_count * channels,
        every,
        *[w_blocks[mask] for mask in range(ctx_count)],
        out_hbm=(0,),
    )


def local(x_gate, x_post, values, decay, residue, w_out):
    tok, width = x_gate.shape
    ctx_count = lax.axis_size("ctx")
    if tok == 128 and width == 512 and ctx_count == 8 and w_out.shape[0] == 64 and lax.axis_size("tp") == 4:
        return blocked(x_gate, x_post, values, decay, residue, w_out)
    return general(x_gate, x_post, values, decay, residue, w_out)


def solution(mesh):
    in_specs = (
        P("ctx", "tp"),
        P("ctx", "tp"),
        P("ctx", "tp"),
        P(None, "tp", None),
        P(None, "tp", None),
        P(("tp", "ctx"), None),
    )
    out_specs = P("ctx", "tp")
    return jax.shard_map(local, mesh=mesh, in_specs=in_specs, out_specs=out_specs, check_vma=False)
```

```python
import functools
import math

import jax
import jax.numpy as jnp
from jax import lax
from jax.experimental import pallas as pl
from jax.experimental.pallas import tpu as pltpu
from jax.sharding import PartitionSpec as P

HIGHEST = lax.Precision.HIGHEST


def partner(value, axis, bit):
    mask = 2**bit
    pairs = [(source, source ^ mask) for source in range(lax.axis_size(axis))]
    return lax.ppermute(value, axis, pairs)


def radices(length_all):
    last_radix = min(128, length_all // 4)
    first_radix = min(32, length_all // last_radix)
    return (first_radix, length_all // (first_radix * last_radix), last_radix)


def rotation(row_count, col_count, modulus):
    product = (
        lax.broadcasted_iota(jnp.int32, (row_count, col_count), 0)
        * lax.broadcasted_iota(jnp.int32, (row_count, col_count), 1)
        % modulus
    )
    angle = product.astype(jnp.float32) * (2.0 * math.pi / modulus)
    return (jnp.cos(angle), -jnp.sin(angle))


def tables(radix_sizes):
    first_radix, mid_radix, last_radix = radix_sizes
    length_all = first_radix * mid_radix * last_radix
    outer_real, outer_imag = rotation(first_radix, first_radix, first_radix)
    mid_real, mid_imag = rotation(mid_radix, mid_radix, mid_radix)
    last_real, last_imag = rotation(last_radix, last_radix, last_radix)
    twist_real, twist_imag = rotation(first_radix, mid_radix * last_radix, length_all)
    twist_real = twist_real.reshape(first_radix, mid_radix, last_radix)
    twist_imag = twist_imag.reshape(first_radix, mid_radix, last_radix)
    inner_real, inner_imag = rotation(mid_radix, last_radix, mid_radix * last_radix)
    return (
        outer_real,
        outer_imag,
        mid_real,
        mid_imag,
        last_real,
        last_imag,
        twist_real,
        twist_imag,
        inner_real,
        inner_imag,
    )


def apply_matrix(pattern, real_part, imag_part, matrix_real, matrix_imag):
    out_real = jnp.einsum(pattern, real_part, matrix_real, precision=HIGHEST) - jnp.einsum(
        pattern, imag_part, matrix_imag, precision=HIGHEST
    )
    out_imag = jnp.einsum(pattern, real_part, matrix_imag, precision=HIGHEST) + jnp.einsum(
        pattern, imag_part, matrix_real, precision=HIGHEST
    )
    return (out_real, out_imag)


def complex_times(left_real, left_imag, right_real, right_imag):
    return (
        left_real * right_real - left_imag * right_imag,
        left_real * right_imag + left_imag * right_real,
    )


def forward(real_part, imag_part, table_set, radix_sizes):
    first_radix, mid_radix, last_radix = radix_sizes
    half_first = first_radix // 2
    batch_rows = real_part.shape[0]
    (
        outer_real,
        outer_imag,
        mid_real,
        mid_imag,
        last_real,
        last_imag,
        twist_real,
        twist_imag,
        inner_real,
        inner_imag,
    ) = table_set
    real_part = real_part.reshape(batch_rows, half_first, mid_radix, last_radix)
    imag_part = imag_part.reshape(batch_rows, half_first, mid_radix, last_radix)
    real_part, imag_part = apply_matrix(
        "banm,ak->bknm", real_part, imag_part, outer_real[:half_first], outer_imag[:half_first]
    )
    real_part, imag_part = complex_times(real_part, imag_part, twist_real, twist_imag)
    real_part, imag_part = apply_matrix("bknm,nj->bkjm", real_part, imag_part, mid_real, mid_imag)
    real_part, imag_part = complex_times(real_part, imag_part, inner_real, inner_imag)
    return apply_matrix("bkjm,mq->bkjq", real_part, imag_part, last_real, last_imag)


def inverse(real_part, imag_part, table_set, radix_sizes):
    first_radix, mid_radix, last_radix = radix_sizes
    half_first = first_radix // 2
    batch_rows = real_part.shape[0]
    (
        outer_real,
        outer_imag,
        mid_real,
        mid_imag,
        last_real,
        last_imag,
        twist_real,
        twist_imag,
        inner_real,
        inner_imag,
    ) = table_set
    real_part, imag_part = apply_matrix(
        "bkjq,mq->bkjm", real_part, imag_part, last_real / last_radix, -last_imag / last_radix
    )
    real_part, imag_part = complex_times(real_part, imag_part, inner_real, -inner_imag)
    real_part, imag_part = apply_matrix(
        "bkjm,nj->bknm", real_part, imag_part, mid_real / mid_radix, -mid_imag / mid_radix
    )
    real_part, imag_part = complex_times(real_part, imag_part, twist_real, -twist_imag)
    matrix_real = outer_real[:half_first] / first_radix
    matrix_imag = -outer_imag[:half_first] / first_radix
    out_real, out_imag = apply_matrix(
        "bknm,ak->banm", real_part, imag_part, matrix_real, matrix_imag
    )
    return (out_real.reshape(batch_rows, -1), out_imag.reshape(batch_rows, -1))


def spectrum(decay_rows, residue_rows, radix_sizes, seq_length):
    first_radix, mid_radix, last_radix = radix_sizes
    length_all = first_radix * mid_radix * last_radix
    poles = decay_rows.shape[1]
    shape_all = (first_radix, mid_radix, last_radix)
    frequency = (
        lax.broadcasted_iota(jnp.int32, shape_all, 0)
        + first_radix * lax.broadcasted_iota(jnp.int32, shape_all, 1)
        + first_radix * mid_radix * lax.broadcasted_iota(jnp.int32, shape_all, 2)
    )
    half_angle = frequency.astype(jnp.float32) * (math.pi / length_all)
    sin_half = jnp.sin(half_angle)
    sin_full = jnp.sin(2.0 * half_angle)
    parity_sign = (1 - 2 * (frequency % 2)).astype(jnp.float32)

    def add_pole(pole_index, running):
        run_real, run_imag = running
        rate_col = lax.dynamic_slice_in_dim(decay_rows, pole_index, 1, 1).reshape(-1, 1, 1, 1)
        weight = lax.dynamic_slice_in_dim(residue_rows, pole_index, 1, 1).reshape(
            -1, 1, 1, 1
        ) * jnp.sqrt(2.0 * rate_col / poles)
        retained = jnp.exp(-rate_col)
        den_real = -jnp.expm1(-rate_col) + 2.0 * retained * sin_half * sin_half
        den_imag = retained * sin_full
        pole_scale = (
            weight
            * (1.0 - jnp.exp(-rate_col * seq_length) * parity_sign)
            / (den_real * den_real + den_imag * den_imag)
        )
        return (run_real + pole_scale * den_real, run_imag - pole_scale * den_imag)

    zeros_all = jnp.zeros((decay_rows.shape[0],) + shape_all, jnp.float32)
    return lax.fori_loop(0, poles, add_pole, (zeros_all, zeros_all))


def general(x_gate, x_post, values, decay, residue, w_out):
    tok_rows, block_width = x_gate.shape
    ctx_count = lax.axis_size("ctx")
    tp_count = lax.axis_size("tp")
    chan_group = block_width // ctx_count
    seq_length = tok_rows * ctx_count
    radix_sizes = radices(2 * seq_length)
    table_set = tables(radix_sizes)
    first_row = lax.axis_index("ctx") * chan_group
    own_rate = lax.dynamic_slice_in_dim(decay, first_row, chan_group, 1)
    own_residue = lax.dynamic_slice_in_dim(residue, first_row, chan_group, 1)
    own_spec = [
        spectrum(own_rate[filter_index], own_residue[filter_index], radix_sizes, seq_length)
        for filter_index in range(2)
    ]
    forward_rows = [x_gate, values] + [x_post]
    row_count = len(forward_rows)
    base_rows = jnp.stack(forward_rows)
    copied = base_rows
    for bit_index in range(tp_count.bit_length() - 1):
        copied = partner(copied, "tp", bit_index)
    sent_rows = jnp.concatenate([base_rows, copied[:, :, ::-1]], axis=0)
    received = lax.all_to_all(
        jnp.swapaxes(sent_rows, 1, 2), "ctx", split_axis=1, concat_axis=2, tiled=True
    )
    gate_fwd = received[0].astype(jnp.float32)
    value_fwd = received[1].astype(jnp.float32)
    mirrored = received[row_count:, :, ::-1].astype(jnp.float32)
    spec_real, spec_imag = forward(value_fwd, mirrored[1], table_set, radix_sizes)
    spec_real, spec_imag = complex_times(spec_real, spec_imag, own_spec[0][0], own_spec[0][1])
    along_fwd, along_rev = inverse(spec_real, spec_imag, table_set, radix_sizes)
    spec_real, spec_imag = forward(
        gate_fwd * along_fwd, mirrored[0] * along_rev, table_set, radix_sizes
    )
    spec_real, spec_imag = complex_times(spec_real, spec_imag, own_spec[1][0], own_spec[1][1])
    sum_fwd, sum_rev = inverse(spec_real, spec_imag, table_set, radix_sizes)
    sum_fwd = received[2].astype(jnp.float32) * sum_fwd
    sum_rev = mirrored[2] * sum_rev
    results = jnp.stack([sum_fwd, sum_rev[:, ::-1]])
    returned = lax.all_to_all(
        results.astype(jnp.bfloat16), "ctx", split_axis=2, concat_axis=1, tiled=True
    ).astype(results.dtype)
    flipped = returned[1, ::-1, :]
    for bit_index in range(tp_count.bit_length() - 1):
        flipped = partner(flipped.astype(jnp.bfloat16), "tp", bit_index).astype(flipped.dtype)
    total_rows = returned[0] + flipped
    total_rows = total_rows.T
    mixed_rows = total_rows.astype(jnp.bfloat16)
    whole_rows = lax.all_gather(mixed_rows, "tp", axis=1, tiled=True)
    projected = lax.dot_general(
        whole_rows,
        lax.all_gather(w_out, "ctx", axis=0, tiled=True),
        (((1,), (1,)), ((), ())),
        preferred_element_type=jnp.float32,
    )
    return projected.astype(jnp.bfloat16)


def cycle(row_factor, col_factor, modulus):
    angle = (row_factor * col_factor % modulus).astype(jnp.float32) * (2.0 * math.pi / modulus)
    return jnp.cos(angle), jnp.sin(angle)


def put_tables(table_ref, back_ref):
    block = table_ref.shape[1]
    modulus = 4 * block
    coarse = 16
    rows = lax.broadcasted_iota(jnp.int32, (coarse, block), 0)
    cols = lax.broadcasted_iota(jnp.int32, (coarse, block), 1)

    def parts(big, small):
        for place in range(block // coarse):
            big_cos, big_sin = (part[place : place + 1] for part in big)
            span = slice(place * coarse, (place + 1) * coarse)
            below = slice(block + place * coarse, block + (place + 1) * coarse)
            cos = halves(big_cos * small[0] - big_sin * small[1])
            sin = halves(-(big_sin * small[0] + big_cos * small[1]))
            yield span, below, cos, sin

    frequency = 2 * cols + 1
    for span, _, cos, sin in parts(cycle(coarse * rows, frequency, modulus), cycle(rows, frequency, modulus)):
        table_ref[0, span, :block], table_ref[1, span, :block] = cos
        table_ref[0, span, block:], table_ref[1, span, block:] = sin
    for span, below, cos, sin in parts(cycle(2 * coarse * rows, cols, modulus), cycle(2 * rows + 1, cols, modulus)):
        back_ref[0, span], back_ref[1, span] = cos
        back_ref[0, below], back_ref[1, below] = sin


def halves(value):
    high = value.astype(jnp.bfloat16)
    return high, (value - high.astype(jnp.float32)).astype(jnp.bfloat16)


def mul(left, right):
    return jnp.dot(left, right, preferred_element_type=jnp.float32)


def mul3(high, low, table_ref):
    return mul(high, table_ref[0]) + (mul(low, table_ref[0]) + mul(high, table_ref[1]))


def pack_kernel(
    gate_hbm, value_hbm, post_hbm, decay_hbm, residue_hbm,
    out_hbm, own_hbm, sent_hbm, held_ref, cut_ref, ready_ref, sems, out_sems,
):
    ctx_count, _, group, tok = out_hbm.shape
    width = gate_hbm.shape[1]
    half = decay_hbm.shape[0]
    position = lax.axis_index("ctx")
    pairs = []
    for place, index in enumerate((position, ctx_count - 1 - position)):
        columns = pl.ds(pl.multiple_of(index * group // tok * tok, tok), tok)
        pairs += [(decay_hbm.at[:, columns], cut_ref.at[place, :half]), (residue_hbm.at[:, columns], cut_ref.at[place, half:])]
    pairs += [(source, held_ref.at[place]) for place, source in enumerate((value_hbm, gate_hbm, post_hbm))]
    copies = [pltpu.make_async_copy(*pair, sems.at[place]) for place, pair in enumerate(pairs)]
    for copy in copies:
        copy.start()
    sends = []
    for place, target in enumerate((own_hbm, sent_hbm)):
        copies[2 * place].wait()
        copies[2 * place + 1].wait()
        sends.append(pltpu.make_async_copy(cut_ref.at[place], target, out_sems.at[3 + place]))
        sends[-1].start()
    for place, copy in enumerate(copies[4:]):
        copy.wait()
        for first in range(0, width, tok):
            turned = held_ref[place, :, first : first + tok].T
            for part in range(tok // group):
                ready_ref[first // group + part, place] = turned[part * group : (part + 1) * group]
        sends.append(pltpu.make_async_copy(ready_ref.at[:, place], out_hbm.at[:, place], out_sems.at[place]))
        sends[-1].start()
    for send in sends:
        send.wait()


def mirror_rows(value):
    row = lax.broadcasted_iota(jnp.int32, (8, value.shape[1]), 0)
    result = []
    for first in range(value.shape[0] - 8, -1, -8):
        part = value[first : first + 8]
        for shift in (1, 2, 4):
            part = jnp.where(row & shift == 0, pltpu.roll(part, 8 - shift, 0), pltpu.roll(part, shift, 0))
        result.append(part)
    return jnp.concatenate(result, axis=0)


def put_spectra(poles, index, turned, out_ref, time_ref, table_ref):
    blocks, group, twice = out_ref.shape
    block = twice // 2
    lanes = 128
    ramp = lax.broadcasted_iota(jnp.int32, (8, lanes), 1).astype(jnp.float32)
    sign = (1 - 2 * (lax.broadcasted_iota(jnp.int32, (group, block), 1) % 2)).astype(jnp.float32)
    for row in range(0, group, 8):
        rows = slice(row, row + 8)
        rate = turned[rows, index * poles : (index + 1) * poles]
        scale = turned[rows, (2 + index) * poles : (3 + index) * poles] * (jnp.sqrt(rate * (2.0 / poles)) / block)
        slope = rate * -math.log2(math.e)
        jump = jnp.exp2(slope * lanes)
        sums = [None] * (blocks * block // lanes)
        for pole in range(poles):
            term = scale[:, pole : pole + 1] * jnp.exp2(slope[:, pole : pole + 1] * ramp)
            step = jnp.broadcast_to(jump[:, pole : pole + 1], (8, lanes))
            for place in range(len(sums)):
                sums[place] = term if pole == 0 else sums[place] + term
                if place + 1 < len(sums):
                    term = term * step
        for place, total in enumerate(sums):
            lag, lane = divmod(place * lanes, block)
            time_ref[lag * group + row : lag * group + row + 8, lane : lane + lanes] = total
    spec = mul3(*halves(time_ref[...]), table_ref)
    for lag in range(blocks):
        real = spec[lag * group : (lag + 1) * group, :block]
        imag = spec[lag * group : (lag + 1) * group, block:]
        if lag > 0:
            real = real - sign * spec[(lag - 1) * group : lag * group, block:]
            imag = imag + sign * spec[(lag - 1) * group : lag * group, :block]
        out_ref[lag, :, :block] = real
        out_ref[lag, :, block:] = imag


def filter_kernel(poles, par_ref, out_ref, table_ref, back_ref, time_ref, turned_ref):
    group = out_ref.shape[2]
    put_tables(table_ref, back_ref)
    turned_ref[...] = par_ref[...].T
    turned = turned_ref[pl.ds(pl.multiple_of(lax.axis_index("ctx") * group % turned_ref.shape[0], group), group)]
    for index in range(2):
        put_spectra(poles, index, turned, out_ref.at[index], time_ref.at[index], table_ref)


def conv_kernel(
    poles, x_ref, own_ref, par_ref, table_ref, back_ref, out_hbm,
    paired_ref, time_ref, turned_ref, spec_ref, high_ref, ready_ref, sems,
):
    turned_ref[...] = par_ref[...].T
    blocks, group, twice = own_ref.shape[1:]
    block = twice // 2
    rows_all = blocks * group
    tall, wide = 16, 128
    pieces = x_ref.shape[0] // blocks
    first = (x_ref.shape[0] - 1 - lax.axis_index("ctx")) * group % turned_ref.shape[0]
    turned = mirror_rows(turned_ref[pl.ds(pl.multiple_of(first, group), group)])

    def rows_of(position):
        return jnp.concatenate(
            [
                jnp.concatenate([x_ref[m * pieces + s, position] for s in range(pieces)], axis=1)
                for m in range(blocks)
            ],
            axis=0,
        )

    def times(index, side, source, row, lane):
        data = []
        for m in range(blocks):
            rows = slice(source + m * group + row, source + m * group + row + tall)
            data.append((spec_ref[rows, lane : lane + wide], spec_ref[rows, block + lane : block + lane + wide]))
        sums = [None] * blocks
        for lag in range(blocks):
            h_ref = (own_ref, paired_ref)[side]
            f_re = h_ref[index, lag, row : row + tall, lane : lane + wide]
            f_im = h_ref[index, lag, row : row + tall, block + lane : block + lane + wide]
            for m in range(blocks - lag):
                target, (d_re, d_im) = (m + lag, data[m]) if side == 0 else (m, data[m + lag])
                if side == 0:
                    real, imag = f_re * d_re - f_im * d_im, f_re * d_im + f_im * d_re
                else:
                    real, imag = f_re * d_re + f_im * d_im, f_re * d_im - f_im * d_re
                if sums[target] is not None:
                    real, imag = sums[target][0] + real, sums[target][1] + imag
                sums[target] = (real, imag)
        return sums

    def to_time(rows):
        return mul(high_ref[rows], back_ref[0]) + mul(high_ref[rows], back_ref[1])

    def keep(target, row, lane, sums):
        for m in range(blocks):
            rows = slice(target + m * group + row, target + m * group + row + tall)
            for part in range(2):
                cols = slice(part * block + lane, part * block + lane + wide)
                high_ref[rows, cols] = sums[m][part].astype(jnp.bfloat16)

    chunks = [(row, lane) for row in range(0, group, tall) for lane in range(0, block, wide)]

    value = rows_of(0)
    gate = rows_of(1).astype(jnp.float32)
    spec_ref[:rows_all] = mul(value, table_ref[0]) + mul(value, table_ref[1])
    sides = [slice(side * rows_all, (side + 1) * rows_all) for side in range(2)]
    gated = []
    put_spectra(poles, 0, turned, paired_ref.at[0], time_ref.at[0], table_ref)
    for side in range(2):
        for row, lane in chunks:
            keep(side * rows_all, row, lane, times(0, side, 0, row, lane))
        gated.append(halves(gate * to_time(sides[side])))
    put_spectra(poles, 1, turned, paired_ref.at[1], time_ref.at[1], table_ref)
    for side in range(2):
        spec_ref[sides[side]] = mul3(*gated[side], table_ref)
    for row, lane in chunks:
        ahead, back = times(1, 0, 0, row, lane), times(1, 1, rows_all, row, lane)
        keep(0, row, lane, [(a[0] + b[0], a[1] + b[1]) for a, b in zip(ahead, back)])
    post = rows_of(2)
    tok = block // pieces
    sends = []
    for part in range(2):
        rows = slice(part * rows_all // 2, (part + 1) * rows_all // 2)
        summed = to_time(rows)
        mixed = (post[rows].astype(jnp.float32) * summed).astype(jnp.bfloat16)
        first = part * blocks // 2 * pieces
        for m in range(blocks // 2):
            for s in range(pieces):
                ready_ref[first + m * pieces + s] = mixed[m * group : (m + 1) * group, s * tok : (s + 1) * tok]
        span = pl.ds(first, blocks // 2 * pieces)
        for copy in range(out_hbm.shape[0]):
            sends.append(pltpu.make_async_copy(ready_ref.at[span], out_hbm.at[copy, span], sems.at[part, copy]))
            sends[-1].start()
    for send in sends:
        send.wait()


def project_kernel(mixed_ref, *refs):
    w_refs, (out_hbm, held_ref, ready_ref, sems) = refs[:-4], refs[-4:]
    rows = w_refs[0].shape[0]
    tile = 2 * rows
    position = lax.axis_index("ctx")
    even = pl.multiple_of(position % 2 * rows, rows)
    odd = pl.multiple_of((1 - position % 2) * rows, rows)
    sends = []
    for part in range(0, len(w_refs), 4):
        total = mul(jnp.concatenate([w_ref[...] for w_ref in w_refs[part : part + 4]], axis=0), mixed_ref[...])
        for pair in range(2):
            place = part // 2 + pair
            held_ref[place, pl.ds(even, rows)] = total[pair * tile : pair * tile + rows]
            held_ref[place, pl.ds(odd, rows)] = total[pair * tile + rows : (pair + 1) * tile]
            ready_ref[place] = held_ref[place].T.astype(jnp.bfloat16)
            columns = pl.ds(pl.multiple_of((position // 2 ^ place) * tile, tile), tile)
            sends.append(pltpu.make_async_copy(ready_ref.at[place], out_hbm.at[:, columns], sems.at[place]))
            sends[-1].start()
    for send in sends:
        send.wait()


def whole_call(kernel, out_shape, scratch, flops, nbytes, *operands, in_hbm=0, out_hbm=()):
    results = pl.pallas_call(
        kernel,
        out_shape=out_shape,
        in_specs=[
            pl.BlockSpec(memory_space=pltpu.HBM if place < in_hbm else pltpu.VMEM) for place in range(len(operands))
        ],
        out_specs=[
            pl.BlockSpec(memory_space=pltpu.HBM if place in out_hbm else pltpu.VMEM) for place in range(len(out_shape))
        ],
        scratch_shapes=scratch,
        cost_estimate=pl.CostEstimate(flops=flops, bytes_accessed=nbytes, transcendentals=0),
        compiler_params=pltpu.CompilerParams(vmem_limit_bytes=None if in_hbm else 32 * 2**20),
    )(*operands)
    return results if len(out_shape) > 1 else results[0]


def blocked(x_gate, x_post, values, decay, residue, w_out):
    tok, width = x_gate.shape
    ctx_count = lax.axis_size("ctx")
    tp_count = lax.axis_size("tp")
    group = width // ctx_count
    poles = decay.shape[2]
    block = 2 * tok
    blocks = tok * ctx_count // block
    rows, channels = w_out.shape
    half = 2 * poles

    packed, own, mirrored = whole_call(
        pack_kernel,
        (
            jax.ShapeDtypeStruct((ctx_count, 3, group, tok), jnp.bfloat16),
            jax.ShapeDtypeStruct((2 * half, tok), jnp.float32),
            jax.ShapeDtypeStruct((2 * half, tok), jnp.float32),
        ),
        [
            pltpu.VMEM((3, tok, width), jnp.bfloat16),
            pltpu.VMEM((2, 2 * half, tok), jnp.float32),
            pltpu.VMEM((ctx_count, 3, group, tok), jnp.bfloat16),
            pltpu.SemaphoreType.DMA((7,)),
            pltpu.SemaphoreType.DMA((5,)),
        ],
        0,
        6 * tok * width * 2,
        x_gate,
        values,
        x_post,
        jnp.swapaxes(decay, 1, 2).reshape(half, width),
        jnp.swapaxes(residue, 1, 2).reshape(half, width),
        in_hbm=5,
        out_hbm=(0, 1, 2),
    )
    paired = lax.ppermute(mirrored, "tp", [(z, tp_count - 1 - z) for z in range(tp_count)])
    received = lax.all_to_all(packed, "ctx", split_axis=0, concat_axis=0, tiled=True)

    w_x, w_y = partner(w_out, "ctx", 1), partner(w_out, "ctx", 2)
    w_x, w_y, own = lax.optimization_barrier((w_x, w_y, own))
    own_spectra, table, back_table = whole_call(
        functools.partial(filter_kernel, poles),
        (
            jax.ShapeDtypeStruct((2, blocks, group, 2 * block), jnp.float32),
            jax.ShapeDtypeStruct((2, block, 2 * block), jnp.bfloat16),
            jax.ShapeDtypeStruct((2, 2 * block, block), jnp.bfloat16),
        ),
        [
            pltpu.VMEM((2, blocks * group, block), jnp.float32),
            pltpu.VMEM((tok, 2 * half), jnp.float32),
        ],
        2 * 2 * blocks * group * block * 2 * block * 3,
        2 * blocks * group * 2 * block * 4,
        own,
    )
    mixed = whole_call(
        functools.partial(conv_kernel, poles),
        (jax.ShapeDtypeStruct((tp_count, ctx_count, group, tok), jnp.bfloat16),),
        [
            pltpu.VMEM((2, blocks, group, 2 * block), jnp.float32),
            pltpu.VMEM((2, blocks * group, block), jnp.float32),
            pltpu.VMEM((tok, 2 * half), jnp.float32),
            pltpu.VMEM((2 * blocks * group, 2 * block), jnp.float32),
            pltpu.VMEM((2 * blocks * group, 2 * block), jnp.bfloat16),
            pltpu.VMEM((ctx_count, group, tok), jnp.bfloat16),
            pltpu.SemaphoreType.DMA((2, tp_count)),
        ],
        2 * 8 * blocks * group * block * 2 * block * 3,
        4 * blocks * group * 2 * block * 4,
        received,
        own_spectra,
        paired,
        table,
        back_table,
        out_hbm=(0,),
    )
    mixed, w_x, w_y, w_own = lax.optimization_barrier((mixed, w_x, w_y, w_out))
    w_far = partner(w_x, "ctx", 2)
    w_blocks = {0: w_own, 2: w_x, 4: w_y, 6: w_far}
    for mask in range(0, ctx_count, 2):
        w_blocks[mask + 1] = partner(w_blocks[mask], "ctx", 0)
    every = lax.all_to_all(
        mixed.reshape(tp_count * ctx_count, group, tok), ("tp", "ctx"), split_axis=0, concat_axis=0, tiled=True
    ).reshape(channels, tok)
    return whole_call(
        project_kernel,
        (jax.ShapeDtypeStruct((tok, rows * ctx_count), jnp.bfloat16),),
        [
            pltpu.VMEM((ctx_count // 2, 2 * rows, tok), jnp.float32),
            pltpu.VMEM((ctx_count // 2, tok, 2 * rows), jnp.bfloat16),
            pltpu.SemaphoreType.DMA((ctx_count // 2,)),
        ],
        2 * tok * rows * ctx_count * channels,
        2 * rows * ctx_count * channels,
        every,
        *[w_blocks[mask] for mask in range(ctx_count)],
        out_hbm=(0,),
    )


def local(x_gate, x_post, values, decay, residue, w_out):
    tok, width = x_gate.shape
    ctx_count = lax.axis_size("ctx")
    if tok == 128 and width == 512 and ctx_count == 8 and w_out.shape[0] == 64 and lax.axis_size("tp") == 4:
        return blocked(x_gate, x_post, values, decay, residue, w_out)
    return general(x_gate, x_post, values, decay, residue, w_out)


def solution(mesh):
    in_specs = (
        P("ctx", "tp"),
        P("ctx", "tp"),
        P("ctx", "tp"),
        P(None, "tp", None),
        P(None, "tp", None),
        P(("tp", "ctx"), None),
    )
    out_specs = P("ctx", "tp")
    return jax.shard_map(local, mesh=mesh, in_specs=in_specs, out_specs=out_specs, check_vma=False)
```

```python
import functools
import math

import jax
import jax.numpy as jnp
from jax import lax
from jax.experimental import pallas as pl
from jax.experimental.pallas import tpu as pltpu
from jax.sharding import PartitionSpec as P

HIGHEST = lax.Precision.HIGHEST


def partner(value, axis, bit):
    mask = 2**bit
    pairs = [(source, source ^ mask) for source in range(lax.axis_size(axis))]
    return lax.ppermute(value, axis, pairs)


def radices(length_all):
    last_radix = min(128, length_all // 4)
    first_radix = min(32, length_all // last_radix)
    return (first_radix, length_all // (first_radix * last_radix), last_radix)


def rotation(row_count, col_count, modulus):
    product = (
        lax.broadcasted_iota(jnp.int32, (row_count, col_count), 0)
        * lax.broadcasted_iota(jnp.int32, (row_count, col_count), 1)
        % modulus
    )
    angle = product.astype(jnp.float32) * (2.0 * math.pi / modulus)
    return (jnp.cos(angle), -jnp.sin(angle))


def tables(radix_sizes):
    first_radix, mid_radix, last_radix = radix_sizes
    length_all = first_radix * mid_radix * last_radix
    outer_real, outer_imag = rotation(first_radix, first_radix, first_radix)
    mid_real, mid_imag = rotation(mid_radix, mid_radix, mid_radix)
    last_real, last_imag = rotation(last_radix, last_radix, last_radix)
    twist_real, twist_imag = rotation(first_radix, mid_radix * last_radix, length_all)
    twist_real = twist_real.reshape(first_radix, mid_radix, last_radix)
    twist_imag = twist_imag.reshape(first_radix, mid_radix, last_radix)
    inner_real, inner_imag = rotation(mid_radix, last_radix, mid_radix * last_radix)
    return (
        outer_real,
        outer_imag,
        mid_real,
        mid_imag,
        last_real,
        last_imag,
        twist_real,
        twist_imag,
        inner_real,
        inner_imag,
    )


def apply_matrix(pattern, real_part, imag_part, matrix_real, matrix_imag):
    out_real = jnp.einsum(pattern, real_part, matrix_real, precision=HIGHEST) - jnp.einsum(
        pattern, imag_part, matrix_imag, precision=HIGHEST
    )
    out_imag = jnp.einsum(pattern, real_part, matrix_imag, precision=HIGHEST) + jnp.einsum(
        pattern, imag_part, matrix_real, precision=HIGHEST
    )
    return (out_real, out_imag)


def complex_times(left_real, left_imag, right_real, right_imag):
    return (
        left_real * right_real - left_imag * right_imag,
        left_real * right_imag + left_imag * right_real,
    )


def forward(real_part, imag_part, table_set, radix_sizes):
    first_radix, mid_radix, last_radix = radix_sizes
    half_first = first_radix // 2
    batch_rows = real_part.shape[0]
    (
        outer_real,
        outer_imag,
        mid_real,
        mid_imag,
        last_real,
        last_imag,
        twist_real,
        twist_imag,
        inner_real,
        inner_imag,
    ) = table_set
    real_part = real_part.reshape(batch_rows, half_first, mid_radix, last_radix)
    imag_part = imag_part.reshape(batch_rows, half_first, mid_radix, last_radix)
    real_part, imag_part = apply_matrix(
        "banm,ak->bknm", real_part, imag_part, outer_real[:half_first], outer_imag[:half_first]
    )
    real_part, imag_part = complex_times(real_part, imag_part, twist_real, twist_imag)
    real_part, imag_part = apply_matrix("bknm,nj->bkjm", real_part, imag_part, mid_real, mid_imag)
    real_part, imag_part = complex_times(real_part, imag_part, inner_real, inner_imag)
    return apply_matrix("bkjm,mq->bkjq", real_part, imag_part, last_real, last_imag)


def inverse(real_part, imag_part, table_set, radix_sizes):
    first_radix, mid_radix, last_radix = radix_sizes
    half_first = first_radix // 2
    batch_rows = real_part.shape[0]
    (
        outer_real,
        outer_imag,
        mid_real,
        mid_imag,
        last_real,
        last_imag,
        twist_real,
        twist_imag,
        inner_real,
        inner_imag,
    ) = table_set
    real_part, imag_part = apply_matrix(
        "bkjq,mq->bkjm", real_part, imag_part, last_real / last_radix, -last_imag / last_radix
    )
    real_part, imag_part = complex_times(real_part, imag_part, inner_real, -inner_imag)
    real_part, imag_part = apply_matrix(
        "bkjm,nj->bknm", real_part, imag_part, mid_real / mid_radix, -mid_imag / mid_radix
    )
    real_part, imag_part = complex_times(real_part, imag_part, twist_real, -twist_imag)
    matrix_real = outer_real[:half_first] / first_radix
    matrix_imag = -outer_imag[:half_first] / first_radix
    out_real, out_imag = apply_matrix(
        "bknm,ak->banm", real_part, imag_part, matrix_real, matrix_imag
    )
    return (out_real.reshape(batch_rows, -1), out_imag.reshape(batch_rows, -1))


def spectrum(decay_rows, residue_rows, radix_sizes, seq_length):
    first_radix, mid_radix, last_radix = radix_sizes
    length_all = first_radix * mid_radix * last_radix
    poles = decay_rows.shape[1]
    shape_all = (first_radix, mid_radix, last_radix)
    frequency = (
        lax.broadcasted_iota(jnp.int32, shape_all, 0)
        + first_radix * lax.broadcasted_iota(jnp.int32, shape_all, 1)
        + first_radix * mid_radix * lax.broadcasted_iota(jnp.int32, shape_all, 2)
    )
    half_angle = frequency.astype(jnp.float32) * (math.pi / length_all)
    sin_half = jnp.sin(half_angle)
    sin_full = jnp.sin(2.0 * half_angle)
    parity_sign = (1 - 2 * (frequency % 2)).astype(jnp.float32)

    def add_pole(pole_index, running):
        run_real, run_imag = running
        rate_col = lax.dynamic_slice_in_dim(decay_rows, pole_index, 1, 1).reshape(-1, 1, 1, 1)
        weight = lax.dynamic_slice_in_dim(residue_rows, pole_index, 1, 1).reshape(
            -1, 1, 1, 1
        ) * jnp.sqrt(2.0 * rate_col / poles)
        retained = jnp.exp(-rate_col)
        den_real = -jnp.expm1(-rate_col) + 2.0 * retained * sin_half * sin_half
        den_imag = retained * sin_full
        pole_scale = (
            weight
            * (1.0 - jnp.exp(-rate_col * seq_length) * parity_sign)
            / (den_real * den_real + den_imag * den_imag)
        )
        return (run_real + pole_scale * den_real, run_imag - pole_scale * den_imag)

    zeros_all = jnp.zeros((decay_rows.shape[0],) + shape_all, jnp.float32)
    return lax.fori_loop(0, poles, add_pole, (zeros_all, zeros_all))


def general(x_gate, x_post, values, decay, residue, w_out):
    tok_rows, block_width = x_gate.shape
    ctx_count = lax.axis_size("ctx")
    tp_count = lax.axis_size("tp")
    chan_group = block_width // ctx_count
    seq_length = tok_rows * ctx_count
    radix_sizes = radices(2 * seq_length)
    table_set = tables(radix_sizes)
    first_row = lax.axis_index("ctx") * chan_group
    own_rate = lax.dynamic_slice_in_dim(decay, first_row, chan_group, 1)
    own_residue = lax.dynamic_slice_in_dim(residue, first_row, chan_group, 1)
    own_spec = [
        spectrum(own_rate[filter_index], own_residue[filter_index], radix_sizes, seq_length)
        for filter_index in range(2)
    ]
    forward_rows = [x_gate, values] + [x_post]
    row_count = len(forward_rows)
    base_rows = jnp.stack(forward_rows)
    copied = base_rows
    for bit_index in range(tp_count.bit_length() - 1):
        copied = partner(copied, "tp", bit_index)
    sent_rows = jnp.concatenate([base_rows, copied[:, :, ::-1]], axis=0)
    received = lax.all_to_all(
        jnp.swapaxes(sent_rows, 1, 2), "ctx", split_axis=1, concat_axis=2, tiled=True
    )
    gate_fwd = received[0].astype(jnp.float32)
    value_fwd = received[1].astype(jnp.float32)
    mirrored = received[row_count:, :, ::-1].astype(jnp.float32)
    spec_real, spec_imag = forward(value_fwd, mirrored[1], table_set, radix_sizes)
    spec_real, spec_imag = complex_times(spec_real, spec_imag, own_spec[0][0], own_spec[0][1])
    along_fwd, along_rev = inverse(spec_real, spec_imag, table_set, radix_sizes)
    spec_real, spec_imag = forward(
        gate_fwd * along_fwd, mirrored[0] * along_rev, table_set, radix_sizes
    )
    spec_real, spec_imag = complex_times(spec_real, spec_imag, own_spec[1][0], own_spec[1][1])
    sum_fwd, sum_rev = inverse(spec_real, spec_imag, table_set, radix_sizes)
    sum_fwd = received[2].astype(jnp.float32) * sum_fwd
    sum_rev = mirrored[2] * sum_rev
    results = jnp.stack([sum_fwd, sum_rev[:, ::-1]])
    returned = lax.all_to_all(
        results.astype(jnp.bfloat16), "ctx", split_axis=2, concat_axis=1, tiled=True
    ).astype(results.dtype)
    flipped = returned[1, ::-1, :]
    for bit_index in range(tp_count.bit_length() - 1):
        flipped = partner(flipped.astype(jnp.bfloat16), "tp", bit_index).astype(flipped.dtype)
    total_rows = returned[0] + flipped
    total_rows = total_rows.T
    mixed_rows = total_rows.astype(jnp.bfloat16)
    whole_rows = lax.all_gather(mixed_rows, "tp", axis=1, tiled=True)
    projected = lax.dot_general(
        whole_rows,
        lax.all_gather(w_out, "ctx", axis=0, tiled=True),
        (((1,), (1,)), ((), ())),
        preferred_element_type=jnp.float32,
    )
    return projected.astype(jnp.bfloat16)


def cycle(row_factor, col_factor, modulus):
    angle = (row_factor * col_factor % modulus).astype(jnp.float32) * (2.0 * math.pi / modulus)
    return jnp.cos(angle), jnp.sin(angle)


def put_tables(table_ref, back_ref):
    block = table_ref.shape[1]
    modulus = 4 * block
    coarse = 16
    rows = lax.broadcasted_iota(jnp.int32, (coarse, block), 0)
    cols = lax.broadcasted_iota(jnp.int32, (coarse, block), 1)

    def parts(big, small):
        for place in range(block // coarse):
            big_cos, big_sin = (part[place : place + 1] for part in big)
            span = slice(place * coarse, (place + 1) * coarse)
            below = slice(block + place * coarse, block + (place + 1) * coarse)
            cos = halves(big_cos * small[0] - big_sin * small[1])
            sin = halves(-(big_sin * small[0] + big_cos * small[1]))
            yield span, below, cos, sin

    frequency = 2 * cols + 1
    for span, _, cos, sin in parts(cycle(coarse * rows, frequency, modulus), cycle(rows, frequency, modulus)):
        table_ref[0, span, :block], table_ref[1, span, :block] = cos
        table_ref[0, span, block:], table_ref[1, span, block:] = sin
    for span, below, cos, sin in parts(cycle(2 * coarse * rows, cols, modulus), cycle(2 * rows + 1, cols, modulus)):
        back_ref[0, span], back_ref[1, span] = cos
        back_ref[0, below], back_ref[1, below] = sin


def halves(value):
    high = value.astype(jnp.bfloat16)
    return high, (value - high.astype(jnp.float32)).astype(jnp.bfloat16)


def mul(left, right):
    return jnp.dot(left, right, preferred_element_type=jnp.float32)


def mul3(high, low, table_ref):
    return mul(high, table_ref[0]) + (mul(low, table_ref[0]) + mul(high, table_ref[1]))


def pack_kernel(
    gate_hbm, value_hbm, post_hbm, decay_hbm, residue_hbm,
    out_hbm, own_hbm, sent_hbm, held_ref, cut_ref, ready_ref, sems, out_sems,
):
    ctx_count, _, group, tok = out_hbm.shape
    width = gate_hbm.shape[1]
    half = decay_hbm.shape[0]
    position = lax.axis_index("ctx")
    pairs = []
    for place, index in enumerate((position, ctx_count - 1 - position)):
        columns = pl.ds(pl.multiple_of(index * group // tok * tok, tok), tok)
        pairs += [(decay_hbm.at[:, columns], cut_ref.at[place, :half]), (residue_hbm.at[:, columns], cut_ref.at[place, half:])]
    pairs += [(source, held_ref.at[place]) for place, source in enumerate((value_hbm, gate_hbm, post_hbm))]
    copies = [pltpu.make_async_copy(*pair, sems.at[place]) for place, pair in enumerate(pairs)]
    for copy in copies:
        copy.start()
    sends = []
    for place, target in enumerate((own_hbm, sent_hbm)):
        copies[2 * place].wait()
        copies[2 * place + 1].wait()
        sends.append(pltpu.make_async_copy(cut_ref.at[place], target, out_sems.at[3 + place]))
        sends[-1].start()
    for place, copy in enumerate(copies[4:]):
        copy.wait()
        for first in range(0, width, tok):
            turned = held_ref[place, :, first : first + tok].T
            for part in range(tok // group):
                ready_ref[first // group + part, place] = turned[part * group : (part + 1) * group]
        sends.append(pltpu.make_async_copy(ready_ref.at[:, place], out_hbm.at[:, place], out_sems.at[place]))
        sends[-1].start()
    for send in sends:
        send.wait()


def mirror_rows(value):
    row = lax.broadcasted_iota(jnp.int32, (8, value.shape[1]), 0)
    result = []
    for first in range(value.shape[0] - 8, -1, -8):
        part = value[first : first + 8]
        for shift in (1, 2, 4):
            part = jnp.where(row & shift == 0, pltpu.roll(part, 8 - shift, 0), pltpu.roll(part, shift, 0))
        result.append(part)
    return jnp.concatenate(result, axis=0)


def put_spectra(poles, index, turned, out_ref, time_ref, table_ref):
    blocks, group, twice = out_ref.shape
    block = twice // 2
    lanes = 128
    ramp = lax.broadcasted_iota(jnp.int32, (8, lanes), 1).astype(jnp.float32)
    sign = (1 - 2 * (lax.broadcasted_iota(jnp.int32, (group, block), 1) % 2)).astype(jnp.float32)
    for row in range(0, group, 8):
        rows = slice(row, row + 8)
        rate = turned[rows, index * poles : (index + 1) * poles]
        scale = turned[rows, (2 + index) * poles : (3 + index) * poles] * (jnp.sqrt(rate * (2.0 / poles)) / block)
        slope = rate * -math.log2(math.e)
        jump = jnp.exp2(slope * lanes)
        sums = [None] * (blocks * block // lanes)
        for pole in range(poles):
            term = scale[:, pole : pole + 1] * jnp.exp2(slope[:, pole : pole + 1] * ramp)
            step = jnp.broadcast_to(jump[:, pole : pole + 1], (8, lanes))
            for place in range(len(sums)):
                sums[place] = term if pole == 0 else sums[place] + term
                if place + 1 < len(sums):
                    term = term * step
        for place, total in enumerate(sums):
            lag, lane = divmod(place * lanes, block)
            time_ref[lag * group + row : lag * group + row + 8, lane : lane + lanes] = total
    spec = mul3(*halves(time_ref[...]), table_ref)
    for lag in range(blocks):
        real = spec[lag * group : (lag + 1) * group, :block]
        imag = spec[lag * group : (lag + 1) * group, block:]
        if lag > 0:
            real = real - sign * spec[(lag - 1) * group : lag * group, block:]
            imag = imag + sign * spec[(lag - 1) * group : lag * group, :block]
        out_ref[lag, :, :block] = real
        out_ref[lag, :, block:] = imag


def filter_kernel(poles, par_ref, out_ref, table_ref, back_ref, time_ref, turned_ref):
    group = out_ref.shape[2]
    put_tables(table_ref, back_ref)
    turned_ref[...] = par_ref[...].T
    turned = turned_ref[pl.ds(pl.multiple_of(lax.axis_index("ctx") * group % turned_ref.shape[0], group), group)]
    for index in range(2):
        put_spectra(poles, index, turned, out_ref.at[index], time_ref.at[index], table_ref)


def conv_kernel(
    poles, x_ref, own_ref, par_ref, table_ref, back_ref, out_hbm,
    paired_ref, time_ref, turned_ref, spec_ref, high_ref, ready_ref, sems,
):
    turned_ref[...] = par_ref[...].T
    blocks, group, twice = own_ref.shape[1:]
    block = twice // 2
    rows_all = blocks * group
    tall, wide = 16, 128
    pieces = x_ref.shape[0] // blocks
    first = (x_ref.shape[0] - 1 - lax.axis_index("ctx")) * group % turned_ref.shape[0]
    turned = mirror_rows(turned_ref[pl.ds(pl.multiple_of(first, group), group)])

    def rows_of(position):
        return jnp.concatenate(
            [
                jnp.concatenate([x_ref[m * pieces + s, position] for s in range(pieces)], axis=1)
                for m in range(blocks)
            ],
            axis=0,
        )

    def times(index, side, source, row, lane):
        data = []
        for m in range(blocks):
            rows = slice(source + m * group + row, source + m * group + row + tall)
            data.append((spec_ref[rows, lane : lane + wide], spec_ref[rows, block + lane : block + lane + wide]))
        sums = [None] * blocks
        for lag in range(blocks):
            h_ref = (own_ref, paired_ref)[side]
            f_re = h_ref[index, lag, row : row + tall, lane : lane + wide]
            f_im = h_ref[index, lag, row : row + tall, block + lane : block + lane + wide]
            for m in range(blocks - lag):
                target, (d_re, d_im) = (m + lag, data[m]) if side == 0 else (m, data[m + lag])
                if side == 0:
                    real, imag = f_re * d_re - f_im * d_im, f_re * d_im + f_im * d_re
                else:
                    real, imag = f_re * d_re + f_im * d_im, f_re * d_im - f_im * d_re
                if sums[target] is not None:
                    real, imag = sums[target][0] + real, sums[target][1] + imag
                sums[target] = (real, imag)
        return sums

    def to_time(rows):
        return mul(high_ref[rows], back_ref[0]) + mul(high_ref[rows], back_ref[1])

    def keep(target, row, lane, sums):
        for m in range(blocks):
            rows = slice(target + m * group + row, target + m * group + row + tall)
            for part in range(2):
                cols = slice(part * block + lane, part * block + lane + wide)
                high_ref[rows, cols] = sums[m][part].astype(jnp.bfloat16)

    chunks = [(row, lane) for row in range(0, group, tall) for lane in range(0, block, wide)]

    value = rows_of(0)
    gate = rows_of(1).astype(jnp.float32)
    spec_ref[:rows_all] = mul(value, table_ref[0]) + mul(value, table_ref[1])
    sides = [slice(side * rows_all, (side + 1) * rows_all) for side in range(2)]
    gated = []
    put_spectra(poles, 0, turned, paired_ref.at[0], time_ref.at[0], table_ref)
    for side in range(2):
        for row, lane in chunks:
            keep(side * rows_all, row, lane, times(0, side, 0, row, lane))
        gated.append(halves(gate * to_time(sides[side])))
    put_spectra(poles, 1, turned, paired_ref.at[1], time_ref.at[1], table_ref)
    for side in range(2):
        spec_ref[sides[side]] = mul3(*gated[side], table_ref)
    for row, lane in chunks:
        ahead, back = times(1, 0, 0, row, lane), times(1, 1, rows_all, row, lane)
        keep(0, row, lane, [(a[0] + b[0], a[1] + b[1]) for a, b in zip(ahead, back)])
    post = rows_of(2)
    tok = block // pieces
    sends = []
    for part in range(2):
        rows = slice(part * rows_all // 2, (part + 1) * rows_all // 2)
        summed = to_time(rows)
        mixed = (post[rows].astype(jnp.float32) * summed).astype(jnp.bfloat16)
        first = part * blocks // 2 * pieces
        for m in range(blocks // 2):
            for s in range(pieces):
                ready_ref[first + m * pieces + s] = mixed[m * group : (m + 1) * group, s * tok : (s + 1) * tok]
        span = pl.ds(first, blocks // 2 * pieces)
        for copy in range(out_hbm.shape[0]):
            sends.append(pltpu.make_async_copy(ready_ref.at[span], out_hbm.at[copy, span], sems.at[part, copy]))
            sends[-1].start()
    for send in sends:
        send.wait()


def project_kernel(mixed_ref, *refs):
    w_refs, (out_hbm, held_ref, ready_ref, sems) = refs[:-4], refs[-4:]
    rows = w_refs[0].shape[0]
    tile = 2 * rows
    position = lax.axis_index("ctx")
    even = pl.multiple_of(position % 2 * rows, rows)
    odd = pl.multiple_of((1 - position % 2) * rows, rows)
    sends = []
    for part in range(0, len(w_refs), 4):
        total = mul(jnp.concatenate([w_ref[...] for w_ref in w_refs[part : part + 4]], axis=0), mixed_ref[...])
        for pair in range(2):
            place = part // 2 + pair
            held_ref[place, pl.ds(even, rows)] = total[pair * tile : pair * tile + rows]
            held_ref[place, pl.ds(odd, rows)] = total[pair * tile + rows : (pair + 1) * tile]
            ready_ref[place] = held_ref[place].T.astype(jnp.bfloat16)
            columns = pl.ds(pl.multiple_of((position // 2 ^ place) * tile, tile), tile)
            sends.append(pltpu.make_async_copy(ready_ref.at[place], out_hbm.at[:, columns], sems.at[place]))
            sends[-1].start()
    for send in sends:
        send.wait()


def whole_call(kernel, out_shape, scratch, flops, nbytes, *operands, in_hbm=0, out_hbm=()):
    results = pl.pallas_call(
        kernel,
        out_shape=out_shape,
        in_specs=[
            pl.BlockSpec(memory_space=pltpu.HBM if place < in_hbm else pltpu.VMEM) for place in range(len(operands))
        ],
        out_specs=[
            pl.BlockSpec(memory_space=pltpu.HBM if place in out_hbm else pltpu.VMEM) for place in range(len(out_shape))
        ],
        scratch_shapes=scratch,
        cost_estimate=pl.CostEstimate(flops=flops, bytes_accessed=nbytes, transcendentals=0),
        compiler_params=pltpu.CompilerParams(vmem_limit_bytes=None if in_hbm else 32 * 2**20),
    )(*operands)
    return results if len(out_shape) > 1 else results[0]


def blocked(x_gate, x_post, values, decay, residue, w_out):
    tok, width = x_gate.shape
    ctx_count = lax.axis_size("ctx")
    tp_count = lax.axis_size("tp")
    group = width // ctx_count
    poles = decay.shape[2]
    block = 2 * tok
    blocks = tok * ctx_count // block
    rows, channels = w_out.shape
    half = 2 * poles

    packed, own, mirrored = whole_call(
        pack_kernel,
        (
            jax.ShapeDtypeStruct((ctx_count, 3, group, tok), jnp.bfloat16),
            jax.ShapeDtypeStruct((2 * half, tok), jnp.float32),
            jax.ShapeDtypeStruct((2 * half, tok), jnp.float32),
        ),
        [
            pltpu.VMEM((3, tok, width), jnp.bfloat16),
            pltpu.VMEM((2, 2 * half, tok), jnp.float32),
            pltpu.VMEM((ctx_count, 3, group, tok), jnp.bfloat16),
            pltpu.SemaphoreType.DMA((7,)),
            pltpu.SemaphoreType.DMA((5,)),
        ],
        0,
        6 * tok * width * 2,
        x_gate,
        values,
        x_post,
        jnp.swapaxes(decay, 1, 2).reshape(half, width),
        jnp.swapaxes(residue, 1, 2).reshape(half, width),
        in_hbm=5,
        out_hbm=(0, 1, 2),
    )
    paired = lax.ppermute(mirrored, "tp", [(z, tp_count - 1 - z) for z in range(tp_count)])
    received = lax.all_to_all(packed, "ctx", split_axis=0, concat_axis=0, tiled=True)

    w_late, mirrored = lax.optimization_barrier((w_out, mirrored))
    w_x, w_y = partner(w_late, "ctx", 1), partner(w_late, "ctx", 2)
    own_spectra, table, back_table = whole_call(
        functools.partial(filter_kernel, poles),
        (
            jax.ShapeDtypeStruct((2, blocks, group, 2 * block), jnp.float32),
            jax.ShapeDtypeStruct((2, block, 2 * block), jnp.bfloat16),
            jax.ShapeDtypeStruct((2, 2 * block, block), jnp.bfloat16),
        ),
        [
            pltpu.VMEM((2, blocks * group, block), jnp.float32),
            pltpu.VMEM((tok, 2 * half), jnp.float32),
        ],
        2 * 2 * blocks * group * block * 2 * block * 3,
        2 * blocks * group * 2 * block * 4,
        own,
    )
    mixed = whole_call(
        functools.partial(conv_kernel, poles),
        (jax.ShapeDtypeStruct((tp_count, ctx_count, group, tok), jnp.bfloat16),),
        [
            pltpu.VMEM((2, blocks, group, 2 * block), jnp.float32),
            pltpu.VMEM((2, blocks * group, block), jnp.float32),
            pltpu.VMEM((tok, 2 * half), jnp.float32),
            pltpu.VMEM((2 * blocks * group, 2 * block), jnp.float32),
            pltpu.VMEM((2 * blocks * group, 2 * block), jnp.bfloat16),
            pltpu.VMEM((ctx_count, group, tok), jnp.bfloat16),
            pltpu.SemaphoreType.DMA((2, tp_count)),
        ],
        2 * 8 * blocks * group * block * 2 * block * 3,
        4 * blocks * group * 2 * block * 4,
        received,
        own_spectra,
        paired,
        table,
        back_table,
        out_hbm=(0,),
    )
    mixed, w_x, w_y, w_own = lax.optimization_barrier((mixed, w_x, w_y, w_out))
    w_far = partner(w_x, "ctx", 2)
    w_blocks = {0: w_own, 2: w_x, 4: w_y, 6: w_far}
    for mask in range(0, ctx_count, 2):
        w_blocks[mask + 1] = partner(w_blocks[mask], "ctx", 0)
    every = lax.all_to_all(
        mixed.reshape(tp_count * ctx_count, group, tok), ("tp", "ctx"), split_axis=0, concat_axis=0, tiled=True
    ).reshape(channels, tok)
    return whole_call(
        project_kernel,
        (jax.ShapeDtypeStruct((tok, rows * ctx_count), jnp.bfloat16),),
        [
            pltpu.VMEM((ctx_count // 2, 2 * rows, tok), jnp.float32),
            pltpu.VMEM((ctx_count // 2, tok, 2 * rows), jnp.bfloat16),
            pltpu.SemaphoreType.DMA((ctx_count // 2,)),
        ],
        2 * tok * rows * ctx_count * channels,
        2 * rows * ctx_count * channels,
        every,
        *[w_blocks[mask] for mask in range(ctx_count)],
        out_hbm=(0,),
    )


def local(x_gate, x_post, values, decay, residue, w_out):
    tok, width = x_gate.shape
    ctx_count = lax.axis_size("ctx")
    if tok == 128 and width == 512 and ctx_count == 8 and w_out.shape[0] == 64 and lax.axis_size("tp") == 4:
        return blocked(x_gate, x_post, values, decay, residue, w_out)
    return general(x_gate, x_post, values, decay, residue, w_out)


def solution(mesh):
    in_specs = (
        P("ctx", "tp"),
        P("ctx", "tp"),
        P("ctx", "tp"),
        P(None, "tp", None),
        P(None, "tp", None),
        P(("tp", "ctx"), None),
    )
    out_specs = P("ctx", "tp")
    return jax.shard_map(local, mesh=mesh, in_specs=in_specs, out_specs=out_specs, check_vma=False)
```

```python
import functools
import math

import jax
import jax.numpy as jnp
from jax import lax
from jax.experimental import pallas as pl
from jax.experimental.pallas import tpu as pltpu
from jax.sharding import PartitionSpec as P

HIGHEST = lax.Precision.HIGHEST


def partner(value, axis, bit):
    mask = 2**bit
    pairs = [(source, source ^ mask) for source in range(lax.axis_size(axis))]
    return lax.ppermute(value, axis, pairs)


def radices(length_all):
    last_radix = min(128, length_all // 4)
    first_radix = min(32, length_all // last_radix)
    return (first_radix, length_all // (first_radix * last_radix), last_radix)


def rotation(row_count, col_count, modulus):
    product = (
        lax.broadcasted_iota(jnp.int32, (row_count, col_count), 0)
        * lax.broadcasted_iota(jnp.int32, (row_count, col_count), 1)
        % modulus
    )
    angle = product.astype(jnp.float32) * (2.0 * math.pi / modulus)
    return (jnp.cos(angle), -jnp.sin(angle))


def tables(radix_sizes):
    first_radix, mid_radix, last_radix = radix_sizes
    length_all = first_radix * mid_radix * last_radix
    outer_real, outer_imag = rotation(first_radix, first_radix, first_radix)
    mid_real, mid_imag = rotation(mid_radix, mid_radix, mid_radix)
    last_real, last_imag = rotation(last_radix, last_radix, last_radix)
    twist_real, twist_imag = rotation(first_radix, mid_radix * last_radix, length_all)
    twist_real = twist_real.reshape(first_radix, mid_radix, last_radix)
    twist_imag = twist_imag.reshape(first_radix, mid_radix, last_radix)
    inner_real, inner_imag = rotation(mid_radix, last_radix, mid_radix * last_radix)
    return (
        outer_real,
        outer_imag,
        mid_real,
        mid_imag,
        last_real,
        last_imag,
        twist_real,
        twist_imag,
        inner_real,
        inner_imag,
    )


def apply_matrix(pattern, real_part, imag_part, matrix_real, matrix_imag):
    out_real = jnp.einsum(pattern, real_part, matrix_real, precision=HIGHEST) - jnp.einsum(
        pattern, imag_part, matrix_imag, precision=HIGHEST
    )
    out_imag = jnp.einsum(pattern, real_part, matrix_imag, precision=HIGHEST) + jnp.einsum(
        pattern, imag_part, matrix_real, precision=HIGHEST
    )
    return (out_real, out_imag)


def complex_times(left_real, left_imag, right_real, right_imag):
    return (
        left_real * right_real - left_imag * right_imag,
        left_real * right_imag + left_imag * right_real,
    )


def forward(real_part, imag_part, table_set, radix_sizes):
    first_radix, mid_radix, last_radix = radix_sizes
    half_first = first_radix // 2
    batch_rows = real_part.shape[0]
    (
        outer_real,
        outer_imag,
        mid_real,
        mid_imag,
        last_real,
        last_imag,
        twist_real,
        twist_imag,
        inner_real,
        inner_imag,
    ) = table_set
    real_part = real_part.reshape(batch_rows, half_first, mid_radix, last_radix)
    imag_part = imag_part.reshape(batch_rows, half_first, mid_radix, last_radix)
    real_part, imag_part = apply_matrix(
        "banm,ak->bknm", real_part, imag_part, outer_real[:half_first], outer_imag[:half_first]
    )
    real_part, imag_part = complex_times(real_part, imag_part, twist_real, twist_imag)
    real_part, imag_part = apply_matrix("bknm,nj->bkjm", real_part, imag_part, mid_real, mid_imag)
    real_part, imag_part = complex_times(real_part, imag_part, inner_real, inner_imag)
    return apply_matrix("bkjm,mq->bkjq", real_part, imag_part, last_real, last_imag)


def inverse(real_part, imag_part, table_set, radix_sizes):
    first_radix, mid_radix, last_radix = radix_sizes
    half_first = first_radix // 2
    batch_rows = real_part.shape[0]
    (
        outer_real,
        outer_imag,
        mid_real,
        mid_imag,
        last_real,
        last_imag,
        twist_real,
        twist_imag,
        inner_real,
        inner_imag,
    ) = table_set
    real_part, imag_part = apply_matrix(
        "bkjq,mq->bkjm", real_part, imag_part, last_real / last_radix, -last_imag / last_radix
    )
    real_part, imag_part = complex_times(real_part, imag_part, inner_real, -inner_imag)
    real_part, imag_part = apply_matrix(
        "bkjm,nj->bknm", real_part, imag_part, mid_real / mid_radix, -mid_imag / mid_radix
    )
    real_part, imag_part = complex_times(real_part, imag_part, twist_real, -twist_imag)
    matrix_real = outer_real[:half_first] / first_radix
    matrix_imag = -outer_imag[:half_first] / first_radix
    out_real, out_imag = apply_matrix(
        "bknm,ak->banm", real_part, imag_part, matrix_real, matrix_imag
    )
    return (out_real.reshape(batch_rows, -1), out_imag.reshape(batch_rows, -1))


def spectrum(decay_rows, residue_rows, radix_sizes, seq_length):
    first_radix, mid_radix, last_radix = radix_sizes
    length_all = first_radix * mid_radix * last_radix
    poles = decay_rows.shape[1]
    shape_all = (first_radix, mid_radix, last_radix)
    frequency = (
        lax.broadcasted_iota(jnp.int32, shape_all, 0)
        + first_radix * lax.broadcasted_iota(jnp.int32, shape_all, 1)
        + first_radix * mid_radix * lax.broadcasted_iota(jnp.int32, shape_all, 2)
    )
    half_angle = frequency.astype(jnp.float32) * (math.pi / length_all)
    sin_half = jnp.sin(half_angle)
    sin_full = jnp.sin(2.0 * half_angle)
    parity_sign = (1 - 2 * (frequency % 2)).astype(jnp.float32)

    def add_pole(pole_index, running):
        run_real, run_imag = running
        rate_col = lax.dynamic_slice_in_dim(decay_rows, pole_index, 1, 1).reshape(-1, 1, 1, 1)
        weight = lax.dynamic_slice_in_dim(residue_rows, pole_index, 1, 1).reshape(
            -1, 1, 1, 1
        ) * jnp.sqrt(2.0 * rate_col / poles)
        retained = jnp.exp(-rate_col)
        den_real = -jnp.expm1(-rate_col) + 2.0 * retained * sin_half * sin_half
        den_imag = retained * sin_full
        pole_scale = (
            weight
            * (1.0 - jnp.exp(-rate_col * seq_length) * parity_sign)
            / (den_real * den_real + den_imag * den_imag)
        )
        return (run_real + pole_scale * den_real, run_imag - pole_scale * den_imag)

    zeros_all = jnp.zeros((decay_rows.shape[0],) + shape_all, jnp.float32)
    return lax.fori_loop(0, poles, add_pole, (zeros_all, zeros_all))


def general(x_gate, x_post, values, decay, residue, w_out):
    tok_rows, block_width = x_gate.shape
    ctx_count = lax.axis_size("ctx")
    tp_count = lax.axis_size("tp")
    chan_group = block_width // ctx_count
    seq_length = tok_rows * ctx_count
    radix_sizes = radices(2 * seq_length)
    table_set = tables(radix_sizes)
    first_row = lax.axis_index("ctx") * chan_group
    own_rate = lax.dynamic_slice_in_dim(decay, first_row, chan_group, 1)
    own_residue = lax.dynamic_slice_in_dim(residue, first_row, chan_group, 1)
    own_spec = [
        spectrum(own_rate[filter_index], own_residue[filter_index], radix_sizes, seq_length)
        for filter_index in range(2)
    ]
    forward_rows = [x_gate, values] + [x_post]
    row_count = len(forward_rows)
    base_rows = jnp.stack(forward_rows)
    copied = base_rows
    for bit_index in range(tp_count.bit_length() - 1):
        copied = partner(copied, "tp", bit_index)
    sent_rows = jnp.concatenate([base_rows, copied[:, :, ::-1]], axis=0)
    received = lax.all_to_all(
        jnp.swapaxes(sent_rows, 1, 2), "ctx", split_axis=1, concat_axis=2, tiled=True
    )
    gate_fwd = received[0].astype(jnp.float32)
    value_fwd = received[1].astype(jnp.float32)
    mirrored = received[row_count:, :, ::-1].astype(jnp.float32)
    spec_real, spec_imag = forward(value_fwd, mirrored[1], table_set, radix_sizes)
    spec_real, spec_imag = complex_times(spec_real, spec_imag, own_spec[0][0], own_spec[0][1])
    along_fwd, along_rev = inverse(spec_real, spec_imag, table_set, radix_sizes)
    spec_real, spec_imag = forward(
        gate_fwd * along_fwd, mirrored[0] * along_rev, table_set, radix_sizes
    )
    spec_real, spec_imag = complex_times(spec_real, spec_imag, own_spec[1][0], own_spec[1][1])
    sum_fwd, sum_rev = inverse(spec_real, spec_imag, table_set, radix_sizes)
    sum_fwd = received[2].astype(jnp.float32) * sum_fwd
    sum_rev = mirrored[2] * sum_rev
    results = jnp.stack([sum_fwd, sum_rev[:, ::-1]])
    returned = lax.all_to_all(
        results.astype(jnp.bfloat16), "ctx", split_axis=2, concat_axis=1, tiled=True
    ).astype(results.dtype)
    flipped = returned[1, ::-1, :]
    for bit_index in range(tp_count.bit_length() - 1):
        flipped = partner(flipped.astype(jnp.bfloat16), "tp", bit_index).astype(flipped.dtype)
    total_rows = returned[0] + flipped
    total_rows = total_rows.T
    mixed_rows = total_rows.astype(jnp.bfloat16)
    whole_rows = lax.all_gather(mixed_rows, "tp", axis=1, tiled=True)
    projected = lax.dot_general(
        whole_rows,
        lax.all_gather(w_out, "ctx", axis=0, tiled=True),
        (((1,), (1,)), ((), ())),
        preferred_element_type=jnp.float32,
    )
    return projected.astype(jnp.bfloat16)


def cycle(row_factor, col_factor, modulus):
    angle = (row_factor * col_factor % modulus).astype(jnp.float32) * (2.0 * math.pi / modulus)
    return jnp.cos(angle), jnp.sin(angle)


def put_tables(table_ref, back_ref):
    block = table_ref.shape[1]
    modulus = 4 * block
    coarse = 16
    rows = lax.broadcasted_iota(jnp.int32, (coarse, block), 0)
    cols = lax.broadcasted_iota(jnp.int32, (coarse, block), 1)

    def parts(big, small):
        for place in range(block // coarse):
            big_cos, big_sin = (part[place : place + 1] for part in big)
            span = slice(place * coarse, (place + 1) * coarse)
            below = slice(block + place * coarse, block + (place + 1) * coarse)
            cos = halves(big_cos * small[0] - big_sin * small[1])
            sin = halves(-(big_sin * small[0] + big_cos * small[1]))
            yield span, below, cos, sin

    frequency = 2 * cols + 1
    for span, _, cos, sin in parts(cycle(coarse * rows, frequency, modulus), cycle(rows, frequency, modulus)):
        table_ref[0, span, :block], table_ref[1, span, :block] = cos
        table_ref[0, span, block:], table_ref[1, span, block:] = sin
    for span, below, cos, sin in parts(cycle(2 * coarse * rows, cols, modulus), cycle(2 * rows + 1, cols, modulus)):
        back_ref[0, span], back_ref[1, span] = cos
        back_ref[0, below], back_ref[1, below] = sin


def halves(value):
    high = value.astype(jnp.bfloat16)
    return high, (value - high.astype(jnp.float32)).astype(jnp.bfloat16)


def mul(left, right):
    return jnp.dot(left, right, preferred_element_type=jnp.float32)


def mul3(high, low, table_ref):
    return mul(high, table_ref[0]) + (mul(low, table_ref[0]) + mul(high, table_ref[1]))


def pack_kernel(
    gate_hbm, value_hbm, post_hbm, decay_hbm, residue_hbm,
    out_hbm, own_hbm, sent_hbm, held_ref, cut_ref, ready_ref, sems, out_sems,
):
    ctx_count, _, group, tok = out_hbm.shape
    width = gate_hbm.shape[1]
    half = decay_hbm.shape[0]
    position = lax.axis_index("ctx")
    pairs = []
    for place, index in enumerate((position, ctx_count - 1 - position)):
        columns = pl.ds(pl.multiple_of(index * group // tok * tok, tok), tok)
        pairs += [(decay_hbm.at[:, columns], cut_ref.at[place, :half]), (residue_hbm.at[:, columns], cut_ref.at[place, half:])]
    pairs += [(source, held_ref.at[place]) for place, source in enumerate((value_hbm, gate_hbm, post_hbm))]
    copies = [pltpu.make_async_copy(*pair, sems.at[place]) for place, pair in enumerate(pairs)]
    for copy in copies:
        copy.start()
    sends = []
    for place, target in enumerate((own_hbm, sent_hbm)):
        copies[2 * place].wait()
        copies[2 * place + 1].wait()
        sends.append(pltpu.make_async_copy(cut_ref.at[place], target, out_sems.at[3 + place]))
        sends[-1].start()
    for place, copy in enumerate(copies[4:]):
        copy.wait()
        for first in range(0, width, tok):
            turned = held_ref[place, :, first : first + tok].T
            for part in range(tok // group):
                ready_ref[first // group + part, place] = turned[part * group : (part + 1) * group]
        sends.append(pltpu.make_async_copy(ready_ref.at[:, place], out_hbm.at[:, place], out_sems.at[place]))
        sends[-1].start()
    for send in sends:
        send.wait()


def mirror_rows(value):
    row = lax.broadcasted_iota(jnp.int32, (8, value.shape[1]), 0)
    result = []
    for first in range(value.shape[0] - 8, -1, -8):
        part = value[first : first + 8]
        for shift in (1, 2, 4):
            part = jnp.where(row & shift == 0, pltpu.roll(part, 8 - shift, 0), pltpu.roll(part, shift, 0))
        result.append(part)
    return jnp.concatenate(result, axis=0)


def put_spectra(poles, index, turned, out_ref, time_ref, table_ref):
    blocks, group, twice = out_ref.shape
    block = twice // 2
    lanes = 128
    ramp = lax.broadcasted_iota(jnp.int32, (8, lanes), 1).astype(jnp.float32)
    sign = (1 - 2 * (lax.broadcasted_iota(jnp.int32, (group, block), 1) % 2)).astype(jnp.float32)
    for row in range(0, group, 8):
        rows = slice(row, row + 8)
        rate = turned[rows, index * poles : (index + 1) * poles]
        scale = turned[rows, (2 + index) * poles : (3 + index) * poles] * (jnp.sqrt(rate * (2.0 / poles)) / block)
        slope = rate * -math.log2(math.e)
        jump = jnp.exp2(slope * lanes)
        sums = [None] * (blocks * block // lanes)
        for pole in range(poles):
            term = scale[:, pole : pole + 1] * jnp.exp2(slope[:, pole : pole + 1] * ramp)
            step = jnp.broadcast_to(jump[:, pole : pole + 1], (8, lanes))
            for place in range(len(sums)):
                sums[place] = term if pole == 0 else sums[place] + term
                if place + 1 < len(sums):
                    term = term * step
        for place, total in enumerate(sums):
            lag, lane = divmod(place * lanes, block)
            time_ref[lag * group + row : lag * group + row + 8, lane : lane + lanes] = total
    spec = mul3(*halves(time_ref[...]), table_ref)
    for lag in range(blocks):
        real = spec[lag * group : (lag + 1) * group, :block]
        imag = spec[lag * group : (lag + 1) * group, block:]
        if lag > 0:
            real = real - sign * spec[(lag - 1) * group : lag * group, block:]
            imag = imag + sign * spec[(lag - 1) * group : lag * group, :block]
        out_ref[lag, :, :block] = real
        out_ref[lag, :, block:] = imag


def filter_kernel(poles, par_ref, out_ref, table_ref, back_ref, time_ref, turned_ref):
    group = out_ref.shape[2]
    put_tables(table_ref, back_ref)
    turned_ref[...] = par_ref[...].T
    turned = turned_ref[pl.ds(pl.multiple_of(lax.axis_index("ctx") * group % turned_ref.shape[0], group), group)]
    for index in range(2):
        put_spectra(poles, index, turned, out_ref.at[index], time_ref.at[index], table_ref)


def conv_kernel(
    poles, x_ref, own_ref, par_ref, table_ref, back_ref, out_hbm,
    paired_ref, time_ref, turned_ref, spec_ref, high_ref, ready_ref, sems,
):
    turned_ref[...] = par_ref[...].T
    blocks, group, twice = own_ref.shape[1:]
    block = twice // 2
    rows_all = blocks * group
    tall, wide = 16, 128
    pieces = x_ref.shape[0] // blocks
    first = (x_ref.shape[0] - 1 - lax.axis_index("ctx")) * group % turned_ref.shape[0]
    turned = mirror_rows(turned_ref[pl.ds(pl.multiple_of(first, group), group)])

    def rows_of(position):
        return jnp.concatenate(
            [
                jnp.concatenate([x_ref[m * pieces + s, position] for s in range(pieces)], axis=1)
                for m in range(blocks)
            ],
            axis=0,
        )

    def times(index, side, source, row, lane):
        data = []
        for m in range(blocks):
            rows = slice(source + m * group + row, source + m * group + row + tall)
            data.append((spec_ref[rows, lane : lane + wide], spec_ref[rows, block + lane : block + lane + wide]))
        sums = [None] * blocks
        for lag in range(blocks):
            h_ref = (own_ref, paired_ref)[side]
            f_re = h_ref[index, lag, row : row + tall, lane : lane + wide]
            f_im = h_ref[index, lag, row : row + tall, block + lane : block + lane + wide]
            for m in range(blocks - lag):
                target, (d_re, d_im) = (m + lag, data[m]) if side == 0 else (m, data[m + lag])
                if side == 0:
                    real, imag = f_re * d_re - f_im * d_im, f_re * d_im + f_im * d_re
                else:
                    real, imag = f_re * d_re + f_im * d_im, f_re * d_im - f_im * d_re
                if sums[target] is not None:
                    real, imag = sums[target][0] + real, sums[target][1] + imag
                sums[target] = (real, imag)
        return sums

    def to_time(rows):
        return mul(high_ref[rows], back_ref[0]) + mul(high_ref[rows], back_ref[1])

    def keep(target, row, lane, sums):
        for m in range(blocks):
            rows = slice(target + m * group + row, target + m * group + row + tall)
            for part in range(2):
                cols = slice(part * block + lane, part * block + lane + wide)
                high_ref[rows, cols] = sums[m][part].astype(jnp.bfloat16)

    chunks = [(row, lane) for row in range(0, group, tall) for lane in range(0, block, wide)]

    value = rows_of(0)
    gate = rows_of(1).astype(jnp.float32)
    spec_ref[:rows_all] = mul(value, table_ref[0]) + mul(value, table_ref[1])
    sides = [slice(side * rows_all, (side + 1) * rows_all) for side in range(2)]
    gated = []
    put_spectra(poles, 0, turned, paired_ref.at[0], time_ref.at[0], table_ref)
    for side in range(2):
        for row, lane in chunks:
            keep(side * rows_all, row, lane, times(0, side, 0, row, lane))
        gated.append(halves(gate * to_time(sides[side])))
    put_spectra(poles, 1, turned, paired_ref.at[1], time_ref.at[1], table_ref)
    for side in range(2):
        spec_ref[sides[side]] = mul3(*gated[side], table_ref)
    for row, lane in chunks:
        ahead, back = times(1, 0, 0, row, lane), times(1, 1, rows_all, row, lane)
        keep(0, row, lane, [(a[0] + b[0], a[1] + b[1]) for a, b in zip(ahead, back)])
    post = rows_of(2)
    tok = block // pieces
    sends = []
    for part in range(2):
        rows = slice(part * rows_all // 2, (part + 1) * rows_all // 2)
        summed = to_time(rows)
        mixed = (post[rows].astype(jnp.float32) * summed).astype(jnp.bfloat16)
        first = part * blocks // 2 * pieces
        for m in range(blocks // 2):
            for s in range(pieces):
                ready_ref[first + m * pieces + s] = mixed[m * group : (m + 1) * group, s * tok : (s + 1) * tok]
        span = pl.ds(first, blocks // 2 * pieces)
        for copy in range(out_hbm.shape[0]):
            sends.append(pltpu.make_async_copy(ready_ref.at[span], out_hbm.at[copy, span], sems.at[part, copy]))
            sends[-1].start()
    for send in sends:
        send.wait()


def project_kernel(mixed_ref, *refs):
    w_refs, (out_hbm, held_ref, ready_ref, sems) = refs[:-4], refs[-4:]
    rows = w_refs[0].shape[0]
    tile = 2 * rows
    position = lax.axis_index("ctx")
    even = pl.multiple_of(position % 2 * rows, rows)
    odd = pl.multiple_of((1 - position % 2) * rows, rows)
    sends = []
    for half, half_refs in enumerate((w_refs[:4], w_refs[4:])):
        total = mul(jnp.concatenate([w_ref[...] for w_ref in half_refs], axis=0), mixed_ref[...])
        for pair in range(2):
            place = 2 * half + pair
            held_ref[place, pl.ds(even, rows)] = total[pair * tile : pair * tile + rows]
            held_ref[place, pl.ds(odd, rows)] = total[pair * tile + rows : (pair + 1) * tile]
            ready_ref[place] = held_ref[place].T.astype(jnp.bfloat16)
            columns = pl.ds(pl.multiple_of((position // 2 ^ place) * tile, tile), tile)
            sends.append(pltpu.make_async_copy(ready_ref.at[place], out_hbm.at[:, columns], sems.at[place]))
            sends[-1].start()
    for send in sends:
        send.wait()


def whole_call(kernel, out_shape, scratch, flops, nbytes, *operands, in_hbm=0, out_hbm=()):
    results = pl.pallas_call(
        kernel,
        out_shape=out_shape,
        in_specs=[
            pl.BlockSpec(memory_space=pltpu.HBM if place < in_hbm else pltpu.VMEM) for place in range(len(operands))
        ],
        out_specs=[
            pl.BlockSpec(memory_space=pltpu.HBM if place in out_hbm else pltpu.VMEM) for place in range(len(out_shape))
        ],
        scratch_shapes=scratch,
        cost_estimate=pl.CostEstimate(flops=flops, bytes_accessed=nbytes, transcendentals=0),
        compiler_params=pltpu.CompilerParams(vmem_limit_bytes=None if in_hbm else 32 * 2**20),
    )(*operands)
    return results if len(out_shape) > 1 else results[0]


def blocked(x_gate, x_post, values, decay, residue, w_out):
    tok, width = x_gate.shape
    ctx_count = lax.axis_size("ctx")
    tp_count = lax.axis_size("tp")
    group = width // ctx_count
    poles = decay.shape[2]
    block = 2 * tok
    blocks = tok * ctx_count // block
    rows, channels = w_out.shape
    half = 2 * poles

    packed, own, mirrored = whole_call(
        pack_kernel,
        (
            jax.ShapeDtypeStruct((ctx_count, 3, group, tok), jnp.bfloat16),
            jax.ShapeDtypeStruct((2 * half, tok), jnp.float32),
            jax.ShapeDtypeStruct((2 * half, tok), jnp.float32),
        ),
        [
            pltpu.VMEM((3, tok, width), jnp.bfloat16),
            pltpu.VMEM((2, 2 * half, tok), jnp.float32),
            pltpu.VMEM((ctx_count, 3, group, tok), jnp.bfloat16),
            pltpu.SemaphoreType.DMA((7,)),
            pltpu.SemaphoreType.DMA((5,)),
        ],
        0,
        6 * tok * width * 2,
        x_gate,
        values,
        x_post,
        jnp.swapaxes(decay, 1, 2).reshape(half, width),
        jnp.swapaxes(residue, 1, 2).reshape(half, width),
        in_hbm=5,
        out_hbm=(0, 1, 2),
    )
    paired = lax.ppermute(mirrored, "tp", [(z, tp_count - 1 - z) for z in range(tp_count)])
    received = lax.all_to_all(packed, "ctx", split_axis=0, concat_axis=0, tiled=True)

    w_late, mirrored = lax.optimization_barrier((w_out, mirrored))
    w_x, w_y = partner(w_late, "ctx", 1), partner(w_late, "ctx", 2)
    own_spectra, table, back_table = whole_call(
        functools.partial(filter_kernel, poles),
        (
            jax.ShapeDtypeStruct((2, blocks, group, 2 * block), jnp.float32),
            jax.ShapeDtypeStruct((2, block, 2 * block), jnp.bfloat16),
            jax.ShapeDtypeStruct((2, 2 * block, block), jnp.bfloat16),
        ),
        [
            pltpu.VMEM((2, blocks * group, block), jnp.float32),
            pltpu.VMEM((tok, 2 * half), jnp.float32),
        ],
        2 * 2 * blocks * group * block * 2 * block * 3,
        2 * blocks * group * 2 * block * 4,
        own,
    )
    mixed = whole_call(
        functools.partial(conv_kernel, poles),
        (jax.ShapeDtypeStruct((tp_count, ctx_count, group, tok), jnp.bfloat16),),
        [
            pltpu.VMEM((2, blocks, group, 2 * block), jnp.float32),
            pltpu.VMEM((2, blocks * group, block), jnp.float32),
            pltpu.VMEM((tok, 2 * half), jnp.float32),
            pltpu.VMEM((2 * blocks * group, 2 * block), jnp.float32),
            pltpu.VMEM((2 * blocks * group, 2 * block), jnp.bfloat16),
            pltpu.VMEM((ctx_count, group, tok), jnp.bfloat16),
            pltpu.SemaphoreType.DMA((2, tp_count)),
        ],
        2 * 8 * blocks * group * block * 2 * block * 3,
        4 * blocks * group * 2 * block * 4,
        received,
        own_spectra,
        paired,
        table,
        back_table,
        out_hbm=(0,),
    )
    mixed, w_x, w_y, w_own = lax.optimization_barrier((mixed, w_x, w_y, w_out))
    lower = rows // 2
    w_far = [partner(w_x[:lower], "ctx", 2), partner(w_y[lower:], "ctx", 1)]
    w_blocks = []
    for block in (w_own, w_x, w_y):
        w_blocks += [block, partner(block, "ctx", 0)]
    w_blocks += w_far + [partner(block, "ctx", 0) for block in w_far]
    every = lax.all_to_all(
        mixed.reshape(tp_count * ctx_count, group, tok), ("tp", "ctx"), split_axis=0, concat_axis=0, tiled=True
    ).reshape(channels, tok)
    return whole_call(
        project_kernel,
        (jax.ShapeDtypeStruct((tok, rows * ctx_count), jnp.bfloat16),),
        [
            pltpu.VMEM((ctx_count // 2, 2 * rows, tok), jnp.float32),
            pltpu.VMEM((ctx_count // 2, tok, 2 * rows), jnp.bfloat16),
            pltpu.SemaphoreType.DMA((ctx_count // 2,)),
        ],
        2 * tok * rows * ctx_count * channels,
        2 * rows * ctx_count * channels,
        every,
        *w_blocks,
        out_hbm=(0,),
    )


def local(x_gate, x_post, values, decay, residue, w_out):
    tok, width = x_gate.shape
    ctx_count = lax.axis_size("ctx")
    if tok == 128 and width == 512 and ctx_count == 8 and w_out.shape[0] == 64 and lax.axis_size("tp") == 4:
        return blocked(x_gate, x_post, values, decay, residue, w_out)
    return general(x_gate, x_post, values, decay, residue, w_out)


def solution(mesh):
    in_specs = (
        P("ctx", "tp"),
        P("ctx", "tp"),
        P("ctx", "tp"),
        P(None, "tp", None),
        P(None, "tp", None),
        P(("tp", "ctx"), None),
    )
    out_specs = P("ctx", "tp")
    return jax.shard_map(local, mesh=mesh, in_specs=in_specs, out_specs=out_specs, check_vma=False)
```

```python
import functools
import math

import jax
import jax.numpy as jnp
from jax import lax
from jax.experimental import pallas as pl
from jax.experimental.pallas import tpu as pltpu
from jax.sharding import PartitionSpec as P

HIGHEST = lax.Precision.HIGHEST


def partner(value, axis, bit):
    mask = 2**bit
    pairs = [(source, source ^ mask) for source in range(lax.axis_size(axis))]
    return lax.ppermute(value, axis, pairs)


def radices(length_all):
    last_radix = min(128, length_all // 4)
    first_radix = min(32, length_all // last_radix)
    return (first_radix, length_all // (first_radix * last_radix), last_radix)


def rotation(row_count, col_count, modulus):
    product = (
        lax.broadcasted_iota(jnp.int32, (row_count, col_count), 0)
        * lax.broadcasted_iota(jnp.int32, (row_count, col_count), 1)
        % modulus
    )
    angle = product.astype(jnp.float32) * (2.0 * math.pi / modulus)
    return (jnp.cos(angle), -jnp.sin(angle))


def tables(radix_sizes):
    first_radix, mid_radix, last_radix = radix_sizes
    length_all = first_radix * mid_radix * last_radix
    outer_real, outer_imag = rotation(first_radix, first_radix, first_radix)
    mid_real, mid_imag = rotation(mid_radix, mid_radix, mid_radix)
    last_real, last_imag = rotation(last_radix, last_radix, last_radix)
    twist_real, twist_imag = rotation(first_radix, mid_radix * last_radix, length_all)
    twist_real = twist_real.reshape(first_radix, mid_radix, last_radix)
    twist_imag = twist_imag.reshape(first_radix, mid_radix, last_radix)
    inner_real, inner_imag = rotation(mid_radix, last_radix, mid_radix * last_radix)
    return (
        outer_real,
        outer_imag,
        mid_real,
        mid_imag,
        last_real,
        last_imag,
        twist_real,
        twist_imag,
        inner_real,
        inner_imag,
    )


def apply_matrix(pattern, real_part, imag_part, matrix_real, matrix_imag):
    out_real = jnp.einsum(pattern, real_part, matrix_real, precision=HIGHEST) - jnp.einsum(
        pattern, imag_part, matrix_imag, precision=HIGHEST
    )
    out_imag = jnp.einsum(pattern, real_part, matrix_imag, precision=HIGHEST) + jnp.einsum(
        pattern, imag_part, matrix_real, precision=HIGHEST
    )
    return (out_real, out_imag)


def complex_times(left_real, left_imag, right_real, right_imag):
    return (
        left_real * right_real - left_imag * right_imag,
        left_real * right_imag + left_imag * right_real,
    )


def forward(real_part, imag_part, table_set, radix_sizes):
    first_radix, mid_radix, last_radix = radix_sizes
    half_first = first_radix // 2
    batch_rows = real_part.shape[0]
    (
        outer_real,
        outer_imag,
        mid_real,
        mid_imag,
        last_real,
        last_imag,
        twist_real,
        twist_imag,
        inner_real,
        inner_imag,
    ) = table_set
    real_part = real_part.reshape(batch_rows, half_first, mid_radix, last_radix)
    imag_part = imag_part.reshape(batch_rows, half_first, mid_radix, last_radix)
    real_part, imag_part = apply_matrix(
        "banm,ak->bknm", real_part, imag_part, outer_real[:half_first], outer_imag[:half_first]
    )
    real_part, imag_part = complex_times(real_part, imag_part, twist_real, twist_imag)
    real_part, imag_part = apply_matrix("bknm,nj->bkjm", real_part, imag_part, mid_real, mid_imag)
    real_part, imag_part = complex_times(real_part, imag_part, inner_real, inner_imag)
    return apply_matrix("bkjm,mq->bkjq", real_part, imag_part, last_real, last_imag)


def inverse(real_part, imag_part, table_set, radix_sizes):
    first_radix, mid_radix, last_radix = radix_sizes
    half_first = first_radix // 2
    batch_rows = real_part.shape[0]
    (
        outer_real,
        outer_imag,
        mid_real,
        mid_imag,
        last_real,
        last_imag,
        twist_real,
        twist_imag,
        inner_real,
        inner_imag,
    ) = table_set
    real_part, imag_part = apply_matrix(
        "bkjq,mq->bkjm", real_part, imag_part, last_real / last_radix, -last_imag / last_radix
    )
    real_part, imag_part = complex_times(real_part, imag_part, inner_real, -inner_imag)
    real_part, imag_part = apply_matrix(
        "bkjm,nj->bknm", real_part, imag_part, mid_real / mid_radix, -mid_imag / mid_radix
    )
    real_part, imag_part = complex_times(real_part, imag_part, twist_real, -twist_imag)
    matrix_real = outer_real[:half_first] / first_radix
    matrix_imag = -outer_imag[:half_first] / first_radix
    out_real, out_imag = apply_matrix(
        "bknm,ak->banm", real_part, imag_part, matrix_real, matrix_imag
    )
    return (out_real.reshape(batch_rows, -1), out_imag.reshape(batch_rows, -1))


def spectrum(decay_rows, residue_rows, radix_sizes, seq_length):
    first_radix, mid_radix, last_radix = radix_sizes
    length_all = first_radix * mid_radix * last_radix
    poles = decay_rows.shape[1]
    shape_all = (first_radix, mid_radix, last_radix)
    frequency = (
        lax.broadcasted_iota(jnp.int32, shape_all, 0)
        + first_radix * lax.broadcasted_iota(jnp.int32, shape_all, 1)
        + first_radix * mid_radix * lax.broadcasted_iota(jnp.int32, shape_all, 2)
    )
    half_angle = frequency.astype(jnp.float32) * (math.pi / length_all)
    sin_half = jnp.sin(half_angle)
    sin_full = jnp.sin(2.0 * half_angle)
    parity_sign = (1 - 2 * (frequency % 2)).astype(jnp.float32)

    def add_pole(pole_index, running):
        run_real, run_imag = running
        rate_col = lax.dynamic_slice_in_dim(decay_rows, pole_index, 1, 1).reshape(-1, 1, 1, 1)
        weight = lax.dynamic_slice_in_dim(residue_rows, pole_index, 1, 1).reshape(
            -1, 1, 1, 1
        ) * jnp.sqrt(2.0 * rate_col / poles)
        retained = jnp.exp(-rate_col)
        den_real = -jnp.expm1(-rate_col) + 2.0 * retained * sin_half * sin_half
        den_imag = retained * sin_full
        pole_scale = (
            weight
            * (1.0 - jnp.exp(-rate_col * seq_length) * parity_sign)
            / (den_real * den_real + den_imag * den_imag)
        )
        return (run_real + pole_scale * den_real, run_imag - pole_scale * den_imag)

    zeros_all = jnp.zeros((decay_rows.shape[0],) + shape_all, jnp.float32)
    return lax.fori_loop(0, poles, add_pole, (zeros_all, zeros_all))


def general(x_gate, x_post, values, decay, residue, w_out):
    tok_rows, block_width = x_gate.shape
    ctx_count = lax.axis_size("ctx")
    tp_count = lax.axis_size("tp")
    chan_group = block_width // ctx_count
    seq_length = tok_rows * ctx_count
    radix_sizes = radices(2 * seq_length)
    table_set = tables(radix_sizes)
    first_row = lax.axis_index("ctx") * chan_group
    own_rate = lax.dynamic_slice_in_dim(decay, first_row, chan_group, 1)
    own_residue = lax.dynamic_slice_in_dim(residue, first_row, chan_group, 1)
    own_spec = [
        spectrum(own_rate[filter_index], own_residue[filter_index], radix_sizes, seq_length)
        for filter_index in range(2)
    ]
    forward_rows = [x_gate, values] + [x_post]
    row_count = len(forward_rows)
    base_rows = jnp.stack(forward_rows)
    copied = base_rows
    for bit_index in range(tp_count.bit_length() - 1):
        copied = partner(copied, "tp", bit_index)
    sent_rows = jnp.concatenate([base_rows, copied[:, :, ::-1]], axis=0)
    received = lax.all_to_all(
        jnp.swapaxes(sent_rows, 1, 2), "ctx", split_axis=1, concat_axis=2, tiled=True
    )
    gate_fwd = received[0].astype(jnp.float32)
    value_fwd = received[1].astype(jnp.float32)
    mirrored = received[row_count:, :, ::-1].astype(jnp.float32)
    spec_real, spec_imag = forward(value_fwd, mirrored[1], table_set, radix_sizes)
    spec_real, spec_imag = complex_times(spec_real, spec_imag, own_spec[0][0], own_spec[0][1])
    along_fwd, along_rev = inverse(spec_real, spec_imag, table_set, radix_sizes)
    spec_real, spec_imag = forward(
        gate_fwd * along_fwd, mirrored[0] * along_rev, table_set, radix_sizes
    )
    spec_real, spec_imag = complex_times(spec_real, spec_imag, own_spec[1][0], own_spec[1][1])
    sum_fwd, sum_rev = inverse(spec_real, spec_imag, table_set, radix_sizes)
    sum_fwd = received[2].astype(jnp.float32) * sum_fwd
    sum_rev = mirrored[2] * sum_rev
    results = jnp.stack([sum_fwd, sum_rev[:, ::-1]])
    returned = lax.all_to_all(
        results.astype(jnp.bfloat16), "ctx", split_axis=2, concat_axis=1, tiled=True
    ).astype(results.dtype)
    flipped = returned[1, ::-1, :]
    for bit_index in range(tp_count.bit_length() - 1):
        flipped = partner(flipped.astype(jnp.bfloat16), "tp", bit_index).astype(flipped.dtype)
    total_rows = returned[0] + flipped
    total_rows = total_rows.T
    mixed_rows = total_rows.astype(jnp.bfloat16)
    whole_rows = lax.all_gather(mixed_rows, "tp", axis=1, tiled=True)
    projected = lax.dot_general(
        whole_rows,
        lax.all_gather(w_out, "ctx", axis=0, tiled=True),
        (((1,), (1,)), ((), ())),
        preferred_element_type=jnp.float32,
    )
    return projected.astype(jnp.bfloat16)


def cycle(row_factor, col_factor, modulus):
    angle = (row_factor * col_factor % modulus).astype(jnp.float32) * (2.0 * math.pi / modulus)
    return jnp.cos(angle), jnp.sin(angle)


def put_tables(table_ref, back_ref):
    block = table_ref.shape[1]
    modulus = 4 * block
    coarse = 16
    rows = lax.broadcasted_iota(jnp.int32, (coarse, block), 0)
    cols = lax.broadcasted_iota(jnp.int32, (coarse, block), 1)

    def parts(big, small):
        for place in range(block // coarse):
            big_cos, big_sin = (part[place : place + 1] for part in big)
            span = slice(place * coarse, (place + 1) * coarse)
            below = slice(block + place * coarse, block + (place + 1) * coarse)
            cos = halves(big_cos * small[0] - big_sin * small[1])
            sin = halves(-(big_sin * small[0] + big_cos * small[1]))
            yield span, below, cos, sin

    frequency = 2 * cols + 1
    for span, _, cos, sin in parts(cycle(coarse * rows, frequency, modulus), cycle(rows, frequency, modulus)):
        table_ref[0, span, :block], table_ref[1, span, :block] = cos
        table_ref[0, span, block:], table_ref[1, span, block:] = sin
    for span, below, cos, sin in parts(cycle(2 * coarse * rows, cols, modulus), cycle(2 * rows + 1, cols, modulus)):
        back_ref[0, span], back_ref[1, span] = cos
        back_ref[0, below], back_ref[1, below] = sin


def halves(value):
    high = value.astype(jnp.bfloat16)
    return high, (value - high.astype(jnp.float32)).astype(jnp.bfloat16)


def mul(left, right):
    return jnp.dot(left, right, preferred_element_type=jnp.float32)


def mul3(high, low, table_ref):
    return mul(high, table_ref[0]) + (mul(low, table_ref[0]) + mul(high, table_ref[1]))


def pack_kernel(
    gate_hbm, value_hbm, post_hbm, decay_hbm, residue_hbm,
    out_hbm, own_hbm, sent_hbm, held_ref, cut_ref, ready_ref, sems, out_sems,
):
    ctx_count, _, group, tok = out_hbm.shape
    width = gate_hbm.shape[1]
    half = decay_hbm.shape[0]
    position = lax.axis_index("ctx")
    pairs = []
    for place, index in enumerate((position, ctx_count - 1 - position)):
        columns = pl.ds(pl.multiple_of(index * group // tok * tok, tok), tok)
        pairs += [(decay_hbm.at[:, columns], cut_ref.at[place, :half]), (residue_hbm.at[:, columns], cut_ref.at[place, half:])]
    pairs += [(source, held_ref.at[place]) for place, source in enumerate((value_hbm, gate_hbm, post_hbm))]
    copies = [pltpu.make_async_copy(*pair, sems.at[place]) for place, pair in enumerate(pairs)]
    for copy in copies:
        copy.start()
    sends = []
    for place, target in enumerate((own_hbm, sent_hbm)):
        copies[2 * place].wait()
        copies[2 * place + 1].wait()
        sends.append(pltpu.make_async_copy(cut_ref.at[place], target, out_sems.at[3 + place]))
        sends[-1].start()
    for place, copy in enumerate(copies[4:]):
        copy.wait()
        for first in range(0, width, tok):
            turned = held_ref[place, :, first : first + tok].T
            for part in range(tok // group):
                ready_ref[first // group + part, place] = turned[part * group : (part + 1) * group]
        sends.append(pltpu.make_async_copy(ready_ref.at[:, place], out_hbm.at[:, place], out_sems.at[place]))
        sends[-1].start()
    for send in sends:
        send.wait()


def mirror_rows(value):
    row = lax.broadcasted_iota(jnp.int32, (8, value.shape[1]), 0)
    result = []
    for first in range(value.shape[0] - 8, -1, -8):
        part = value[first : first + 8]
        for shift in (1, 2, 4):
            part = jnp.where(row & shift == 0, pltpu.roll(part, 8 - shift, 0), pltpu.roll(part, shift, 0))
        result.append(part)
    return jnp.concatenate(result, axis=0)


def put_spectra(poles, index, turned, out_ref, time_ref, table_ref):
    blocks, group, twice = out_ref.shape
    block = twice // 2
    lanes = 128
    ramp = lax.broadcasted_iota(jnp.int32, (8, lanes), 1).astype(jnp.float32)
    sign = (1 - 2 * (lax.broadcasted_iota(jnp.int32, (group, block), 1) % 2)).astype(jnp.float32)
    for row in range(0, group, 8):
        rows = slice(row, row + 8)
        rate = turned[rows, index * poles : (index + 1) * poles]
        scale = turned[rows, (2 + index) * poles : (3 + index) * poles] * (jnp.sqrt(rate * (2.0 / poles)) / block)
        slope = rate * -math.log2(math.e)
        jump = jnp.exp2(slope * lanes)
        sums = [None] * (blocks * block // lanes)
        for pole in range(poles):
            term = scale[:, pole : pole + 1] * jnp.exp2(slope[:, pole : pole + 1] * ramp)
            step = jnp.broadcast_to(jump[:, pole : pole + 1], (8, lanes))
            for place in range(len(sums)):
                sums[place] = term if pole == 0 else sums[place] + term
                if place + 1 < len(sums):
                    term = term * step
        for place, total in enumerate(sums):
            lag, lane = divmod(place * lanes, block)
            time_ref[lag * group + row : lag * group + row + 8, lane : lane + lanes] = total
    spec = mul3(*halves(time_ref[...]), table_ref)
    for lag in range(blocks):
        real = spec[lag * group : (lag + 1) * group, :block]
        imag = spec[lag * group : (lag + 1) * group, block:]
        if lag > 0:
            real = real - sign * spec[(lag - 1) * group : lag * group, block:]
            imag = imag + sign * spec[(lag - 1) * group : lag * group, :block]
        out_ref[lag, :, :block] = real
        out_ref[lag, :, block:] = imag


def filter_kernel(poles, par_ref, out_ref, table_ref, back_ref, time_ref, turned_ref):
    group = out_ref.shape[2]
    put_tables(table_ref, back_ref)
    turned_ref[...] = par_ref[...].T
    turned = turned_ref[pl.ds(pl.multiple_of(lax.axis_index("ctx") * group % turned_ref.shape[0], group), group)]
    for index in range(2):
        put_spectra(poles, index, turned, out_ref.at[index], time_ref.at[index], table_ref)


def conv_kernel(
    poles, x_ref, own_ref, par_ref, table_ref, back_ref, out_hbm,
    paired_ref, time_ref, turned_ref, spec_ref, high_ref, ready_ref, sems,
):
    turned_ref[...] = par_ref[...].T
    blocks, group, twice = own_ref.shape[1:]
    block = twice // 2
    rows_all = blocks * group
    tall, wide = 16, 128
    pieces = x_ref.shape[0] // blocks
    first = (x_ref.shape[0] - 1 - lax.axis_index("ctx")) * group % turned_ref.shape[0]
    turned = mirror_rows(turned_ref[pl.ds(pl.multiple_of(first, group), group)])

    def rows_of(position):
        return jnp.concatenate(
            [
                jnp.concatenate([x_ref[m * pieces + s, position] for s in range(pieces)], axis=1)
                for m in range(blocks)
            ],
            axis=0,
        )

    def times(index, side, source, row, lane):
        data = []
        for m in range(blocks):
            rows = slice(source + m * group + row, source + m * group + row + tall)
            data.append((spec_ref[rows, lane : lane + wide], spec_ref[rows, block + lane : block + lane + wide]))
        sums = [None] * blocks
        for lag in range(blocks):
            h_ref = (own_ref, paired_ref)[side]
            f_re = h_ref[index, lag, row : row + tall, lane : lane + wide]
            f_im = h_ref[index, lag, row : row + tall, block + lane : block + lane + wide]
            for m in range(blocks - lag):
                target, (d_re, d_im) = (m + lag, data[m]) if side == 0 else (m, data[m + lag])
                if side == 0:
                    real, imag = f_re * d_re - f_im * d_im, f_re * d_im + f_im * d_re
                else:
                    real, imag = f_re * d_re + f_im * d_im, f_re * d_im - f_im * d_re
                if sums[target] is not None:
                    real, imag = sums[target][0] + real, sums[target][1] + imag
                sums[target] = (real, imag)
        return sums

    def to_time(rows):
        return mul(high_ref[rows], back_ref[0]) + mul(high_ref[rows], back_ref[1])

    def keep(target, row, lane, sums):
        for m in range(blocks):
            rows = slice(target + m * group + row, target + m * group + row + tall)
            for part in range(2):
                cols = slice(part * block + lane, part * block + lane + wide)
                high_ref[rows, cols] = sums[m][part].astype(jnp.bfloat16)

    chunks = [(row, lane) for row in range(0, group, tall) for lane in range(0, block, wide)]

    value = rows_of(0)
    gate = rows_of(1).astype(jnp.float32)
    spec_ref[:rows_all] = mul(value, table_ref[0]) + mul(value, table_ref[1])
    sides = [slice(side * rows_all, (side + 1) * rows_all) for side in range(2)]
    gated = []
    put_spectra(poles, 0, turned, paired_ref.at[0], time_ref.at[0], table_ref)
    for side in range(2):
        for row, lane in chunks:
            keep(side * rows_all, row, lane, times(0, side, 0, row, lane))
        gated.append(halves(gate * to_time(sides[side])))
    put_spectra(poles, 1, turned, paired_ref.at[1], time_ref.at[1], table_ref)
    for side in range(2):
        spec_ref[sides[side]] = mul3(*gated[side], table_ref)
    for row, lane in chunks:
        ahead, back = times(1, 0, 0, row, lane), times(1, 1, rows_all, row, lane)
        keep(0, row, lane, [(a[0] + b[0], a[1] + b[1]) for a, b in zip(ahead, back)])
    post = rows_of(2)
    tok = block // pieces
    sends = []
    for part in range(2):
        rows = slice(part * rows_all // 2, (part + 1) * rows_all // 2)
        summed = to_time(rows)
        mixed = (post[rows].astype(jnp.float32) * summed).astype(jnp.bfloat16)
        first = part * blocks // 2 * pieces
        for m in range(blocks // 2):
            for s in range(pieces):
                ready_ref[first + m * pieces + s] = mixed[m * group : (m + 1) * group, s * tok : (s + 1) * tok]
        span = pl.ds(first, blocks // 2 * pieces)
        for copy in range(out_hbm.shape[1]):
            sends.append(pltpu.make_async_copy(ready_ref.at[span], out_hbm.at[span, copy], sems.at[part, copy]))
            sends[-1].start()
    for send in sends:
        send.wait()


def project_kernel(mixed_ref, *refs):
    w_refs, (out_hbm, held_ref, ready_ref, sems) = refs[:-4], refs[-4:]
    rows = w_refs[0].shape[0]
    tile = 2 * rows
    position = lax.axis_index("ctx")
    even = pl.multiple_of(position % 2 * rows, rows)
    odd = pl.multiple_of((1 - position % 2) * rows, rows)
    ctx_count, tp_count = mixed_ref.shape[:2]
    mixed = jnp.concatenate([mixed_ref[i, z] for z in range(tp_count) for i in range(ctx_count)], axis=0)
    sends = []
    for half, half_refs in enumerate((w_refs[:4], w_refs[4:])):
        total = mul(jnp.concatenate([w_ref[...] for w_ref in half_refs], axis=0), mixed)
        for pair in range(2):
            place = 2 * half + pair
            held_ref[place, pl.ds(even, rows)] = total[pair * tile : pair * tile + rows]
            held_ref[place, pl.ds(odd, rows)] = total[pair * tile + rows : (pair + 1) * tile]
            ready_ref[place] = held_ref[place].T.astype(jnp.bfloat16)
            columns = pl.ds(pl.multiple_of((position // 2 ^ place) * tile, tile), tile)
            sends.append(pltpu.make_async_copy(ready_ref.at[place], out_hbm.at[:, columns], sems.at[place]))
            sends[-1].start()
    for send in sends:
        send.wait()


def whole_call(kernel, out_shape, scratch, flops, nbytes, *operands, in_hbm=0, out_hbm=()):
    results = pl.pallas_call(
        kernel,
        out_shape=out_shape,
        in_specs=[
            pl.BlockSpec(memory_space=pltpu.HBM if place < in_hbm else pltpu.VMEM) for place in range(len(operands))
        ],
        out_specs=[
            pl.BlockSpec(memory_space=pltpu.HBM if place in out_hbm else pltpu.VMEM) for place in range(len(out_shape))
        ],
        scratch_shapes=scratch,
        cost_estimate=pl.CostEstimate(flops=flops, bytes_accessed=nbytes, transcendentals=0),
        compiler_params=pltpu.CompilerParams(vmem_limit_bytes=None if in_hbm else 32 * 2**20),
    )(*operands)
    return results if len(out_shape) > 1 else results[0]


def blocked(x_gate, x_post, values, decay, residue, w_out):
    tok, width = x_gate.shape
    ctx_count = lax.axis_size("ctx")
    tp_count = lax.axis_size("tp")
    group = width // ctx_count
    poles = decay.shape[2]
    block = 2 * tok
    blocks = tok * ctx_count // block
    rows, channels = w_out.shape
    half = 2 * poles

    packed, own, mirrored = whole_call(
        pack_kernel,
        (
            jax.ShapeDtypeStruct((ctx_count, 3, group, tok), jnp.bfloat16),
            jax.ShapeDtypeStruct((2 * half, tok), jnp.float32),
            jax.ShapeDtypeStruct((2 * half, tok), jnp.float32),
        ),
        [
            pltpu.VMEM((3, tok, width), jnp.bfloat16),
            pltpu.VMEM((2, 2 * half, tok), jnp.float32),
            pltpu.VMEM((ctx_count, 3, group, tok), jnp.bfloat16),
            pltpu.SemaphoreType.DMA((7,)),
            pltpu.SemaphoreType.DMA((5,)),
        ],
        0,
        6 * tok * width * 2,
        x_gate,
        values,
        x_post,
        jnp.swapaxes(decay, 1, 2).reshape(half, width),
        jnp.swapaxes(residue, 1, 2).reshape(half, width),
        in_hbm=5,
        out_hbm=(0, 1, 2),
    )
    paired = lax.ppermute(mirrored, "tp", [(z, tp_count - 1 - z) for z in range(tp_count)])
    received = lax.all_to_all(packed, "ctx", split_axis=0, concat_axis=0, tiled=True)

    w_late, mirrored = lax.optimization_barrier((w_out, mirrored))
    w_x, w_y = partner(w_late, "ctx", 1), partner(w_late, "ctx", 2)
    own_spectra, table, back_table = whole_call(
        functools.partial(filter_kernel, poles),
        (
            jax.ShapeDtypeStruct((2, blocks, group, 2 * block), jnp.float32),
            jax.ShapeDtypeStruct((2, block, 2 * block), jnp.bfloat16),
            jax.ShapeDtypeStruct((2, 2 * block, block), jnp.bfloat16),
        ),
        [
            pltpu.VMEM((2, blocks * group, block), jnp.float32),
            pltpu.VMEM((tok, 2 * half), jnp.float32),
        ],
        2 * 2 * blocks * group * block * 2 * block * 3,
        2 * blocks * group * 2 * block * 4,
        own,
    )
    mixed = whole_call(
        functools.partial(conv_kernel, poles),
        (jax.ShapeDtypeStruct((ctx_count, tp_count, group, tok), jnp.bfloat16),),
        [
            pltpu.VMEM((2, blocks, group, 2 * block), jnp.float32),
            pltpu.VMEM((2, blocks * group, block), jnp.float32),
            pltpu.VMEM((tok, 2 * half), jnp.float32),
            pltpu.VMEM((2 * blocks * group, 2 * block), jnp.float32),
            pltpu.VMEM((2 * blocks * group, 2 * block), jnp.bfloat16),
            pltpu.VMEM((ctx_count, group, tok), jnp.bfloat16),
            pltpu.SemaphoreType.DMA((2, tp_count)),
        ],
        2 * 8 * blocks * group * block * 2 * block * 3,
        4 * blocks * group * 2 * block * 4,
        received,
        own_spectra,
        paired,
        table,
        back_table,
        out_hbm=(0,),
    )
    mixed, w_x, w_y, w_own = lax.optimization_barrier((mixed, w_x, w_y, w_out))
    lower = rows // 2
    w_far = [partner(w_x[:lower], "ctx", 2), partner(w_y[lower:], "ctx", 1)]
    w_blocks = []
    for block in (w_own, w_x, w_y):
        w_blocks += [block, partner(block, "ctx", 0)]
    w_blocks += w_far + [partner(block, "ctx", 0) for block in w_far]
    every = lax.all_to_all(
        mixed.reshape(ctx_count * tp_count, group, tok), ("ctx", "tp"), split_axis=0, concat_axis=0, tiled=True
    ).reshape(ctx_count, tp_count, group, tok)
    return whole_call(
        project_kernel,
        (jax.ShapeDtypeStruct((tok, rows * ctx_count), jnp.bfloat16),),
        [
            pltpu.VMEM((ctx_count // 2, 2 * rows, tok), jnp.float32),
            pltpu.VMEM((ctx_count // 2, tok, 2 * rows), jnp.bfloat16),
            pltpu.SemaphoreType.DMA((ctx_count // 2,)),
        ],
        2 * tok * rows * ctx_count * channels,
        2 * rows * ctx_count * channels,
        every,
        *w_blocks,
        out_hbm=(0,),
    )


def local(x_gate, x_post, values, decay, residue, w_out):
    tok, width = x_gate.shape
    ctx_count = lax.axis_size("ctx")
    if tok == 128 and width == 512 and ctx_count == 8 and w_out.shape[0] == 64 and lax.axis_size("tp") == 4:
        return blocked(x_gate, x_post, values, decay, residue, w_out)
    return general(x_gate, x_post, values, decay, residue, w_out)


def solution(mesh):
    in_specs = (
        P("ctx", "tp"),
        P("ctx", "tp"),
        P("ctx", "tp"),
        P(None, "tp", None),
        P(None, "tp", None),
        P(("tp", "ctx"), None),
    )
    out_specs = P("ctx", "tp")
    return jax.shard_map(local, mesh=mesh, in_specs=in_specs, out_specs=out_specs, check_vma=False)
```

```python
import functools
import math

import jax
import jax.numpy as jnp
from jax import lax
from jax.experimental import pallas as pl
from jax.experimental.pallas import tpu as pltpu
from jax.sharding import PartitionSpec as P

HIGHEST = lax.Precision.HIGHEST


def partner(value, axis, bit):
    mask = 2**bit
    pairs = [(source, source ^ mask) for source in range(lax.axis_size(axis))]
    return lax.ppermute(value, axis, pairs)


def radices(length_all):
    last_radix = min(128, length_all // 4)
    first_radix = min(32, length_all // last_radix)
    return (first_radix, length_all // (first_radix * last_radix), last_radix)


def rotation(row_count, col_count, modulus):
    product = (
        lax.broadcasted_iota(jnp.int32, (row_count, col_count), 0)
        * lax.broadcasted_iota(jnp.int32, (row_count, col_count), 1)
        % modulus
    )
    angle = product.astype(jnp.float32) * (2.0 * math.pi / modulus)
    return (jnp.cos(angle), -jnp.sin(angle))


def tables(radix_sizes):
    first_radix, mid_radix, last_radix = radix_sizes
    length_all = first_radix * mid_radix * last_radix
    outer_real, outer_imag = rotation(first_radix, first_radix, first_radix)
    mid_real, mid_imag = rotation(mid_radix, mid_radix, mid_radix)
    last_real, last_imag = rotation(last_radix, last_radix, last_radix)
    twist_real, twist_imag = rotation(first_radix, mid_radix * last_radix, length_all)
    twist_real = twist_real.reshape(first_radix, mid_radix, last_radix)
    twist_imag = twist_imag.reshape(first_radix, mid_radix, last_radix)
    inner_real, inner_imag = rotation(mid_radix, last_radix, mid_radix * last_radix)
    return (
        outer_real,
        outer_imag,
        mid_real,
        mid_imag,
        last_real,
        last_imag,
        twist_real,
        twist_imag,
        inner_real,
        inner_imag,
    )


def apply_matrix(pattern, real_part, imag_part, matrix_real, matrix_imag):
    out_real = jnp.einsum(pattern, real_part, matrix_real, precision=HIGHEST) - jnp.einsum(
        pattern, imag_part, matrix_imag, precision=HIGHEST
    )
    out_imag = jnp.einsum(pattern, real_part, matrix_imag, precision=HIGHEST) + jnp.einsum(
        pattern, imag_part, matrix_real, precision=HIGHEST
    )
    return (out_real, out_imag)


def complex_times(left_real, left_imag, right_real, right_imag):
    return (
        left_real * right_real - left_imag * right_imag,
        left_real * right_imag + left_imag * right_real,
    )


def forward(real_part, imag_part, table_set, radix_sizes):
    first_radix, mid_radix, last_radix = radix_sizes
    half_first = first_radix // 2
    batch_rows = real_part.shape[0]
    (
        outer_real,
        outer_imag,
        mid_real,
        mid_imag,
        last_real,
        last_imag,
        twist_real,
        twist_imag,
        inner_real,
        inner_imag,
    ) = table_set
    real_part = real_part.reshape(batch_rows, half_first, mid_radix, last_radix)
    imag_part = imag_part.reshape(batch_rows, half_first, mid_radix, last_radix)
    real_part, imag_part = apply_matrix(
        "banm,ak->bknm", real_part, imag_part, outer_real[:half_first], outer_imag[:half_first]
    )
    real_part, imag_part = complex_times(real_part, imag_part, twist_real, twist_imag)
    real_part, imag_part = apply_matrix("bknm,nj->bkjm", real_part, imag_part, mid_real, mid_imag)
    real_part, imag_part = complex_times(real_part, imag_part, inner_real, inner_imag)
    return apply_matrix("bkjm,mq->bkjq", real_part, imag_part, last_real, last_imag)


def inverse(real_part, imag_part, table_set, radix_sizes):
    first_radix, mid_radix, last_radix = radix_sizes
    half_first = first_radix // 2
    batch_rows = real_part.shape[0]
    (
        outer_real,
        outer_imag,
        mid_real,
        mid_imag,
        last_real,
        last_imag,
        twist_real,
        twist_imag,
        inner_real,
        inner_imag,
    ) = table_set
    real_part, imag_part = apply_matrix(
        "bkjq,mq->bkjm", real_part, imag_part, last_real / last_radix, -last_imag / last_radix
    )
    real_part, imag_part = complex_times(real_part, imag_part, inner_real, -inner_imag)
    real_part, imag_part = apply_matrix(
        "bkjm,nj->bknm", real_part, imag_part, mid_real / mid_radix, -mid_imag / mid_radix
    )
    real_part, imag_part = complex_times(real_part, imag_part, twist_real, -twist_imag)
    matrix_real = outer_real[:half_first] / first_radix
    matrix_imag = -outer_imag[:half_first] / first_radix
    out_real, out_imag = apply_matrix(
        "bknm,ak->banm", real_part, imag_part, matrix_real, matrix_imag
    )
    return (out_real.reshape(batch_rows, -1), out_imag.reshape(batch_rows, -1))


def spectrum(decay_rows, residue_rows, radix_sizes, seq_length):
    first_radix, mid_radix, last_radix = radix_sizes
    length_all = first_radix * mid_radix * last_radix
    poles = decay_rows.shape[1]
    shape_all = (first_radix, mid_radix, last_radix)
    frequency = (
        lax.broadcasted_iota(jnp.int32, shape_all, 0)
        + first_radix * lax.broadcasted_iota(jnp.int32, shape_all, 1)
        + first_radix * mid_radix * lax.broadcasted_iota(jnp.int32, shape_all, 2)
    )
    half_angle = frequency.astype(jnp.float32) * (math.pi / length_all)
    sin_half = jnp.sin(half_angle)
    sin_full = jnp.sin(2.0 * half_angle)
    parity_sign = (1 - 2 * (frequency % 2)).astype(jnp.float32)

    def add_pole(pole_index, running):
        run_real, run_imag = running
        rate_col = lax.dynamic_slice_in_dim(decay_rows, pole_index, 1, 1).reshape(-1, 1, 1, 1)
        weight = lax.dynamic_slice_in_dim(residue_rows, pole_index, 1, 1).reshape(
            -1, 1, 1, 1
        ) * jnp.sqrt(2.0 * rate_col / poles)
        retained = jnp.exp(-rate_col)
        den_real = -jnp.expm1(-rate_col) + 2.0 * retained * sin_half * sin_half
        den_imag = retained * sin_full
        pole_scale = (
            weight
            * (1.0 - jnp.exp(-rate_col * seq_length) * parity_sign)
            / (den_real * den_real + den_imag * den_imag)
        )
        return (run_real + pole_scale * den_real, run_imag - pole_scale * den_imag)

    zeros_all = jnp.zeros((decay_rows.shape[0],) + shape_all, jnp.float32)
    return lax.fori_loop(0, poles, add_pole, (zeros_all, zeros_all))


def general(x_gate, x_post, values, decay, residue, w_out):
    tok_rows, block_width = x_gate.shape
    ctx_count = lax.axis_size("ctx")
    tp_count = lax.axis_size("tp")
    chan_group = block_width // ctx_count
    seq_length = tok_rows * ctx_count
    radix_sizes = radices(2 * seq_length)
    table_set = tables(radix_sizes)
    first_row = lax.axis_index("ctx") * chan_group
    own_rate = lax.dynamic_slice_in_dim(decay, first_row, chan_group, 1)
    own_residue = lax.dynamic_slice_in_dim(residue, first_row, chan_group, 1)
    own_spec = [
        spectrum(own_rate[filter_index], own_residue[filter_index], radix_sizes, seq_length)
        for filter_index in range(2)
    ]
    forward_rows = [x_gate, values] + [x_post]
    row_count = len(forward_rows)
    base_rows = jnp.stack(forward_rows)
    copied = base_rows
    for bit_index in range(tp_count.bit_length() - 1):
        copied = partner(copied, "tp", bit_index)
    sent_rows = jnp.concatenate([base_rows, copied[:, :, ::-1]], axis=0)
    received = lax.all_to_all(
        jnp.swapaxes(sent_rows, 1, 2), "ctx", split_axis=1, concat_axis=2, tiled=True
    )
    gate_fwd = received[0].astype(jnp.float32)
    value_fwd = received[1].astype(jnp.float32)
    mirrored = received[row_count:, :, ::-1].astype(jnp.float32)
    spec_real, spec_imag = forward(value_fwd, mirrored[1], table_set, radix_sizes)
    spec_real, spec_imag = complex_times(spec_real, spec_imag, own_spec[0][0], own_spec[0][1])
    along_fwd, along_rev = inverse(spec_real, spec_imag, table_set, radix_sizes)
    spec_real, spec_imag = forward(
        gate_fwd * along_fwd, mirrored[0] * along_rev, table_set, radix_sizes
    )
    spec_real, spec_imag = complex_times(spec_real, spec_imag, own_spec[1][0], own_spec[1][1])
    sum_fwd, sum_rev = inverse(spec_real, spec_imag, table_set, radix_sizes)
    sum_fwd = received[2].astype(jnp.float32) * sum_fwd
    sum_rev = mirrored[2] * sum_rev
    results = jnp.stack([sum_fwd, sum_rev[:, ::-1]])
    returned = lax.all_to_all(
        results.astype(jnp.bfloat16), "ctx", split_axis=2, concat_axis=1, tiled=True
    ).astype(results.dtype)
    flipped = returned[1, ::-1, :]
    for bit_index in range(tp_count.bit_length() - 1):
        flipped = partner(flipped.astype(jnp.bfloat16), "tp", bit_index).astype(flipped.dtype)
    total_rows = returned[0] + flipped
    total_rows = total_rows.T
    mixed_rows = total_rows.astype(jnp.bfloat16)
    whole_rows = lax.all_gather(mixed_rows, "tp", axis=1, tiled=True)
    projected = lax.dot_general(
        whole_rows,
        lax.all_gather(w_out, "ctx", axis=0, tiled=True),
        (((1,), (1,)), ((), ())),
        preferred_element_type=jnp.float32,
    )
    return projected.astype(jnp.bfloat16)


def cycle(row_factor, col_factor, modulus):
    angle = (row_factor * col_factor % modulus).astype(jnp.float32) * (2.0 * math.pi / modulus)
    return jnp.cos(angle), jnp.sin(angle)


def put_tables(table_ref, back_ref):
    block = table_ref.shape[1]
    modulus = 4 * block
    coarse = 16
    rows = lax.broadcasted_iota(jnp.int32, (coarse, block), 0)
    cols = lax.broadcasted_iota(jnp.int32, (coarse, block), 1)

    def parts(big, small):
        for place in range(block // coarse):
            big_cos, big_sin = (part[place : place + 1] for part in big)
            span = slice(place * coarse, (place + 1) * coarse)
            below = slice(block + place * coarse, block + (place + 1) * coarse)
            cos = halves(big_cos * small[0] - big_sin * small[1])
            sin = halves(-(big_sin * small[0] + big_cos * small[1]))
            yield span, below, cos, sin

    frequency = 2 * cols + 1
    for span, _, cos, sin in parts(cycle(coarse * rows, frequency, modulus), cycle(rows, frequency, modulus)):
        table_ref[0, span, :block], table_ref[1, span, :block] = cos
        table_ref[0, span, block:], table_ref[1, span, block:] = sin
    for span, below, cos, sin in parts(cycle(2 * coarse * rows, cols, modulus), cycle(2 * rows + 1, cols, modulus)):
        back_ref[0, span], back_ref[1, span] = cos
        back_ref[0, below], back_ref[1, below] = sin


def halves(value):
    high = value.astype(jnp.bfloat16)
    return high, (value - high.astype(jnp.float32)).astype(jnp.bfloat16)


def mul(left, right):
    return jnp.dot(left, right, preferred_element_type=jnp.float32)


def mul3(high, low, table_ref):
    return mul(high, table_ref[0]) + (mul(low, table_ref[0]) + mul(high, table_ref[1]))


def pack_kernel(
    gate_hbm, value_hbm, post_hbm, decay_hbm, residue_hbm,
    out_hbm, own_hbm, sent_hbm, held_ref, cut_ref, ready_ref, sems, out_sems,
):
    ctx_count, _, group, tok = out_hbm.shape
    width = gate_hbm.shape[1]
    half = decay_hbm.shape[0]
    position = lax.axis_index("ctx")
    pairs = []
    for place, index in enumerate((position, ctx_count - 1 - position)):
        columns = pl.ds(pl.multiple_of(index * group // tok * tok, tok), tok)
        pairs += [(decay_hbm.at[:, columns], cut_ref.at[place, :half]), (residue_hbm.at[:, columns], cut_ref.at[place, half:])]
    pairs += [(source, held_ref.at[place]) for place, source in enumerate((value_hbm, gate_hbm, post_hbm))]
    copies = [pltpu.make_async_copy(*pair, sems.at[place]) for place, pair in enumerate(pairs)]
    for copy in copies:
        copy.start()
    sends = []
    for place, target in enumerate((own_hbm, sent_hbm)):
        copies[2 * place].wait()
        copies[2 * place + 1].wait()
        sends.append(pltpu.make_async_copy(cut_ref.at[place], target, out_sems.at[3 + place]))
        sends[-1].start()
    for place, copy in enumerate(copies[4:]):
        copy.wait()
        for first in range(0, width, tok):
            turned = held_ref[place, :, first : first + tok].T
            for part in range(tok // group):
                ready_ref[first // group + part, place] = turned[part * group : (part + 1) * group]
        sends.append(pltpu.make_async_copy(ready_ref.at[:, place], out_hbm.at[:, place], out_sems.at[place]))
        sends[-1].start()
    for send in sends:
        send.wait()


def mirror_rows(value):
    row = lax.broadcasted_iota(jnp.int32, (8, value.shape[1]), 0)
    result = []
    for first in range(value.shape[0] - 8, -1, -8):
        part = value[first : first + 8]
        for shift in (1, 2, 4):
            part = jnp.where(row & shift == 0, pltpu.roll(part, 8 - shift, 0), pltpu.roll(part, shift, 0))
        result.append(part)
    return jnp.concatenate(result, axis=0)


def put_spectra(poles, index, turned, out_ref, time_ref, table_ref):
    blocks, group, twice = out_ref.shape
    block = twice // 2
    lanes = 128
    ramp = lax.broadcasted_iota(jnp.int32, (8, lanes), 1).astype(jnp.float32)
    sign = (1 - 2 * (lax.broadcasted_iota(jnp.int32, (group, block), 1) % 2)).astype(jnp.float32)
    for row in range(0, group, 8):
        rows = slice(row, row + 8)
        rate = turned[rows, index * poles : (index + 1) * poles]
        scale = turned[rows, (2 + index) * poles : (3 + index) * poles] * (jnp.sqrt(rate * (2.0 / poles)) / block)
        slope = rate * -math.log2(math.e)
        jump = jnp.exp2(slope * lanes)
        sums = [None] * (blocks * block // lanes)
        for pole in range(poles):
            term = scale[:, pole : pole + 1] * jnp.exp2(slope[:, pole : pole + 1] * ramp)
            step = jnp.broadcast_to(jump[:, pole : pole + 1], (8, lanes))
            for place in range(len(sums)):
                sums[place] = term if pole == 0 else sums[place] + term
                if place + 1 < len(sums):
                    term = term * step
        for place, total in enumerate(sums):
            lag, lane = divmod(place * lanes, block)
            time_ref[lag * group + row : lag * group + row + 8, lane : lane + lanes] = total
    spec = mul3(*halves(time_ref[...]), table_ref)
    for lag in range(blocks):
        real = spec[lag * group : (lag + 1) * group, :block]
        imag = spec[lag * group : (lag + 1) * group, block:]
        if lag > 0:
            real = real - sign * spec[(lag - 1) * group : lag * group, block:]
            imag = imag + sign * spec[(lag - 1) * group : lag * group, :block]
        out_ref[lag, :, :block] = real
        out_ref[lag, :, block:] = imag


def filter_kernel(poles, par_ref, out_ref, table_ref, back_ref, time_ref, turned_ref):
    group = out_ref.shape[2]
    put_tables(table_ref, back_ref)
    turned_ref[...] = par_ref[...].T
    turned = turned_ref[pl.ds(pl.multiple_of(lax.axis_index("ctx") * group % turned_ref.shape[0], group), group)]
    for index in range(2):
        put_spectra(poles, index, turned, out_ref.at[index], time_ref.at[index], table_ref)


def conv_kernel(
    poles, x_ref, own_ref, par_ref, table_ref, back_ref, out_hbm,
    paired_ref, time_ref, turned_ref, spec_ref, high_ref, ready_ref, sems,
):
    turned_ref[...] = par_ref[...].T
    blocks, group, twice = own_ref.shape[1:]
    block = twice // 2
    rows_all = blocks * group
    tall, wide = 16, 128
    pieces = x_ref.shape[0] // blocks
    first = (x_ref.shape[0] - 1 - lax.axis_index("ctx")) * group % turned_ref.shape[0]
    turned = mirror_rows(turned_ref[pl.ds(pl.multiple_of(first, group), group)])

    def rows_of(position):
        return jnp.concatenate(
            [
                jnp.concatenate([x_ref[m * pieces + s, position] for s in range(pieces)], axis=1)
                for m in range(blocks)
            ],
            axis=0,
        )

    def times(index, side, source, row, lane):
        data = []
        for m in range(blocks):
            rows = slice(source + m * group + row, source + m * group + row + tall)
            data.append((spec_ref[rows, lane : lane + wide], spec_ref[rows, block + lane : block + lane + wide]))
        sums = [None] * blocks
        for lag in range(blocks):
            h_ref = (own_ref, paired_ref)[side]
            f_re = h_ref[index, lag, row : row + tall, lane : lane + wide]
            f_im = h_ref[index, lag, row : row + tall, block + lane : block + lane + wide]
            for m in range(blocks - lag):
                target, (d_re, d_im) = (m + lag, data[m]) if side == 0 else (m, data[m + lag])
                if side == 0:
                    real, imag = f_re * d_re - f_im * d_im, f_re * d_im + f_im * d_re
                else:
                    real, imag = f_re * d_re + f_im * d_im, f_re * d_im - f_im * d_re
                if sums[target] is not None:
                    real, imag = sums[target][0] + real, sums[target][1] + imag
                sums[target] = (real, imag)
        return sums

    def to_time(rows):
        return mul(high_ref[rows], back_ref[0]) + mul(high_ref[rows], back_ref[1])

    def keep(target, row, lane, sums):
        for m in range(blocks):
            rows = slice(target + m * group + row, target + m * group + row + tall)
            for part in range(2):
                cols = slice(part * block + lane, part * block + lane + wide)
                high_ref[rows, cols] = sums[m][part].astype(jnp.bfloat16)

    chunks = [(row, lane) for row in range(0, group, tall) for lane in range(0, block, wide)]

    value = rows_of(0)
    gate = rows_of(1).astype(jnp.float32)
    spec_ref[:rows_all] = mul(value, table_ref[0]) + mul(value, table_ref[1])
    sides = [slice(side * rows_all, (side + 1) * rows_all) for side in range(2)]
    gated = []
    put_spectra(poles, 0, turned, paired_ref.at[0], time_ref.at[0], table_ref)
    for side in range(2):
        for row, lane in chunks:
            keep(side * rows_all, row, lane, times(0, side, 0, row, lane))
        gated.append(halves(gate * to_time(sides[side])))
    put_spectra(poles, 1, turned, paired_ref.at[1], time_ref.at[1], table_ref)
    for side in range(2):
        spec_ref[sides[side]] = mul3(*gated[side], table_ref)
    for row, lane in chunks:
        ahead, back = times(1, 0, 0, row, lane), times(1, 1, rows_all, row, lane)
        keep(0, row, lane, [(a[0] + b[0], a[1] + b[1]) for a, b in zip(ahead, back)])
    post = rows_of(2)
    tok = block // pieces
    sends = []
    for part in range(2):
        rows = slice(part * rows_all // 2, (part + 1) * rows_all // 2)
        summed = to_time(rows)
        mixed = (post[rows].astype(jnp.float32) * summed).astype(jnp.bfloat16)
        first = part * blocks // 2 * pieces
        for m in range(blocks // 2):
            for s in range(pieces):
                ready_ref[first + m * pieces + s] = mixed[m * group : (m + 1) * group, s * tok : (s + 1) * tok]
        span = pl.ds(first, blocks // 2 * pieces)
        for copy in range(out_hbm.shape[1]):
            sends.append(pltpu.make_async_copy(ready_ref.at[span], out_hbm.at[span, copy], sems.at[part, copy]))
            sends[-1].start()
    for send in sends:
        send.wait()


def project_kernel(mixed_ref, *refs):
    w_refs, (out_hbm, held_ref, ready_ref, sems) = refs[:-4], refs[-4:]
    rows = w_refs[0].shape[0]
    tile = 2 * rows
    position = lax.axis_index("ctx")
    even = pl.multiple_of(position % 2 * rows, rows)
    odd = pl.multiple_of((1 - position % 2) * rows, rows)
    ctx_count, tp_count = mixed_ref.shape[:2]
    mixed = jnp.concatenate([mixed_ref[i, z] for z in range(tp_count) for i in range(ctx_count)], axis=0)
    sends = []
    for half, half_refs in enumerate((w_refs[:4], w_refs[4:])):
        total = mul(jnp.concatenate([w_ref[...] for w_ref in half_refs], axis=0), mixed)
        for pair in range(2):
            place = 2 * half + pair
            held_ref[place, pl.ds(even, rows)] = total[pair * tile : pair * tile + rows]
            held_ref[place, pl.ds(odd, rows)] = total[pair * tile + rows : (pair + 1) * tile]
            ready_ref[place] = held_ref[place].T.astype(jnp.bfloat16)
            columns = pl.ds(pl.multiple_of((position // 2 ^ place) * tile, tile), tile)
            sends.append(pltpu.make_async_copy(ready_ref.at[place], out_hbm.at[:, columns], sems.at[place]))
            sends[-1].start()
    for send in sends:
        send.wait()


def whole_call(kernel, out_shape, scratch, flops, nbytes, *operands, in_hbm=0, out_hbm=()):
    results = pl.pallas_call(
        kernel,
        out_shape=out_shape,
        in_specs=[
            pl.BlockSpec(memory_space=pltpu.HBM if place < in_hbm else pltpu.VMEM) for place in range(len(operands))
        ],
        out_specs=[
            pl.BlockSpec(memory_space=pltpu.HBM if place in out_hbm else pltpu.VMEM) for place in range(len(out_shape))
        ],
        scratch_shapes=scratch,
        cost_estimate=pl.CostEstimate(flops=flops, bytes_accessed=nbytes, transcendentals=0),
        compiler_params=pltpu.CompilerParams(vmem_limit_bytes=None if in_hbm else 32 * 2**20),
    )(*operands)
    return results if len(out_shape) > 1 else results[0]


def blocked(x_gate, x_post, values, decay, residue, w_out):
    tok, width = x_gate.shape
    ctx_count = lax.axis_size("ctx")
    tp_count = lax.axis_size("tp")
    group = width // ctx_count
    poles = decay.shape[2]
    block = 2 * tok
    blocks = tok * ctx_count // block
    rows, channels = w_out.shape
    half = 2 * poles

    packed, own, mirrored = whole_call(
        pack_kernel,
        (
            jax.ShapeDtypeStruct((ctx_count, 3, group, tok), jnp.bfloat16),
            jax.ShapeDtypeStruct((2 * half, tok), jnp.float32),
            jax.ShapeDtypeStruct((2 * half, tok), jnp.float32),
        ),
        [
            pltpu.VMEM((3, tok, width), jnp.bfloat16),
            pltpu.VMEM((2, 2 * half, tok), jnp.float32),
            pltpu.VMEM((ctx_count, 3, group, tok), jnp.bfloat16),
            pltpu.SemaphoreType.DMA((7,)),
            pltpu.SemaphoreType.DMA((5,)),
        ],
        0,
        6 * tok * width * 2,
        x_gate,
        values,
        x_post,
        jnp.swapaxes(decay, 1, 2).reshape(half, width),
        jnp.swapaxes(residue, 1, 2).reshape(half, width),
        in_hbm=5,
        out_hbm=(0, 1, 2),
    )
    received = lax.all_to_all(packed, "ctx", split_axis=0, concat_axis=0, tiled=True)
    w_x, w_y = partner(w_out, "ctx", 1), partner(w_out, "ctx", 2)
    w_x, w_y, own, mirrored = lax.optimization_barrier((w_x, w_y, own, mirrored))
    paired = lax.ppermute(mirrored, "tp", [(z, tp_count - 1 - z) for z in range(tp_count)])
    own_spectra, table, back_table = whole_call(
        functools.partial(filter_kernel, poles),
        (
            jax.ShapeDtypeStruct((2, blocks, group, 2 * block), jnp.float32),
            jax.ShapeDtypeStruct((2, block, 2 * block), jnp.bfloat16),
            jax.ShapeDtypeStruct((2, 2 * block, block), jnp.bfloat16),
        ),
        [
            pltpu.VMEM((2, blocks * group, block), jnp.float32),
            pltpu.VMEM((tok, 2 * half), jnp.float32),
        ],
        2 * 2 * blocks * group * block * 2 * block * 3,
        2 * blocks * group * 2 * block * 4,
        own,
    )
    mixed = whole_call(
        functools.partial(conv_kernel, poles),
        (jax.ShapeDtypeStruct((ctx_count, tp_count, group, tok), jnp.bfloat16),),
        [
            pltpu.VMEM((2, blocks, group, 2 * block), jnp.float32),
            pltpu.VMEM((2, blocks * group, block), jnp.float32),
            pltpu.VMEM((tok, 2 * half), jnp.float32),
            pltpu.VMEM((2 * blocks * group, 2 * block), jnp.float32),
            pltpu.VMEM((2 * blocks * group, 2 * block), jnp.bfloat16),
            pltpu.VMEM((ctx_count, group, tok), jnp.bfloat16),
            pltpu.SemaphoreType.DMA((2, tp_count)),
        ],
        2 * 8 * blocks * group * block * 2 * block * 3,
        4 * blocks * group * 2 * block * 4,
        received,
        own_spectra,
        paired,
        table,
        back_table,
        out_hbm=(0,),
    )
    mixed, w_x, w_y, w_own = lax.optimization_barrier((mixed, w_x, w_y, w_out))
    lower = rows // 2
    w_far = [partner(w_x[:lower], "ctx", 2), partner(w_y[lower:], "ctx", 1)]
    w_blocks = []
    for block in (w_own, w_x, w_y):
        w_blocks += [block, partner(block, "ctx", 0)]
    w_blocks += w_far + [partner(block, "ctx", 0) for block in w_far]
    every = lax.all_to_all(
        mixed.reshape(ctx_count * tp_count, group, tok), ("ctx", "tp"), split_axis=0, concat_axis=0, tiled=True
    ).reshape(ctx_count, tp_count, group, tok)
    return whole_call(
        project_kernel,
        (jax.ShapeDtypeStruct((tok, rows * ctx_count), jnp.bfloat16),),
        [
            pltpu.VMEM((ctx_count // 2, 2 * rows, tok), jnp.float32),
            pltpu.VMEM((ctx_count // 2, tok, 2 * rows), jnp.bfloat16),
            pltpu.SemaphoreType.DMA((ctx_count // 2,)),
        ],
        2 * tok * rows * ctx_count * channels,
        2 * rows * ctx_count * channels,
        every,
        *w_blocks,
        out_hbm=(0,),
    )


def local(x_gate, x_post, values, decay, residue, w_out):
    tok, width = x_gate.shape
    ctx_count = lax.axis_size("ctx")
    if tok == 128 and width == 512 and ctx_count == 8 and w_out.shape[0] == 64 and lax.axis_size("tp") == 4:
        return blocked(x_gate, x_post, values, decay, residue, w_out)
    return general(x_gate, x_post, values, decay, residue, w_out)


def solution(mesh):
    in_specs = (
        P("ctx", "tp"),
        P("ctx", "tp"),
        P("ctx", "tp"),
        P(None, "tp", None),
        P(None, "tp", None),
        P(("tp", "ctx"), None),
    )
    out_specs = P("ctx", "tp")
    return jax.shard_map(local, mesh=mesh, in_specs=in_specs, out_specs=out_specs, check_vma=False)
```

```python
import functools
import math

import jax
import jax.numpy as jnp
from jax import lax
from jax.experimental import pallas as pl
from jax.experimental.pallas import tpu as pltpu
from jax.sharding import PartitionSpec as P

HIGHEST = lax.Precision.HIGHEST


def partner(value, axis, bit):
    mask = 2**bit
    pairs = [(source, source ^ mask) for source in range(lax.axis_size(axis))]
    return lax.ppermute(value, axis, pairs)


def radices(length_all):
    last_radix = min(128, length_all // 4)
    first_radix = min(32, length_all // last_radix)
    return (first_radix, length_all // (first_radix * last_radix), last_radix)


def rotation(row_count, col_count, modulus):
    product = (
        lax.broadcasted_iota(jnp.int32, (row_count, col_count), 0)
        * lax.broadcasted_iota(jnp.int32, (row_count, col_count), 1)
        % modulus
    )
    angle = product.astype(jnp.float32) * (2.0 * math.pi / modulus)
    return (jnp.cos(angle), -jnp.sin(angle))


def tables(radix_sizes):
    first_radix, mid_radix, last_radix = radix_sizes
    length_all = first_radix * mid_radix * last_radix
    outer_real, outer_imag = rotation(first_radix, first_radix, first_radix)
    mid_real, mid_imag = rotation(mid_radix, mid_radix, mid_radix)
    last_real, last_imag = rotation(last_radix, last_radix, last_radix)
    twist_real, twist_imag = rotation(first_radix, mid_radix * last_radix, length_all)
    twist_real = twist_real.reshape(first_radix, mid_radix, last_radix)
    twist_imag = twist_imag.reshape(first_radix, mid_radix, last_radix)
    inner_real, inner_imag = rotation(mid_radix, last_radix, mid_radix * last_radix)
    return (
        outer_real,
        outer_imag,
        mid_real,
        mid_imag,
        last_real,
        last_imag,
        twist_real,
        twist_imag,
        inner_real,
        inner_imag,
    )


def apply_matrix(pattern, real_part, imag_part, matrix_real, matrix_imag):
    out_real = jnp.einsum(pattern, real_part, matrix_real, precision=HIGHEST) - jnp.einsum(
        pattern, imag_part, matrix_imag, precision=HIGHEST
    )
    out_imag = jnp.einsum(pattern, real_part, matrix_imag, precision=HIGHEST) + jnp.einsum(
        pattern, imag_part, matrix_real, precision=HIGHEST
    )
    return (out_real, out_imag)


def complex_times(left_real, left_imag, right_real, right_imag):
    return (
        left_real * right_real - left_imag * right_imag,
        left_real * right_imag + left_imag * right_real,
    )


def forward(real_part, imag_part, table_set, radix_sizes):
    first_radix, mid_radix, last_radix = radix_sizes
    half_first = first_radix // 2
    batch_rows = real_part.shape[0]
    (
        outer_real,
        outer_imag,
        mid_real,
        mid_imag,
        last_real,
        last_imag,
        twist_real,
        twist_imag,
        inner_real,
        inner_imag,
    ) = table_set
    real_part = real_part.reshape(batch_rows, half_first, mid_radix, last_radix)
    imag_part = imag_part.reshape(batch_rows, half_first, mid_radix, last_radix)
    real_part, imag_part = apply_matrix(
        "banm,ak->bknm", real_part, imag_part, outer_real[:half_first], outer_imag[:half_first]
    )
    real_part, imag_part = complex_times(real_part, imag_part, twist_real, twist_imag)
    real_part, imag_part = apply_matrix("bknm,nj->bkjm", real_part, imag_part, mid_real, mid_imag)
    real_part, imag_part = complex_times(real_part, imag_part, inner_real, inner_imag)
    return apply_matrix("bkjm,mq->bkjq", real_part, imag_part, last_real, last_imag)


def inverse(real_part, imag_part, table_set, radix_sizes):
    first_radix, mid_radix, last_radix = radix_sizes
    half_first = first_radix // 2
    batch_rows = real_part.shape[0]
    (
        outer_real,
        outer_imag,
        mid_real,
        mid_imag,
        last_real,
        last_imag,
        twist_real,
        twist_imag,
        inner_real,
        inner_imag,
    ) = table_set
    real_part, imag_part = apply_matrix(
        "bkjq,mq->bkjm", real_part, imag_part, last_real / last_radix, -last_imag / last_radix
    )
    real_part, imag_part = complex_times(real_part, imag_part, inner_real, -inner_imag)
    real_part, imag_part = apply_matrix(
        "bkjm,nj->bknm", real_part, imag_part, mid_real / mid_radix, -mid_imag / mid_radix
    )
    real_part, imag_part = complex_times(real_part, imag_part, twist_real, -twist_imag)
    matrix_real = outer_real[:half_first] / first_radix
    matrix_imag = -outer_imag[:half_first] / first_radix
    out_real, out_imag = apply_matrix(
        "bknm,ak->banm", real_part, imag_part, matrix_real, matrix_imag
    )
    return (out_real.reshape(batch_rows, -1), out_imag.reshape(batch_rows, -1))


def spectrum(decay_rows, residue_rows, radix_sizes, seq_length):
    first_radix, mid_radix, last_radix = radix_sizes
    length_all = first_radix * mid_radix * last_radix
    poles = decay_rows.shape[1]
    shape_all = (first_radix, mid_radix, last_radix)
    frequency = (
        lax.broadcasted_iota(jnp.int32, shape_all, 0)
        + first_radix * lax.broadcasted_iota(jnp.int32, shape_all, 1)
        + first_radix * mid_radix * lax.broadcasted_iota(jnp.int32, shape_all, 2)
    )
    half_angle = frequency.astype(jnp.float32) * (math.pi / length_all)
    sin_half = jnp.sin(half_angle)
    sin_full = jnp.sin(2.0 * half_angle)
    parity_sign = (1 - 2 * (frequency % 2)).astype(jnp.float32)

    def add_pole(pole_index, running):
        run_real, run_imag = running
        rate_col = lax.dynamic_slice_in_dim(decay_rows, pole_index, 1, 1).reshape(-1, 1, 1, 1)
        weight = lax.dynamic_slice_in_dim(residue_rows, pole_index, 1, 1).reshape(
            -1, 1, 1, 1
        ) * jnp.sqrt(2.0 * rate_col / poles)
        retained = jnp.exp(-rate_col)
        den_real = -jnp.expm1(-rate_col) + 2.0 * retained * sin_half * sin_half
        den_imag = retained * sin_full
        pole_scale = (
            weight
            * (1.0 - jnp.exp(-rate_col * seq_length) * parity_sign)
            / (den_real * den_real + den_imag * den_imag)
        )
        return (run_real + pole_scale * den_real, run_imag - pole_scale * den_imag)

    zeros_all = jnp.zeros((decay_rows.shape[0],) + shape_all, jnp.float32)
    return lax.fori_loop(0, poles, add_pole, (zeros_all, zeros_all))


def general(x_gate, x_post, values, decay, residue, w_out):
    tok_rows, block_width = x_gate.shape
    ctx_count = lax.axis_size("ctx")
    tp_count = lax.axis_size("tp")
    chan_group = block_width // ctx_count
    seq_length = tok_rows * ctx_count
    radix_sizes = radices(2 * seq_length)
    table_set = tables(radix_sizes)
    first_row = lax.axis_index("ctx") * chan_group
    own_rate = lax.dynamic_slice_in_dim(decay, first_row, chan_group, 1)
    own_residue = lax.dynamic_slice_in_dim(residue, first_row, chan_group, 1)
    own_spec = [
        spectrum(own_rate[filter_index], own_residue[filter_index], radix_sizes, seq_length)
        for filter_index in range(2)
    ]
    forward_rows = [x_gate, values] + [x_post]
    row_count = len(forward_rows)
    base_rows = jnp.stack(forward_rows)
    copied = base_rows
    for bit_index in range(tp_count.bit_length() - 1):
        copied = partner(copied, "tp", bit_index)
    sent_rows = jnp.concatenate([base_rows, copied[:, :, ::-1]], axis=0)
    received = lax.all_to_all(
        jnp.swapaxes(sent_rows, 1, 2), "ctx", split_axis=1, concat_axis=2, tiled=True
    )
    gate_fwd = received[0].astype(jnp.float32)
    value_fwd = received[1].astype(jnp.float32)
    mirrored = received[row_count:, :, ::-1].astype(jnp.float32)
    spec_real, spec_imag = forward(value_fwd, mirrored[1], table_set, radix_sizes)
    spec_real, spec_imag = complex_times(spec_real, spec_imag, own_spec[0][0], own_spec[0][1])
    along_fwd, along_rev = inverse(spec_real, spec_imag, table_set, radix_sizes)
    spec_real, spec_imag = forward(
        gate_fwd * along_fwd, mirrored[0] * along_rev, table_set, radix_sizes
    )
    spec_real, spec_imag = complex_times(spec_real, spec_imag, own_spec[1][0], own_spec[1][1])
    sum_fwd, sum_rev = inverse(spec_real, spec_imag, table_set, radix_sizes)
    sum_fwd = received[2].astype(jnp.float32) * sum_fwd
    sum_rev = mirrored[2] * sum_rev
    results = jnp.stack([sum_fwd, sum_rev[:, ::-1]])
    returned = lax.all_to_all(
        results.astype(jnp.bfloat16), "ctx", split_axis=2, concat_axis=1, tiled=True
    ).astype(results.dtype)
    flipped = returned[1, ::-1, :]
    for bit_index in range(tp_count.bit_length() - 1):
        flipped = partner(flipped.astype(jnp.bfloat16), "tp", bit_index).astype(flipped.dtype)
    total_rows = returned[0] + flipped
    total_rows = total_rows.T
    mixed_rows = total_rows.astype(jnp.bfloat16)
    whole_rows = lax.all_gather(mixed_rows, "tp", axis=1, tiled=True)
    projected = lax.dot_general(
        whole_rows,
        lax.all_gather(w_out, "ctx", axis=0, tiled=True),
        (((1,), (1,)), ((), ())),
        preferred_element_type=jnp.float32,
    )
    return projected.astype(jnp.bfloat16)


def cycle(row_factor, col_factor, modulus):
    quarter = modulus // 4
    turned = row_factor * col_factor + quarter // 2
    quadrant = turned // quarter % 4
    angle = (turned % quarter - quarter // 2).astype(jnp.float32) * (2.0 * math.pi / modulus)
    square = angle * angle

    def series(first):
        total = jnp.zeros_like(square)
        for power in range(first + 10, first, -2):
            total = (total + (-1.0) ** ((power - first) // 2) / math.factorial(power)) * square
        return total

    cos = 1.0 + series(0)
    sin = angle + angle * series(1)
    odd = quadrant % 2 == 1
    cos, sin = jnp.where(odd, sin, cos), jnp.where(odd, cos, sin)
    return jnp.where((quadrant == 1) | (quadrant == 2), -cos, cos), jnp.where(quadrant >= 2, -sin, sin)


def put_tables(table_ref, back_ref):
    block = table_ref.shape[1]
    modulus = 4 * block
    coarse = 16
    rows = lax.broadcasted_iota(jnp.int32, (coarse, block), 0)
    cols = lax.broadcasted_iota(jnp.int32, (coarse, block), 1)

    def parts(big, small):
        for place in range(block // coarse):
            big_cos, big_sin = (part[place : place + 1] for part in big)
            span = slice(place * coarse, (place + 1) * coarse)
            below = slice(block + place * coarse, block + (place + 1) * coarse)
            cos = halves(big_cos * small[0] - big_sin * small[1])
            sin = halves(-(big_sin * small[0] + big_cos * small[1]))
            yield span, below, cos, sin

    frequency = 2 * cols + 1
    for span, _, cos, sin in parts(cycle(coarse * rows, frequency, modulus), cycle(rows, frequency, modulus)):
        table_ref[0, span, :block], table_ref[1, span, :block] = cos
        table_ref[0, span, block:], table_ref[1, span, block:] = sin
    for span, below, cos, sin in parts(cycle(2 * coarse * rows, cols, modulus), cycle(2 * rows + 1, cols, modulus)):
        back_ref[0, span], back_ref[1, span] = cos
        back_ref[0, below], back_ref[1, below] = sin


def halves(value):
    high = value.astype(jnp.bfloat16)
    return high, (value - high.astype(jnp.float32)).astype(jnp.bfloat16)


def mul(left, right):
    return jnp.dot(left, right, preferred_element_type=jnp.float32)


def mul3(high, low, table_ref):
    return mul(high, table_ref[0]) + (mul(low, table_ref[0]) + mul(high, table_ref[1]))


def pack_kernel(
    gate_hbm, value_hbm, post_hbm, decay_hbm, residue_hbm, w_hbm,
    out_hbm, own_hbm, sent_hbm, lower_hbm, upper_hbm, held_ref, cut_ref, w_ref, ready_ref, sems, out_sems,
):
    ctx_count, _, group, tok = out_hbm.shape
    width = gate_hbm.shape[1]
    half = decay_hbm.shape[0]
    position = lax.axis_index("ctx")
    pairs = []
    for place, index in enumerate((position, ctx_count - 1 - position)):
        columns = pl.ds(pl.multiple_of(index * group // tok * tok, tok), tok)
        pairs += [(decay_hbm.at[:, columns], cut_ref.at[place, :half]), (residue_hbm.at[:, columns], cut_ref.at[place, half:])]
    pairs += [(source, held_ref.at[place]) for place, source in enumerate((value_hbm, gate_hbm, post_hbm))]
    lower = w_hbm.shape[0] // 2
    pairs += [(w_hbm.at[:lower], w_ref.at[0]), (w_hbm.at[lower:], w_ref.at[1])]
    copies = [pltpu.make_async_copy(*pair, sems.at[place]) for place, pair in enumerate(pairs)]
    for copy in copies:
        copy.start()
    sends = []
    for place, target in enumerate((own_hbm, sent_hbm)):
        copies[2 * place].wait()
        copies[2 * place + 1].wait()
        sends.append(pltpu.make_async_copy(cut_ref.at[place], target, out_sems.at[3 + place]))
        sends[-1].start()
    for place, copy in enumerate(copies[4:7]):
        copy.wait()
        for first in range(0, width, tok):
            turned = held_ref[place, :, first : first + tok].T
            for part in range(tok // group):
                ready_ref[first // group + part, place] = turned[part * group : (part + 1) * group]
        sends.append(pltpu.make_async_copy(ready_ref.at[:, place], out_hbm.at[:, place], out_sems.at[place]))
        sends[-1].start()
    for place, target in enumerate((lower_hbm, upper_hbm)):
        copies[7 + place].wait()
        sends.append(pltpu.make_async_copy(w_ref.at[place], target, out_sems.at[5 + place]))
        sends[-1].start()
    for send in sends:
        send.wait()


def mirror_rows(value):
    row = lax.broadcasted_iota(jnp.int32, (8, value.shape[1]), 0)
    result = []
    for first in range(value.shape[0] - 8, -1, -8):
        part = value[first : first + 8]
        for shift in (1, 2, 4):
            part = jnp.where(row & shift == 0, pltpu.roll(part, 8 - shift, 0), pltpu.roll(part, shift, 0))
        result.append(part)
    return jnp.concatenate(result, axis=0)


def put_spectra(poles, index, turned, out_ref, time_ref, table_ref):
    blocks, group, twice = out_ref.shape
    block = twice // 2
    lanes = 128
    ramp = lax.broadcasted_iota(jnp.int32, (8, lanes), 1).astype(jnp.float32)
    sign = (1 - 2 * (lax.broadcasted_iota(jnp.int32, (group, block), 1) % 2)).astype(jnp.float32)
    for row in range(0, group, 8):
        rows = slice(row, row + 8)
        rate = turned[rows, index * poles : (index + 1) * poles]
        scale = turned[rows, (2 + index) * poles : (3 + index) * poles] * (jnp.sqrt(rate * (2.0 / poles)) / block)
        slope = rate * -math.log2(math.e)
        jump = jnp.exp2(slope * lanes)
        sums = [None] * (blocks * block // lanes)
        for pole in range(poles):
            term = scale[:, pole : pole + 1] * jnp.exp2(slope[:, pole : pole + 1] * ramp)
            step = jnp.broadcast_to(jump[:, pole : pole + 1], (8, lanes))
            for place in range(len(sums)):
                sums[place] = term if pole == 0 else sums[place] + term
                if place + 1 < len(sums):
                    term = term * step
        for place, total in enumerate(sums):
            lag, lane = divmod(place * lanes, block)
            time_ref[lag * group + row : lag * group + row + 8, lane : lane + lanes] = total
    spec = mul3(*halves(time_ref[...]), table_ref)
    for lag in range(blocks):
        real = spec[lag * group : (lag + 1) * group, :block]
        imag = spec[lag * group : (lag + 1) * group, block:]
        if lag > 0:
            real = real - sign * spec[(lag - 1) * group : lag * group, block:]
            imag = imag + sign * spec[(lag - 1) * group : lag * group, :block]
        out_ref[lag, :, :block] = real
        out_ref[lag, :, block:] = imag


def filter_kernel(poles, par_ref, out_ref, table_ref, back_ref, time_ref, turned_ref):
    group = out_ref.shape[1]
    put_tables(table_ref, back_ref)
    turned_ref[...] = par_ref[...].T
    turned = turned_ref[pl.ds(pl.multiple_of(lax.axis_index("ctx") * group % turned_ref.shape[0], group), group)]
    put_spectra(poles, 0, turned, out_ref, time_ref, table_ref)


def conv_kernel(
    poles, x_ref, own_ref, own_par_ref, par_ref, table_ref, back_ref, out_hbm,
    next_ref, paired_ref, time_ref, turned_ref, own_turned_ref, spec_ref, high_ref, ready_ref, sems,
):
    turned_ref[...] = par_ref[...].T
    blocks, group, twice = own_ref.shape
    block = twice // 2
    rows_all = blocks * group
    tall, wide = 16, 128
    pieces = x_ref.shape[0] // blocks
    first = (x_ref.shape[0] - 1 - lax.axis_index("ctx")) * group % turned_ref.shape[0]
    turned = mirror_rows(turned_ref[pl.ds(pl.multiple_of(first, group), group)])
    own_turned_ref[...] = own_par_ref[...].T
    first = lax.axis_index("ctx") * group % turned_ref.shape[0]
    own_turned = own_turned_ref[pl.ds(pl.multiple_of(first, group), group)]

    def rows_of(position):
        return jnp.concatenate(
            [
                jnp.concatenate([x_ref[m * pieces + s, position] for s in range(pieces)], axis=1)
                for m in range(blocks)
            ],
            axis=0,
        )

    def times(index, side, source, row, lane):
        data = []
        for m in range(blocks):
            rows = slice(source + m * group + row, source + m * group + row + tall)
            data.append((spec_ref[rows, lane : lane + wide], spec_ref[rows, block + lane : block + lane + wide]))
        sums = [None] * blocks
        for lag in range(blocks):
            h_ref = paired_ref.at[index] if side else (own_ref, next_ref)[index]
            f_re = h_ref[lag, row : row + tall, lane : lane + wide]
            f_im = h_ref[lag, row : row + tall, block + lane : block + lane + wide]
            for m in range(blocks - lag):
                target, (d_re, d_im) = (m + lag, data[m]) if side == 0 else (m, data[m + lag])
                if side == 0:
                    real, imag = f_re * d_re - f_im * d_im, f_re * d_im + f_im * d_re
                else:
                    real, imag = f_re * d_re + f_im * d_im, f_re * d_im - f_im * d_re
                if sums[target] is not None:
                    real, imag = sums[target][0] + real, sums[target][1] + imag
                sums[target] = (real, imag)
        return sums

    def to_time(rows):
        return mul(high_ref[rows], back_ref[0]) + mul(high_ref[rows], back_ref[1])

    def keep(target, row, lane, sums):
        for m in range(blocks):
            rows = slice(target + m * group + row, target + m * group + row + tall)
            for part in range(2):
                cols = slice(part * block + lane, part * block + lane + wide)
                high_ref[rows, cols] = sums[m][part].astype(jnp.bfloat16)

    chunks = [(row, lane) for row in range(0, group, tall) for lane in range(0, block, wide)]

    value = rows_of(0)
    gate = rows_of(1).astype(jnp.float32)
    spec_ref[:rows_all] = mul(value, table_ref[0]) + mul(value, table_ref[1])
    sides = [slice(side * rows_all, (side + 1) * rows_all) for side in range(2)]
    gated = []
    put_spectra(poles, 0, turned, paired_ref.at[0], time_ref.at[0], table_ref)
    for side in range(2):
        for row, lane in chunks:
            keep(side * rows_all, row, lane, times(0, side, 0, row, lane))
        gated.append(halves(gate * to_time(sides[side])))
    put_spectra(poles, 1, turned, paired_ref.at[1], time_ref.at[1], table_ref)
    put_spectra(poles, 1, own_turned, next_ref, time_ref.at[2], table_ref)
    for side in range(2):
        spec_ref[sides[side]] = mul3(*gated[side], table_ref)
    for row, lane in chunks:
        ahead, back = times(1, 0, 0, row, lane), times(1, 1, rows_all, row, lane)
        keep(0, row, lane, [(a[0] + b[0], a[1] + b[1]) for a, b in zip(ahead, back)])
    post = rows_of(2)
    tok = block // pieces
    sends = []
    for part in range(2):
        rows = slice(part * rows_all // 2, (part + 1) * rows_all // 2)
        summed = to_time(rows)
        mixed = (post[rows].astype(jnp.float32) * summed).astype(jnp.bfloat16)
        first = part * blocks // 2 * pieces
        for m in range(blocks // 2):
            for s in range(pieces):
                ready_ref[first + m * pieces + s] = mixed[m * group : (m + 1) * group, s * tok : (s + 1) * tok]
        span = pl.ds(first, blocks // 2 * pieces)
        for copy in range(out_hbm.shape[1]):
            sends.append(pltpu.make_async_copy(ready_ref.at[span], out_hbm.at[span, copy], sems.at[part, copy]))
            sends[-1].start()
    for send in sends:
        send.wait()


def project_kernel(mixed_ref, *refs):
    w_refs, (out_hbm, held_ref, ready_ref, sems) = refs[:-4], refs[-4:]
    rows = w_refs[0].shape[0]
    tile = 2 * rows
    position = lax.axis_index("ctx")
    even = pl.multiple_of(position % 2 * rows, rows)
    odd = pl.multiple_of((1 - position % 2) * rows, rows)
    ctx_count, tp_count = mixed_ref.shape[:2]
    mixed = jnp.concatenate([mixed_ref[i, z] for z in range(tp_count) for i in range(ctx_count)], axis=0)
    sends = []
    for half, half_refs in enumerate((w_refs[:6], w_refs[6:])):
        total = mul(jnp.concatenate([w_ref[...] for w_ref in half_refs], axis=0), mixed)
        for pair in range(2):
            place = 2 * half + pair
            held_ref[place, pl.ds(even, rows)] = total[pair * tile : pair * tile + rows]
            held_ref[place, pl.ds(odd, rows)] = total[pair * tile + rows : (pair + 1) * tile]
            ready_ref[place] = held_ref[place].T.astype(jnp.bfloat16)
            columns = pl.ds(pl.multiple_of((position // 2 ^ place) * tile, tile), tile)
            sends.append(pltpu.make_async_copy(ready_ref.at[place], out_hbm.at[:, columns], sems.at[place]))
            sends[-1].start()
    for send in sends:
        send.wait()


def whole_call(kernel, out_shape, scratch, flops, nbytes, *operands, in_hbm=0, out_hbm=()):
    results = pl.pallas_call(
        kernel,
        out_shape=out_shape,
        in_specs=[
            pl.BlockSpec(memory_space=pltpu.HBM if place < in_hbm else pltpu.VMEM) for place in range(len(operands))
        ],
        out_specs=[
            pl.BlockSpec(memory_space=pltpu.HBM if place in out_hbm else pltpu.VMEM) for place in range(len(out_shape))
        ],
        scratch_shapes=scratch,
        cost_estimate=pl.CostEstimate(flops=flops, bytes_accessed=nbytes, transcendentals=0),
        compiler_params=pltpu.CompilerParams(vmem_limit_bytes=None if in_hbm else 32 * 2**20),
    )(*operands)
    return results if len(out_shape) > 1 else results[0]


def blocked(x_gate, x_post, values, decay, residue, w_out):
    tok, width = x_gate.shape
    ctx_count = lax.axis_size("ctx")
    tp_count = lax.axis_size("tp")
    group = width // ctx_count
    poles = decay.shape[2]
    block = 2 * tok
    blocks = tok * ctx_count // block
    rows, channels = w_out.shape
    half = 2 * poles

    packed, own, mirrored, w_lower, w_upper = whole_call(
        pack_kernel,
        (
            jax.ShapeDtypeStruct((ctx_count, 3, group, tok), jnp.bfloat16),
            jax.ShapeDtypeStruct((2 * half, tok), jnp.float32),
            jax.ShapeDtypeStruct((2 * half, tok), jnp.float32),
            jax.ShapeDtypeStruct((rows // 2, channels), jnp.bfloat16),
            jax.ShapeDtypeStruct((rows // 2, channels), jnp.bfloat16),
        ),
        [
            pltpu.VMEM((3, tok, width), jnp.bfloat16),
            pltpu.VMEM((2, 2 * half, tok), jnp.float32),
            pltpu.VMEM((2, rows // 2, channels), jnp.bfloat16),
            pltpu.VMEM((ctx_count, 3, group, tok), jnp.bfloat16),
            pltpu.SemaphoreType.DMA((9,)),
            pltpu.SemaphoreType.DMA((7,)),
        ],
        0,
        6 * tok * width * 2,
        x_gate,
        values,
        x_post,
        jnp.swapaxes(decay, 1, 2).reshape(half, width),
        jnp.swapaxes(residue, 1, 2).reshape(half, width),
        w_out,
        in_hbm=6,
        out_hbm=(0, 1, 2, 3, 4),
    )
    paired = lax.ppermute(mirrored, "tp", [(z, tp_count - 1 - z) for z in range(tp_count)])
    received = lax.all_to_all(packed, "ctx", split_axis=0, concat_axis=0, tiled=True)

    w_x, w_y = partner(w_lower, "ctx", 1), partner(w_upper, "ctx", 2)
    own_spectra, table, back_table = whole_call(
        functools.partial(filter_kernel, poles),
        (
            jax.ShapeDtypeStruct((blocks, group, 2 * block), jnp.float32),
            jax.ShapeDtypeStruct((2, block, 2 * block), jnp.bfloat16),
            jax.ShapeDtypeStruct((2, 2 * block, block), jnp.bfloat16),
        ),
        [
            pltpu.VMEM((blocks * group, block), jnp.float32),
            pltpu.VMEM((tok, 2 * half), jnp.float32),
        ],
        2 * blocks * group * block * 2 * block * 3,
        blocks * group * 2 * block * 4,
        own,
    )
    mixed = whole_call(
        functools.partial(conv_kernel, poles),
        (jax.ShapeDtypeStruct((ctx_count, tp_count, group, tok), jnp.bfloat16),),
        [
            pltpu.VMEM((blocks, group, 2 * block), jnp.float32),
            pltpu.VMEM((2, blocks, group, 2 * block), jnp.float32),
            pltpu.VMEM((3, blocks * group, block), jnp.float32),
            pltpu.VMEM((tok, 2 * half), jnp.float32),
            pltpu.VMEM((tok, 2 * half), jnp.float32),
            pltpu.VMEM((2 * blocks * group, 2 * block), jnp.float32),
            pltpu.VMEM((2 * blocks * group, 2 * block), jnp.bfloat16),
            pltpu.VMEM((ctx_count, group, tok), jnp.bfloat16),
            pltpu.SemaphoreType.DMA((2, tp_count)),
        ],
        2 * 9 * blocks * group * block * 2 * block * 3,
        4 * blocks * group * 2 * block * 4,
        received,
        own_spectra,
        own,
        paired,
        table,
        back_table,
        out_hbm=(0,),
    )
    mixed, w_x, w_y, w_own, w_lower, w_upper = lax.optimization_barrier((mixed, w_x, w_y, w_out, w_lower, w_upper))
    w_blocks = []
    for block in (
        [w_own],
        [w_x, partner(w_upper, "ctx", 1)],
        [partner(w_lower, "ctx", 2), w_y],
        [partner(w_x, "ctx", 2), partner(w_y, "ctx", 1)],
    ):
        w_blocks += block + [partner(part, "ctx", 0) for part in block]
    every = lax.all_to_all(
        mixed.reshape(ctx_count * tp_count, group, tok), ("ctx", "tp"), split_axis=0, concat_axis=0, tiled=True
    ).reshape(ctx_count, tp_count, group, tok)
    return whole_call(
        project_kernel,
        (jax.ShapeDtypeStruct((tok, rows * ctx_count), jnp.bfloat16),),
        [
            pltpu.VMEM((ctx_count // 2, 2 * rows, tok), jnp.float32),
            pltpu.VMEM((ctx_count // 2, tok, 2 * rows), jnp.bfloat16),
            pltpu.SemaphoreType.DMA((ctx_count // 2,)),
        ],
        2 * tok * rows * ctx_count * channels,
        2 * rows * ctx_count * channels,
        every,
        *w_blocks,
        out_hbm=(0,),
    )


def local(x_gate, x_post, values, decay, residue, w_out):
    tok, width = x_gate.shape
    ctx_count = lax.axis_size("ctx")
    if tok == 128 and width == 512 and ctx_count == 8 and w_out.shape[0] == 64 and lax.axis_size("tp") == 4:
        return blocked(x_gate, x_post, values, decay, residue, w_out)
    return general(x_gate, x_post, values, decay, residue, w_out)


def solution(mesh):
    in_specs = (
        P("ctx", "tp"),
        P("ctx", "tp"),
        P("ctx", "tp"),
        P(None, "tp", None),
        P(None, "tp", None),
        P(("tp", "ctx"), None),
    )
    out_specs = P("ctx", "tp")
    return jax.shard_map(local, mesh=mesh, in_specs=in_specs, out_specs=out_specs, check_vma=False)
```

```python
import functools
import math

import jax
import jax.numpy as jnp
from jax import lax
from jax.experimental import pallas as pl
from jax.experimental.pallas import tpu as pltpu
from jax.sharding import PartitionSpec as P

HIGHEST = lax.Precision.HIGHEST


def partner(value, axis, bit):
    mask = 2**bit
    pairs = [(source, source ^ mask) for source in range(lax.axis_size(axis))]
    return lax.ppermute(value, axis, pairs)


def radices(length_all):
    last_radix = min(128, length_all // 4)
    first_radix = min(32, length_all // last_radix)
    return (first_radix, length_all // (first_radix * last_radix), last_radix)


def rotation(row_count, col_count, modulus):
    product = (
        lax.broadcasted_iota(jnp.int32, (row_count, col_count), 0)
        * lax.broadcasted_iota(jnp.int32, (row_count, col_count), 1)
        % modulus
    )
    angle = product.astype(jnp.float32) * (2.0 * math.pi / modulus)
    return (jnp.cos(angle), -jnp.sin(angle))


def tables(radix_sizes):
    first_radix, mid_radix, last_radix = radix_sizes
    length_all = first_radix * mid_radix * last_radix
    outer_real, outer_imag = rotation(first_radix, first_radix, first_radix)
    mid_real, mid_imag = rotation(mid_radix, mid_radix, mid_radix)
    last_real, last_imag = rotation(last_radix, last_radix, last_radix)
    twist_real, twist_imag = rotation(first_radix, mid_radix * last_radix, length_all)
    twist_real = twist_real.reshape(first_radix, mid_radix, last_radix)
    twist_imag = twist_imag.reshape(first_radix, mid_radix, last_radix)
    inner_real, inner_imag = rotation(mid_radix, last_radix, mid_radix * last_radix)
    return (
        outer_real,
        outer_imag,
        mid_real,
        mid_imag,
        last_real,
        last_imag,
        twist_real,
        twist_imag,
        inner_real,
        inner_imag,
    )


def apply_matrix(pattern, real_part, imag_part, matrix_real, matrix_imag):
    out_real = jnp.einsum(pattern, real_part, matrix_real, precision=HIGHEST) - jnp.einsum(
        pattern, imag_part, matrix_imag, precision=HIGHEST
    )
    out_imag = jnp.einsum(pattern, real_part, matrix_imag, precision=HIGHEST) + jnp.einsum(
        pattern, imag_part, matrix_real, precision=HIGHEST
    )
    return (out_real, out_imag)


def complex_times(left_real, left_imag, right_real, right_imag):
    return (
        left_real * right_real - left_imag * right_imag,
        left_real * right_imag + left_imag * right_real,
    )


def forward(real_part, imag_part, table_set, radix_sizes):
    first_radix, mid_radix, last_radix = radix_sizes
    half_first = first_radix // 2
    batch_rows = real_part.shape[0]
    (
        outer_real,
        outer_imag,
        mid_real,
        mid_imag,
        last_real,
        last_imag,
        twist_real,
        twist_imag,
        inner_real,
        inner_imag,
    ) = table_set
    real_part = real_part.reshape(batch_rows, half_first, mid_radix, last_radix)
    imag_part = imag_part.reshape(batch_rows, half_first, mid_radix, last_radix)
    real_part, imag_part = apply_matrix(
        "banm,ak->bknm", real_part, imag_part, outer_real[:half_first], outer_imag[:half_first]
    )
    real_part, imag_part = complex_times(real_part, imag_part, twist_real, twist_imag)
    real_part, imag_part = apply_matrix("bknm,nj->bkjm", real_part, imag_part, mid_real, mid_imag)
    real_part, imag_part = complex_times(real_part, imag_part, inner_real, inner_imag)
    return apply_matrix("bkjm,mq->bkjq", real_part, imag_part, last_real, last_imag)


def inverse(real_part, imag_part, table_set, radix_sizes):
    first_radix, mid_radix, last_radix = radix_sizes
    half_first = first_radix // 2
    batch_rows = real_part.shape[0]
    (
        outer_real,
        outer_imag,
        mid_real,
        mid_imag,
        last_real,
        last_imag,
        twist_real,
        twist_imag,
        inner_real,
        inner_imag,
    ) = table_set
    real_part, imag_part = apply_matrix(
        "bkjq,mq->bkjm", real_part, imag_part, last_real / last_radix, -last_imag / last_radix
    )
    real_part, imag_part = complex_times(real_part, imag_part, inner_real, -inner_imag)
    real_part, imag_part = apply_matrix(
        "bkjm,nj->bknm", real_part, imag_part, mid_real / mid_radix, -mid_imag / mid_radix
    )
    real_part, imag_part = complex_times(real_part, imag_part, twist_real, -twist_imag)
    matrix_real = outer_real[:half_first] / first_radix
    matrix_imag = -outer_imag[:half_first] / first_radix
    out_real, out_imag = apply_matrix(
        "bknm,ak->banm", real_part, imag_part, matrix_real, matrix_imag
    )
    return (out_real.reshape(batch_rows, -1), out_imag.reshape(batch_rows, -1))


def spectrum(decay_rows, residue_rows, radix_sizes, seq_length):
    first_radix, mid_radix, last_radix = radix_sizes
    length_all = first_radix * mid_radix * last_radix
    poles = decay_rows.shape[1]
    shape_all = (first_radix, mid_radix, last_radix)
    frequency = (
        lax.broadcasted_iota(jnp.int32, shape_all, 0)
        + first_radix * lax.broadcasted_iota(jnp.int32, shape_all, 1)
        + first_radix * mid_radix * lax.broadcasted_iota(jnp.int32, shape_all, 2)
    )
    half_angle = frequency.astype(jnp.float32) * (math.pi / length_all)
    sin_half = jnp.sin(half_angle)
    sin_full = jnp.sin(2.0 * half_angle)
    parity_sign = (1 - 2 * (frequency % 2)).astype(jnp.float32)

    def add_pole(pole_index, running):
        run_real, run_imag = running
        rate_col = lax.dynamic_slice_in_dim(decay_rows, pole_index, 1, 1).reshape(-1, 1, 1, 1)
        weight = lax.dynamic_slice_in_dim(residue_rows, pole_index, 1, 1).reshape(
            -1, 1, 1, 1
        ) * jnp.sqrt(2.0 * rate_col / poles)
        retained = jnp.exp(-rate_col)
        den_real = -jnp.expm1(-rate_col) + 2.0 * retained * sin_half * sin_half
        den_imag = retained * sin_full
        pole_scale = (
            weight
            * (1.0 - jnp.exp(-rate_col * seq_length) * parity_sign)
            / (den_real * den_real + den_imag * den_imag)
        )
        return (run_real + pole_scale * den_real, run_imag - pole_scale * den_imag)

    zeros_all = jnp.zeros((decay_rows.shape[0],) + shape_all, jnp.float32)
    return lax.fori_loop(0, poles, add_pole, (zeros_all, zeros_all))


def general(x_gate, x_post, values, decay, residue, w_out):
    tok_rows, block_width = x_gate.shape
    ctx_count = lax.axis_size("ctx")
    tp_count = lax.axis_size("tp")
    chan_group = block_width // ctx_count
    seq_length = tok_rows * ctx_count
    radix_sizes = radices(2 * seq_length)
    table_set = tables(radix_sizes)
    first_row = lax.axis_index("ctx") * chan_group
    own_rate = lax.dynamic_slice_in_dim(decay, first_row, chan_group, 1)
    own_residue = lax.dynamic_slice_in_dim(residue, first_row, chan_group, 1)
    own_spec = [
        spectrum(own_rate[filter_index], own_residue[filter_index], radix_sizes, seq_length)
        for filter_index in range(2)
    ]
    forward_rows = [x_gate, values] + [x_post]
    row_count = len(forward_rows)
    base_rows = jnp.stack(forward_rows)
    copied = base_rows
    for bit_index in range(tp_count.bit_length() - 1):
        copied = partner(copied, "tp", bit_index)
    sent_rows = jnp.concatenate([base_rows, copied[:, :, ::-1]], axis=0)
    received = lax.all_to_all(
        jnp.swapaxes(sent_rows, 1, 2), "ctx", split_axis=1, concat_axis=2, tiled=True
    )
    gate_fwd = received[0].astype(jnp.float32)
    value_fwd = received[1].astype(jnp.float32)
    mirrored = received[row_count:, :, ::-1].astype(jnp.float32)
    spec_real, spec_imag = forward(value_fwd, mirrored[1], table_set, radix_sizes)
    spec_real, spec_imag = complex_times(spec_real, spec_imag, own_spec[0][0], own_spec[0][1])
    along_fwd, along_rev = inverse(spec_real, spec_imag, table_set, radix_sizes)
    spec_real, spec_imag = forward(
        gate_fwd * along_fwd, mirrored[0] * along_rev, table_set, radix_sizes
    )
    spec_real, spec_imag = complex_times(spec_real, spec_imag, own_spec[1][0], own_spec[1][1])
    sum_fwd, sum_rev = inverse(spec_real, spec_imag, table_set, radix_sizes)
    sum_fwd = received[2].astype(jnp.float32) * sum_fwd
    sum_rev = mirrored[2] * sum_rev
    results = jnp.stack([sum_fwd, sum_rev[:, ::-1]])
    returned = lax.all_to_all(
        results.astype(jnp.bfloat16), "ctx", split_axis=2, concat_axis=1, tiled=True
    ).astype(results.dtype)
    flipped = returned[1, ::-1, :]
    for bit_index in range(tp_count.bit_length() - 1):
        flipped = partner(flipped.astype(jnp.bfloat16), "tp", bit_index).astype(flipped.dtype)
    total_rows = returned[0] + flipped
    total_rows = total_rows.T
    mixed_rows = total_rows.astype(jnp.bfloat16)
    whole_rows = lax.all_gather(mixed_rows, "tp", axis=1, tiled=True)
    projected = lax.dot_general(
        whole_rows,
        lax.all_gather(w_out, "ctx", axis=0, tiled=True),
        (((1,), (1,)), ((), ())),
        preferred_element_type=jnp.float32,
    )
    return projected.astype(jnp.bfloat16)


def cycle(row_factor, col_factor, modulus):
    quarter = modulus // 4
    turned = row_factor * col_factor + quarter // 2
    quadrant = turned // quarter % 4
    angle = (turned % quarter - quarter // 2).astype(jnp.float32) * (2.0 * math.pi / modulus)
    square = angle * angle

    def series(first):
        total = jnp.zeros_like(square)
        for power in range(first + 10, first, -2):
            total = (total + (-1.0) ** ((power - first) // 2) / math.factorial(power)) * square
        return total

    cos = 1.0 + series(0)
    sin = angle + angle * series(1)
    odd = quadrant % 2 == 1
    cos, sin = jnp.where(odd, sin, cos), jnp.where(odd, cos, sin)
    return jnp.where((quadrant == 1) | (quadrant == 2), -cos, cos), jnp.where(quadrant >= 2, -sin, sin)


def put_tables(table_ref, back_ref):
    block = table_ref.shape[1]
    modulus = 4 * block
    coarse = 16
    rows = lax.broadcasted_iota(jnp.int32, (coarse, block), 0)
    cols = lax.broadcasted_iota(jnp.int32, (coarse, block), 1)

    def parts(big, small):
        for place in range(block // coarse):
            big_cos, big_sin = (part[place : place + 1] for part in big)
            span = slice(place * coarse, (place + 1) * coarse)
            below = slice(block + place * coarse, block + (place + 1) * coarse)
            cos = halves(big_cos * small[0] - big_sin * small[1])
            sin = halves(-(big_sin * small[0] + big_cos * small[1]))
            yield span, below, cos, sin

    frequency = 2 * cols + 1
    for span, _, cos, sin in parts(cycle(coarse * rows, frequency, modulus), cycle(rows, frequency, modulus)):
        table_ref[0, span, :block], table_ref[1, span, :block] = cos
        table_ref[0, span, block:], table_ref[1, span, block:] = sin
    for span, below, cos, sin in parts(cycle(2 * coarse * rows, cols, modulus), cycle(2 * rows + 1, cols, modulus)):
        back_ref[0, span], back_ref[1, span] = cos
        back_ref[0, below], back_ref[1, below] = sin


def halves(value):
    high = value.astype(jnp.bfloat16)
    return high, (value - high.astype(jnp.float32)).astype(jnp.bfloat16)


def mul(left, right):
    return jnp.dot(left, right, preferred_element_type=jnp.float32)


def mul3(high, low, table_ref):
    return mul(high, table_ref[0]) + (mul(low, table_ref[0]) + mul(high, table_ref[1]))


def pack_kernel(
    gate_hbm, value_hbm, post_hbm, decay_hbm, residue_hbm,
    out_hbm, own_hbm, sent_hbm, held_ref, cut_ref, ready_ref, sems, out_sems,
):
    ctx_count, _, group, tok = out_hbm.shape
    width = gate_hbm.shape[1]
    half = decay_hbm.shape[0]
    position = lax.axis_index("ctx")
    pairs = []
    for place, index in enumerate((position, ctx_count - 1 - position)):
        columns = pl.ds(pl.multiple_of(index * group // tok * tok, tok), tok)
        pairs += [(decay_hbm.at[:, columns], cut_ref.at[place, :half]), (residue_hbm.at[:, columns], cut_ref.at[place, half:])]
    pairs += [(source, held_ref.at[place]) for place, source in enumerate((value_hbm, gate_hbm, post_hbm))]
    copies = [pltpu.make_async_copy(*pair, sems.at[place]) for place, pair in enumerate(pairs)]
    for copy in copies:
        copy.start()
    sends = []
    for place, target in enumerate((own_hbm, sent_hbm)):
        copies[2 * place].wait()
        copies[2 * place + 1].wait()
        sends.append(pltpu.make_async_copy(cut_ref.at[place], target, out_sems.at[3 + place]))
        sends[-1].start()
    for place, copy in enumerate(copies[4:]):
        copy.wait()
        for first in range(0, width, tok):
            turned = held_ref[place, :, first : first + tok].T
            for part in range(tok // group):
                ready_ref[first // group + part, place] = turned[part * group : (part + 1) * group]
        sends.append(pltpu.make_async_copy(ready_ref.at[:, place], out_hbm.at[:, place], out_sems.at[place]))
        sends[-1].start()
    for send in sends:
        send.wait()


def mirror_rows(value):
    row = lax.broadcasted_iota(jnp.int32, (8, value.shape[1]), 0)
    result = []
    for first in range(value.shape[0] - 8, -1, -8):
        part = value[first : first + 8]
        for shift in (1, 2, 4):
            part = jnp.where(row & shift == 0, pltpu.roll(part, 8 - shift, 0), pltpu.roll(part, shift, 0))
        result.append(part)
    return jnp.concatenate(result, axis=0)


def put_filter(poles, index, turned, time_ref):
    lanes = 128
    rows_all, block = time_ref.shape
    group = turned.shape[0]
    ramp = lax.broadcasted_iota(jnp.int32, (8, lanes), 1).astype(jnp.float32)
    for row in range(0, group, 8):
        rows = slice(row, row + 8)
        rate = turned[rows, index * poles : (index + 1) * poles]
        scale = turned[rows, (2 + index) * poles : (3 + index) * poles] * (jnp.sqrt(rate * (2.0 / poles)) / block)
        slope = rate * -math.log2(math.e)
        jump = jnp.exp2(slope * lanes)
        sums = [None] * (rows_all // group * block // lanes)
        for pole in range(poles):
            term = scale[:, pole : pole + 1] * jnp.exp2(slope[:, pole : pole + 1] * ramp)
            step = jnp.broadcast_to(jump[:, pole : pole + 1], (8, lanes))
            for place in range(len(sums)):
                sums[place] = term if pole == 0 else sums[place] + term
                if place + 1 < len(sums):
                    term = term * step
        for place, total in enumerate(sums):
            lag, lane = divmod(place * lanes, block)
            time_ref[lag * group + row : lag * group + row + 8, lane : lane + lanes] = total


def put_spectra(spec, out_ref):
    blocks, group, twice = out_ref.shape
    block = twice // 2
    sign = (1 - 2 * (lax.broadcasted_iota(jnp.int32, (group, block), 1) % 2)).astype(jnp.float32)
    for lag in range(blocks):
        real = spec[lag * group : (lag + 1) * group, :block]
        imag = spec[lag * group : (lag + 1) * group, block:]
        if lag > 0:
            real = real - sign * spec[(lag - 1) * group : lag * group, block:]
            imag = imag + sign * spec[(lag - 1) * group : lag * group, :block]
        out_ref[lag, :, :block] = real
        out_ref[lag, :, block:] = imag


def filter_kernel(poles, par_ref, out_ref, table_ref, back_ref, time_ref, turned_ref):
    group = out_ref.shape[2]
    put_tables(table_ref, back_ref)
    turned_ref[...] = par_ref[...].T
    turned = turned_ref[pl.ds(pl.multiple_of(lax.axis_index("ctx") * group % turned_ref.shape[0], group), group)]
    put_filter(poles, 0, turned, time_ref.at[0])
    spec = mul3(*halves(time_ref[0]), table_ref)
    put_filter(poles, 1, turned, time_ref.at[1])
    put_spectra(spec, out_ref.at[0])
    put_spectra(mul3(*halves(time_ref[1]), table_ref), out_ref.at[1])


def conv_kernel(
    poles, x_ref, own_ref, par_ref, table_ref, back_ref, out_hbm,
    paired_ref, time_ref, turned_ref, spec_ref, high_ref, ready_ref, sems,
):
    turned_ref[...] = par_ref[...].T
    blocks, group, twice = own_ref.shape[1:]
    block = twice // 2
    rows_all = blocks * group
    tall, wide = 16, 128
    pieces = x_ref.shape[0] // blocks
    first = (x_ref.shape[0] - 1 - lax.axis_index("ctx")) * group % turned_ref.shape[0]
    turned = mirror_rows(turned_ref[pl.ds(pl.multiple_of(first, group), group)])

    def rows_of(position):
        return jnp.concatenate(
            [
                jnp.concatenate([x_ref[m * pieces + s, position] for s in range(pieces)], axis=1)
                for m in range(blocks)
            ],
            axis=0,
        )

    def times(index, side, source, row, lane):
        data = []
        for m in range(blocks):
            rows = slice(source + m * group + row, source + m * group + row + tall)
            data.append((spec_ref[rows, lane : lane + wide], spec_ref[rows, block + lane : block + lane + wide]))
        sums = [None] * blocks
        for lag in range(blocks):
            h_ref = (own_ref, paired_ref)[side]
            f_re = h_ref[index, lag, row : row + tall, lane : lane + wide]
            f_im = h_ref[index, lag, row : row + tall, block + lane : block + lane + wide]
            for m in range(blocks - lag):
                target, (d_re, d_im) = (m + lag, data[m]) if side == 0 else (m, data[m + lag])
                if side == 0:
                    real, imag = f_re * d_re - f_im * d_im, f_re * d_im + f_im * d_re
                else:
                    real, imag = f_re * d_re + f_im * d_im, f_re * d_im - f_im * d_re
                if sums[target] is not None:
                    real, imag = sums[target][0] + real, sums[target][1] + imag
                sums[target] = (real, imag)
        return sums

    def to_time(rows):
        return mul(high_ref[rows], back_ref[0]) + mul(high_ref[rows], back_ref[1])

    def keep(target, row, lane, sums):
        for m in range(blocks):
            rows = slice(target + m * group + row, target + m * group + row + tall)
            for part in range(2):
                cols = slice(part * block + lane, part * block + lane + wide)
                high_ref[rows, cols] = sums[m][part].astype(jnp.bfloat16)

    chunks = [(row, lane) for row in range(0, group, tall) for lane in range(0, block, wide)]

    value = rows_of(0)
    gate = rows_of(1).astype(jnp.float32)
    spec_ref[:rows_all] = mul(value, table_ref[0]) + mul(value, table_ref[1])
    sides = [slice(side * rows_all, (side + 1) * rows_all) for side in range(2)]
    put_filter(poles, 0, turned, time_ref.at[0])
    spec = mul3(*halves(time_ref[0]), table_ref)
    for row, lane in chunks:
        keep(0, row, lane, times(0, 0, 0, row, lane))
    put_spectra(spec, paired_ref.at[0])
    gated = [gate * to_time(sides[0])]
    put_filter(poles, 1, turned, time_ref.at[1])
    for row, lane in chunks:
        keep(rows_all, row, lane, times(0, 1, 0, row, lane))
    gated.append(gate * to_time(sides[1]))
    spec = mul3(*halves(time_ref[1]), table_ref)
    for side in range(2):
        spec_ref[sides[side]] = mul3(*halves(gated[side]), table_ref)
    put_spectra(spec, paired_ref.at[1])
    for row, lane in chunks:
        ahead, back = times(1, 0, 0, row, lane), times(1, 1, rows_all, row, lane)
        keep(0, row, lane, [(a[0] + b[0], a[1] + b[1]) for a, b in zip(ahead, back)])
    post = rows_of(2)
    tok = block // pieces
    sends = []
    for part in range(2):
        rows = slice(part * rows_all // 2, (part + 1) * rows_all // 2)
        summed = to_time(rows)
        mixed = (post[rows].astype(jnp.float32) * summed).astype(jnp.bfloat16)
        first = part * blocks // 2 * pieces
        for m in range(blocks // 2):
            for s in range(pieces):
                ready_ref[first + m * pieces + s] = mixed[m * group : (m + 1) * group, s * tok : (s + 1) * tok]
        span = pl.ds(first, blocks // 2 * pieces)
        for copy in range(out_hbm.shape[1]):
            sends.append(pltpu.make_async_copy(ready_ref.at[span], out_hbm.at[span, copy], sems.at[part, copy]))
            sends[-1].start()
    for send in sends:
        send.wait()


def project_kernel(mixed_ref, *refs):
    w_refs, (out_hbm, held_ref, ready_ref, sems) = refs[:-4], refs[-4:]
    rows = w_refs[0].shape[0]
    tile = 2 * rows
    position = lax.axis_index("ctx")
    even = pl.multiple_of(position % 2 * rows, rows)
    odd = pl.multiple_of((1 - position % 2) * rows, rows)
    ctx_count, tp_count = mixed_ref.shape[:2]
    mixed = jnp.concatenate([mixed_ref[i, z] for z in range(tp_count) for i in range(ctx_count)], axis=0)
    sends = []
    for half, half_refs in enumerate((w_refs[:4], w_refs[4:])):
        total = mul(jnp.concatenate([w_ref[...] for w_ref in half_refs], axis=0), mixed)
        for pair in range(2):
            place = 2 * half + pair
            held_ref[place, pl.ds(even, rows)] = total[pair * tile : pair * tile + rows]
            held_ref[place, pl.ds(odd, rows)] = total[pair * tile + rows : (pair + 1) * tile]
            ready_ref[place] = held_ref[place].T.astype(jnp.bfloat16)
            columns = pl.ds(pl.multiple_of((position // 2 ^ place) * tile, tile), tile)
            sends.append(pltpu.make_async_copy(ready_ref.at[place], out_hbm.at[:, columns], sems.at[place]))
            sends[-1].start()
    for send in sends:
        send.wait()


def whole_call(kernel, out_shape, scratch, flops, nbytes, *operands, in_hbm=0, out_hbm=()):
    results = pl.pallas_call(
        kernel,
        out_shape=out_shape,
        in_specs=[
            pl.BlockSpec(memory_space=pltpu.HBM if place < in_hbm else pltpu.VMEM) for place in range(len(operands))
        ],
        out_specs=[
            pl.BlockSpec(memory_space=pltpu.HBM if place in out_hbm else pltpu.VMEM) for place in range(len(out_shape))
        ],
        scratch_shapes=scratch,
        cost_estimate=pl.CostEstimate(flops=flops, bytes_accessed=nbytes, transcendentals=0),
        compiler_params=pltpu.CompilerParams(vmem_limit_bytes=None if in_hbm else 32 * 2**20),
    )(*operands)
    return results if len(out_shape) > 1 else results[0]


def blocked(x_gate, x_post, values, decay, residue, w_out):
    tok, width = x_gate.shape
    ctx_count = lax.axis_size("ctx")
    tp_count = lax.axis_size("tp")
    group = width // ctx_count
    poles = decay.shape[2]
    block = 2 * tok
    blocks = tok * ctx_count // block
    rows, channels = w_out.shape
    half = 2 * poles

    packed, own, mirrored = whole_call(
        pack_kernel,
        (
            jax.ShapeDtypeStruct((ctx_count, 3, group, tok), jnp.bfloat16),
            jax.ShapeDtypeStruct((2 * half, tok), jnp.float32),
            jax.ShapeDtypeStruct((2 * half, tok), jnp.float32),
        ),
        [
            pltpu.VMEM((3, tok, width), jnp.bfloat16),
            pltpu.VMEM((2, 2 * half, tok), jnp.float32),
            pltpu.VMEM((ctx_count, 3, group, tok), jnp.bfloat16),
            pltpu.SemaphoreType.DMA((7,)),
            pltpu.SemaphoreType.DMA((5,)),
        ],
        0,
        6 * tok * width * 2,
        x_gate,
        values,
        x_post,
        jnp.swapaxes(decay, 1, 2).reshape(half, width),
        jnp.swapaxes(residue, 1, 2).reshape(half, width),
        in_hbm=5,
        out_hbm=(0, 1, 2),
    )
    paired = lax.ppermute(mirrored, "tp", [(z, tp_count - 1 - z) for z in range(tp_count)])
    received = lax.all_to_all(packed, "ctx", split_axis=0, concat_axis=0, tiled=True)

    w_late, mirrored = lax.optimization_barrier((w_out, mirrored))
    w_x, w_y = partner(w_late, "ctx", 1), partner(w_late, "ctx", 2)
    own_spectra, table, back_table = whole_call(
        functools.partial(filter_kernel, poles),
        (
            jax.ShapeDtypeStruct((2, blocks, group, 2 * block), jnp.float32),
            jax.ShapeDtypeStruct((2, block, 2 * block), jnp.bfloat16),
            jax.ShapeDtypeStruct((2, 2 * block, block), jnp.bfloat16),
        ),
        [
            pltpu.VMEM((2, blocks * group, block), jnp.float32),
            pltpu.VMEM((tok, 2 * half), jnp.float32),
        ],
        2 * 2 * blocks * group * block * 2 * block * 3,
        2 * blocks * group * 2 * block * 4,
        own,
    )
    mixed = whole_call(
        functools.partial(conv_kernel, poles),
        (jax.ShapeDtypeStruct((ctx_count, tp_count, group, tok), jnp.bfloat16),),
        [
            pltpu.VMEM((2, blocks, group, 2 * block), jnp.float32),
            pltpu.VMEM((2, blocks * group, block), jnp.float32),
            pltpu.VMEM((tok, 2 * half), jnp.float32),
            pltpu.VMEM((2 * blocks * group, 2 * block), jnp.float32),
            pltpu.VMEM((2 * blocks * group, 2 * block), jnp.bfloat16),
            pltpu.VMEM((ctx_count, group, tok), jnp.bfloat16),
            pltpu.SemaphoreType.DMA((2, tp_count)),
        ],
        2 * 8 * blocks * group * block * 2 * block * 3,
        4 * blocks * group * 2 * block * 4,
        received,
        own_spectra,
        paired,
        table,
        back_table,
        out_hbm=(0,),
    )
    mixed, w_x, w_y, w_own = lax.optimization_barrier((mixed, w_x, w_y, w_out))
    lower = rows // 2
    w_far = [partner(w_x[:lower], "ctx", 2), partner(w_y[lower:], "ctx", 1)]
    w_blocks = []
    for block in (w_own, w_x, w_y):
        w_blocks += [block, partner(block, "ctx", 0)]
    w_blocks += w_far + [partner(block, "ctx", 0) for block in w_far]
    every = lax.all_to_all(
        mixed.reshape(ctx_count * tp_count, group, tok), ("ctx", "tp"), split_axis=0, concat_axis=0, tiled=True
    ).reshape(ctx_count, tp_count, group, tok)
    return whole_call(
        project_kernel,
        (jax.ShapeDtypeStruct((tok, rows * ctx_count), jnp.bfloat16),),
        [
            pltpu.VMEM((ctx_count // 2, 2 * rows, tok), jnp.float32),
            pltpu.VMEM((ctx_count // 2, tok, 2 * rows), jnp.bfloat16),
            pltpu.SemaphoreType.DMA((ctx_count // 2,)),
        ],
        2 * tok * rows * ctx_count * channels,
        2 * rows * ctx_count * channels,
        every,
        *w_blocks,
        out_hbm=(0,),
    )


def local(x_gate, x_post, values, decay, residue, w_out):
    tok, width = x_gate.shape
    ctx_count = lax.axis_size("ctx")
    if tok == 128 and width == 512 and ctx_count == 8 and w_out.shape[0] == 64 and lax.axis_size("tp") == 4:
        return blocked(x_gate, x_post, values, decay, residue, w_out)
    return general(x_gate, x_post, values, decay, residue, w_out)


def solution(mesh):
    in_specs = (
        P("ctx", "tp"),
        P("ctx", "tp"),
        P("ctx", "tp"),
        P(None, "tp", None),
        P(None, "tp", None),
        P(("tp", "ctx"), None),
    )
    out_specs = P("ctx", "tp")
    return jax.shard_map(local, mesh=mesh, in_specs=in_specs, out_specs=out_specs, check_vma=False)
```

```python
import functools
import math

import jax
import jax.numpy as jnp
from jax import lax
from jax.experimental import pallas as pl
from jax.experimental.pallas import tpu as pltpu
from jax.sharding import PartitionSpec as P

HIGHEST = lax.Precision.HIGHEST


def partner(value, axis, bit):
    mask = 2**bit
    pairs = [(source, source ^ mask) for source in range(lax.axis_size(axis))]
    return lax.ppermute(value, axis, pairs)


def radices(length_all):
    last_radix = min(128, length_all // 4)
    first_radix = min(32, length_all // last_radix)
    return (first_radix, length_all // (first_radix * last_radix), last_radix)


def rotation(row_count, col_count, modulus):
    product = (
        lax.broadcasted_iota(jnp.int32, (row_count, col_count), 0)
        * lax.broadcasted_iota(jnp.int32, (row_count, col_count), 1)
        % modulus
    )
    angle = product.astype(jnp.float32) * (2.0 * math.pi / modulus)
    return (jnp.cos(angle), -jnp.sin(angle))


def tables(radix_sizes):
    first_radix, mid_radix, last_radix = radix_sizes
    length_all = first_radix * mid_radix * last_radix
    outer_real, outer_imag = rotation(first_radix, first_radix, first_radix)
    mid_real, mid_imag = rotation(mid_radix, mid_radix, mid_radix)
    last_real, last_imag = rotation(last_radix, last_radix, last_radix)
    twist_real, twist_imag = rotation(first_radix, mid_radix * last_radix, length_all)
    twist_real = twist_real.reshape(first_radix, mid_radix, last_radix)
    twist_imag = twist_imag.reshape(first_radix, mid_radix, last_radix)
    inner_real, inner_imag = rotation(mid_radix, last_radix, mid_radix * last_radix)
    return (
        outer_real,
        outer_imag,
        mid_real,
        mid_imag,
        last_real,
        last_imag,
        twist_real,
        twist_imag,
        inner_real,
        inner_imag,
    )


def apply_matrix(pattern, real_part, imag_part, matrix_real, matrix_imag):
    out_real = jnp.einsum(pattern, real_part, matrix_real, precision=HIGHEST) - jnp.einsum(
        pattern, imag_part, matrix_imag, precision=HIGHEST
    )
    out_imag = jnp.einsum(pattern, real_part, matrix_imag, precision=HIGHEST) + jnp.einsum(
        pattern, imag_part, matrix_real, precision=HIGHEST
    )
    return (out_real, out_imag)


def complex_times(left_real, left_imag, right_real, right_imag):
    return (
        left_real * right_real - left_imag * right_imag,
        left_real * right_imag + left_imag * right_real,
    )


def forward(real_part, imag_part, table_set, radix_sizes):
    first_radix, mid_radix, last_radix = radix_sizes
    half_first = first_radix // 2
    batch_rows = real_part.shape[0]
    (
        outer_real,
        outer_imag,
        mid_real,
        mid_imag,
        last_real,
        last_imag,
        twist_real,
        twist_imag,
        inner_real,
        inner_imag,
    ) = table_set
    real_part = real_part.reshape(batch_rows, half_first, mid_radix, last_radix)
    imag_part = imag_part.reshape(batch_rows, half_first, mid_radix, last_radix)
    real_part, imag_part = apply_matrix(
        "banm,ak->bknm", real_part, imag_part, outer_real[:half_first], outer_imag[:half_first]
    )
    real_part, imag_part = complex_times(real_part, imag_part, twist_real, twist_imag)
    real_part, imag_part = apply_matrix("bknm,nj->bkjm", real_part, imag_part, mid_real, mid_imag)
    real_part, imag_part = complex_times(real_part, imag_part, inner_real, inner_imag)
    return apply_matrix("bkjm,mq->bkjq", real_part, imag_part, last_real, last_imag)


def inverse(real_part, imag_part, table_set, radix_sizes):
    first_radix, mid_radix, last_radix = radix_sizes
    half_first = first_radix // 2
    batch_rows = real_part.shape[0]
    (
        outer_real,
        outer_imag,
        mid_real,
        mid_imag,
        last_real,
        last_imag,
        twist_real,
        twist_imag,
        inner_real,
        inner_imag,
    ) = table_set
    real_part, imag_part = apply_matrix(
        "bkjq,mq->bkjm", real_part, imag_part, last_real / last_radix, -last_imag / last_radix
    )
    real_part, imag_part = complex_times(real_part, imag_part, inner_real, -inner_imag)
    real_part, imag_part = apply_matrix(
        "bkjm,nj->bknm", real_part, imag_part, mid_real / mid_radix, -mid_imag / mid_radix
    )
    real_part, imag_part = complex_times(real_part, imag_part, twist_real, -twist_imag)
    matrix_real = outer_real[:half_first] / first_radix
    matrix_imag = -outer_imag[:half_first] / first_radix
    out_real, out_imag = apply_matrix(
        "bknm,ak->banm", real_part, imag_part, matrix_real, matrix_imag
    )
    return (out_real.reshape(batch_rows, -1), out_imag.reshape(batch_rows, -1))


def spectrum(decay_rows, residue_rows, radix_sizes, seq_length):
    first_radix, mid_radix, last_radix = radix_sizes
    length_all = first_radix * mid_radix * last_radix
    poles = decay_rows.shape[1]
    shape_all = (first_radix, mid_radix, last_radix)
    frequency = (
        lax.broadcasted_iota(jnp.int32, shape_all, 0)
        + first_radix * lax.broadcasted_iota(jnp.int32, shape_all, 1)
        + first_radix * mid_radix * lax.broadcasted_iota(jnp.int32, shape_all, 2)
    )
    half_angle = frequency.astype(jnp.float32) * (math.pi / length_all)
    sin_half = jnp.sin(half_angle)
    sin_full = jnp.sin(2.0 * half_angle)
    parity_sign = (1 - 2 * (frequency % 2)).astype(jnp.float32)

    def add_pole(pole_index, running):
        run_real, run_imag = running
        rate_col = lax.dynamic_slice_in_dim(decay_rows, pole_index, 1, 1).reshape(-1, 1, 1, 1)
        weight = lax.dynamic_slice_in_dim(residue_rows, pole_index, 1, 1).reshape(
            -1, 1, 1, 1
        ) * jnp.sqrt(2.0 * rate_col / poles)
        retained = jnp.exp(-rate_col)
        den_real = -jnp.expm1(-rate_col) + 2.0 * retained * sin_half * sin_half
        den_imag = retained * sin_full
        pole_scale = (
            weight
            * (1.0 - jnp.exp(-rate_col * seq_length) * parity_sign)
            / (den_real * den_real + den_imag * den_imag)
        )
        return (run_real + pole_scale * den_real, run_imag - pole_scale * den_imag)

    zeros_all = jnp.zeros((decay_rows.shape[0],) + shape_all, jnp.float32)
    return lax.fori_loop(0, poles, add_pole, (zeros_all, zeros_all))


def general(x_gate, x_post, values, decay, residue, w_out):
    tok_rows, block_width = x_gate.shape
    ctx_count = lax.axis_size("ctx")
    tp_count = lax.axis_size("tp")
    chan_group = block_width // ctx_count
    seq_length = tok_rows * ctx_count
    radix_sizes = radices(2 * seq_length)
    table_set = tables(radix_sizes)
    first_row = lax.axis_index("ctx") * chan_group
    own_rate = lax.dynamic_slice_in_dim(decay, first_row, chan_group, 1)
    own_residue = lax.dynamic_slice_in_dim(residue, first_row, chan_group, 1)
    own_spec = [
        spectrum(own_rate[filter_index], own_residue[filter_index], radix_sizes, seq_length)
        for filter_index in range(2)
    ]
    forward_rows = [x_gate, values] + [x_post]
    row_count = len(forward_rows)
    base_rows = jnp.stack(forward_rows)
    copied = base_rows
    for bit_index in range(tp_count.bit_length() - 1):
        copied = partner(copied, "tp", bit_index)
    sent_rows = jnp.concatenate([base_rows, copied[:, :, ::-1]], axis=0)
    received = lax.all_to_all(
        jnp.swapaxes(sent_rows, 1, 2), "ctx", split_axis=1, concat_axis=2, tiled=True
    )
    gate_fwd = received[0].astype(jnp.float32)
    value_fwd = received[1].astype(jnp.float32)
    mirrored = received[row_count:, :, ::-1].astype(jnp.float32)
    spec_real, spec_imag = forward(value_fwd, mirrored[1], table_set, radix_sizes)
    spec_real, spec_imag = complex_times(spec_real, spec_imag, own_spec[0][0], own_spec[0][1])
    along_fwd, along_rev = inverse(spec_real, spec_imag, table_set, radix_sizes)
    spec_real, spec_imag = forward(
        gate_fwd * along_fwd, mirrored[0] * along_rev, table_set, radix_sizes
    )
    spec_real, spec_imag = complex_times(spec_real, spec_imag, own_spec[1][0], own_spec[1][1])
    sum_fwd, sum_rev = inverse(spec_real, spec_imag, table_set, radix_sizes)
    sum_fwd = received[2].astype(jnp.float32) * sum_fwd
    sum_rev = mirrored[2] * sum_rev
    results = jnp.stack([sum_fwd, sum_rev[:, ::-1]])
    returned = lax.all_to_all(
        results.astype(jnp.bfloat16), "ctx", split_axis=2, concat_axis=1, tiled=True
    ).astype(results.dtype)
    flipped = returned[1, ::-1, :]
    for bit_index in range(tp_count.bit_length() - 1):
        flipped = partner(flipped.astype(jnp.bfloat16), "tp", bit_index).astype(flipped.dtype)
    total_rows = returned[0] + flipped
    total_rows = total_rows.T
    mixed_rows = total_rows.astype(jnp.bfloat16)
    whole_rows = lax.all_gather(mixed_rows, "tp", axis=1, tiled=True)
    projected = lax.dot_general(
        whole_rows,
        lax.all_gather(w_out, "ctx", axis=0, tiled=True),
        (((1,), (1,)), ((), ())),
        preferred_element_type=jnp.float32,
    )
    return projected.astype(jnp.bfloat16)


def cycle(row_factor, col_factor, modulus):
    quarter = modulus // 4
    turned = row_factor * col_factor + quarter // 2
    quadrant = turned // quarter % 4
    angle = (turned % quarter - quarter // 2).astype(jnp.float32) * (2.0 * math.pi / modulus)
    square = angle * angle

    def series(first):
        total = jnp.zeros_like(square)
        for power in range(first + 10, first, -2):
            total = (total + (-1.0) ** ((power - first) // 2) / math.factorial(power)) * square
        return total

    cos = 1.0 + series(0)
    sin = angle + angle * series(1)
    odd = quadrant % 2 == 1
    cos, sin = jnp.where(odd, sin, cos), jnp.where(odd, cos, sin)
    return jnp.where((quadrant == 1) | (quadrant == 2), -cos, cos), jnp.where(quadrant >= 2, -sin, sin)


def put_tables(table_ref, back_ref):
    block = back_ref.shape[1]
    modulus = 4 * block
    coarse = 16
    rows = lax.broadcasted_iota(jnp.int32, (coarse, block), 0)
    cols = lax.broadcasted_iota(jnp.int32, (coarse, block), 1)

    def parts(big, small):
        for place in range(block // coarse):
            big_cos, big_sin = (part[place : place + 1] for part in big)
            cos = halves(big_cos * small[0] - big_sin * small[1])
            sin = halves(-(big_sin * small[0] + big_cos * small[1]))
            yield place * coarse, cos, sin

    def put(ref, first, columns, value):
        ref[first : first + coarse, columns] = value[0]
        low = first + ref.shape[0] // 2
        ref[low : low + coarse, columns] = value[1]

    frequency = 2 * cols + 1
    for first, cos, sin in parts(cycle(coarse * rows, frequency, modulus), cycle(rows, frequency, modulus)):
        put(table_ref, first, slice(0, block), cos)
        put(table_ref, first, slice(block, 2 * block), sin)
    for first, cos, sin in parts(cycle(2 * coarse * rows, cols, modulus), cycle(2 * rows + 1, cols, modulus)):
        put(back_ref, first, slice(0, block), cos)
        put(back_ref, block + first, slice(0, block), sin)


def halves(value):
    high = value.astype(jnp.bfloat16)
    return high, (value - high.astype(jnp.float32)).astype(jnp.bfloat16)


def mul(left, right):
    return jnp.dot(left, right, preferred_element_type=jnp.float32)


def mul3(high, low, table_ref):
    left = jnp.concatenate([high, high, low], axis=1)
    return mul(left, jnp.concatenate([table_ref[...], table_ref[: table_ref.shape[0] // 2]], axis=0))


def mul2(value, table_ref):
    return mul(jnp.concatenate([value, value], axis=1), table_ref[...])


def pack_kernel(
    gate_hbm, value_hbm, post_hbm, decay_hbm, residue_hbm,
    out_hbm, own_hbm, sent_hbm, held_ref, cut_ref, ready_ref, sems, out_sems,
):
    ctx_count, _, group, tok = out_hbm.shape
    width = gate_hbm.shape[1]
    half = decay_hbm.shape[0]
    position = lax.axis_index("ctx")
    pairs = []
    for place, index in enumerate((position, ctx_count - 1 - position)):
        columns = pl.ds(pl.multiple_of(index * group // tok * tok, tok), tok)
        pairs += [(decay_hbm.at[:, columns], cut_ref.at[place, :half]), (residue_hbm.at[:, columns], cut_ref.at[place, half:])]
    pairs += [(source, held_ref.at[place]) for place, source in enumerate((value_hbm, gate_hbm, post_hbm))]
    copies = [pltpu.make_async_copy(*pair, sems.at[place]) for place, pair in enumerate(pairs)]
    for copy in copies:
        copy.start()
    sends = []
    for place, target in enumerate((own_hbm, sent_hbm)):
        copies[2 * place].wait()
        copies[2 * place + 1].wait()
        sends.append(pltpu.make_async_copy(cut_ref.at[place], target, out_sems.at[3 + place]))
        sends[-1].start()
    for place, copy in enumerate(copies[4:]):
        copy.wait()
        for first in range(0, width, tok):
            turned = held_ref[place, :, first : first + tok].T
            for part in range(tok // group):
                ready_ref[first // group + part, place] = turned[part * group : (part + 1) * group]
        sends.append(pltpu.make_async_copy(ready_ref.at[:, place], out_hbm.at[:, place], out_sems.at[place]))
        sends[-1].start()
    for send in sends:
        send.wait()


def mirror_rows(value):
    row = lax.broadcasted_iota(jnp.int32, (8, value.shape[1]), 0)
    result = []
    for first in range(value.shape[0] - 8, -1, -8):
        part = value[first : first + 8]
        for shift in (1, 2, 4):
            part = jnp.where(row & shift == 0, pltpu.roll(part, 8 - shift, 0), pltpu.roll(part, shift, 0))
        result.append(part)
    return jnp.concatenate(result, axis=0)


def put_filter(poles, index, turned, time_ref):
    lanes = 128
    rows_all, block = time_ref.shape
    group = turned.shape[0]
    ramp = lax.broadcasted_iota(jnp.int32, (8, lanes), 1).astype(jnp.float32)
    for row in range(0, group, 8):
        rows = slice(row, row + 8)
        rate = turned[rows, index * poles : (index + 1) * poles]
        scale = turned[rows, (2 + index) * poles : (3 + index) * poles] * (jnp.sqrt(rate * (2.0 / poles)) / block)
        slope = rate * -math.log2(math.e)
        jump = jnp.exp2(slope * lanes)
        sums = [None] * (rows_all // group * block // lanes)
        for pole in range(poles):
            term = scale[:, pole : pole + 1] * jnp.exp2(slope[:, pole : pole + 1] * ramp)
            step = jnp.broadcast_to(jump[:, pole : pole + 1], (8, lanes))
            for place in range(len(sums)):
                sums[place] = term if pole == 0 else sums[place] + term
                if place + 1 < len(sums):
                    term = term * step
        for place, total in enumerate(sums):
            lag, lane = divmod(place * lanes, block)
            time_ref[lag * group + row : lag * group + row + 8, lane : lane + lanes] = total


def put_spectra(spec, out_ref):
    blocks, group, twice = out_ref.shape
    block = twice // 2
    sign = (1 - 2 * (lax.broadcasted_iota(jnp.int32, (group, block), 1) % 2)).astype(jnp.float32)
    for lag in range(blocks):
        real = spec[lag * group : (lag + 1) * group, :block]
        imag = spec[lag * group : (lag + 1) * group, block:]
        if lag > 0:
            real = real - sign * spec[(lag - 1) * group : lag * group, block:]
            imag = imag + sign * spec[(lag - 1) * group : lag * group, :block]
        out_ref[lag, :, :block] = real
        out_ref[lag, :, block:] = imag


def filter_kernel(poles, par_ref, out_ref, table_ref, back_ref, time_ref, turned_ref):
    group = out_ref.shape[2]
    put_tables(table_ref, back_ref)
    turned_ref[...] = par_ref[...].T
    turned = turned_ref[pl.ds(pl.multiple_of(lax.axis_index("ctx") * group % turned_ref.shape[0], group), group)]
    put_filter(poles, 0, turned, time_ref.at[0])
    spec = mul3(*halves(time_ref[0]), table_ref)
    put_filter(poles, 1, turned, time_ref.at[1])
    put_spectra(spec, out_ref.at[0])
    put_spectra(mul3(*halves(time_ref[1]), table_ref), out_ref.at[1])


def conv_kernel(
    poles, x_ref, own_ref, par_ref, table_ref, back_ref, out_hbm,
    paired_ref, time_ref, turned_ref, spec_ref, high_ref, ready_ref, sems,
):
    turned_ref[...] = par_ref[...].T
    blocks, group, twice = own_ref.shape[1:]
    block = twice // 2
    rows_all = blocks * group
    tall, wide = 16, 128
    pieces = x_ref.shape[0] // blocks
    first = (x_ref.shape[0] - 1 - lax.axis_index("ctx")) * group % turned_ref.shape[0]
    turned = mirror_rows(turned_ref[pl.ds(pl.multiple_of(first, group), group)])

    def rows_of(position):
        return jnp.concatenate(
            [
                jnp.concatenate([x_ref[m * pieces + s, position] for s in range(pieces)], axis=1)
                for m in range(blocks)
            ],
            axis=0,
        )

    def times(index, side, source, row, lane):
        data = []
        for m in range(blocks):
            rows = slice(source + m * group + row, source + m * group + row + tall)
            data.append((spec_ref[rows, lane : lane + wide], spec_ref[rows, block + lane : block + lane + wide]))
        sums = [None] * blocks
        for lag in range(blocks):
            h_ref = (own_ref, paired_ref)[side]
            f_re = h_ref[index, lag, row : row + tall, lane : lane + wide]
            f_im = h_ref[index, lag, row : row + tall, block + lane : block + lane + wide]
            for m in range(blocks - lag):
                target, (d_re, d_im) = (m + lag, data[m]) if side == 0 else (m, data[m + lag])
                if side == 0:
                    real, imag = f_re * d_re - f_im * d_im, f_re * d_im + f_im * d_re
                else:
                    real, imag = f_re * d_re + f_im * d_im, f_re * d_im - f_im * d_re
                if sums[target] is not None:
                    real, imag = sums[target][0] + real, sums[target][1] + imag
                sums[target] = (real, imag)
        return sums

    def to_time(rows):
        return mul2(high_ref[rows], back_ref)

    def keep(target, row, lane, sums):
        for m in range(blocks):
            rows = slice(target + m * group + row, target + m * group + row + tall)
            for part in range(2):
                cols = slice(part * block + lane, part * block + lane + wide)
                high_ref[rows, cols] = sums[m][part].astype(jnp.bfloat16)

    chunks = [(row, lane) for row in range(0, group, tall) for lane in range(0, block, wide)]

    value = rows_of(0)
    gate = rows_of(1).astype(jnp.float32)
    spec_ref[:rows_all] = mul2(value, table_ref)
    sides = [slice(side * rows_all, (side + 1) * rows_all) for side in range(2)]
    put_filter(poles, 0, turned, time_ref.at[0])
    spec = mul3(*halves(time_ref[0]), table_ref)
    for row, lane in chunks:
        keep(0, row, lane, times(0, 0, 0, row, lane))
    put_spectra(spec, paired_ref.at[0])
    gated = [gate * to_time(sides[0])]
    put_filter(poles, 1, turned, time_ref.at[1])
    for row, lane in chunks:
        keep(rows_all, row, lane, times(0, 1, 0, row, lane))
    gated.append(gate * to_time(sides[1]))
    spec = mul3(*halves(time_ref[1]), table_ref)
    for side in range(2):
        spec_ref[sides[side]] = mul3(*halves(gated[side]), table_ref)
    put_spectra(spec, paired_ref.at[1])
    for row, lane in chunks:
        ahead, back = times(1, 0, 0, row, lane), times(1, 1, rows_all, row, lane)
        keep(0, row, lane, [(a[0] + b[0], a[1] + b[1]) for a, b in zip(ahead, back)])
    post = rows_of(2)
    tok = block // pieces
    sends = []
    for part in range(2):
        rows = slice(part * rows_all // 2, (part + 1) * rows_all // 2)
        summed = to_time(rows)
        mixed = (post[rows].astype(jnp.float32) * summed).astype(jnp.bfloat16)
        first = part * blocks // 2 * pieces
        for m in range(blocks // 2):
            for s in range(pieces):
                ready_ref[first + m * pieces + s] = mixed[m * group : (m + 1) * group, s * tok : (s + 1) * tok]
        span = pl.ds(first, blocks // 2 * pieces)
        for copy in range(out_hbm.shape[1]):
            sends.append(pltpu.make_async_copy(ready_ref.at[span], out_hbm.at[span, copy], sems.at[part, copy]))
            sends[-1].start()
    for send in sends:
        send.wait()


def project_kernel(mixed_ref, *refs):
    w_refs, (out_hbm, held_ref, ready_ref, sems) = refs[:-4], refs[-4:]
    rows = w_refs[0].shape[0]
    tile = 2 * rows
    position = lax.axis_index("ctx")
    even = pl.multiple_of(position % 2 * rows, rows)
    odd = pl.multiple_of((1 - position % 2) * rows, rows)
    ctx_count, tp_count = mixed_ref.shape[:2]
    mixed = jnp.concatenate([mixed_ref[i, z] for z in range(tp_count) for i in range(ctx_count)], axis=0)
    sends = []
    for half, half_refs in enumerate((w_refs[:4], w_refs[4:])):
        total = mul(jnp.concatenate([w_ref[...] for w_ref in half_refs], axis=0), mixed)
        for pair in range(2):
            place = 2 * half + pair
            held_ref[place, pl.ds(even, rows)] = total[pair * tile : pair * tile + rows]
            held_ref[place, pl.ds(odd, rows)] = total[pair * tile + rows : (pair + 1) * tile]
            ready_ref[place] = held_ref[place].T.astype(jnp.bfloat16)
            columns = pl.ds(pl.multiple_of((position // 2 ^ place) * tile, tile), tile)
            sends.append(pltpu.make_async_copy(ready_ref.at[place], out_hbm.at[:, columns], sems.at[place]))
            sends[-1].start()
    for send in sends:
        send.wait()


def whole_call(kernel, out_shape, scratch, flops, nbytes, *operands, in_hbm=0, out_hbm=()):
    results = pl.pallas_call(
        kernel,
        out_shape=out_shape,
        in_specs=[
            pl.BlockSpec(memory_space=pltpu.HBM if place < in_hbm else pltpu.VMEM) for place in range(len(operands))
        ],
        out_specs=[
            pl.BlockSpec(memory_space=pltpu.HBM if place in out_hbm else pltpu.VMEM) for place in range(len(out_shape))
        ],
        scratch_shapes=scratch,
        cost_estimate=pl.CostEstimate(flops=flops, bytes_accessed=nbytes, transcendentals=0),
        compiler_params=pltpu.CompilerParams(vmem_limit_bytes=None if in_hbm else 32 * 2**20),
    )(*operands)
    return results if len(out_shape) > 1 else results[0]


def blocked(x_gate, x_post, values, decay, residue, w_out):
    tok, width = x_gate.shape
    ctx_count = lax.axis_size("ctx")
    tp_count = lax.axis_size("tp")
    group = width // ctx_count
    poles = decay.shape[2]
    block = 2 * tok
    blocks = tok * ctx_count // block
    rows, channels = w_out.shape
    half = 2 * poles

    packed, own, mirrored = whole_call(
        pack_kernel,
        (
            jax.ShapeDtypeStruct((ctx_count, 3, group, tok), jnp.bfloat16),
            jax.ShapeDtypeStruct((2 * half, tok), jnp.float32),
            jax.ShapeDtypeStruct((2 * half, tok), jnp.float32),
        ),
        [
            pltpu.VMEM((3, tok, width), jnp.bfloat16),
            pltpu.VMEM((2, 2 * half, tok), jnp.float32),
            pltpu.VMEM((ctx_count, 3, group, tok), jnp.bfloat16),
            pltpu.SemaphoreType.DMA((7,)),
            pltpu.SemaphoreType.DMA((5,)),
        ],
        0,
        6 * tok * width * 2,
        x_gate,
        values,
        x_post,
        jnp.swapaxes(decay, 1, 2).reshape(half, width),
        jnp.swapaxes(residue, 1, 2).reshape(half, width),
        in_hbm=5,
        out_hbm=(0, 1, 2),
    )
    paired = lax.ppermute(mirrored, "tp", [(z, tp_count - 1 - z) for z in range(tp_count)])
    received = lax.all_to_all(packed, "ctx", split_axis=0, concat_axis=0, tiled=True)

    w_late, mirrored = lax.optimization_barrier((w_out, mirrored))
    w_x, w_y = partner(w_late, "ctx", 1), partner(w_late, "ctx", 2)
    own_spectra, table, back_table = whole_call(
        functools.partial(filter_kernel, poles),
        (
            jax.ShapeDtypeStruct((2, blocks, group, 2 * block), jnp.float32),
            jax.ShapeDtypeStruct((2 * block, 2 * block), jnp.bfloat16),
            jax.ShapeDtypeStruct((4 * block, block), jnp.bfloat16),
        ),
        [
            pltpu.VMEM((2, blocks * group, block), jnp.float32),
            pltpu.VMEM((tok, 2 * half), jnp.float32),
        ],
        2 * 2 * blocks * group * block * 2 * block * 3,
        2 * blocks * group * 2 * block * 4,
        own,
    )
    mixed = whole_call(
        functools.partial(conv_kernel, poles),
        (jax.ShapeDtypeStruct((ctx_count, tp_count, group, tok), jnp.bfloat16),),
        [
            pltpu.VMEM((2, blocks, group, 2 * block), jnp.float32),
            pltpu.VMEM((2, blocks * group, block), jnp.float32),
            pltpu.VMEM((tok, 2 * half), jnp.float32),
            pltpu.VMEM((2 * blocks * group, 2 * block), jnp.float32),
            pltpu.VMEM((2 * blocks * group, 2 * block), jnp.bfloat16),
            pltpu.VMEM((ctx_count, group, tok), jnp.bfloat16),
            pltpu.SemaphoreType.DMA((2, tp_count)),
        ],
        2 * 8 * blocks * group * block * 2 * block * 3,
        4 * blocks * group * 2 * block * 4,
        received,
        own_spectra,
        paired,
        table,
        back_table,
        out_hbm=(0,),
    )
    mixed, w_x, w_y, w_own = lax.optimization_barrier((mixed, w_x, w_y, w_out))
    lower = rows // 2
    w_far = [partner(w_x[:lower], "ctx", 2), partner(w_y[lower:], "ctx", 1)]
    w_blocks = []
    for block in (w_own, w_x, w_y):
        w_blocks += [block, partner(block, "ctx", 0)]
    w_blocks += w_far + [partner(block, "ctx", 0) for block in w_far]
    every = lax.all_to_all(
        mixed.reshape(ctx_count * tp_count, group, tok), ("ctx", "tp"), split_axis=0, concat_axis=0, tiled=True
    ).reshape(ctx_count, tp_count, group, tok)
    return whole_call(
        project_kernel,
        (jax.ShapeDtypeStruct((tok, rows * ctx_count), jnp.bfloat16),),
        [
            pltpu.VMEM((ctx_count // 2, 2 * rows, tok), jnp.float32),
            pltpu.VMEM((ctx_count // 2, tok, 2 * rows), jnp.bfloat16),
            pltpu.SemaphoreType.DMA((ctx_count // 2,)),
        ],
        2 * tok * rows * ctx_count * channels,
        2 * rows * ctx_count * channels,
        every,
        *w_blocks,
        out_hbm=(0,),
    )


def local(x_gate, x_post, values, decay, residue, w_out):
    tok, width = x_gate.shape
    ctx_count = lax.axis_size("ctx")
    if tok == 128 and width == 512 and ctx_count == 8 and w_out.shape[0] == 64 and lax.axis_size("tp") == 4:
        return blocked(x_gate, x_post, values, decay, residue, w_out)
    return general(x_gate, x_post, values, decay, residue, w_out)


def solution(mesh):
    in_specs = (
        P("ctx", "tp"),
        P("ctx", "tp"),
        P("ctx", "tp"),
        P(None, "tp", None),
        P(None, "tp", None),
        P(("tp", "ctx"), None),
    )
    out_specs = P("ctx", "tp")
    return jax.shard_map(local, mesh=mesh, in_specs=in_specs, out_specs=out_specs, check_vma=False)
```

```python
import functools
import math

import jax
import jax.numpy as jnp
from jax import lax
from jax.experimental import pallas as pl
from jax.experimental.pallas import tpu as pltpu
from jax.sharding import PartitionSpec as P

HIGHEST = lax.Precision.HIGHEST


def partner(value, axis, bit):
    mask = 2**bit
    pairs = [(source, source ^ mask) for source in range(lax.axis_size(axis))]
    return lax.ppermute(value, axis, pairs)


def radices(length_all):
    last_radix = min(128, length_all // 4)
    first_radix = min(32, length_all // last_radix)
    return (first_radix, length_all // (first_radix * last_radix), last_radix)


def rotation(row_count, col_count, modulus):
    product = (
        lax.broadcasted_iota(jnp.int32, (row_count, col_count), 0)
        * lax.broadcasted_iota(jnp.int32, (row_count, col_count), 1)
        % modulus
    )
    angle = product.astype(jnp.float32) * (2.0 * math.pi / modulus)
    return (jnp.cos(angle), -jnp.sin(angle))


def tables(radix_sizes):
    first_radix, mid_radix, last_radix = radix_sizes
    length_all = first_radix * mid_radix * last_radix
    outer_real, outer_imag = rotation(first_radix, first_radix, first_radix)
    mid_real, mid_imag = rotation(mid_radix, mid_radix, mid_radix)
    last_real, last_imag = rotation(last_radix, last_radix, last_radix)
    twist_real, twist_imag = rotation(first_radix, mid_radix * last_radix, length_all)
    twist_real = twist_real.reshape(first_radix, mid_radix, last_radix)
    twist_imag = twist_imag.reshape(first_radix, mid_radix, last_radix)
    inner_real, inner_imag = rotation(mid_radix, last_radix, mid_radix * last_radix)
    return (
        outer_real,
        outer_imag,
        mid_real,
        mid_imag,
        last_real,
        last_imag,
        twist_real,
        twist_imag,
        inner_real,
        inner_imag,
    )


def apply_matrix(pattern, real_part, imag_part, matrix_real, matrix_imag):
    out_real = jnp.einsum(pattern, real_part, matrix_real, precision=HIGHEST) - jnp.einsum(
        pattern, imag_part, matrix_imag, precision=HIGHEST
    )
    out_imag = jnp.einsum(pattern, real_part, matrix_imag, precision=HIGHEST) + jnp.einsum(
        pattern, imag_part, matrix_real, precision=HIGHEST
    )
    return (out_real, out_imag)


def complex_times(left_real, left_imag, right_real, right_imag):
    return (
        left_real * right_real - left_imag * right_imag,
        left_real * right_imag + left_imag * right_real,
    )


def forward(real_part, imag_part, table_set, radix_sizes):
    first_radix, mid_radix, last_radix = radix_sizes
    half_first = first_radix // 2
    batch_rows = real_part.shape[0]
    (
        outer_real,
        outer_imag,
        mid_real,
        mid_imag,
        last_real,
        last_imag,
        twist_real,
        twist_imag,
        inner_real,
        inner_imag,
    ) = table_set
    real_part = real_part.reshape(batch_rows, half_first, mid_radix, last_radix)
    imag_part = imag_part.reshape(batch_rows, half_first, mid_radix, last_radix)
    real_part, imag_part = apply_matrix(
        "banm,ak->bknm", real_part, imag_part, outer_real[:half_first], outer_imag[:half_first]
    )
    real_part, imag_part = complex_times(real_part, imag_part, twist_real, twist_imag)
    real_part, imag_part = apply_matrix("bknm,nj->bkjm", real_part, imag_part, mid_real, mid_imag)
    real_part, imag_part = complex_times(real_part, imag_part, inner_real, inner_imag)
    return apply_matrix("bkjm,mq->bkjq", real_part, imag_part, last_real, last_imag)


def inverse(real_part, imag_part, table_set, radix_sizes):
    first_radix, mid_radix, last_radix = radix_sizes
    half_first = first_radix // 2
    batch_rows = real_part.shape[0]
    (
        outer_real,
        outer_imag,
        mid_real,
        mid_imag,
        last_real,
        last_imag,
        twist_real,
        twist_imag,
        inner_real,
        inner_imag,
    ) = table_set
    real_part, imag_part = apply_matrix(
        "bkjq,mq->bkjm", real_part, imag_part, last_real / last_radix, -last_imag / last_radix
    )
    real_part, imag_part = complex_times(real_part, imag_part, inner_real, -inner_imag)
    real_part, imag_part = apply_matrix(
        "bkjm,nj->bknm", real_part, imag_part, mid_real / mid_radix, -mid_imag / mid_radix
    )
    real_part, imag_part = complex_times(real_part, imag_part, twist_real, -twist_imag)
    matrix_real = outer_real[:half_first] / first_radix
    matrix_imag = -outer_imag[:half_first] / first_radix
    out_real, out_imag = apply_matrix(
        "bknm,ak->banm", real_part, imag_part, matrix_real, matrix_imag
    )
    return (out_real.reshape(batch_rows, -1), out_imag.reshape(batch_rows, -1))


def spectrum(decay_rows, residue_rows, radix_sizes, seq_length):
    first_radix, mid_radix, last_radix = radix_sizes
    length_all = first_radix * mid_radix * last_radix
    poles = decay_rows.shape[1]
    shape_all = (first_radix, mid_radix, last_radix)
    frequency = (
        lax.broadcasted_iota(jnp.int32, shape_all, 0)
        + first_radix * lax.broadcasted_iota(jnp.int32, shape_all, 1)
        + first_radix * mid_radix * lax.broadcasted_iota(jnp.int32, shape_all, 2)
    )
    half_angle = frequency.astype(jnp.float32) * (math.pi / length_all)
    sin_half = jnp.sin(half_angle)
    sin_full = jnp.sin(2.0 * half_angle)
    parity_sign = (1 - 2 * (frequency % 2)).astype(jnp.float32)

    def add_pole(pole_index, running):
        run_real, run_imag = running
        rate_col = lax.dynamic_slice_in_dim(decay_rows, pole_index, 1, 1).reshape(-1, 1, 1, 1)
        weight = lax.dynamic_slice_in_dim(residue_rows, pole_index, 1, 1).reshape(
            -1, 1, 1, 1
        ) * jnp.sqrt(2.0 * rate_col / poles)
        retained = jnp.exp(-rate_col)
        den_real = -jnp.expm1(-rate_col) + 2.0 * retained * sin_half * sin_half
        den_imag = retained * sin_full
        pole_scale = (
            weight
            * (1.0 - jnp.exp(-rate_col * seq_length) * parity_sign)
            / (den_real * den_real + den_imag * den_imag)
        )
        return (run_real + pole_scale * den_real, run_imag - pole_scale * den_imag)

    zeros_all = jnp.zeros((decay_rows.shape[0],) + shape_all, jnp.float32)
    return lax.fori_loop(0, poles, add_pole, (zeros_all, zeros_all))


def general(x_gate, x_post, values, decay, residue, w_out):
    tok_rows, block_width = x_gate.shape
    ctx_count = lax.axis_size("ctx")
    tp_count = lax.axis_size("tp")
    chan_group = block_width // ctx_count
    seq_length = tok_rows * ctx_count
    radix_sizes = radices(2 * seq_length)
    table_set = tables(radix_sizes)
    first_row = lax.axis_index("ctx") * chan_group
    own_rate = lax.dynamic_slice_in_dim(decay, first_row, chan_group, 1)
    own_residue = lax.dynamic_slice_in_dim(residue, first_row, chan_group, 1)
    own_spec = [
        spectrum(own_rate[filter_index], own_residue[filter_index], radix_sizes, seq_length)
        for filter_index in range(2)
    ]
    forward_rows = [x_gate, values] + [x_post]
    row_count = len(forward_rows)
    base_rows = jnp.stack(forward_rows)
    copied = base_rows
    for bit_index in range(tp_count.bit_length() - 1):
        copied = partner(copied, "tp", bit_index)
    sent_rows = jnp.concatenate([base_rows, copied[:, :, ::-1]], axis=0)
    received = lax.all_to_all(
        jnp.swapaxes(sent_rows, 1, 2), "ctx", split_axis=1, concat_axis=2, tiled=True
    )
    gate_fwd = received[0].astype(jnp.float32)
    value_fwd = received[1].astype(jnp.float32)
    mirrored = received[row_count:, :, ::-1].astype(jnp.float32)
    spec_real, spec_imag = forward(value_fwd, mirrored[1], table_set, radix_sizes)
    spec_real, spec_imag = complex_times(spec_real, spec_imag, own_spec[0][0], own_spec[0][1])
    along_fwd, along_rev = inverse(spec_real, spec_imag, table_set, radix_sizes)
    spec_real, spec_imag = forward(
        gate_fwd * along_fwd, mirrored[0] * along_rev, table_set, radix_sizes
    )
    spec_real, spec_imag = complex_times(spec_real, spec_imag, own_spec[1][0], own_spec[1][1])
    sum_fwd, sum_rev = inverse(spec_real, spec_imag, table_set, radix_sizes)
    sum_fwd = received[2].astype(jnp.float32) * sum_fwd
    sum_rev = mirrored[2] * sum_rev
    results = jnp.stack([sum_fwd, sum_rev[:, ::-1]])
    returned = lax.all_to_all(
        results.astype(jnp.bfloat16), "ctx", split_axis=2, concat_axis=1, tiled=True
    ).astype(results.dtype)
    flipped = returned[1, ::-1, :]
    for bit_index in range(tp_count.bit_length() - 1):
        flipped = partner(flipped.astype(jnp.bfloat16), "tp", bit_index).astype(flipped.dtype)
    total_rows = returned[0] + flipped
    total_rows = total_rows.T
    mixed_rows = total_rows.astype(jnp.bfloat16)
    whole_rows = lax.all_gather(mixed_rows, "tp", axis=1, tiled=True)
    projected = lax.dot_general(
        whole_rows,
        lax.all_gather(w_out, "ctx", axis=0, tiled=True),
        (((1,), (1,)), ((), ())),
        preferred_element_type=jnp.float32,
    )
    return projected.astype(jnp.bfloat16)


def cycle(row_factor, col_factor, modulus):
    quarter = modulus // 4
    turned = row_factor * col_factor + quarter // 2
    quadrant = turned // quarter % 4
    angle = (turned % quarter - quarter // 2).astype(jnp.float32) * (2.0 * math.pi / modulus)
    square = angle * angle

    def series(first):
        total = jnp.zeros_like(square)
        for power in range(first + 10, first, -2):
            total = (total + (-1.0) ** ((power - first) // 2) / math.factorial(power)) * square
        return total

    cos = 1.0 + series(0)
    sin = angle + angle * series(1)
    odd = quadrant % 2 == 1
    cos, sin = jnp.where(odd, sin, cos), jnp.where(odd, cos, sin)
    return jnp.where((quadrant == 1) | (quadrant == 2), -cos, cos), jnp.where(quadrant >= 2, -sin, sin)


def put_tables(table_ref, back_ref):
    block = back_ref.shape[1]
    modulus = 4 * block
    coarse = 16
    rows = lax.broadcasted_iota(jnp.int32, (coarse, block), 0)
    cols = lax.broadcasted_iota(jnp.int32, (coarse, block), 1)

    def parts(big, small):
        for place in range(block // coarse):
            big_cos, big_sin = (part[place : place + 1] for part in big)
            cos = halves(big_cos * small[0] - big_sin * small[1])
            sin = halves(-(big_sin * small[0] + big_cos * small[1]))
            yield place * coarse, cos, sin

    def put(ref, first, columns, value):
        ref[first : first + coarse, columns] = value[0]
        low = first + ref.shape[0] // 2
        ref[low : low + coarse, columns] = value[1]

    frequency = 2 * cols + 1
    for first, cos, sin in parts(cycle(coarse * rows, frequency, modulus), cycle(rows, frequency, modulus)):
        put(table_ref, first, slice(0, block), cos)
        put(table_ref, first, slice(block, 2 * block), sin)
    for first, cos, sin in parts(cycle(2 * coarse * rows, cols, modulus), cycle(2 * rows + 1, cols, modulus)):
        put(back_ref, first, slice(0, block), cos)
        put(back_ref, block + first, slice(0, block), sin)


def halves(value):
    high = value.astype(jnp.bfloat16)
    return high, (value - high.astype(jnp.float32)).astype(jnp.bfloat16)


def mul(left, right):
    return jnp.dot(left, right, preferred_element_type=jnp.float32)


def mul3(high, low, table_ref):
    left = jnp.concatenate([high, high, low], axis=1)
    return mul(left, jnp.concatenate([table_ref[...], table_ref[: table_ref.shape[0] // 2]], axis=0))


def mul2(value, table_ref):
    return mul(jnp.concatenate([value, value], axis=1), table_ref[...])


def pack_kernel(
    gate_hbm, value_hbm, post_hbm, decay_hbm, residue_hbm,
    out_hbm, own_hbm, sent_hbm, held_ref, cut_ref, ready_ref, sems, out_sems,
):
    ctx_count, _, group, tok = out_hbm.shape
    width = gate_hbm.shape[1]
    half = decay_hbm.shape[0]
    position = lax.axis_index("ctx")
    pairs = []
    for place, index in enumerate((position, ctx_count - 1 - position)):
        columns = pl.ds(pl.multiple_of(index * group // tok * tok, tok), tok)
        pairs += [(decay_hbm.at[:, columns], cut_ref.at[place, :half]), (residue_hbm.at[:, columns], cut_ref.at[place, half:])]
    pairs += [(source, held_ref.at[place]) for place, source in enumerate((value_hbm, gate_hbm, post_hbm))]
    copies = [pltpu.make_async_copy(*pair, sems.at[place]) for place, pair in enumerate(pairs)]
    for copy in copies:
        copy.start()
    sends = []
    for place, target in enumerate((own_hbm, sent_hbm)):
        copies[2 * place].wait()
        copies[2 * place + 1].wait()
        sends.append(pltpu.make_async_copy(cut_ref.at[place], target, out_sems.at[3 + place]))
        sends[-1].start()
    for place, copy in enumerate(copies[4:]):
        copy.wait()
        for first in range(0, width, tok):
            turned = held_ref[place, :, first : first + tok].T
            for part in range(tok // group):
                ready_ref[first // group + part, place] = turned[part * group : (part + 1) * group]
        sends.append(pltpu.make_async_copy(ready_ref.at[:, place], out_hbm.at[:, place], out_sems.at[place]))
        sends[-1].start()
    for send in sends:
        send.wait()


def mirror_rows(value):
    row = lax.broadcasted_iota(jnp.int32, (8, value.shape[1]), 0)
    result = []
    for first in range(value.shape[0] - 8, -1, -8):
        part = value[first : first + 8]
        for shift in (1, 2, 4):
            part = jnp.where(row & shift == 0, pltpu.roll(part, 8 - shift, 0), pltpu.roll(part, shift, 0))
        result.append(part)
    return jnp.concatenate(result, axis=0)


def put_filter(poles, index, turned, time_ref):
    lanes = 128
    rows_all, block = time_ref.shape
    group = turned.shape[0]
    ramp = lax.broadcasted_iota(jnp.int32, (8, lanes), 1).astype(jnp.float32)
    for row in range(0, group, 8):
        rows = slice(row, row + 8)
        rate = turned[rows, index * poles : (index + 1) * poles]
        scale = turned[rows, (2 + index) * poles : (3 + index) * poles] * (jnp.sqrt(rate * (2.0 / poles)) / block)
        slope = rate * -math.log2(math.e)
        sums = [None] * (rows_all // group * block // lanes)
        for pole in range(poles):
            level = jnp.broadcast_to(slope[:, pole : pole + 1], (8, lanes))
            term = scale[:, pole : pole + 1] * jnp.exp2(level * ramp)
            step = jnp.exp2(level * lanes)
            for place in range(len(sums)):
                sums[place] = term if pole == 0 else sums[place] + term
                if place + 1 < len(sums):
                    term = term * step
        for place, total in enumerate(sums):
            lag, lane = divmod(place * lanes, block)
            time_ref[lag * group + row : lag * group + row + 8, lane : lane + lanes] = total


def put_spectra(spec, out_ref):
    blocks, group, twice = out_ref.shape
    block = twice // 2
    sign = (1 - 2 * (lax.broadcasted_iota(jnp.int32, (group, block), 1) % 2)).astype(jnp.float32)
    for lag in range(blocks):
        real = spec[lag * group : (lag + 1) * group, :block]
        imag = spec[lag * group : (lag + 1) * group, block:]
        if lag > 0:
            real = real - sign * spec[(lag - 1) * group : lag * group, block:]
            imag = imag + sign * spec[(lag - 1) * group : lag * group, :block]
        out_ref[lag, :, :block] = real
        out_ref[lag, :, block:] = imag


def filter_kernel(poles, par_ref, out_ref, table_ref, back_ref, time_ref, turned_ref):
    group = out_ref.shape[2]
    put_tables(table_ref, back_ref)
    turned_ref[...] = par_ref[...].T
    turned = turned_ref[pl.ds(pl.multiple_of(lax.axis_index("ctx") * group % turned_ref.shape[0], group), group)]
    put_filter(poles, 0, turned, time_ref.at[0])
    spec = mul3(*halves(time_ref[0]), table_ref)
    put_filter(poles, 1, turned, time_ref.at[1])
    put_spectra(spec, out_ref.at[0])
    put_spectra(mul3(*halves(time_ref[1]), table_ref), out_ref.at[1])


def conv_kernel(
    poles, x_ref, own_ref, par_ref, table_ref, back_ref, out_hbm,
    paired_ref, time_ref, turned_ref, spec_ref, high_ref, low_ref, ready_ref, sems,
):
    turned_ref[...] = par_ref[...].T
    blocks, group, twice = own_ref.shape[1:]
    block = twice // 2
    rows_all = blocks * group
    tall, wide = 16, 128
    pieces = x_ref.shape[0] // blocks
    first = (x_ref.shape[0] - 1 - lax.axis_index("ctx")) * group % turned_ref.shape[0]
    turned = mirror_rows(turned_ref[pl.ds(pl.multiple_of(first, group), group)])

    def rows_of(position):
        return jnp.concatenate(
            [
                jnp.concatenate([x_ref[m * pieces + s, position] for s in range(pieces)], axis=1)
                for m in range(blocks)
            ],
            axis=0,
        )

    def times(index, side, source, row, lane):
        data = []
        for m in range(blocks):
            rows = slice(source + m * group + row, source + m * group + row + tall)
            data.append((spec_ref[rows, lane : lane + wide], spec_ref[rows, block + lane : block + lane + wide]))
        sums = [None] * blocks
        for lag in range(blocks):
            h_ref = (own_ref, paired_ref)[side]
            f_re = h_ref[index, lag, row : row + tall, lane : lane + wide]
            f_im = h_ref[index, lag, row : row + tall, block + lane : block + lane + wide]
            for m in range(blocks - lag):
                target, (d_re, d_im) = (m + lag, data[m]) if side == 0 else (m, data[m + lag])
                if side == 0:
                    real, imag = f_re * d_re - f_im * d_im, f_re * d_im + f_im * d_re
                else:
                    real, imag = f_re * d_re + f_im * d_im, f_re * d_im - f_im * d_re
                if sums[target] is not None:
                    real, imag = sums[target][0] + real, sums[target][1] + imag
                sums[target] = (real, imag)
        return sums

    def keep(target, row, lane, sums, both_parts):
        for m in range(blocks):
            rows = slice(target + m * group + row, target + m * group + row + tall)
            for part in range(2):
                cols = slice(part * block + lane, part * block + lane + wide)
                high_ref[rows, cols], low = halves(sums[m][part])
                if both_parts:
                    low_ref[rows, cols] = low

    chunks = [(row, lane) for row in range(0, group, tall) for lane in range(0, block, wide)]

    value = rows_of(0)
    gate = rows_of(1).astype(jnp.float32)
    spec_ref[:rows_all] = mul2(value, table_ref)
    sides = [slice(side * rows_all, (side + 1) * rows_all) for side in range(2)]
    put_filter(poles, 0, turned, time_ref.at[0])
    spec = mul3(*halves(time_ref[0]), table_ref)
    for row, lane in chunks:
        keep(0, row, lane, times(0, 0, 0, row, lane), True)
    put_spectra(spec, paired_ref.at[0])
    gated = [gate * mul3(high_ref[sides[0]], low_ref[sides[0]], back_ref)]
    put_filter(poles, 1, turned, time_ref.at[1])
    for row, lane in chunks:
        keep(rows_all, row, lane, times(0, 1, 0, row, lane), True)
    gated.append(gate * mul3(high_ref[sides[1]], low_ref[sides[1]], back_ref))
    spec = mul3(*halves(time_ref[1]), table_ref)
    for side in range(2):
        spec_ref[sides[side]] = mul3(*halves(gated[side]), table_ref)
    put_spectra(spec, paired_ref.at[1])
    for row, lane in chunks:
        ahead, back = times(1, 0, 0, row, lane), times(1, 1, rows_all, row, lane)
        keep(0, row, lane, [(a[0] + b[0], a[1] + b[1]) for a, b in zip(ahead, back)], False)
    post = rows_of(2)
    tok = block // pieces
    sends = []
    for part in range(2):
        rows = slice(part * rows_all // 2, (part + 1) * rows_all // 2)
        summed = mul2(high_ref[rows], back_ref)
        mixed = (post[rows].astype(jnp.float32) * summed).astype(jnp.bfloat16)
        first = part * blocks // 2 * pieces
        for m in range(blocks // 2):
            for s in range(pieces):
                ready_ref[first + m * pieces + s] = mixed[m * group : (m + 1) * group, s * tok : (s + 1) * tok]
        span = pl.ds(first, blocks // 2 * pieces)
        for copy in range(out_hbm.shape[1]):
            sends.append(pltpu.make_async_copy(ready_ref.at[span], out_hbm.at[span, copy], sems.at[part, copy]))
            sends[-1].start()
    for send in sends:
        send.wait()


def project_kernel(mixed_ref, *refs):
    w_refs, (out_hbm, held_ref, ready_ref, sems) = refs[:-4], refs[-4:]
    rows = w_refs[0].shape[0]
    tile = 2 * rows
    position = lax.axis_index("ctx")
    even = pl.multiple_of(position % 2 * rows, rows)
    odd = pl.multiple_of((1 - position % 2) * rows, rows)
    ctx_count, tp_count = mixed_ref.shape[:2]
    mixed = jnp.concatenate([mixed_ref[i, z] for z in range(tp_count) for i in range(ctx_count)], axis=0)
    sends = []
    for half, half_refs in enumerate((w_refs[:4], w_refs[4:])):
        total = mul(jnp.concatenate([w_ref[...] for w_ref in half_refs], axis=0), mixed)
        for pair in range(2):
            place = 2 * half + pair
            held_ref[place, pl.ds(even, rows)] = total[pair * tile : pair * tile + rows]
            held_ref[place, pl.ds(odd, rows)] = total[pair * tile + rows : (pair + 1) * tile]
            ready_ref[place] = held_ref[place].T.astype(jnp.bfloat16)
            columns = pl.ds(pl.multiple_of((position // 2 ^ place) * tile, tile), tile)
            sends.append(pltpu.make_async_copy(ready_ref.at[place], out_hbm.at[:, columns], sems.at[place]))
            sends[-1].start()
    for send in sends:
        send.wait()


def whole_call(kernel, out_shape, scratch, flops, nbytes, *operands, in_hbm=0, out_hbm=()):
    results = pl.pallas_call(
        kernel,
        out_shape=out_shape,
        in_specs=[
            pl.BlockSpec(memory_space=pltpu.HBM if place < in_hbm else pltpu.VMEM) for place in range(len(operands))
        ],
        out_specs=[
            pl.BlockSpec(memory_space=pltpu.HBM if place in out_hbm else pltpu.VMEM) for place in range(len(out_shape))
        ],
        scratch_shapes=scratch,
        cost_estimate=pl.CostEstimate(flops=flops, bytes_accessed=nbytes, transcendentals=0),
        compiler_params=pltpu.CompilerParams(vmem_limit_bytes=None if in_hbm else 32 * 2**20),
    )(*operands)
    return results if len(out_shape) > 1 else results[0]


def blocked(x_gate, x_post, values, decay, residue, w_out):
    tok, width = x_gate.shape
    ctx_count = lax.axis_size("ctx")
    tp_count = lax.axis_size("tp")
    group = width // ctx_count
    poles = decay.shape[2]
    block = 2 * tok
    blocks = tok * ctx_count // block
    rows, channels = w_out.shape
    half = 2 * poles

    packed, own, mirrored = whole_call(
        pack_kernel,
        (
            jax.ShapeDtypeStruct((ctx_count, 3, group, tok), jnp.bfloat16),
            jax.ShapeDtypeStruct((2 * half, tok), jnp.float32),
            jax.ShapeDtypeStruct((2 * half, tok), jnp.float32),
        ),
        [
            pltpu.VMEM((3, tok, width), jnp.bfloat16),
            pltpu.VMEM((2, 2 * half, tok), jnp.float32),
            pltpu.VMEM((ctx_count, 3, group, tok), jnp.bfloat16),
            pltpu.SemaphoreType.DMA((7,)),
            pltpu.SemaphoreType.DMA((5,)),
        ],
        0,
        6 * tok * width * 2,
        x_gate,
        values,
        x_post,
        jnp.swapaxes(decay, 1, 2).reshape(half, width),
        jnp.swapaxes(residue, 1, 2).reshape(half, width),
        in_hbm=5,
        out_hbm=(0, 1, 2),
    )
    paired = lax.ppermute(mirrored, "tp", [(z, tp_count - 1 - z) for z in range(tp_count)])
    received = lax.all_to_all(packed, "ctx", split_axis=0, concat_axis=0, tiled=True)

    w_late, mirrored = lax.optimization_barrier((w_out, mirrored))
    w_x, w_y = partner(w_late, "ctx", 1), partner(w_late, "ctx", 2)
    own_spectra, table, back_table = whole_call(
        functools.partial(filter_kernel, poles),
        (
            jax.ShapeDtypeStruct((2, blocks, group, 2 * block), jnp.float32),
            jax.ShapeDtypeStruct((2 * block, 2 * block), jnp.bfloat16),
            jax.ShapeDtypeStruct((4 * block, block), jnp.bfloat16),
        ),
        [
            pltpu.VMEM((2, blocks * group, block), jnp.float32),
            pltpu.VMEM((tok, 2 * half), jnp.float32),
        ],
        2 * 2 * blocks * group * block * 2 * block * 3,
        2 * blocks * group * 2 * block * 4,
        own,
    )
    mixed = whole_call(
        functools.partial(conv_kernel, poles),
        (jax.ShapeDtypeStruct((ctx_count, tp_count, group, tok), jnp.bfloat16),),
        [
            pltpu.VMEM((2, blocks, group, 2 * block), jnp.float32),
            pltpu.VMEM((2, blocks * group, block), jnp.float32),
            pltpu.VMEM((tok, 2 * half), jnp.float32),
            pltpu.VMEM((2 * blocks * group, 2 * block), jnp.float32),
            pltpu.VMEM((2 * blocks * group, 2 * block), jnp.bfloat16),
            pltpu.VMEM((2 * blocks * group, 2 * block), jnp.bfloat16),
            pltpu.VMEM((ctx_count, group, tok), jnp.bfloat16),
            pltpu.SemaphoreType.DMA((2, tp_count)),
        ],
        2 * 8 * blocks * group * block * 2 * block * 3,
        4 * blocks * group * 2 * block * 4,
        received,
        own_spectra,
        paired,
        table,
        back_table,
        out_hbm=(0,),
    )
    mixed, w_x, w_y, w_own = lax.optimization_barrier((mixed, w_x, w_y, w_out))
    lower = rows // 2
    w_far = [partner(w_x[:lower], "ctx", 2), partner(w_y[lower:], "ctx", 1)]
    w_blocks = []
    for block in (w_own, w_x, w_y):
        w_blocks += [block, partner(block, "ctx", 0)]
    w_blocks += w_far + [partner(block, "ctx", 0) for block in w_far]
    every = lax.all_to_all(
        mixed.reshape(ctx_count * tp_count, group, tok), ("ctx", "tp"), split_axis=0, concat_axis=0, tiled=True
    ).reshape(ctx_count, tp_count, group, tok)
    return whole_call(
        project_kernel,
        (jax.ShapeDtypeStruct((tok, rows * ctx_count), jnp.bfloat16),),
        [
            pltpu.VMEM((ctx_count // 2, 2 * rows, tok), jnp.float32),
            pltpu.VMEM((ctx_count // 2, tok, 2 * rows), jnp.bfloat16),
            pltpu.SemaphoreType.DMA((ctx_count // 2,)),
        ],
        2 * tok * rows * ctx_count * channels,
        2 * rows * ctx_count * channels,
        every,
        *w_blocks,
        out_hbm=(0,),
    )


def local(x_gate, x_post, values, decay, residue, w_out):
    tok, width = x_gate.shape
    ctx_count = lax.axis_size("ctx")
    if tok == 128 and width == 512 and ctx_count == 8 and w_out.shape[0] == 64 and lax.axis_size("tp") == 4:
        return blocked(x_gate, x_post, values, decay, residue, w_out)
    return general(x_gate, x_post, values, decay, residue, w_out)


def solution(mesh):
    in_specs = (
        P("ctx", "tp"),
        P("ctx", "tp"),
        P("ctx", "tp"),
        P(None, "tp", None),
        P(None, "tp", None),
        P(("tp", "ctx"), None),
    )
    out_specs = P("ctx", "tp")
    return jax.shard_map(local, mesh=mesh, in_specs=in_specs, out_specs=out_specs, check_vma=False)
```

```python
import functools
import math

import jax
import jax.numpy as jnp
from jax import lax
from jax.experimental import pallas as pl
from jax.experimental.pallas import tpu as pltpu
from jax.sharding import PartitionSpec as P

HIGHEST = lax.Precision.HIGHEST


def partner(value, axis, bit):
    mask = 2**bit
    pairs = [(source, source ^ mask) for source in range(lax.axis_size(axis))]
    return lax.ppermute(value, axis, pairs)


def radices(length_all):
    last_radix = min(128, length_all // 4)
    first_radix = min(32, length_all // last_radix)
    return (first_radix, length_all // (first_radix * last_radix), last_radix)


def rotation(row_count, col_count, modulus):
    product = (
        lax.broadcasted_iota(jnp.int32, (row_count, col_count), 0)
        * lax.broadcasted_iota(jnp.int32, (row_count, col_count), 1)
        % modulus
    )
    angle = product.astype(jnp.float32) * (2.0 * math.pi / modulus)
    return (jnp.cos(angle), -jnp.sin(angle))


def tables(radix_sizes):
    first_radix, mid_radix, last_radix = radix_sizes
    length_all = first_radix * mid_radix * last_radix
    outer_real, outer_imag = rotation(first_radix, first_radix, first_radix)
    mid_real, mid_imag = rotation(mid_radix, mid_radix, mid_radix)
    last_real, last_imag = rotation(last_radix, last_radix, last_radix)
    twist_real, twist_imag = rotation(first_radix, mid_radix * last_radix, length_all)
    twist_real = twist_real.reshape(first_radix, mid_radix, last_radix)
    twist_imag = twist_imag.reshape(first_radix, mid_radix, last_radix)
    inner_real, inner_imag = rotation(mid_radix, last_radix, mid_radix * last_radix)
    return (
        outer_real,
        outer_imag,
        mid_real,
        mid_imag,
        last_real,
        last_imag,
        twist_real,
        twist_imag,
        inner_real,
        inner_imag,
    )


def apply_matrix(pattern, real_part, imag_part, matrix_real, matrix_imag):
    out_real = jnp.einsum(pattern, real_part, matrix_real, precision=HIGHEST) - jnp.einsum(
        pattern, imag_part, matrix_imag, precision=HIGHEST
    )
    out_imag = jnp.einsum(pattern, real_part, matrix_imag, precision=HIGHEST) + jnp.einsum(
        pattern, imag_part, matrix_real, precision=HIGHEST
    )
    return (out_real, out_imag)


def complex_times(left_real, left_imag, right_real, right_imag):
    return (
        left_real * right_real - left_imag * right_imag,
        left_real * right_imag + left_imag * right_real,
    )


def forward(real_part, imag_part, table_set, radix_sizes):
    first_radix, mid_radix, last_radix = radix_sizes
    half_first = first_radix // 2
    batch_rows = real_part.shape[0]
    (
        outer_real,
        outer_imag,
        mid_real,
        mid_imag,
        last_real,
        last_imag,
        twist_real,
        twist_imag,
        inner_real,
        inner_imag,
    ) = table_set
    real_part = real_part.reshape(batch_rows, half_first, mid_radix, last_radix)
    imag_part = imag_part.reshape(batch_rows, half_first, mid_radix, last_radix)
    real_part, imag_part = apply_matrix(
        "banm,ak->bknm", real_part, imag_part, outer_real[:half_first], outer_imag[:half_first]
    )
    real_part, imag_part = complex_times(real_part, imag_part, twist_real, twist_imag)
    real_part, imag_part = apply_matrix("bknm,nj->bkjm", real_part, imag_part, mid_real, mid_imag)
    real_part, imag_part = complex_times(real_part, imag_part, inner_real, inner_imag)
    return apply_matrix("bkjm,mq->bkjq", real_part, imag_part, last_real, last_imag)


def inverse(real_part, imag_part, table_set, radix_sizes):
    first_radix, mid_radix, last_radix = radix_sizes
    half_first = first_radix // 2
    batch_rows = real_part.shape[0]
    (
        outer_real,
        outer_imag,
        mid_real,
        mid_imag,
        last_real,
        last_imag,
        twist_real,
        twist_imag,
        inner_real,
        inner_imag,
    ) = table_set
    real_part, imag_part = apply_matrix(
        "bkjq,mq->bkjm", real_part, imag_part, last_real / last_radix, -last_imag / last_radix
    )
    real_part, imag_part = complex_times(real_part, imag_part, inner_real, -inner_imag)
    real_part, imag_part = apply_matrix(
        "bkjm,nj->bknm", real_part, imag_part, mid_real / mid_radix, -mid_imag / mid_radix
    )
    real_part, imag_part = complex_times(real_part, imag_part, twist_real, -twist_imag)
    matrix_real = outer_real[:half_first] / first_radix
    matrix_imag = -outer_imag[:half_first] / first_radix
    out_real, out_imag = apply_matrix(
        "bknm,ak->banm", real_part, imag_part, matrix_real, matrix_imag
    )
    return (out_real.reshape(batch_rows, -1), out_imag.reshape(batch_rows, -1))


def spectrum(decay_rows, residue_rows, radix_sizes, seq_length):
    first_radix, mid_radix, last_radix = radix_sizes
    length_all = first_radix * mid_radix * last_radix
    poles = decay_rows.shape[1]
    shape_all = (first_radix, mid_radix, last_radix)
    frequency = (
        lax.broadcasted_iota(jnp.int32, shape_all, 0)
        + first_radix * lax.broadcasted_iota(jnp.int32, shape_all, 1)
        + first_radix * mid_radix * lax.broadcasted_iota(jnp.int32, shape_all, 2)
    )
    half_angle = frequency.astype(jnp.float32) * (math.pi / length_all)
    sin_half = jnp.sin(half_angle)
    sin_full = jnp.sin(2.0 * half_angle)
    parity_sign = (1 - 2 * (frequency % 2)).astype(jnp.float32)

    def add_pole(pole_index, running):
        run_real, run_imag = running
        rate_col = lax.dynamic_slice_in_dim(decay_rows, pole_index, 1, 1).reshape(-1, 1, 1, 1)
        weight = lax.dynamic_slice_in_dim(residue_rows, pole_index, 1, 1).reshape(
            -1, 1, 1, 1
        ) * jnp.sqrt(2.0 * rate_col / poles)
        retained = jnp.exp(-rate_col)
        den_real = -jnp.expm1(-rate_col) + 2.0 * retained * sin_half * sin_half
        den_imag = retained * sin_full
        pole_scale = (
            weight
            * (1.0 - jnp.exp(-rate_col * seq_length) * parity_sign)
            / (den_real * den_real + den_imag * den_imag)
        )
        return (run_real + pole_scale * den_real, run_imag - pole_scale * den_imag)

    zeros_all = jnp.zeros((decay_rows.shape[0],) + shape_all, jnp.float32)
    return lax.fori_loop(0, poles, add_pole, (zeros_all, zeros_all))


def general(x_gate, x_post, values, decay, residue, w_out):
    tok_rows, block_width = x_gate.shape
    ctx_count = lax.axis_size("ctx")
    tp_count = lax.axis_size("tp")
    chan_group = block_width // ctx_count
    seq_length = tok_rows * ctx_count
    radix_sizes = radices(2 * seq_length)
    table_set = tables(radix_sizes)
    first_row = lax.axis_index("ctx") * chan_group
    own_rate = lax.dynamic_slice_in_dim(decay, first_row, chan_group, 1)
    own_residue = lax.dynamic_slice_in_dim(residue, first_row, chan_group, 1)
    own_spec = [
        spectrum(own_rate[filter_index], own_residue[filter_index], radix_sizes, seq_length)
        for filter_index in range(2)
    ]
    forward_rows = [x_gate, values] + [x_post]
    row_count = len(forward_rows)
    base_rows = jnp.stack(forward_rows)
    copied = base_rows
    for bit_index in range(tp_count.bit_length() - 1):
        copied = partner(copied, "tp", bit_index)
    sent_rows = jnp.concatenate([base_rows, copied[:, :, ::-1]], axis=0)
    received = lax.all_to_all(
        jnp.swapaxes(sent_rows, 1, 2), "ctx", split_axis=1, concat_axis=2, tiled=True
    )
    gate_fwd = received[0].astype(jnp.float32)
    value_fwd = received[1].astype(jnp.float32)
    mirrored = received[row_count:, :, ::-1].astype(jnp.float32)
    spec_real, spec_imag = forward(value_fwd, mirrored[1], table_set, radix_sizes)
    spec_real, spec_imag = complex_times(spec_real, spec_imag, own_spec[0][0], own_spec[0][1])
    along_fwd, along_rev = inverse(spec_real, spec_imag, table_set, radix_sizes)
    spec_real, spec_imag = forward(
        gate_fwd * along_fwd, mirrored[0] * along_rev, table_set, radix_sizes
    )
    spec_real, spec_imag = complex_times(spec_real, spec_imag, own_spec[1][0], own_spec[1][1])
    sum_fwd, sum_rev = inverse(spec_real, spec_imag, table_set, radix_sizes)
    sum_fwd = received[2].astype(jnp.float32) * sum_fwd
    sum_rev = mirrored[2] * sum_rev
    results = jnp.stack([sum_fwd, sum_rev[:, ::-1]])
    returned = lax.all_to_all(
        results.astype(jnp.bfloat16), "ctx", split_axis=2, concat_axis=1, tiled=True
    ).astype(results.dtype)
    flipped = returned[1, ::-1, :]
    for bit_index in range(tp_count.bit_length() - 1):
        flipped = partner(flipped.astype(jnp.bfloat16), "tp", bit_index).astype(flipped.dtype)
    total_rows = returned[0] + flipped
    total_rows = total_rows.T
    mixed_rows = total_rows.astype(jnp.bfloat16)
    whole_rows = lax.all_gather(mixed_rows, "tp", axis=1, tiled=True)
    projected = lax.dot_general(
        whole_rows,
        lax.all_gather(w_out, "ctx", axis=0, tiled=True),
        (((1,), (1,)), ((), ())),
        preferred_element_type=jnp.float32,
    )
    return projected.astype(jnp.bfloat16)


def cycle(row_factor, col_factor, modulus):
    quarter = modulus // 4
    turned = row_factor * col_factor + quarter // 2
    quadrant = turned // quarter % 4
    angle = (turned % quarter - quarter // 2).astype(jnp.float32) * (2.0 * math.pi / modulus)
    square = angle * angle

    def series(first):
        total = jnp.zeros_like(square)
        for power in range(first + 10, first, -2):
            total = (total + (-1.0) ** ((power - first) // 2) / math.factorial(power)) * square
        return total

    cos = 1.0 + series(0)
    sin = angle + angle * series(1)
    odd = quadrant % 2 == 1
    cos, sin = jnp.where(odd, sin, cos), jnp.where(odd, cos, sin)
    return jnp.where((quadrant == 1) | (quadrant == 2), -cos, cos), jnp.where(quadrant >= 2, -sin, sin)


def put_tables(table_ref, back_ref):
    block = back_ref.shape[1]
    modulus = 4 * block
    coarse = 16
    rows = lax.broadcasted_iota(jnp.int32, (coarse, block), 0)
    cols = lax.broadcasted_iota(jnp.int32, (coarse, block), 1)

    def parts(big, small):
        for place in range(block // coarse):
            big_cos, big_sin = (part[place : place + 1] for part in big)
            cos = halves(big_cos * small[0] - big_sin * small[1])
            sin = halves(-(big_sin * small[0] + big_cos * small[1]))
            yield place * coarse, cos, sin

    def put(ref, first, columns, value):
        ref[first : first + coarse, columns] = value[0]
        low = first + ref.shape[0] // 2
        ref[low : low + coarse, columns] = value[1]

    frequency = 2 * cols + 1
    for first, cos, sin in parts(cycle(coarse * rows, frequency, modulus), cycle(rows, frequency, modulus)):
        put(table_ref, first, slice(0, block), cos)
        put(table_ref, first, slice(block, 2 * block), sin)
    for first, cos, sin in parts(cycle(2 * coarse * rows, cols, modulus), cycle(2 * rows + 1, cols, modulus)):
        put(back_ref, first, slice(0, block), cos)
        put(back_ref, block + first, slice(0, block), sin)


def halves(value):
    high = value.astype(jnp.bfloat16)
    return high, (value - high.astype(jnp.float32)).astype(jnp.bfloat16)


def mul(left, right):
    return jnp.dot(left, right, preferred_element_type=jnp.float32)


def mul3(high, low, table_ref):
    left = jnp.concatenate([high, high, low], axis=1)
    return mul(left, jnp.concatenate([table_ref[...], table_ref[: table_ref.shape[0] // 2]], axis=0))


def mul2(value, table_ref):
    return mul(jnp.concatenate([value, value], axis=1), table_ref[...])


def pack_kernel(
    gate_hbm, value_hbm, post_hbm, decay_hbm, residue_hbm,
    out_hbm, own_hbm, sent_hbm, held_ref, cut_ref, ready_ref, sems, out_sems,
):
    ctx_count, _, group, tok = out_hbm.shape
    width = gate_hbm.shape[1]
    half = decay_hbm.shape[0]
    position = lax.axis_index("ctx")
    pairs = []
    for place, index in enumerate((position, ctx_count - 1 - position)):
        columns = pl.ds(pl.multiple_of(index * group // tok * tok, tok), tok)
        pairs += [(decay_hbm.at[:, columns], cut_ref.at[place, :half]), (residue_hbm.at[:, columns], cut_ref.at[place, half:])]
    pairs += [(source, held_ref.at[place]) for place, source in enumerate((value_hbm, gate_hbm, post_hbm))]
    copies = [pltpu.make_async_copy(*pair, sems.at[place]) for place, pair in enumerate(pairs)]
    for copy in copies:
        copy.start()
    sends = []
    for place, target in enumerate((own_hbm, sent_hbm)):
        copies[2 * place].wait()
        copies[2 * place + 1].wait()
        sends.append(pltpu.make_async_copy(cut_ref.at[place], target, out_sems.at[3 + place]))
        sends[-1].start()
    for place, copy in enumerate(copies[4:]):
        copy.wait()
        for first in range(0, width, tok):
            turned = held_ref[place, :, first : first + tok].T
            for part in range(tok // group):
                ready_ref[first // group + part, place] = turned[part * group : (part + 1) * group]
        sends.append(pltpu.make_async_copy(ready_ref.at[:, place], out_hbm.at[:, place], out_sems.at[place]))
        sends[-1].start()
    for send in sends:
        send.wait()


def mirror_rows(value):
    row = lax.broadcasted_iota(jnp.int32, (8, value.shape[1]), 0)
    result = []
    for first in range(value.shape[0] - 8, -1, -8):
        part = value[first : first + 8]
        for shift in (1, 2, 4):
            part = jnp.where(row & shift == 0, pltpu.roll(part, 8 - shift, 0), pltpu.roll(part, shift, 0))
        result.append(part)
    return jnp.concatenate(result, axis=0)


def put_filter(poles, index, turned, time_ref):
    lanes = 128
    rows_all, block = time_ref.shape
    group = turned.shape[0]
    ramp = lax.broadcasted_iota(jnp.int32, (8, lanes), 1).astype(jnp.float32)
    for row in range(0, group, 8):
        rows = slice(row, row + 8)
        rate = turned[rows, index * poles : (index + 1) * poles]
        scale = turned[rows, (2 + index) * poles : (3 + index) * poles] * (jnp.sqrt(rate * (2.0 / poles)) / block)
        slope = rate * -math.log2(math.e)
        sums = [None] * (rows_all // group * block // lanes)
        for pole in range(poles):
            level = jnp.broadcast_to(slope[:, pole : pole + 1], (8, lanes))
            term = scale[:, pole : pole + 1] * jnp.exp2(level * ramp)
            step = jnp.exp2(level * lanes)
            for place in range(len(sums)):
                sums[place] = term if pole == 0 else sums[place] + term
                if place + 1 < len(sums):
                    term = term * step
        for place, total in enumerate(sums):
            lag, lane = divmod(place * lanes, block)
            time_ref[lag * group + row : lag * group + row + 8, lane : lane + lanes] = total


def put_spectra(spec, out_ref):
    blocks, group, twice = out_ref.shape
    block = twice // 2
    sign = (1 - 2 * (lax.broadcasted_iota(jnp.int32, (group, block), 1) % 2)).astype(jnp.float32)
    for lag in range(blocks):
        real = spec[lag * group : (lag + 1) * group, :block]
        imag = spec[lag * group : (lag + 1) * group, block:]
        if lag > 0:
            real = real - sign * spec[(lag - 1) * group : lag * group, block:]
            imag = imag + sign * spec[(lag - 1) * group : lag * group, :block]
        out_ref[lag, :, :block] = real
        out_ref[lag, :, block:] = imag


def filter_kernel(poles, par_ref, out_ref, table_ref, back_ref, time_ref, turned_ref):
    group = out_ref.shape[2]
    put_tables(table_ref, back_ref)
    turned_ref[...] = par_ref[...].T
    turned = turned_ref[pl.ds(pl.multiple_of(lax.axis_index("ctx") * group % turned_ref.shape[0], group), group)]
    put_filter(poles, 0, turned, time_ref.at[0])
    spec = mul3(*halves(time_ref[0]), table_ref)
    put_filter(poles, 1, turned, time_ref.at[1])
    put_spectra(spec, out_ref.at[0])
    put_spectra(mul3(*halves(time_ref[1]), table_ref), out_ref.at[1])


def conv_kernel(
    poles, x_ref, own_ref, par_ref, table_ref, back_ref, out_hbm,
    paired_ref, time_ref, turned_ref, spec_ref, high_ref, low_ref, ready_ref, sems,
):
    turned_ref[...] = par_ref[...].T
    blocks, group, twice = own_ref.shape[1:]
    block = twice // 2
    rows_all = blocks * group
    tall, wide = 16, 128
    pieces = x_ref.shape[0] // blocks
    first = (x_ref.shape[0] - 1 - lax.axis_index("ctx")) * group % turned_ref.shape[0]
    turned = mirror_rows(turned_ref[pl.ds(pl.multiple_of(first, group), group)])

    def rows_of(position):
        return jnp.concatenate(
            [
                jnp.concatenate([x_ref[m * pieces + s, position] for s in range(pieces)], axis=1)
                for m in range(blocks)
            ],
            axis=0,
        )

    def times(index, side, source, row, lane):
        data = []
        for m in range(blocks):
            rows = slice(source + m * group + row, source + m * group + row + tall)
            data.append((spec_ref[rows, lane : lane + wide], spec_ref[rows, block + lane : block + lane + wide]))
        sums = [None] * blocks
        for lag in range(blocks):
            h_ref = (own_ref, paired_ref)[side]
            f_re = h_ref[index, lag, row : row + tall, lane : lane + wide]
            f_im = h_ref[index, lag, row : row + tall, block + lane : block + lane + wide]
            for m in range(blocks - lag):
                target, (d_re, d_im) = (m + lag, data[m]) if side == 0 else (m, data[m + lag])
                if side == 0:
                    real, imag = f_re * d_re - f_im * d_im, f_re * d_im + f_im * d_re
                else:
                    real, imag = f_re * d_re + f_im * d_im, f_re * d_im - f_im * d_re
                if sums[target] is not None:
                    real, imag = sums[target][0] + real, sums[target][1] + imag
                sums[target] = (real, imag)
        return sums

    def keep(target, row, lane, sums, both_parts):
        for m in range(blocks):
            rows = slice(target + m * group + row, target + m * group + row + tall)
            for part in range(2):
                cols = slice(part * block + lane, part * block + lane + wide)
                high_ref[rows, cols], low = halves(sums[m][part])
                if both_parts:
                    low_ref[rows, cols] = low

    chunks = [(row, lane) for row in range(0, group, tall) for lane in range(0, block, wide)]

    value = rows_of(0)
    gate = rows_of(1).astype(jnp.float32)
    spec_ref[:rows_all] = mul2(value, table_ref)
    sides = [slice(side * rows_all, (side + 1) * rows_all) for side in range(2)]
    put_filter(poles, 0, turned, time_ref.at[0])
    spec = mul3(*halves(time_ref[0]), table_ref)
    for row, lane in chunks:
        keep(0, row, lane, times(0, 0, 0, row, lane), True)
    put_spectra(spec, paired_ref.at[0])
    gated = [gate * mul3(high_ref[sides[0]], low_ref[sides[0]], back_ref)]
    put_filter(poles, 1, turned, time_ref.at[1])
    for row, lane in chunks:
        keep(rows_all, row, lane, times(0, 1, 0, row, lane), True)
    gated.append(gate * mul3(high_ref[sides[1]], low_ref[sides[1]], back_ref))
    spec = mul3(*halves(time_ref[1]), table_ref)
    for side in range(2):
        spec_ref[sides[side]] = mul3(*halves(gated[side]), table_ref)
    put_spectra(spec, paired_ref.at[1])
    for row, lane in chunks:
        ahead, back = times(1, 0, 0, row, lane), times(1, 1, rows_all, row, lane)
        keep(0, row, lane, [(a[0] + b[0], a[1] + b[1]) for a, b in zip(ahead, back)], False)
    post = rows_of(2)
    tok = block // pieces
    sends = []
    for part in range(2):
        rows = slice(part * rows_all // 2, (part + 1) * rows_all // 2)
        summed = mul2(high_ref[rows], back_ref)
        mixed = (post[rows].astype(jnp.float32) * summed).astype(jnp.bfloat16)
        first = part * blocks // 2 * pieces
        for m in range(blocks // 2):
            for s in range(pieces):
                ready_ref[first + m * pieces + s] = mixed[m * group : (m + 1) * group, s * tok : (s + 1) * tok]
        span = pl.ds(first, blocks // 2 * pieces)
        for copy in range(out_hbm.shape[1]):
            sends.append(pltpu.make_async_copy(ready_ref.at[span], out_hbm.at[span, copy], sems.at[part, copy]))
            sends[-1].start()
    for send in sends:
        send.wait()


def project_kernel(mixed_ref, *refs):
    w_refs, (out_hbm, held_ref, ready_ref, sems) = refs[:-4], refs[-4:]
    rows = w_refs[0].shape[0]
    tile = 2 * rows
    position = lax.axis_index("ctx")
    parity = position % 2
    even = pl.multiple_of(parity * rows, rows)
    odd = pl.multiple_of((1 - parity) * rows, rows)
    masks = (0, 1 + parity, 2 - parity, 3)
    ctx_count, tp_count = mixed_ref.shape[:2]
    mixed = jnp.concatenate([mixed_ref[i, z] for z in range(tp_count) for i in range(ctx_count)], axis=0)
    sends = []
    for half in range(2):
        total = mul(jnp.concatenate([w_ref[...] for w_ref in w_refs[4 * half : 4 * half + 4]], axis=0), mixed)
        for pair in range(2):
            place = 2 * half + pair
            held_ref[place, pl.ds(even, rows)] = total[pair * tile : pair * tile + rows]
            held_ref[place, pl.ds(odd, rows)] = total[pair * tile + rows : (pair + 1) * tile]
            ready_ref[place] = held_ref[place].T.astype(jnp.bfloat16)
            columns = pl.ds(pl.multiple_of((position // 2 ^ masks[place]) * tile, tile), tile)
            sends.append(pltpu.make_async_copy(ready_ref.at[place], out_hbm.at[:, columns], sems.at[place]))
            sends[-1].start()
    for send in sends:
        send.wait()


def whole_call(kernel, out_shape, scratch, flops, nbytes, *operands, in_hbm=0, out_hbm=()):
    results = pl.pallas_call(
        kernel,
        out_shape=out_shape,
        in_specs=[
            pl.BlockSpec(memory_space=pltpu.HBM if place < in_hbm else pltpu.VMEM) for place in range(len(operands))
        ],
        out_specs=[
            pl.BlockSpec(memory_space=pltpu.HBM if place in out_hbm else pltpu.VMEM) for place in range(len(out_shape))
        ],
        scratch_shapes=scratch,
        cost_estimate=pl.CostEstimate(flops=flops, bytes_accessed=nbytes, transcendentals=0),
        compiler_params=pltpu.CompilerParams(vmem_limit_bytes=None if in_hbm else 32 * 2**20),
    )(*operands)
    return results if len(out_shape) > 1 else results[0]


def blocked(x_gate, x_post, values, decay, residue, w_out):
    tok, width = x_gate.shape
    ctx_count = lax.axis_size("ctx")
    tp_count = lax.axis_size("tp")
    group = width // ctx_count
    poles = decay.shape[2]
    block = 2 * tok
    blocks = tok * ctx_count // block
    rows, channels = w_out.shape
    half = 2 * poles

    packed, own, mirrored = whole_call(
        pack_kernel,
        (
            jax.ShapeDtypeStruct((ctx_count, 3, group, tok), jnp.bfloat16),
            jax.ShapeDtypeStruct((2 * half, tok), jnp.float32),
            jax.ShapeDtypeStruct((2 * half, tok), jnp.float32),
        ),
        [
            pltpu.VMEM((3, tok, width), jnp.bfloat16),
            pltpu.VMEM((2, 2 * half, tok), jnp.float32),
            pltpu.VMEM((ctx_count, 3, group, tok), jnp.bfloat16),
            pltpu.SemaphoreType.DMA((7,)),
            pltpu.SemaphoreType.DMA((5,)),
        ],
        0,
        6 * tok * width * 2,
        x_gate,
        values,
        x_post,
        jnp.swapaxes(decay, 1, 2).reshape(half, width),
        jnp.swapaxes(residue, 1, 2).reshape(half, width),
        in_hbm=5,
        out_hbm=(0, 1, 2),
    )
    paired = lax.ppermute(mirrored, "tp", [(z, tp_count - 1 - z) for z in range(tp_count)])
    received = lax.all_to_all(packed, "ctx", split_axis=0, concat_axis=0, tiled=True)

    w_late, mirrored = lax.optimization_barrier((w_out, mirrored))

    def cross(block, even_mask, odd_mask):
        return lax.ppermute(block, "ctx", [(i, i ^ (odd_mask if i % 2 else even_mask)) for i in range(ctx_count)])

    w_first = cross(w_late, 2, 4)
    own_spectra, table, back_table = whole_call(
        functools.partial(filter_kernel, poles),
        (
            jax.ShapeDtypeStruct((2, blocks, group, 2 * block), jnp.float32),
            jax.ShapeDtypeStruct((2 * block, 2 * block), jnp.bfloat16),
            jax.ShapeDtypeStruct((4 * block, block), jnp.bfloat16),
        ),
        [
            pltpu.VMEM((2, blocks * group, block), jnp.float32),
            pltpu.VMEM((tok, 2 * half), jnp.float32),
        ],
        2 * 2 * blocks * group * block * 2 * block * 3,
        2 * blocks * group * 2 * block * 4,
        own,
    )
    mixed = whole_call(
        functools.partial(conv_kernel, poles),
        (jax.ShapeDtypeStruct((ctx_count, tp_count, group, tok), jnp.bfloat16),),
        [
            pltpu.VMEM((2, blocks, group, 2 * block), jnp.float32),
            pltpu.VMEM((2, blocks * group, block), jnp.float32),
            pltpu.VMEM((tok, 2 * half), jnp.float32),
            pltpu.VMEM((2 * blocks * group, 2 * block), jnp.float32),
            pltpu.VMEM((2 * blocks * group, 2 * block), jnp.bfloat16),
            pltpu.VMEM((2 * blocks * group, 2 * block), jnp.bfloat16),
            pltpu.VMEM((ctx_count, group, tok), jnp.bfloat16),
            pltpu.SemaphoreType.DMA((2, tp_count)),
        ],
        2 * 8 * blocks * group * block * 2 * block * 3,
        4 * blocks * group * 2 * block * 4,
        received,
        own_spectra,
        paired,
        table,
        back_table,
        out_hbm=(0,),
    )
    mixed, w_first, w_own = lax.optimization_barrier((mixed, w_first, w_out))
    w_third = cross(w_first, 4, 2)
    w_second = cross(w_own, 4, 2)
    w_other = [partner(block, "ctx", 0) for block in (w_own, w_first, w_second, w_third)]
    w_blocks = [w_own, w_other[0], w_first, w_other[2], w_second, w_other[1], w_third, w_other[3]]
    every = lax.all_to_all(
        mixed.reshape(ctx_count * tp_count, group, tok), ("ctx", "tp"), split_axis=0, concat_axis=0, tiled=True
    ).reshape(ctx_count, tp_count, group, tok)
    return whole_call(
        project_kernel,
        (jax.ShapeDtypeStruct((tok, rows * ctx_count), jnp.bfloat16),),
        [
            pltpu.VMEM((ctx_count // 2, 2 * rows, tok), jnp.float32),
            pltpu.VMEM((ctx_count // 2, tok, 2 * rows), jnp.bfloat16),
            pltpu.SemaphoreType.DMA((ctx_count // 2,)),
        ],
        2 * tok * rows * ctx_count * channels,
        2 * rows * ctx_count * channels,
        every,
        *w_blocks,
        out_hbm=(0,),
    )


def local(x_gate, x_post, values, decay, residue, w_out):
    tok, width = x_gate.shape
    ctx_count = lax.axis_size("ctx")
    if tok == 128 and width == 512 and ctx_count == 8 and w_out.shape[0] == 64 and lax.axis_size("tp") == 4:
        return blocked(x_gate, x_post, values, decay, residue, w_out)
    return general(x_gate, x_post, values, decay, residue, w_out)


def solution(mesh):
    in_specs = (
        P("ctx", "tp"),
        P("ctx", "tp"),
        P("ctx", "tp"),
        P(None, "tp", None),
        P(None, "tp", None),
        P(("tp", "ctx"), None),
    )
    out_specs = P("ctx", "tp")
    return jax.shard_map(local, mesh=mesh, in_specs=in_specs, out_specs=out_specs, check_vma=False)
```

```python
import functools
import math

import jax
import jax.numpy as jnp
from jax import lax
from jax.experimental import pallas as pl
from jax.experimental.pallas import tpu as pltpu
from jax.sharding import PartitionSpec as P

HIGHEST = lax.Precision.HIGHEST


def partner(value, axis, bit):
    mask = 2**bit
    pairs = [(source, source ^ mask) for source in range(lax.axis_size(axis))]
    return lax.ppermute(value, axis, pairs)


def radices(length_all):
    last_radix = min(128, length_all // 4)
    first_radix = min(32, length_all // last_radix)
    return (first_radix, length_all // (first_radix * last_radix), last_radix)


def rotation(row_count, col_count, modulus):
    product = (
        lax.broadcasted_iota(jnp.int32, (row_count, col_count), 0)
        * lax.broadcasted_iota(jnp.int32, (row_count, col_count), 1)
        % modulus
    )
    angle = product.astype(jnp.float32) * (2.0 * math.pi / modulus)
    return (jnp.cos(angle), -jnp.sin(angle))


def tables(radix_sizes):
    first_radix, mid_radix, last_radix = radix_sizes
    length_all = first_radix * mid_radix * last_radix
    outer_real, outer_imag = rotation(first_radix, first_radix, first_radix)
    mid_real, mid_imag = rotation(mid_radix, mid_radix, mid_radix)
    last_real, last_imag = rotation(last_radix, last_radix, last_radix)
    twist_real, twist_imag = rotation(first_radix, mid_radix * last_radix, length_all)
    twist_real = twist_real.reshape(first_radix, mid_radix, last_radix)
    twist_imag = twist_imag.reshape(first_radix, mid_radix, last_radix)
    inner_real, inner_imag = rotation(mid_radix, last_radix, mid_radix * last_radix)
    return (
        outer_real,
        outer_imag,
        mid_real,
        mid_imag,
        last_real,
        last_imag,
        twist_real,
        twist_imag,
        inner_real,
        inner_imag,
    )


def apply_matrix(pattern, real_part, imag_part, matrix_real, matrix_imag):
    out_real = jnp.einsum(pattern, real_part, matrix_real, precision=HIGHEST) - jnp.einsum(
        pattern, imag_part, matrix_imag, precision=HIGHEST
    )
    out_imag = jnp.einsum(pattern, real_part, matrix_imag, precision=HIGHEST) + jnp.einsum(
        pattern, imag_part, matrix_real, precision=HIGHEST
    )
    return (out_real, out_imag)


def complex_times(left_real, left_imag, right_real, right_imag):
    return (
        left_real * right_real - left_imag * right_imag,
        left_real * right_imag + left_imag * right_real,
    )


def forward(real_part, imag_part, table_set, radix_sizes):
    first_radix, mid_radix, last_radix = radix_sizes
    half_first = first_radix // 2
    batch_rows = real_part.shape[0]
    (
        outer_real,
        outer_imag,
        mid_real,
        mid_imag,
        last_real,
        last_imag,
        twist_real,
        twist_imag,
        inner_real,
        inner_imag,
    ) = table_set
    real_part = real_part.reshape(batch_rows, half_first, mid_radix, last_radix)
    imag_part = imag_part.reshape(batch_rows, half_first, mid_radix, last_radix)
    real_part, imag_part = apply_matrix(
        "banm,ak->bknm", real_part, imag_part, outer_real[:half_first], outer_imag[:half_first]
    )
    real_part, imag_part = complex_times(real_part, imag_part, twist_real, twist_imag)
    real_part, imag_part = apply_matrix("bknm,nj->bkjm", real_part, imag_part, mid_real, mid_imag)
    real_part, imag_part = complex_times(real_part, imag_part, inner_real, inner_imag)
    return apply_matrix("bkjm,mq->bkjq", real_part, imag_part, last_real, last_imag)


def inverse(real_part, imag_part, table_set, radix_sizes):
    first_radix, mid_radix, last_radix = radix_sizes
    half_first = first_radix // 2
    batch_rows = real_part.shape[0]
    (
        outer_real,
        outer_imag,
        mid_real,
        mid_imag,
        last_real,
        last_imag,
        twist_real,
        twist_imag,
        inner_real,
        inner_imag,
    ) = table_set
    real_part, imag_part = apply_matrix(
        "bkjq,mq->bkjm", real_part, imag_part, last_real / last_radix, -last_imag / last_radix
    )
    real_part, imag_part = complex_times(real_part, imag_part, inner_real, -inner_imag)
    real_part, imag_part = apply_matrix(
        "bkjm,nj->bknm", real_part, imag_part, mid_real / mid_radix, -mid_imag / mid_radix
    )
    real_part, imag_part = complex_times(real_part, imag_part, twist_real, -twist_imag)
    matrix_real = outer_real[:half_first] / first_radix
    matrix_imag = -outer_imag[:half_first] / first_radix
    out_real, out_imag = apply_matrix(
        "bknm,ak->banm", real_part, imag_part, matrix_real, matrix_imag
    )
    return (out_real.reshape(batch_rows, -1), out_imag.reshape(batch_rows, -1))


def spectrum(decay_rows, residue_rows, radix_sizes, seq_length):
    first_radix, mid_radix, last_radix = radix_sizes
    length_all = first_radix * mid_radix * last_radix
    poles = decay_rows.shape[1]
    shape_all = (first_radix, mid_radix, last_radix)
    frequency = (
        lax.broadcasted_iota(jnp.int32, shape_all, 0)
        + first_radix * lax.broadcasted_iota(jnp.int32, shape_all, 1)
        + first_radix * mid_radix * lax.broadcasted_iota(jnp.int32, shape_all, 2)
    )
    half_angle = frequency.astype(jnp.float32) * (math.pi / length_all)
    sin_half = jnp.sin(half_angle)
    sin_full = jnp.sin(2.0 * half_angle)
    parity_sign = (1 - 2 * (frequency % 2)).astype(jnp.float32)

    def add_pole(pole_index, running):
        run_real, run_imag = running
        rate_col = lax.dynamic_slice_in_dim(decay_rows, pole_index, 1, 1).reshape(-1, 1, 1, 1)
        weight = lax.dynamic_slice_in_dim(residue_rows, pole_index, 1, 1).reshape(
            -1, 1, 1, 1
        ) * jnp.sqrt(2.0 * rate_col / poles)
        retained = jnp.exp(-rate_col)
        den_real = -jnp.expm1(-rate_col) + 2.0 * retained * sin_half * sin_half
        den_imag = retained * sin_full
        pole_scale = (
            weight
            * (1.0 - jnp.exp(-rate_col * seq_length) * parity_sign)
            / (den_real * den_real + den_imag * den_imag)
        )
        return (run_real + pole_scale * den_real, run_imag - pole_scale * den_imag)

    zeros_all = jnp.zeros((decay_rows.shape[0],) + shape_all, jnp.float32)
    return lax.fori_loop(0, poles, add_pole, (zeros_all, zeros_all))


def general(x_gate, x_post, values, decay, residue, w_out):
    tok_rows, block_width = x_gate.shape
    ctx_count = lax.axis_size("ctx")
    tp_count = lax.axis_size("tp")
    chan_group = block_width // ctx_count
    seq_length = tok_rows * ctx_count
    radix_sizes = radices(2 * seq_length)
    table_set = tables(radix_sizes)
    first_row = lax.axis_index("ctx") * chan_group
    own_rate = lax.dynamic_slice_in_dim(decay, first_row, chan_group, 1)
    own_residue = lax.dynamic_slice_in_dim(residue, first_row, chan_group, 1)
    own_spec = [
        spectrum(own_rate[filter_index], own_residue[filter_index], radix_sizes, seq_length)
        for filter_index in range(2)
    ]
    forward_rows = [x_gate, values] + [x_post]
    row_count = len(forward_rows)
    base_rows = jnp.stack(forward_rows)
    copied = base_rows
    for bit_index in range(tp_count.bit_length() - 1):
        copied = partner(copied, "tp", bit_index)
    sent_rows = jnp.concatenate([base_rows, copied[:, :, ::-1]], axis=0)
    received = lax.all_to_all(
        jnp.swapaxes(sent_rows, 1, 2), "ctx", split_axis=1, concat_axis=2, tiled=True
    )
    gate_fwd = received[0].astype(jnp.float32)
    value_fwd = received[1].astype(jnp.float32)
    mirrored = received[row_count:, :, ::-1].astype(jnp.float32)
    spec_real, spec_imag = forward(value_fwd, mirrored[1], table_set, radix_sizes)
    spec_real, spec_imag = complex_times(spec_real, spec_imag, own_spec[0][0], own_spec[0][1])
    along_fwd, along_rev = inverse(spec_real, spec_imag, table_set, radix_sizes)
    spec_real, spec_imag = forward(
        gate_fwd * along_fwd, mirrored[0] * along_rev, table_set, radix_sizes
    )
    spec_real, spec_imag = complex_times(spec_real, spec_imag, own_spec[1][0], own_spec[1][1])
    sum_fwd, sum_rev = inverse(spec_real, spec_imag, table_set, radix_sizes)
    sum_fwd = received[2].astype(jnp.float32) * sum_fwd
    sum_rev = mirrored[2] * sum_rev
    results = jnp.stack([sum_fwd, sum_rev[:, ::-1]])
    returned = lax.all_to_all(
        results.astype(jnp.bfloat16), "ctx", split_axis=2, concat_axis=1, tiled=True
    ).astype(results.dtype)
    flipped = returned[1, ::-1, :]
    for bit_index in range(tp_count.bit_length() - 1):
        flipped = partner(flipped.astype(jnp.bfloat16), "tp", bit_index).astype(flipped.dtype)
    total_rows = returned[0] + flipped
    total_rows = total_rows.T
    mixed_rows = total_rows.astype(jnp.bfloat16)
    whole_rows = lax.all_gather(mixed_rows, "tp", axis=1, tiled=True)
    projected = lax.dot_general(
        whole_rows,
        lax.all_gather(w_out, "ctx", axis=0, tiled=True),
        (((1,), (1,)), ((), ())),
        preferred_element_type=jnp.float32,
    )
    return projected.astype(jnp.bfloat16)


def cycle(row_factor, col_factor, modulus):
    quarter = modulus // 4
    turned = row_factor * col_factor + quarter // 2
    quadrant = turned // quarter % 4
    angle = (turned % quarter - quarter // 2).astype(jnp.float32) * (2.0 * math.pi / modulus)
    square = angle * angle

    def series(first):
        total = jnp.zeros_like(square)
        for power in range(first + 10, first, -2):
            total = (total + (-1.0) ** ((power - first) // 2) / math.factorial(power)) * square
        return total

    cos = 1.0 + series(0)
    sin = angle + angle * series(1)
    odd = quadrant % 2 == 1
    cos, sin = jnp.where(odd, sin, cos), jnp.where(odd, cos, sin)
    return jnp.where((quadrant == 1) | (quadrant == 2), -cos, cos), jnp.where(quadrant >= 2, -sin, sin)


def put_tables(table_ref, back_ref):
    block = back_ref.shape[1]
    modulus = 4 * block
    coarse = 16
    rows = lax.broadcasted_iota(jnp.int32, (coarse, block), 0)
    cols = lax.broadcasted_iota(jnp.int32, (coarse, block), 1)

    def parts(big, small):
        for place in range(block // coarse):
            big_cos, big_sin = (part[place : place + 1] for part in big)
            cos = halves(big_cos * small[0] - big_sin * small[1])
            sin = halves(-(big_sin * small[0] + big_cos * small[1]))
            yield place * coarse, cos, sin

    def put(ref, first, columns, value):
        ref[first : first + coarse, columns] = value[0]
        low = first + ref.shape[0] // 2
        ref[low : low + coarse, columns] = value[1]

    frequency = 2 * cols + 1
    for first, cos, sin in parts(cycle(coarse * rows, frequency, modulus), cycle(rows, frequency, modulus)):
        put(table_ref, first, slice(0, block), cos)
        put(table_ref, first, slice(block, 2 * block), sin)
    for first, cos, sin in parts(cycle(2 * coarse * rows, cols, modulus), cycle(2 * rows + 1, cols, modulus)):
        put(back_ref, first, slice(0, block), cos)
        put(back_ref, block + first, slice(0, block), sin)


def halves(value):
    high = value.astype(jnp.bfloat16)
    return high, (value - high.astype(jnp.float32)).astype(jnp.bfloat16)


def mul(left, right):
    return jnp.dot(left, right, preferred_element_type=jnp.float32)


def mul3(high, low, table_ref):
    left = jnp.concatenate([high, high, low], axis=1)
    return mul(left, jnp.concatenate([table_ref[...], table_ref[: table_ref.shape[0] // 2]], axis=0))


def mul2(value, table_ref):
    return mul(jnp.concatenate([value, value], axis=1), table_ref[...])


def pack_kernel(
    gate_hbm, value_hbm, post_hbm, decay_hbm, residue_hbm,
    out_hbm, own_hbm, sent_hbm, held_ref, cut_ref, ready_ref, sems, out_sems,
):
    ctx_count, _, group, tok = out_hbm.shape
    width = gate_hbm.shape[1]
    half = decay_hbm.shape[0]
    position = lax.axis_index("ctx")
    pairs = []
    for place, index in enumerate((position, ctx_count - 1 - position)):
        columns = pl.ds(pl.multiple_of(index * group // tok * tok, tok), tok)
        pairs += [(decay_hbm.at[:, columns], cut_ref.at[place, :half]), (residue_hbm.at[:, columns], cut_ref.at[place, half:])]
    pairs += [(source, held_ref.at[place]) for place, source in enumerate((value_hbm, gate_hbm, post_hbm))]
    copies = [pltpu.make_async_copy(*pair, sems.at[place]) for place, pair in enumerate(pairs)]
    for copy in copies:
        copy.start()
    sends = []
    for place, target in enumerate((own_hbm, sent_hbm)):
        copies[2 * place].wait()
        copies[2 * place + 1].wait()
        sends.append(pltpu.make_async_copy(cut_ref.at[place], target, out_sems.at[3 + place]))
        sends[-1].start()
    for place, copy in enumerate(copies[4:]):
        copy.wait()
        for first in range(0, width, tok):
            turned = held_ref[place, :, first : first + tok].T
            for part in range(tok // group):
                ready_ref[first // group + part, place] = turned[part * group : (part + 1) * group]
        sends.append(pltpu.make_async_copy(ready_ref.at[:, place], out_hbm.at[:, place], out_sems.at[place]))
        sends[-1].start()
    for send in sends:
        send.wait()


def mirror_rows(value):
    row = lax.broadcasted_iota(jnp.int32, (8, value.shape[1]), 0)
    result = []
    for first in range(value.shape[0] - 8, -1, -8):
        part = value[first : first + 8]
        for shift in (1, 2, 4):
            part = jnp.where(row & shift == 0, pltpu.roll(part, 8 - shift, 0), pltpu.roll(part, shift, 0))
        result.append(part)
    return jnp.concatenate(result, axis=0)


def put_filter(poles, index, turned, time_ref):
    lanes = 128
    rows_all, block = time_ref.shape
    group = turned.shape[0]
    ramp = lax.broadcasted_iota(jnp.int32, (8, lanes), 1).astype(jnp.float32)
    for row in range(0, group, 8):
        rows = slice(row, row + 8)
        rate = turned[rows, index * poles : (index + 1) * poles]
        scale = turned[rows, (2 + index) * poles : (3 + index) * poles] * (jnp.sqrt(rate * (2.0 / poles)) / block)
        slope = rate * -math.log2(math.e)
        sums = [None] * (rows_all // group * block // lanes)
        for pole in range(poles):
            level = jnp.broadcast_to(slope[:, pole : pole + 1], (8, lanes))
            term = scale[:, pole : pole + 1] * jnp.exp2(level * ramp)
            step = jnp.exp2(level * lanes)
            for place in range(len(sums)):
                sums[place] = term if pole == 0 else sums[place] + term
                if place + 1 < len(sums):
                    term = term * step
        for place, total in enumerate(sums):
            lag, lane = divmod(place * lanes, block)
            time_ref[lag * group + row : lag * group + row + 8, lane : lane + lanes] = total


def put_spectra(spec, out_ref):
    blocks, group, twice = out_ref.shape
    block = twice // 2
    sign = (1 - 2 * (lax.broadcasted_iota(jnp.int32, (group, block), 1) % 2)).astype(jnp.float32)
    for lag in range(blocks):
        real = spec[lag * group : (lag + 1) * group, :block]
        imag = spec[lag * group : (lag + 1) * group, block:]
        if lag > 0:
            real = real - sign * spec[(lag - 1) * group : lag * group, block:]
            imag = imag + sign * spec[(lag - 1) * group : lag * group, :block]
        out_ref[lag, :, :block] = real
        out_ref[lag, :, block:] = imag


def filter_kernel(poles, par_ref, out_ref, table_ref, back_ref, time_ref, turned_ref):
    group = out_ref.shape[2]
    put_tables(table_ref, back_ref)
    turned_ref[...] = par_ref[...].T
    turned = turned_ref[pl.ds(pl.multiple_of(lax.axis_index("ctx") * group % turned_ref.shape[0], group), group)]
    put_filter(poles, 0, turned, time_ref.at[0])
    spec = mul3(*halves(time_ref[0]), table_ref)
    put_filter(poles, 1, turned, time_ref.at[1])
    put_spectra(spec, out_ref.at[0])
    put_spectra(mul3(*halves(time_ref[1]), table_ref), out_ref.at[1])


def conv_kernel(
    poles, x_ref, own_ref, par_ref, table_ref, back_ref, out_hbm,
    paired_ref, time_ref, turned_ref, spec_ref, high_ref, low_ref, ready_ref, sems,
):
    turned_ref[...] = par_ref[...].T
    blocks, group, twice = own_ref.shape[1:]
    block = twice // 2
    rows_all = blocks * group
    tall, wide = 16, 128
    pieces = x_ref.shape[0] // blocks
    first = (x_ref.shape[0] - 1 - lax.axis_index("ctx")) * group % turned_ref.shape[0]
    turned = mirror_rows(turned_ref[pl.ds(pl.multiple_of(first, group), group)])

    def rows_of(position):
        return jnp.concatenate(
            [
                jnp.concatenate([x_ref[m * pieces + s, position] for s in range(pieces)], axis=1)
                for m in range(blocks)
            ],
            axis=0,
        )

    def times(index, side, source, row, lane):
        data = []
        for m in range(blocks):
            rows = slice(source + m * group + row, source + m * group + row + tall)
            data.append((spec_ref[rows, lane : lane + wide], spec_ref[rows, block + lane : block + lane + wide]))
        sums = [None] * blocks
        for lag in range(blocks):
            h_ref = (own_ref, paired_ref)[side]
            f_re = h_ref[index, lag, row : row + tall, lane : lane + wide]
            f_im = h_ref[index, lag, row : row + tall, block + lane : block + lane + wide]
            for m in range(blocks - lag):
                target, (d_re, d_im) = (m + lag, data[m]) if side == 0 else (m, data[m + lag])
                if side == 0:
                    real, imag = f_re * d_re - f_im * d_im, f_re * d_im + f_im * d_re
                else:
                    real, imag = f_re * d_re + f_im * d_im, f_re * d_im - f_im * d_re
                if sums[target] is not None:
                    real, imag = sums[target][0] + real, sums[target][1] + imag
                sums[target] = (real, imag)
        return sums

    def keep(target, row, lane, sums, both_parts):
        for m in range(blocks):
            rows = slice(target + m * group + row, target + m * group + row + tall)
            for part in range(2):
                cols = slice(part * block + lane, part * block + lane + wide)
                high_ref[rows, cols], low = halves(sums[m][part])
                if both_parts:
                    low_ref[rows, cols] = low

    chunks = [(row, lane) for row in range(0, group, tall) for lane in range(0, block, wide)]

    value = rows_of(0)
    gate = rows_of(1).astype(jnp.float32)
    spec_ref[:rows_all] = mul2(value, table_ref)
    sides = [slice(side * rows_all, (side + 1) * rows_all) for side in range(2)]
    put_filter(poles, 0, turned, time_ref.at[0])
    spec = mul3(*halves(time_ref[0]), table_ref)
    for row, lane in chunks:
        keep(0, row, lane, times(0, 0, 0, row, lane), True)
    put_spectra(spec, paired_ref.at[0])
    gated = [gate * mul3(high_ref[sides[0]], low_ref[sides[0]], back_ref)]
    put_filter(poles, 1, turned, time_ref.at[1])
    for row, lane in chunks:
        keep(rows_all, row, lane, times(0, 1, 0, row, lane), True)
    gated.append(gate * mul3(high_ref[sides[1]], low_ref[sides[1]], back_ref))
    spec = mul3(*halves(time_ref[1]), table_ref)
    for side in range(2):
        spec_ref[sides[side]] = mul3(*halves(gated[side]), table_ref)
    put_spectra(spec, paired_ref.at[1])
    for row, lane in chunks:
        ahead, back = times(1, 0, 0, row, lane), times(1, 1, rows_all, row, lane)
        keep(0, row, lane, [(a[0] + b[0], a[1] + b[1]) for a, b in zip(ahead, back)], False)
    post = rows_of(2)
    tok = block // pieces
    sends = []
    for part in range(2):
        rows = slice(part * rows_all // 2, (part + 1) * rows_all // 2)
        summed = mul2(high_ref[rows], back_ref)
        mixed = (post[rows].astype(jnp.float32) * summed).astype(jnp.bfloat16)
        first = part * blocks // 2 * pieces
        for m in range(blocks // 2):
            for s in range(pieces):
                ready_ref[first + m * pieces + s] = mixed[m * group : (m + 1) * group, s * tok : (s + 1) * tok]
        span = pl.ds(first, blocks // 2 * pieces)
        for copy in range(out_hbm.shape[1]):
            sends.append(pltpu.make_async_copy(ready_ref.at[span], out_hbm.at[span, copy], sems.at[part, copy]))
            sends[-1].start()
    for send in sends:
        send.wait()


def project_kernel(mixed_ref, *refs):
    w_refs, (out_hbm, held_ref, ready_ref, sems) = refs[:-4], refs[-4:]
    rows = w_refs[0].shape[0]
    tile = 2 * rows
    position = lax.axis_index("ctx")
    parity = position % 2
    even = pl.multiple_of(parity * rows, rows)
    odd = pl.multiple_of((1 - parity) * rows, rows)
    masks = (0, 1 + parity, 2 - parity, 3)
    ctx_count, tp_count = mixed_ref.shape[:2]
    mixed = jnp.concatenate([mixed_ref[i, z] for z in range(tp_count) for i in range(ctx_count)], axis=0)
    sends = []
    for half in range(2):
        total = mul(jnp.concatenate([w_ref[...] for w_ref in w_refs[4 * half : 4 * half + 4]], axis=0), mixed)
        for pair in range(2):
            place = 2 * half + pair
            held_ref[place, pl.ds(even, rows)] = total[pair * tile : pair * tile + rows]
            held_ref[place, pl.ds(odd, rows)] = total[pair * tile + rows : (pair + 1) * tile]
            ready_ref[place] = held_ref[place].T.astype(jnp.bfloat16)
            columns = pl.ds(pl.multiple_of((position // 2 ^ masks[place]) * tile, tile), tile)
            sends.append(pltpu.make_async_copy(ready_ref.at[place], out_hbm.at[:, columns], sems.at[place]))
            sends[-1].start()
    for send in sends:
        send.wait()


def whole_call(kernel, out_shape, scratch, flops, nbytes, *operands, in_hbm=0, out_hbm=()):
    results = pl.pallas_call(
        kernel,
        out_shape=out_shape,
        in_specs=[
            pl.BlockSpec(memory_space=pltpu.HBM if place < in_hbm else pltpu.VMEM) for place in range(len(operands))
        ],
        out_specs=[
            pl.BlockSpec(memory_space=pltpu.HBM if place in out_hbm else pltpu.VMEM) for place in range(len(out_shape))
        ],
        scratch_shapes=scratch,
        cost_estimate=pl.CostEstimate(flops=flops, bytes_accessed=nbytes, transcendentals=0),
        compiler_params=pltpu.CompilerParams(vmem_limit_bytes=None if in_hbm else 32 * 2**20),
    )(*operands)
    return results if len(out_shape) > 1 else results[0]


def blocked(x_gate, x_post, values, decay, residue, w_out):
    tok, width = x_gate.shape
    ctx_count = lax.axis_size("ctx")
    tp_count = lax.axis_size("tp")
    group = width // ctx_count
    poles = decay.shape[2]
    block = 2 * tok
    blocks = tok * ctx_count // block
    rows, channels = w_out.shape
    half = 2 * poles

    packed, own, mirrored = whole_call(
        pack_kernel,
        (
            jax.ShapeDtypeStruct((ctx_count, 3, group, tok), jnp.bfloat16),
            jax.ShapeDtypeStruct((2 * half, tok), jnp.float32),
            jax.ShapeDtypeStruct((2 * half, tok), jnp.float32),
        ),
        [
            pltpu.VMEM((3, tok, width), jnp.bfloat16),
            pltpu.VMEM((2, 2 * half, tok), jnp.float32),
            pltpu.VMEM((ctx_count, 3, group, tok), jnp.bfloat16),
            pltpu.SemaphoreType.DMA((7,)),
            pltpu.SemaphoreType.DMA((5,)),
        ],
        0,
        6 * tok * width * 2,
        x_gate,
        values,
        x_post,
        jnp.swapaxes(decay, 1, 2).reshape(half, width),
        jnp.swapaxes(residue, 1, 2).reshape(half, width),
        in_hbm=5,
        out_hbm=(0, 1, 2),
    )
    paired = lax.ppermute(mirrored, "tp", [(z, tp_count - 1 - z) for z in range(tp_count)])
    received = lax.all_to_all(packed, "ctx", split_axis=0, concat_axis=0, tiled=True)

    own_spectra, table, back_table = whole_call(
        functools.partial(filter_kernel, poles),
        (
            jax.ShapeDtypeStruct((2, blocks, group, 2 * block), jnp.float32),
            jax.ShapeDtypeStruct((2 * block, 2 * block), jnp.bfloat16),
            jax.ShapeDtypeStruct((4 * block, block), jnp.bfloat16),
        ),
        [
            pltpu.VMEM((2, blocks * group, block), jnp.float32),
            pltpu.VMEM((tok, 2 * half), jnp.float32),
        ],
        2 * 2 * blocks * group * block * 2 * block * 3,
        2 * blocks * group * 2 * block * 4,
        own,
    )
    w_late, own_spectra = lax.optimization_barrier((w_out, own_spectra))

    def cross(block, even_mask, odd_mask):
        return lax.ppermute(block, "ctx", [(i, i ^ (odd_mask if i % 2 else even_mask)) for i in range(ctx_count)])

    w_first = cross(w_late, 2, 4)
    mixed = whole_call(
        functools.partial(conv_kernel, poles),
        (jax.ShapeDtypeStruct((ctx_count, tp_count, group, tok), jnp.bfloat16),),
        [
            pltpu.VMEM((2, blocks, group, 2 * block), jnp.float32),
            pltpu.VMEM((2, blocks * group, block), jnp.float32),
            pltpu.VMEM((tok, 2 * half), jnp.float32),
            pltpu.VMEM((2 * blocks * group, 2 * block), jnp.float32),
            pltpu.VMEM((2 * blocks * group, 2 * block), jnp.bfloat16),
            pltpu.VMEM((2 * blocks * group, 2 * block), jnp.bfloat16),
            pltpu.VMEM((ctx_count, group, tok), jnp.bfloat16),
            pltpu.SemaphoreType.DMA((2, tp_count)),
        ],
        2 * 8 * blocks * group * block * 2 * block * 3,
        4 * blocks * group * 2 * block * 4,
        received,
        own_spectra,
        paired,
        table,
        back_table,
        out_hbm=(0,),
    )
    mixed, w_first, w_own = lax.optimization_barrier((mixed, w_first, w_out))
    w_third = cross(w_first, 4, 2)
    w_second = cross(w_own, 4, 2)
    w_other = [partner(block, "ctx", 0) for block in (w_own, w_first, w_second, w_third)]
    w_blocks = [w_own, w_other[0], w_first, w_other[2], w_second, w_other[1], w_third, w_other[3]]
    every = lax.all_to_all(
        mixed.reshape(ctx_count * tp_count, group, tok), ("ctx", "tp"), split_axis=0, concat_axis=0, tiled=True
    ).reshape(ctx_count, tp_count, group, tok)
    return whole_call(
        project_kernel,
        (jax.ShapeDtypeStruct((tok, rows * ctx_count), jnp.bfloat16),),
        [
            pltpu.VMEM((ctx_count // 2, 2 * rows, tok), jnp.float32),
            pltpu.VMEM((ctx_count // 2, tok, 2 * rows), jnp.bfloat16),
            pltpu.SemaphoreType.DMA((ctx_count // 2,)),
        ],
        2 * tok * rows * ctx_count * channels,
        2 * rows * ctx_count * channels,
        every,
        *w_blocks,
        out_hbm=(0,),
    )


def local(x_gate, x_post, values, decay, residue, w_out):
    tok, width = x_gate.shape
    ctx_count = lax.axis_size("ctx")
    if tok == 128 and width == 512 and ctx_count == 8 and w_out.shape[0] == 64 and lax.axis_size("tp") == 4:
        return blocked(x_gate, x_post, values, decay, residue, w_out)
    return general(x_gate, x_post, values, decay, residue, w_out)


def solution(mesh):
    in_specs = (
        P("ctx", "tp"),
        P("ctx", "tp"),
        P("ctx", "tp"),
        P(None, "tp", None),
        P(None, "tp", None),
        P(("tp", "ctx"), None),
    )
    out_specs = P("ctx", "tp")
    return jax.shard_map(local, mesh=mesh, in_specs=in_specs, out_specs=out_specs, check_vma=False)
```

```python
import functools
import math

import jax
import jax.numpy as jnp
from jax import lax
from jax.experimental import pallas as pl
from jax.experimental.pallas import tpu as pltpu
from jax.sharding import PartitionSpec as P

HIGHEST = lax.Precision.HIGHEST


def partner(value, axis, bit):
    mask = 2**bit
    pairs = [(source, source ^ mask) for source in range(lax.axis_size(axis))]
    return lax.ppermute(value, axis, pairs)


def radices(length_all):
    last_radix = min(128, length_all // 4)
    first_radix = min(32, length_all // last_radix)
    return (first_radix, length_all // (first_radix * last_radix), last_radix)


def rotation(row_count, col_count, modulus):
    product = (
        lax.broadcasted_iota(jnp.int32, (row_count, col_count), 0)
        * lax.broadcasted_iota(jnp.int32, (row_count, col_count), 1)
        % modulus
    )
    angle = product.astype(jnp.float32) * (2.0 * math.pi / modulus)
    return (jnp.cos(angle), -jnp.sin(angle))


def tables(radix_sizes):
    first_radix, mid_radix, last_radix = radix_sizes
    length_all = first_radix * mid_radix * last_radix
    outer_real, outer_imag = rotation(first_radix, first_radix, first_radix)
    mid_real, mid_imag = rotation(mid_radix, mid_radix, mid_radix)
    last_real, last_imag = rotation(last_radix, last_radix, last_radix)
    twist_real, twist_imag = rotation(first_radix, mid_radix * last_radix, length_all)
    twist_real = twist_real.reshape(first_radix, mid_radix, last_radix)
    twist_imag = twist_imag.reshape(first_radix, mid_radix, last_radix)
    inner_real, inner_imag = rotation(mid_radix, last_radix, mid_radix * last_radix)
    return (
        outer_real,
        outer_imag,
        mid_real,
        mid_imag,
        last_real,
        last_imag,
        twist_real,
        twist_imag,
        inner_real,
        inner_imag,
    )


def apply_matrix(pattern, real_part, imag_part, matrix_real, matrix_imag):
    out_real = jnp.einsum(pattern, real_part, matrix_real, precision=HIGHEST) - jnp.einsum(
        pattern, imag_part, matrix_imag, precision=HIGHEST
    )
    out_imag = jnp.einsum(pattern, real_part, matrix_imag, precision=HIGHEST) + jnp.einsum(
        pattern, imag_part, matrix_real, precision=HIGHEST
    )
    return (out_real, out_imag)


def complex_times(left_real, left_imag, right_real, right_imag):
    return (
        left_real * right_real - left_imag * right_imag,
        left_real * right_imag + left_imag * right_real,
    )


def forward(real_part, imag_part, table_set, radix_sizes):
    first_radix, mid_radix, last_radix = radix_sizes
    half_first = first_radix // 2
    batch_rows = real_part.shape[0]
    (
        outer_real,
        outer_imag,
        mid_real,
        mid_imag,
        last_real,
        last_imag,
        twist_real,
        twist_imag,
        inner_real,
        inner_imag,
    ) = table_set
    real_part = real_part.reshape(batch_rows, half_first, mid_radix, last_radix)
    imag_part = imag_part.reshape(batch_rows, half_first, mid_radix, last_radix)
    real_part, imag_part = apply_matrix(
        "banm,ak->bknm", real_part, imag_part, outer_real[:half_first], outer_imag[:half_first]
    )
    real_part, imag_part = complex_times(real_part, imag_part, twist_real, twist_imag)
    real_part, imag_part = apply_matrix("bknm,nj->bkjm", real_part, imag_part, mid_real, mid_imag)
    real_part, imag_part = complex_times(real_part, imag_part, inner_real, inner_imag)
    return apply_matrix("bkjm,mq->bkjq", real_part, imag_part, last_real, last_imag)


def inverse(real_part, imag_part, table_set, radix_sizes):
    first_radix, mid_radix, last_radix = radix_sizes
    half_first = first_radix // 2
    batch_rows = real_part.shape[0]
    (
        outer_real,
        outer_imag,
        mid_real,
        mid_imag,
        last_real,
        last_imag,
        twist_real,
        twist_imag,
        inner_real,
        inner_imag,
    ) = table_set
    real_part, imag_part = apply_matrix(
        "bkjq,mq->bkjm", real_part, imag_part, last_real / last_radix, -last_imag / last_radix
    )
    real_part, imag_part = complex_times(real_part, imag_part, inner_real, -inner_imag)
    real_part, imag_part = apply_matrix(
        "bkjm,nj->bknm", real_part, imag_part, mid_real / mid_radix, -mid_imag / mid_radix
    )
    real_part, imag_part = complex_times(real_part, imag_part, twist_real, -twist_imag)
    matrix_real = outer_real[:half_first] / first_radix
    matrix_imag = -outer_imag[:half_first] / first_radix
    out_real, out_imag = apply_matrix(
        "bknm,ak->banm", real_part, imag_part, matrix_real, matrix_imag
    )
    return (out_real.reshape(batch_rows, -1), out_imag.reshape(batch_rows, -1))


def spectrum(decay_rows, residue_rows, radix_sizes, seq_length):
    first_radix, mid_radix, last_radix = radix_sizes
    length_all = first_radix * mid_radix * last_radix
    poles = decay_rows.shape[1]
    shape_all = (first_radix, mid_radix, last_radix)
    frequency = (
        lax.broadcasted_iota(jnp.int32, shape_all, 0)
        + first_radix * lax.broadcasted_iota(jnp.int32, shape_all, 1)
        + first_radix * mid_radix * lax.broadcasted_iota(jnp.int32, shape_all, 2)
    )
    half_angle = frequency.astype(jnp.float32) * (math.pi / length_all)
    sin_half = jnp.sin(half_angle)
    sin_full = jnp.sin(2.0 * half_angle)
    parity_sign = (1 - 2 * (frequency % 2)).astype(jnp.float32)

    def add_pole(pole_index, running):
        run_real, run_imag = running
        rate_col = lax.dynamic_slice_in_dim(decay_rows, pole_index, 1, 1).reshape(-1, 1, 1, 1)
        weight = lax.dynamic_slice_in_dim(residue_rows, pole_index, 1, 1).reshape(
            -1, 1, 1, 1
        ) * jnp.sqrt(2.0 * rate_col / poles)
        retained = jnp.exp(-rate_col)
        den_real = -jnp.expm1(-rate_col) + 2.0 * retained * sin_half * sin_half
        den_imag = retained * sin_full
        pole_scale = (
            weight
            * (1.0 - jnp.exp(-rate_col * seq_length) * parity_sign)
            / (den_real * den_real + den_imag * den_imag)
        )
        return (run_real + pole_scale * den_real, run_imag - pole_scale * den_imag)

    zeros_all = jnp.zeros((decay_rows.shape[0],) + shape_all, jnp.float32)
    return lax.fori_loop(0, poles, add_pole, (zeros_all, zeros_all))


def general(x_gate, x_post, values, decay, residue, w_out):
    tok_rows, block_width = x_gate.shape
    ctx_count = lax.axis_size("ctx")
    tp_count = lax.axis_size("tp")
    chan_group = block_width // ctx_count
    seq_length = tok_rows * ctx_count
    radix_sizes = radices(2 * seq_length)
    table_set = tables(radix_sizes)
    first_row = lax.axis_index("ctx") * chan_group
    own_rate = lax.dynamic_slice_in_dim(decay, first_row, chan_group, 1)
    own_residue = lax.dynamic_slice_in_dim(residue, first_row, chan_group, 1)
    own_spec = [
        spectrum(own_rate[filter_index], own_residue[filter_index], radix_sizes, seq_length)
        for filter_index in range(2)
    ]
    forward_rows = [x_gate, values] + [x_post]
    row_count = len(forward_rows)
    base_rows = jnp.stack(forward_rows)
    copied = base_rows
    for bit_index in range(tp_count.bit_length() - 1):
        copied = partner(copied, "tp", bit_index)
    sent_rows = jnp.concatenate([base_rows, copied[:, :, ::-1]], axis=0)
    received = lax.all_to_all(
        jnp.swapaxes(sent_rows, 1, 2), "ctx", split_axis=1, concat_axis=2, tiled=True
    )
    gate_fwd = received[0].astype(jnp.float32)
    value_fwd = received[1].astype(jnp.float32)
    mirrored = received[row_count:, :, ::-1].astype(jnp.float32)
    spec_real, spec_imag = forward(value_fwd, mirrored[1], table_set, radix_sizes)
    spec_real, spec_imag = complex_times(spec_real, spec_imag, own_spec[0][0], own_spec[0][1])
    along_fwd, along_rev = inverse(spec_real, spec_imag, table_set, radix_sizes)
    spec_real, spec_imag = forward(
        gate_fwd * along_fwd, mirrored[0] * along_rev, table_set, radix_sizes
    )
    spec_real, spec_imag = complex_times(spec_real, spec_imag, own_spec[1][0], own_spec[1][1])
    sum_fwd, sum_rev = inverse(spec_real, spec_imag, table_set, radix_sizes)
    sum_fwd = received[2].astype(jnp.float32) * sum_fwd
    sum_rev = mirrored[2] * sum_rev
    results = jnp.stack([sum_fwd, sum_rev[:, ::-1]])
    returned = lax.all_to_all(
        results.astype(jnp.bfloat16), "ctx", split_axis=2, concat_axis=1, tiled=True
    ).astype(results.dtype)
    flipped = returned[1, ::-1, :]
    for bit_index in range(tp_count.bit_length() - 1):
        flipped = partner(flipped.astype(jnp.bfloat16), "tp", bit_index).astype(flipped.dtype)
    total_rows = returned[0] + flipped
    total_rows = total_rows.T
    mixed_rows = total_rows.astype(jnp.bfloat16)
    whole_rows = lax.all_gather(mixed_rows, "tp", axis=1, tiled=True)
    projected = lax.dot_general(
        whole_rows,
        lax.all_gather(w_out, "ctx", axis=0, tiled=True),
        (((1,), (1,)), ((), ())),
        preferred_element_type=jnp.float32,
    )
    return projected.astype(jnp.bfloat16)


def cycle(row_factor, col_factor, modulus):
    quarter = modulus // 4
    turned = row_factor * col_factor + quarter // 2
    quadrant = turned // quarter % 4
    angle = (turned % quarter - quarter // 2).astype(jnp.float32) * (2.0 * math.pi / modulus)
    square = angle * angle

    def series(first):
        total = jnp.zeros_like(square)
        for power in range(first + 10, first, -2):
            total = (total + (-1.0) ** ((power - first) // 2) / math.factorial(power)) * square
        return total

    cos = 1.0 + series(0)
    sin = angle + angle * series(1)
    odd = quadrant % 2 == 1
    cos, sin = jnp.where(odd, sin, cos), jnp.where(odd, cos, sin)
    return jnp.where((quadrant == 1) | (quadrant == 2), -cos, cos), jnp.where(quadrant >= 2, -sin, sin)


def put_tables(table_ref, back_ref):
    block = back_ref.shape[1]
    modulus = 4 * block
    coarse = 16
    rows = lax.broadcasted_iota(jnp.int32, (coarse, block), 0)
    cols = lax.broadcasted_iota(jnp.int32, (coarse, block), 1)

    def parts(big, small):
        for place in range(block // coarse):
            big_cos, big_sin = (part[place : place + 1] for part in big)
            cos = halves(big_cos * small[0] - big_sin * small[1])
            sin = halves(-(big_sin * small[0] + big_cos * small[1]))
            yield place * coarse, cos, sin

    def put(ref, first, columns, value):
        ref[first : first + coarse, columns] = value[0]
        low = first + ref.shape[0] // 2
        ref[low : low + coarse, columns] = value[1]

    frequency = 2 * cols + 1
    for first, cos, sin in parts(cycle(coarse * rows, frequency, modulus), cycle(rows, frequency, modulus)):
        put(table_ref, first, slice(0, block), cos)
        put(table_ref, first, slice(block, 2 * block), sin)
    for first, cos, sin in parts(cycle(2 * coarse * rows, cols, modulus), cycle(2 * rows + 1, cols, modulus)):
        put(back_ref, first, slice(0, block), cos)
        put(back_ref, block + first, slice(0, block), sin)


def halves(value):
    high = value.astype(jnp.bfloat16)
    return high, (value - high.astype(jnp.float32)).astype(jnp.bfloat16)


def mul(left, right):
    return jnp.dot(left, right, preferred_element_type=jnp.float32)


def mul3(high, low, table_ref):
    left = jnp.concatenate([high, high, low], axis=1)
    return mul(left, jnp.concatenate([table_ref[...], table_ref[: table_ref.shape[0] // 2]], axis=0))


def mul2(value, table_ref):
    return mul(jnp.concatenate([value, value], axis=1), table_ref[...])


def pack_kernel(
    gate_hbm, value_hbm, post_hbm, decay_hbm, residue_hbm,
    out_hbm, own_hbm, sent_hbm, held_ref, cut_ref, ready_ref, sems, out_sems,
):
    ctx_count, _, group, tok = out_hbm.shape
    width = gate_hbm.shape[1]
    half = decay_hbm.shape[0]
    position = lax.axis_index("ctx")
    pairs = []
    for place, index in enumerate((position, ctx_count - 1 - position)):
        columns = pl.ds(pl.multiple_of(index * group // tok * tok, tok), tok)
        pairs += [(decay_hbm.at[:, columns], cut_ref.at[place, :half]), (residue_hbm.at[:, columns], cut_ref.at[place, half:])]
    pairs += [(source, held_ref.at[place]) for place, source in enumerate((value_hbm, gate_hbm, post_hbm))]
    copies = [pltpu.make_async_copy(*pair, sems.at[place]) for place, pair in enumerate(pairs)]
    for copy in copies:
        copy.start()
    sends = []
    for place, target in enumerate((own_hbm, sent_hbm)):
        copies[2 * place].wait()
        copies[2 * place + 1].wait()
        sends.append(pltpu.make_async_copy(cut_ref.at[place], target, out_sems.at[3 + place]))
        sends[-1].start()
    for place, copy in enumerate(copies[4:]):
        copy.wait()
        for first in range(0, width, tok):
            turned = held_ref[place, :, first : first + tok].T
            for part in range(tok // group):
                ready_ref[first // group + part, place] = turned[part * group : (part + 1) * group]
        sends.append(pltpu.make_async_copy(ready_ref.at[:, place], out_hbm.at[:, place], out_sems.at[place]))
        sends[-1].start()
    for send in sends:
        send.wait()


def mirror_rows(value):
    row = lax.broadcasted_iota(jnp.int32, (8, value.shape[1]), 0)
    result = []
    for first in range(value.shape[0] - 8, -1, -8):
        part = value[first : first + 8]
        for shift in (1, 2, 4):
            part = jnp.where(row & shift == 0, pltpu.roll(part, 8 - shift, 0), pltpu.roll(part, shift, 0))
        result.append(part)
    return jnp.concatenate(result, axis=0)


def put_filter(poles, index, turned, time_ref):
    lanes = 128
    rows_all, block = time_ref.shape
    group = turned.shape[0]
    ramp = lax.broadcasted_iota(jnp.int32, (8, lanes), 1).astype(jnp.float32)
    for row in range(0, group, 8):
        rows = slice(row, row + 8)
        rate = turned[rows, index * poles : (index + 1) * poles]
        scale = turned[rows, (2 + index) * poles : (3 + index) * poles] * (jnp.sqrt(rate * (2.0 / poles)) / block)
        slope = rate * -math.log2(math.e)
        sums = [None] * (rows_all // group * block // lanes)
        for pole in range(poles):
            level = jnp.broadcast_to(slope[:, pole : pole + 1], (8, lanes))
            term = scale[:, pole : pole + 1] * jnp.exp2(level * ramp)
            step = jnp.exp2(level * lanes)
            for place in range(len(sums)):
                sums[place] = term if pole == 0 else sums[place] + term
                if place + 1 < len(sums):
                    term = term * step
        for place, total in enumerate(sums):
            lag, lane = divmod(place * lanes, block)
            time_ref[lag * group + row : lag * group + row + 8, lane : lane + lanes] = total


def put_spectra(spec, out_ref):
    blocks, group, twice = out_ref.shape
    block = twice // 2
    sign = (1 - 2 * (lax.broadcasted_iota(jnp.int32, (group, block), 1) % 2)).astype(jnp.float32)
    for lag in range(blocks):
        real = spec[lag * group : (lag + 1) * group, :block]
        imag = spec[lag * group : (lag + 1) * group, block:]
        if lag > 0:
            real = real - sign * spec[(lag - 1) * group : lag * group, block:]
            imag = imag + sign * spec[(lag - 1) * group : lag * group, :block]
        out_ref[lag, :, :block] = real
        out_ref[lag, :, block:] = imag


def filter_kernel(poles, par_ref, out_ref, table_ref, back_ref, time_ref, turned_ref):
    group = out_ref.shape[2]
    put_tables(table_ref, back_ref)
    turned_ref[...] = par_ref[...].T
    turned = turned_ref[pl.ds(pl.multiple_of(lax.axis_index("ctx") * group % turned_ref.shape[0], group), group)]
    put_filter(poles, 0, turned, time_ref.at[0])
    spec = mul3(*halves(time_ref[0]), table_ref)
    put_filter(poles, 1, turned, time_ref.at[1])
    put_spectra(spec, out_ref.at[0])
    put_spectra(mul3(*halves(time_ref[1]), table_ref), out_ref.at[1])


def conv_kernel(
    poles, x_ref, own_ref, par_ref, table_ref, back_ref, out_hbm,
    paired_ref, time_ref, turned_ref, spec_ref, high_ref, low_ref, ready_ref, sems,
):
    turned_ref[...] = par_ref[...].T
    blocks, group, twice = own_ref.shape[1:]
    block = twice // 2
    rows_all = blocks * group
    tall, wide = 16, 128
    pieces = x_ref.shape[0] // blocks
    first = (x_ref.shape[0] - 1 - lax.axis_index("ctx")) * group % turned_ref.shape[0]
    turned = mirror_rows(turned_ref[pl.ds(pl.multiple_of(first, group), group)])

    def rows_of(position):
        return jnp.concatenate(
            [
                jnp.concatenate([x_ref[m * pieces + s, position] for s in range(pieces)], axis=1)
                for m in range(blocks)
            ],
            axis=0,
        )

    def times(index, side, source, row, lane):
        data = []
        for m in range(blocks):
            rows = slice(source + m * group + row, source + m * group + row + tall)
            data.append((spec_ref[rows, lane : lane + wide], spec_ref[rows, block + lane : block + lane + wide]))
        sums = [None] * blocks
        for lag in range(blocks):
            h_ref = (own_ref, paired_ref)[side]
            f_re = h_ref[index, lag, row : row + tall, lane : lane + wide]
            f_im = h_ref[index, lag, row : row + tall, block + lane : block + lane + wide]
            for m in range(blocks - lag):
                target, (d_re, d_im) = (m + lag, data[m]) if side == 0 else (m, data[m + lag])
                if side == 0:
                    real, imag = f_re * d_re - f_im * d_im, f_re * d_im + f_im * d_re
                else:
                    real, imag = f_re * d_re + f_im * d_im, f_re * d_im - f_im * d_re
                if sums[target] is not None:
                    real, imag = sums[target][0] + real, sums[target][1] + imag
                sums[target] = (real, imag)
        return sums

    def keep(target, row, lane, sums, both_parts):
        for m in range(blocks):
            rows = slice(target + m * group + row, target + m * group + row + tall)
            for part in range(2):
                cols = slice(part * block + lane, part * block + lane + wide)
                high_ref[rows, cols], low = halves(sums[m][part])
                if both_parts:
                    low_ref[rows, cols] = low

    chunks = [(row, lane) for row in range(0, group, tall) for lane in range(0, block, wide)]

    value = rows_of(0)
    gate = rows_of(1).astype(jnp.float32)
    spec_ref[:rows_all] = mul2(value, table_ref)
    sides = [slice(side * rows_all, (side + 1) * rows_all) for side in range(2)]
    put_filter(poles, 0, turned, time_ref.at[0])
    spec = mul3(*halves(time_ref[0]), table_ref)
    for row, lane in chunks:
        keep(0, row, lane, times(0, 0, 0, row, lane), True)
    put_spectra(spec, paired_ref.at[0])
    gated = [gate * mul3(high_ref[sides[0]], low_ref[sides[0]], back_ref)]
    put_filter(poles, 1, turned, time_ref.at[1])
    for row, lane in chunks:
        keep(rows_all, row, lane, times(0, 1, 0, row, lane), True)
    gated.append(gate * mul3(high_ref[sides[1]], low_ref[sides[1]], back_ref))
    spec = mul3(*halves(time_ref[1]), table_ref)
    for side in range(2):
        spec_ref[sides[side]] = mul3(*halves(gated[side]), table_ref)
    put_spectra(spec, paired_ref.at[1])
    for row, lane in chunks:
        ahead, back = times(1, 0, 0, row, lane), times(1, 1, rows_all, row, lane)
        keep(0, row, lane, [(a[0] + b[0], a[1] + b[1]) for a, b in zip(ahead, back)], False)
    post = rows_of(2)
    tok = block // pieces
    sends = []
    for part in range(2):
        rows = slice(part * rows_all // 2, (part + 1) * rows_all // 2)
        summed = mul2(high_ref[rows], back_ref)
        mixed = (post[rows].astype(jnp.float32) * summed).astype(jnp.bfloat16)
        first = part * blocks // 2 * pieces
        for m in range(blocks // 2):
            for s in range(pieces):
                ready_ref[first + m * pieces + s] = mixed[m * group : (m + 1) * group, s * tok : (s + 1) * tok]
        span = pl.ds(first, blocks // 2 * pieces)
        for copy in range(out_hbm.shape[1]):
            sends.append(pltpu.make_async_copy(ready_ref.at[span], out_hbm.at[span, copy], sems.at[part, copy]))
            sends[-1].start()
    for send in sends:
        send.wait()


def project_kernel(places, mixed_ref, *refs):
    w_refs, (out_hbm, held_ref, ready_ref, sems) = refs[: 2 * len(places)], refs[-4:]
    rows = w_refs[0].shape[0]
    tile = 2 * rows
    position = lax.axis_index("ctx")
    parity = position % 2
    even = pl.multiple_of(parity * rows, rows)
    odd = pl.multiple_of((1 - parity) * rows, rows)
    masks = (0, 1 + parity, 2 - parity, 3)
    ctx_count, tp_count = mixed_ref.shape[:2]
    mixed = jnp.concatenate([mixed_ref[i, z] for z in range(tp_count) for i in range(ctx_count)], axis=0)
    sends = []
    for first in range(0, len(places), 2):
        part = places[first : first + 2]
        total = mul(jnp.concatenate([w_ref[...] for w_ref in w_refs[2 * first : 2 * first + 4]], axis=0), mixed)
        for pair, place in enumerate(part):
            slot = first + pair
            held_ref[slot, pl.ds(even, rows)] = total[pair * tile : pair * tile + rows]
            held_ref[slot, pl.ds(odd, rows)] = total[pair * tile + rows : (pair + 1) * tile]
            ready_ref[slot] = held_ref[slot].T.astype(jnp.bfloat16)
            columns = pl.ds(pl.multiple_of((position // 2 ^ masks[place]) * tile, tile), tile)
            sends.append(pltpu.make_async_copy(ready_ref.at[slot], out_hbm.at[:, columns], sems.at[slot]))
            sends[-1].start()
    for send in sends:
        send.wait()


def whole_call(kernel, out_shape, scratch, flops, nbytes, *operands, in_hbm=0, out_hbm=(), into=None):
    spaces = [pltpu.HBM if place < in_hbm else pltpu.VMEM for place in range(len(operands))]
    aliases = {}
    if into is not None:
        aliases = {len(operands): 0}
        operands += (into,)
        spaces.append(pltpu.HBM)
    results = pl.pallas_call(
        kernel,
        out_shape=out_shape,
        in_specs=[pl.BlockSpec(memory_space=space) for space in spaces],
        input_output_aliases=aliases,
        out_specs=[
            pl.BlockSpec(memory_space=pltpu.HBM if place in out_hbm else pltpu.VMEM) for place in range(len(out_shape))
        ],
        scratch_shapes=scratch,
        cost_estimate=pl.CostEstimate(flops=flops, bytes_accessed=nbytes, transcendentals=0),
        compiler_params=pltpu.CompilerParams(vmem_limit_bytes=None if in_hbm else 32 * 2**20),
    )(*operands)
    return results if len(out_shape) > 1 else results[0]


def blocked(x_gate, x_post, values, decay, residue, w_out):
    tok, width = x_gate.shape
    ctx_count = lax.axis_size("ctx")
    tp_count = lax.axis_size("tp")
    group = width // ctx_count
    poles = decay.shape[2]
    block = 2 * tok
    blocks = tok * ctx_count // block
    rows, channels = w_out.shape
    half = 2 * poles

    packed, own, mirrored = whole_call(
        pack_kernel,
        (
            jax.ShapeDtypeStruct((ctx_count, 3, group, tok), jnp.bfloat16),
            jax.ShapeDtypeStruct((2 * half, tok), jnp.float32),
            jax.ShapeDtypeStruct((2 * half, tok), jnp.float32),
        ),
        [
            pltpu.VMEM((3, tok, width), jnp.bfloat16),
            pltpu.VMEM((2, 2 * half, tok), jnp.float32),
            pltpu.VMEM((ctx_count, 3, group, tok), jnp.bfloat16),
            pltpu.SemaphoreType.DMA((7,)),
            pltpu.SemaphoreType.DMA((5,)),
        ],
        0,
        6 * tok * width * 2,
        x_gate,
        values,
        x_post,
        jnp.swapaxes(decay, 1, 2).reshape(half, width),
        jnp.swapaxes(residue, 1, 2).reshape(half, width),
        in_hbm=5,
        out_hbm=(0, 1, 2),
    )
    paired = lax.ppermute(mirrored, "tp", [(z, tp_count - 1 - z) for z in range(tp_count)])
    received = lax.all_to_all(packed, "ctx", split_axis=0, concat_axis=0, tiled=True)

    w_late, mirrored = lax.optimization_barrier((w_out, mirrored))

    def cross(block, even_mask, odd_mask):
        return lax.ppermute(block, "ctx", [(i, i ^ (odd_mask if i % 2 else even_mask)) for i in range(ctx_count)])

    w_first = cross(w_late, 2, 4)
    own_spectra, table, back_table = whole_call(
        functools.partial(filter_kernel, poles),
        (
            jax.ShapeDtypeStruct((2, blocks, group, 2 * block), jnp.float32),
            jax.ShapeDtypeStruct((2 * block, 2 * block), jnp.bfloat16),
            jax.ShapeDtypeStruct((4 * block, block), jnp.bfloat16),
        ),
        [
            pltpu.VMEM((2, blocks * group, block), jnp.float32),
            pltpu.VMEM((tok, 2 * half), jnp.float32),
        ],
        2 * 2 * blocks * group * block * 2 * block * 3,
        2 * blocks * group * 2 * block * 4,
        own,
    )
    mixed = whole_call(
        functools.partial(conv_kernel, poles),
        (jax.ShapeDtypeStruct((ctx_count, tp_count, group, tok), jnp.bfloat16),),
        [
            pltpu.VMEM((2, blocks, group, 2 * block), jnp.float32),
            pltpu.VMEM((2, blocks * group, block), jnp.float32),
            pltpu.VMEM((tok, 2 * half), jnp.float32),
            pltpu.VMEM((2 * blocks * group, 2 * block), jnp.float32),
            pltpu.VMEM((2 * blocks * group, 2 * block), jnp.bfloat16),
            pltpu.VMEM((2 * blocks * group, 2 * block), jnp.bfloat16),
            pltpu.VMEM((ctx_count, group, tok), jnp.bfloat16),
            pltpu.SemaphoreType.DMA((2, tp_count)),
        ],
        2 * 8 * blocks * group * block * 2 * block * 3,
        4 * blocks * group * 2 * block * 4,
        received,
        own_spectra,
        paired,
        table,
        back_table,
        out_hbm=(0,),
    )
    mixed, w_first, w_own = lax.optimization_barrier((mixed, w_first, w_out))
    w_third = cross(w_first, 4, 2)
    w_second = cross(w_own, 4, 2)
    w_other = [partner(block, "ctx", 0) for block in (w_own, w_first, w_second, w_third)]
    w_blocks = [w_own, w_other[0], w_first, w_other[2], w_second, w_other[1], w_third, w_other[3]]
    every = lax.all_to_all(
        mixed.reshape(ctx_count * tp_count, group, tok), ("ctx", "tp"), split_axis=0, concat_axis=0, tiled=True
    ).reshape(ctx_count, tp_count, group, tok)

    def project(places, into):
        return whole_call(
            functools.partial(project_kernel, places),
            (jax.ShapeDtypeStruct((tok, rows * ctx_count), jnp.bfloat16),),
            [
                pltpu.VMEM((len(places), 2 * rows, tok), jnp.float32),
                pltpu.VMEM((len(places), tok, 2 * rows), jnp.bfloat16),
                pltpu.SemaphoreType.DMA((len(places),)),
            ],
            2 * tok * 2 * rows * len(places) * channels,
            2 * 2 * rows * len(places) * channels,
            every,
            *w_blocks[2 * places[0] : 2 * places[-1] + 2],
            out_hbm=(0,),
            into=into,
        )

    return project((3,), project((0, 1, 2), None))


def local(x_gate, x_post, values, decay, residue, w_out):
    tok, width = x_gate.shape
    ctx_count = lax.axis_size("ctx")
    if tok == 128 and width == 512 and ctx_count == 8 and w_out.shape[0] == 64 and lax.axis_size("tp") == 4:
        return blocked(x_gate, x_post, values, decay, residue, w_out)
    return general(x_gate, x_post, values, decay, residue, w_out)


def solution(mesh):
    in_specs = (
        P("ctx", "tp"),
        P("ctx", "tp"),
        P("ctx", "tp"),
        P(None, "tp", None),
        P(None, "tp", None),
        P(("tp", "ctx"), None),
    )
    out_specs = P("ctx", "tp")
    return jax.shard_map(local, mesh=mesh, in_specs=in_specs, out_specs=out_specs, check_vma=False)
```

```python
import functools
import math

import jax
import jax.numpy as jnp
from jax import lax
from jax.experimental import pallas as pl
from jax.experimental.pallas import tpu as pltpu
from jax.sharding import PartitionSpec as P

HIGHEST = lax.Precision.HIGHEST


def partner(value, axis, bit):
    mask = 2**bit
    pairs = [(source, source ^ mask) for source in range(lax.axis_size(axis))]
    return lax.ppermute(value, axis, pairs)


def radices(length_all):
    last_radix = min(128, length_all // 4)
    first_radix = min(32, length_all // last_radix)
    return (first_radix, length_all // (first_radix * last_radix), last_radix)


def rotation(row_count, col_count, modulus):
    product = (
        lax.broadcasted_iota(jnp.int32, (row_count, col_count), 0)
        * lax.broadcasted_iota(jnp.int32, (row_count, col_count), 1)
        % modulus
    )
    angle = product.astype(jnp.float32) * (2.0 * math.pi / modulus)
    return (jnp.cos(angle), -jnp.sin(angle))


def tables(radix_sizes):
    first_radix, mid_radix, last_radix = radix_sizes
    length_all = first_radix * mid_radix * last_radix
    outer_real, outer_imag = rotation(first_radix, first_radix, first_radix)
    mid_real, mid_imag = rotation(mid_radix, mid_radix, mid_radix)
    last_real, last_imag = rotation(last_radix, last_radix, last_radix)
    twist_real, twist_imag = rotation(first_radix, mid_radix * last_radix, length_all)
    twist_real = twist_real.reshape(first_radix, mid_radix, last_radix)
    twist_imag = twist_imag.reshape(first_radix, mid_radix, last_radix)
    inner_real, inner_imag = rotation(mid_radix, last_radix, mid_radix * last_radix)
    return (
        outer_real,
        outer_imag,
        mid_real,
        mid_imag,
        last_real,
        last_imag,
        twist_real,
        twist_imag,
        inner_real,
        inner_imag,
    )


def apply_matrix(pattern, real_part, imag_part, matrix_real, matrix_imag):
    out_real = jnp.einsum(pattern, real_part, matrix_real, precision=HIGHEST) - jnp.einsum(
        pattern, imag_part, matrix_imag, precision=HIGHEST
    )
    out_imag = jnp.einsum(pattern, real_part, matrix_imag, precision=HIGHEST) + jnp.einsum(
        pattern, imag_part, matrix_real, precision=HIGHEST
    )
    return (out_real, out_imag)


def complex_times(left_real, left_imag, right_real, right_imag):
    return (
        left_real * right_real - left_imag * right_imag,
        left_real * right_imag + left_imag * right_real,
    )


def forward(real_part, imag_part, table_set, radix_sizes):
    first_radix, mid_radix, last_radix = radix_sizes
    half_first = first_radix // 2
    batch_rows = real_part.shape[0]
    (
        outer_real,
        outer_imag,
        mid_real,
        mid_imag,
        last_real,
        last_imag,
        twist_real,
        twist_imag,
        inner_real,
        inner_imag,
    ) = table_set
    real_part = real_part.reshape(batch_rows, half_first, mid_radix, last_radix)
    imag_part = imag_part.reshape(batch_rows, half_first, mid_radix, last_radix)
    real_part, imag_part = apply_matrix(
        "banm,ak->bknm", real_part, imag_part, outer_real[:half_first], outer_imag[:half_first]
    )
    real_part, imag_part = complex_times(real_part, imag_part, twist_real, twist_imag)
    real_part, imag_part = apply_matrix("bknm,nj->bkjm", real_part, imag_part, mid_real, mid_imag)
    real_part, imag_part = complex_times(real_part, imag_part, inner_real, inner_imag)
    return apply_matrix("bkjm,mq->bkjq", real_part, imag_part, last_real, last_imag)


def inverse(real_part, imag_part, table_set, radix_sizes):
    first_radix, mid_radix, last_radix = radix_sizes
    half_first = first_radix // 2
    batch_rows = real_part.shape[0]
    (
        outer_real,
        outer_imag,
        mid_real,
        mid_imag,
        last_real,
        last_imag,
        twist_real,
        twist_imag,
        inner_real,
        inner_imag,
    ) = table_set
    real_part, imag_part = apply_matrix(
        "bkjq,mq->bkjm", real_part, imag_part, last_real / last_radix, -last_imag / last_radix
    )
    real_part, imag_part = complex_times(real_part, imag_part, inner_real, -inner_imag)
    real_part, imag_part = apply_matrix(
        "bkjm,nj->bknm", real_part, imag_part, mid_real / mid_radix, -mid_imag / mid_radix
    )
    real_part, imag_part = complex_times(real_part, imag_part, twist_real, -twist_imag)
    matrix_real = outer_real[:half_first] / first_radix
    matrix_imag = -outer_imag[:half_first] / first_radix
    out_real, out_imag = apply_matrix(
        "bknm,ak->banm", real_part, imag_part, matrix_real, matrix_imag
    )
    return (out_real.reshape(batch_rows, -1), out_imag.reshape(batch_rows, -1))


def spectrum(decay_rows, residue_rows, radix_sizes, seq_length):
    first_radix, mid_radix, last_radix = radix_sizes
    length_all = first_radix * mid_radix * last_radix
    poles = decay_rows.shape[1]
    shape_all = (first_radix, mid_radix, last_radix)
    frequency = (
        lax.broadcasted_iota(jnp.int32, shape_all, 0)
        + first_radix * lax.broadcasted_iota(jnp.int32, shape_all, 1)
        + first_radix * mid_radix * lax.broadcasted_iota(jnp.int32, shape_all, 2)
    )
    half_angle = frequency.astype(jnp.float32) * (math.pi / length_all)
    sin_half = jnp.sin(half_angle)
    sin_full = jnp.sin(2.0 * half_angle)
    parity_sign = (1 - 2 * (frequency % 2)).astype(jnp.float32)

    def add_pole(pole_index, running):
        run_real, run_imag = running
        rate_col = lax.dynamic_slice_in_dim(decay_rows, pole_index, 1, 1).reshape(-1, 1, 1, 1)
        weight = lax.dynamic_slice_in_dim(residue_rows, pole_index, 1, 1).reshape(
            -1, 1, 1, 1
        ) * jnp.sqrt(2.0 * rate_col / poles)
        retained = jnp.exp(-rate_col)
        den_real = -jnp.expm1(-rate_col) + 2.0 * retained * sin_half * sin_half
        den_imag = retained * sin_full
        pole_scale = (
            weight
            * (1.0 - jnp.exp(-rate_col * seq_length) * parity_sign)
            / (den_real * den_real + den_imag * den_imag)
        )
        return (run_real + pole_scale * den_real, run_imag - pole_scale * den_imag)

    zeros_all = jnp.zeros((decay_rows.shape[0],) + shape_all, jnp.float32)
    return lax.fori_loop(0, poles, add_pole, (zeros_all, zeros_all))


def general(x_gate, x_post, values, decay, residue, w_out):
    tok_rows, block_width = x_gate.shape
    ctx_count = lax.axis_size("ctx")
    tp_count = lax.axis_size("tp")
    chan_group = block_width // ctx_count
    seq_length = tok_rows * ctx_count
    radix_sizes = radices(2 * seq_length)
    table_set = tables(radix_sizes)
    first_row = lax.axis_index("ctx") * chan_group
    own_rate = lax.dynamic_slice_in_dim(decay, first_row, chan_group, 1)
    own_residue = lax.dynamic_slice_in_dim(residue, first_row, chan_group, 1)
    own_spec = [
        spectrum(own_rate[filter_index], own_residue[filter_index], radix_sizes, seq_length)
        for filter_index in range(2)
    ]
    forward_rows = [x_gate, values] + [x_post]
    row_count = len(forward_rows)
    base_rows = jnp.stack(forward_rows)
    copied = base_rows
    for bit_index in range(tp_count.bit_length() - 1):
        copied = partner(copied, "tp", bit_index)
    sent_rows = jnp.concatenate([base_rows, copied[:, :, ::-1]], axis=0)
    received = lax.all_to_all(
        jnp.swapaxes(sent_rows, 1, 2), "ctx", split_axis=1, concat_axis=2, tiled=True
    )
    gate_fwd = received[0].astype(jnp.float32)
    value_fwd = received[1].astype(jnp.float32)
    mirrored = received[row_count:, :, ::-1].astype(jnp.float32)
    spec_real, spec_imag = forward(value_fwd, mirrored[1], table_set, radix_sizes)
    spec_real, spec_imag = complex_times(spec_real, spec_imag, own_spec[0][0], own_spec[0][1])
    along_fwd, along_rev = inverse(spec_real, spec_imag, table_set, radix_sizes)
    spec_real, spec_imag = forward(
        gate_fwd * along_fwd, mirrored[0] * along_rev, table_set, radix_sizes
    )
    spec_real, spec_imag = complex_times(spec_real, spec_imag, own_spec[1][0], own_spec[1][1])
    sum_fwd, sum_rev = inverse(spec_real, spec_imag, table_set, radix_sizes)
    sum_fwd = received[2].astype(jnp.float32) * sum_fwd
    sum_rev = mirrored[2] * sum_rev
    results = jnp.stack([sum_fwd, sum_rev[:, ::-1]])
    returned = lax.all_to_all(
        results.astype(jnp.bfloat16), "ctx", split_axis=2, concat_axis=1, tiled=True
    ).astype(results.dtype)
    flipped = returned[1, ::-1, :]
    for bit_index in range(tp_count.bit_length() - 1):
        flipped = partner(flipped.astype(jnp.bfloat16), "tp", bit_index).astype(flipped.dtype)
    total_rows = returned[0] + flipped
    total_rows = total_rows.T
    mixed_rows = total_rows.astype(jnp.bfloat16)
    whole_rows = lax.all_gather(mixed_rows, "tp", axis=1, tiled=True)
    projected = lax.dot_general(
        whole_rows,
        lax.all_gather(w_out, "ctx", axis=0, tiled=True),
        (((1,), (1,)), ((), ())),
        preferred_element_type=jnp.float32,
    )
    return projected.astype(jnp.bfloat16)


def cycle(row_factor, col_factor, modulus):
    quarter = modulus // 4
    turned = row_factor * col_factor + quarter // 2
    quadrant = turned // quarter % 4
    angle = (turned % quarter - quarter // 2).astype(jnp.float32) * (2.0 * math.pi / modulus)
    square = angle * angle

    def series(first):
        total = jnp.zeros_like(square)
        for power in range(first + 10, first, -2):
            total = (total + (-1.0) ** ((power - first) // 2) / math.factorial(power)) * square
        return total

    cos = 1.0 + series(0)
    sin = angle + angle * series(1)
    odd = quadrant % 2 == 1
    cos, sin = jnp.where(odd, sin, cos), jnp.where(odd, cos, sin)
    return jnp.where((quadrant == 1) | (quadrant == 2), -cos, cos), jnp.where(quadrant >= 2, -sin, sin)


def put_tables(table_ref, back_ref):
    block = back_ref.shape[1]
    modulus = 4 * block
    coarse = 16
    rows = lax.broadcasted_iota(jnp.int32, (coarse, block), 0)
    cols = lax.broadcasted_iota(jnp.int32, (coarse, block), 1)

    def parts(big, small):
        for place in range(block // coarse):
            big_cos, big_sin = (part[place : place + 1] for part in big)
            cos = halves(big_cos * small[0] - big_sin * small[1])
            sin = halves(-(big_sin * small[0] + big_cos * small[1]))
            yield place * coarse, cos, sin

    def put(ref, first, columns, value):
        ref[first : first + coarse, columns] = value[0]
        low = first + ref.shape[0] // 2
        ref[low : low + coarse, columns] = value[1]

    frequency = 2 * cols + 1
    for first, cos, sin in parts(cycle(coarse * rows, frequency, modulus), cycle(rows, frequency, modulus)):
        put(table_ref, first, slice(0, block), cos)
        put(table_ref, first, slice(block, 2 * block), sin)
    for first, cos, sin in parts(cycle(2 * coarse * rows, cols, modulus), cycle(2 * rows + 1, cols, modulus)):
        put(back_ref, first, slice(0, block), cos)
        put(back_ref, block + first, slice(0, block), sin)


def halves(value):
    high = value.astype(jnp.bfloat16)
    return high, (value - high.astype(jnp.float32)).astype(jnp.bfloat16)


def mul(left, right):
    return jnp.dot(left, right, preferred_element_type=jnp.float32)


def mul3(high, low, table_ref):
    left = jnp.concatenate([high, high, low], axis=1)
    return mul(left, jnp.concatenate([table_ref[...], table_ref[: table_ref.shape[0] // 2]], axis=0))


def mul2(value, table_ref):
    return mul(jnp.concatenate([value, value], axis=1), table_ref[...])


def pack_kernel(
    gate_hbm, value_hbm, post_hbm, decay_hbm, residue_hbm,
    out_hbm, own_hbm, sent_hbm, held_ref, cut_ref, ready_ref, sems, out_sems,
):
    ctx_count, _, group, tok = out_hbm.shape
    width = gate_hbm.shape[1]
    half = decay_hbm.shape[0]
    position = lax.axis_index("ctx")
    pairs = []
    for place, index in enumerate((position, ctx_count - 1 - position)):
        columns = pl.ds(pl.multiple_of(index * group // tok * tok, tok), tok)
        pairs += [(decay_hbm.at[:, columns], cut_ref.at[place, :half]), (residue_hbm.at[:, columns], cut_ref.at[place, half:])]
    pairs += [(source, held_ref.at[place]) for place, source in enumerate((value_hbm, gate_hbm, post_hbm))]
    copies = [pltpu.make_async_copy(*pair, sems.at[place]) for place, pair in enumerate(pairs)]
    for copy in copies:
        copy.start()
    sends = []
    for place, target in enumerate((own_hbm, sent_hbm)):
        copies[2 * place].wait()
        copies[2 * place + 1].wait()
        sends.append(pltpu.make_async_copy(cut_ref.at[place], target, out_sems.at[3 + place]))
        sends[-1].start()
    for place, copy in enumerate(copies[4:]):
        copy.wait()
        for first in range(0, width, tok):
            turned = held_ref[place, :, first : first + tok].T
            for part in range(tok // group):
                ready_ref[first // group + part, place] = turned[part * group : (part + 1) * group]
        sends.append(pltpu.make_async_copy(ready_ref.at[:, place], out_hbm.at[:, place], out_sems.at[place]))
        sends[-1].start()
    for send in sends:
        send.wait()


def mirror_rows(value):
    row = lax.broadcasted_iota(jnp.int32, (8, value.shape[1]), 0)
    result = []
    for first in range(value.shape[0] - 8, -1, -8):
        part = value[first : first + 8]
        for shift in (1, 2, 4):
            part = jnp.where(row & shift == 0, pltpu.roll(part, 8 - shift, 0), pltpu.roll(part, shift, 0))
        result.append(part)
    return jnp.concatenate(result, axis=0)


def put_filter(poles, index, turned, time_ref):
    lanes = 128
    rows_all, block = time_ref.shape
    group = turned.shape[0]
    ramp = lax.broadcasted_iota(jnp.int32, (8, lanes), 1).astype(jnp.float32)
    for row in range(0, group, 8):
        rows = slice(row, row + 8)
        rate = turned[rows, index * poles : (index + 1) * poles]
        scale = turned[rows, (2 + index) * poles : (3 + index) * poles] * (jnp.sqrt(rate * (2.0 / poles)) / block)
        slope = rate * -math.log2(math.e)
        sums = [None] * (rows_all // group * block // lanes)
        for pole in range(poles):
            level = jnp.broadcast_to(slope[:, pole : pole + 1], (8, lanes))
            term = scale[:, pole : pole + 1] * jnp.exp2(level * ramp)
            step = jnp.exp2(level * lanes)
            for place in range(len(sums)):
                sums[place] = term if pole == 0 else sums[place] + term
                if place + 1 < len(sums):
                    term = term * step
        for place, total in enumerate(sums):
            lag, lane = divmod(place * lanes, block)
            time_ref[lag * group + row : lag * group + row + 8, lane : lane + lanes] = total


def put_spectra(spec, out_ref):
    blocks, group, twice = out_ref.shape
    block = twice // 2
    sign = (1 - 2 * (lax.broadcasted_iota(jnp.int32, (group, block), 1) % 2)).astype(jnp.float32)
    for lag in range(blocks):
        real = spec[lag * group : (lag + 1) * group, :block]
        imag = spec[lag * group : (lag + 1) * group, block:]
        if lag > 0:
            real = real - sign * spec[(lag - 1) * group : lag * group, block:]
            imag = imag + sign * spec[(lag - 1) * group : lag * group, :block]
        out_ref[lag, :, :block] = real
        out_ref[lag, :, block:] = imag


def filter_kernel(poles, par_ref, out_ref, table_ref, back_ref, time_ref, turned_ref):
    group = out_ref.shape[2]
    put_tables(table_ref, back_ref)
    turned_ref[...] = par_ref[...].T
    turned = turned_ref[pl.ds(pl.multiple_of(lax.axis_index("ctx") * group % turned_ref.shape[0], group), group)]
    put_filter(poles, 0, turned, time_ref.at[0])
    spec = mul3(*halves(time_ref[0]), table_ref)
    put_filter(poles, 1, turned, time_ref.at[1])
    put_spectra(spec, out_ref.at[0])
    put_spectra(mul3(*halves(time_ref[1]), table_ref), out_ref.at[1])


def conv_kernel(
    poles, x_ref, own_ref, par_ref, table_ref, back_ref, out_hbm,
    paired_ref, time_ref, turned_ref, spec_ref, high_ref, low_ref, ready_ref, sems,
):
    turned_ref[...] = par_ref[...].T
    blocks, group, twice = own_ref.shape[1:]
    block = twice // 2
    rows_all = blocks * group
    tall, wide = 16, 128
    pieces = x_ref.shape[0] // blocks
    first = (x_ref.shape[0] - 1 - lax.axis_index("ctx")) * group % turned_ref.shape[0]
    turned = mirror_rows(turned_ref[pl.ds(pl.multiple_of(first, group), group)])

    def rows_of(position):
        return jnp.concatenate(
            [
                jnp.concatenate([x_ref[m * pieces + s, position] for s in range(pieces)], axis=1)
                for m in range(blocks)
            ],
            axis=0,
        )

    def times(index, side, source, row, lane):
        data = []
        for m in range(blocks):
            rows = slice(source + m * group + row, source + m * group + row + tall)
            data.append((spec_ref[rows, lane : lane + wide], spec_ref[rows, block + lane : block + lane + wide]))
        sums = [None] * blocks
        for lag in range(blocks):
            h_ref = (own_ref, paired_ref)[side]
            f_re = h_ref[index, lag, row : row + tall, lane : lane + wide]
            f_im = h_ref[index, lag, row : row + tall, block + lane : block + lane + wide]
            for m in range(blocks - lag):
                target, (d_re, d_im) = (m + lag, data[m]) if side == 0 else (m, data[m + lag])
                if side == 0:
                    real, imag = f_re * d_re - f_im * d_im, f_re * d_im + f_im * d_re
                else:
                    real, imag = f_re * d_re + f_im * d_im, f_re * d_im - f_im * d_re
                if sums[target] is not None:
                    real, imag = sums[target][0] + real, sums[target][1] + imag
                sums[target] = (real, imag)
        return sums

    def keep(target, row, lane, sums):
        for m in range(blocks):
            rows = slice(target + m * group + row, target + m * group + row + tall)
            for part in range(2):
                cols = slice(part * block + lane, part * block + lane + wide)
                high_ref[rows, cols], low_ref[rows, cols] = halves(sums[m][part])

    chunks = [(row, lane) for row in range(0, group, tall) for lane in range(0, block, wide)]

    value = rows_of(0)
    gate = rows_of(1).astype(jnp.float32)
    spec_ref[:rows_all] = mul2(value, table_ref)
    sides = [slice(side * rows_all, (side + 1) * rows_all) for side in range(2)]
    put_filter(poles, 0, turned, time_ref.at[0])
    spec = mul3(*halves(time_ref[0]), table_ref)
    for row, lane in chunks:
        keep(0, row, lane, times(0, 0, 0, row, lane))
    put_spectra(spec, paired_ref.at[0])
    gated = [gate * mul3(high_ref[sides[0]], low_ref[sides[0]], back_ref)]
    put_filter(poles, 1, turned, time_ref.at[1])
    for row, lane in chunks:
        keep(rows_all, row, lane, times(0, 1, 0, row, lane))
    gated.append(gate * mul3(high_ref[sides[1]], low_ref[sides[1]], back_ref))
    spec = mul3(*halves(time_ref[1]), table_ref)
    for side in range(2):
        spec_ref[sides[side]] = mul3(*halves(gated[side]), table_ref)
    put_spectra(spec, paired_ref.at[1])
    for row, lane in chunks:
        ahead, back = times(1, 0, 0, row, lane), times(1, 1, rows_all, row, lane)
        keep(0, row, lane, [(a[0] + b[0], a[1] + b[1]) for a, b in zip(ahead, back)])
    post = rows_of(2)
    tok = block // pieces
    sends = []
    for part in range(2):
        rows = slice(part * rows_all // 2, (part + 1) * rows_all // 2)
        summed = mul3(high_ref[rows], low_ref[rows], back_ref)
        mixed = (post[rows].astype(jnp.float32) * summed).astype(jnp.bfloat16)
        first = part * blocks // 2 * pieces
        for m in range(blocks // 2):
            for s in range(pieces):
                ready_ref[first + m * pieces + s] = mixed[m * group : (m + 1) * group, s * tok : (s + 1) * tok]
        span = pl.ds(first, blocks // 2 * pieces)
        for copy in range(out_hbm.shape[1]):
            sends.append(pltpu.make_async_copy(ready_ref.at[span], out_hbm.at[span, copy], sems.at[part, copy]))
            sends[-1].start()
    for send in sends:
        send.wait()


def project_kernel(mixed_ref, *refs):
    w_refs, (out_hbm, held_ref, ready_ref, sems) = refs[:-4], refs[-4:]
    rows = w_refs[0].shape[0]
    tile = 2 * rows
    position = lax.axis_index("ctx")
    parity = position % 2
    even = pl.multiple_of(parity * rows, rows)
    odd = pl.multiple_of((1 - parity) * rows, rows)
    masks = (0, 1 + parity, 2 - parity, 3)
    ctx_count, tp_count = mixed_ref.shape[:2]
    mixed = jnp.concatenate([mixed_ref[i, z] for z in range(tp_count) for i in range(ctx_count)], axis=0)
    sends = []
    for half in range(2):
        total = mul(jnp.concatenate([w_ref[...] for w_ref in w_refs[4 * half : 4 * half + 4]], axis=0), mixed)
        for pair in range(2):
            place = 2 * half + pair
            held_ref[place, pl.ds(even, rows)] = total[pair * tile : pair * tile + rows]
            held_ref[place, pl.ds(odd, rows)] = total[pair * tile + rows : (pair + 1) * tile]
            ready_ref[place] = held_ref[place].T.astype(jnp.bfloat16)
            columns = pl.ds(pl.multiple_of((position // 2 ^ masks[place]) * tile, tile), tile)
            sends.append(pltpu.make_async_copy(ready_ref.at[place], out_hbm.at[:, columns], sems.at[place]))
            sends[-1].start()
    for send in sends:
        send.wait()


def whole_call(kernel, out_shape, scratch, flops, nbytes, *operands, in_hbm=0, out_hbm=()):
    results = pl.pallas_call(
        kernel,
        out_shape=out_shape,
        in_specs=[
            pl.BlockSpec(memory_space=pltpu.HBM if place < in_hbm else pltpu.VMEM) for place in range(len(operands))
        ],
        out_specs=[
            pl.BlockSpec(memory_space=pltpu.HBM if place in out_hbm else pltpu.VMEM) for place in range(len(out_shape))
        ],
        scratch_shapes=scratch,
        cost_estimate=pl.CostEstimate(flops=flops, bytes_accessed=nbytes, transcendentals=0),
        compiler_params=pltpu.CompilerParams(vmem_limit_bytes=None if in_hbm else 32 * 2**20),
    )(*operands)
    return results if len(out_shape) > 1 else results[0]


def blocked(x_gate, x_post, values, decay, residue, w_out):
    tok, width = x_gate.shape
    ctx_count = lax.axis_size("ctx")
    tp_count = lax.axis_size("tp")
    group = width // ctx_count
    poles = decay.shape[2]
    block = 2 * tok
    blocks = tok * ctx_count // block
    rows, channels = w_out.shape
    half = 2 * poles

    packed, own, mirrored = whole_call(
        pack_kernel,
        (
            jax.ShapeDtypeStruct((ctx_count, 3, group, tok), jnp.bfloat16),
            jax.ShapeDtypeStruct((2 * half, tok), jnp.float32),
            jax.ShapeDtypeStruct((2 * half, tok), jnp.float32),
        ),
        [
            pltpu.VMEM((3, tok, width), jnp.bfloat16),
            pltpu.VMEM((2, 2 * half, tok), jnp.float32),
            pltpu.VMEM((ctx_count, 3, group, tok), jnp.bfloat16),
            pltpu.SemaphoreType.DMA((7,)),
            pltpu.SemaphoreType.DMA((5,)),
        ],
        0,
        6 * tok * width * 2,
        x_gate,
        values,
        x_post,
        jnp.swapaxes(decay, 1, 2).reshape(half, width),
        jnp.swapaxes(residue, 1, 2).reshape(half, width),
        in_hbm=5,
        out_hbm=(0, 1, 2),
    )
    paired = lax.ppermute(mirrored, "tp", [(z, tp_count - 1 - z) for z in range(tp_count)])
    received = lax.all_to_all(packed, "ctx", split_axis=0, concat_axis=0, tiled=True)

    w_late, mirrored = lax.optimization_barrier((w_out, mirrored))

    def cross(block, even_mask, odd_mask):
        return lax.ppermute(block, "ctx", [(i, i ^ (odd_mask if i % 2 else even_mask)) for i in range(ctx_count)])

    w_first = cross(w_late, 2, 4)
    own_spectra, table, back_table = whole_call(
        functools.partial(filter_kernel, poles),
        (
            jax.ShapeDtypeStruct((2, blocks, group, 2 * block), jnp.float32),
            jax.ShapeDtypeStruct((2 * block, 2 * block), jnp.bfloat16),
            jax.ShapeDtypeStruct((4 * block, block), jnp.bfloat16),
        ),
        [
            pltpu.VMEM((2, blocks * group, block), jnp.float32),
            pltpu.VMEM((tok, 2 * half), jnp.float32),
        ],
        2 * 2 * blocks * group * block * 2 * block * 3,
        2 * blocks * group * 2 * block * 4,
        own,
    )
    mixed = whole_call(
        functools.partial(conv_kernel, poles),
        (jax.ShapeDtypeStruct((ctx_count, tp_count, group, tok), jnp.bfloat16),),
        [
            pltpu.VMEM((2, blocks, group, 2 * block), jnp.float32),
            pltpu.VMEM((2, blocks * group, block), jnp.float32),
            pltpu.VMEM((tok, 2 * half), jnp.float32),
            pltpu.VMEM((2 * blocks * group, 2 * block), jnp.float32),
            pltpu.VMEM((2 * blocks * group, 2 * block), jnp.bfloat16),
            pltpu.VMEM((2 * blocks * group, 2 * block), jnp.bfloat16),
            pltpu.VMEM((ctx_count, group, tok), jnp.bfloat16),
            pltpu.SemaphoreType.DMA((2, tp_count)),
        ],
        2 * 8 * blocks * group * block * 2 * block * 3,
        4 * blocks * group * 2 * block * 4,
        received,
        own_spectra,
        paired,
        table,
        back_table,
        out_hbm=(0,),
    )
    mixed, w_first, w_own = lax.optimization_barrier((mixed, w_first, w_out))
    w_third = cross(w_first, 4, 2)
    w_second = cross(w_own, 4, 2)
    w_other = [partner(block, "ctx", 0) for block in (w_own, w_first, w_second, w_third)]
    w_blocks = [w_own, w_other[0], w_first, w_other[2], w_second, w_other[1], w_third, w_other[3]]
    every = lax.all_to_all(
        mixed.reshape(ctx_count * tp_count, group, tok), ("ctx", "tp"), split_axis=0, concat_axis=0, tiled=True
    ).reshape(ctx_count, tp_count, group, tok)
    return whole_call(
        project_kernel,
        (jax.ShapeDtypeStruct((tok, rows * ctx_count), jnp.bfloat16),),
        [
            pltpu.VMEM((ctx_count // 2, 2 * rows, tok), jnp.float32),
            pltpu.VMEM((ctx_count // 2, tok, 2 * rows), jnp.bfloat16),
            pltpu.SemaphoreType.DMA((ctx_count // 2,)),
        ],
        2 * tok * rows * ctx_count * channels,
        2 * rows * ctx_count * channels,
        every,
        *w_blocks,
        out_hbm=(0,),
    )


def local(x_gate, x_post, values, decay, residue, w_out):
    tok, width = x_gate.shape
    ctx_count = lax.axis_size("ctx")
    if tok == 128 and width == 512 and ctx_count == 8 and w_out.shape[0] == 64 and lax.axis_size("tp") == 4:
        return blocked(x_gate, x_post, values, decay, residue, w_out)
    return general(x_gate, x_post, values, decay, residue, w_out)


def solution(mesh):
    in_specs = (
        P("ctx", "tp"),
        P("ctx", "tp"),
        P("ctx", "tp"),
        P(None, "tp", None),
        P(None, "tp", None),
        P(("tp", "ctx"), None),
    )
    out_specs = P("ctx", "tp")
    return jax.shard_map(local, mesh=mesh, in_specs=in_specs, out_specs=out_specs, check_vma=False)
```

```python
import functools
import math

import jax
import jax.numpy as jnp
from jax import lax
from jax.experimental import pallas as pl
from jax.experimental.pallas import tpu as pltpu
from jax.sharding import PartitionSpec as P

HIGHEST = lax.Precision.HIGHEST


def partner(value, axis, bit):
    mask = 2**bit
    pairs = [(source, source ^ mask) for source in range(lax.axis_size(axis))]
    return lax.ppermute(value, axis, pairs)


def radices(length_all):
    last_radix = min(128, length_all // 4)
    first_radix = min(32, length_all // last_radix)
    return (first_radix, length_all // (first_radix * last_radix), last_radix)


def rotation(row_count, col_count, modulus):
    product = (
        lax.broadcasted_iota(jnp.int32, (row_count, col_count), 0)
        * lax.broadcasted_iota(jnp.int32, (row_count, col_count), 1)
        % modulus
    )
    angle = product.astype(jnp.float32) * (2.0 * math.pi / modulus)
    return (jnp.cos(angle), -jnp.sin(angle))


def tables(radix_sizes):
    first_radix, mid_radix, last_radix = radix_sizes
    length_all = first_radix * mid_radix * last_radix
    outer_real, outer_imag = rotation(first_radix, first_radix, first_radix)
    mid_real, mid_imag = rotation(mid_radix, mid_radix, mid_radix)
    last_real, last_imag = rotation(last_radix, last_radix, last_radix)
    twist_real, twist_imag = rotation(first_radix, mid_radix * last_radix, length_all)
    twist_real = twist_real.reshape(first_radix, mid_radix, last_radix)
    twist_imag = twist_imag.reshape(first_radix, mid_radix, last_radix)
    inner_real, inner_imag = rotation(mid_radix, last_radix, mid_radix * last_radix)
    return (
        outer_real,
        outer_imag,
        mid_real,
        mid_imag,
        last_real,
        last_imag,
        twist_real,
        twist_imag,
        inner_real,
        inner_imag,
    )


def apply_matrix(pattern, real_part, imag_part, matrix_real, matrix_imag):
    out_real = jnp.einsum(pattern, real_part, matrix_real, precision=HIGHEST) - jnp.einsum(
        pattern, imag_part, matrix_imag, precision=HIGHEST
    )
    out_imag = jnp.einsum(pattern, real_part, matrix_imag, precision=HIGHEST) + jnp.einsum(
        pattern, imag_part, matrix_real, precision=HIGHEST
    )
    return (out_real, out_imag)


def complex_times(left_real, left_imag, right_real, right_imag):
    return (
        left_real * right_real - left_imag * right_imag,
        left_real * right_imag + left_imag * right_real,
    )


def forward(real_part, imag_part, table_set, radix_sizes):
    first_radix, mid_radix, last_radix = radix_sizes
    half_first = first_radix // 2
    batch_rows = real_part.shape[0]
    (
        outer_real,
        outer_imag,
        mid_real,
        mid_imag,
        last_real,
        last_imag,
        twist_real,
        twist_imag,
        inner_real,
        inner_imag,
    ) = table_set
    real_part = real_part.reshape(batch_rows, half_first, mid_radix, last_radix)
    imag_part = imag_part.reshape(batch_rows, half_first, mid_radix, last_radix)
    real_part, imag_part = apply_matrix(
        "banm,ak->bknm", real_part, imag_part, outer_real[:half_first], outer_imag[:half_first]
    )
    real_part, imag_part = complex_times(real_part, imag_part, twist_real, twist_imag)
    real_part, imag_part = apply_matrix("bknm,nj->bkjm", real_part, imag_part, mid_real, mid_imag)
    real_part, imag_part = complex_times(real_part, imag_part, inner_real, inner_imag)
    return apply_matrix("bkjm,mq->bkjq", real_part, imag_part, last_real, last_imag)


def inverse(real_part, imag_part, table_set, radix_sizes):
    first_radix, mid_radix, last_radix = radix_sizes
    half_first = first_radix // 2
    batch_rows = real_part.shape[0]
    (
        outer_real,
        outer_imag,
        mid_real,
        mid_imag,
        last_real,
        last_imag,
        twist_real,
        twist_imag,
        inner_real,
        inner_imag,
    ) = table_set
    real_part, imag_part = apply_matrix(
        "bkjq,mq->bkjm", real_part, imag_part, last_real / last_radix, -last_imag / last_radix
    )
    real_part, imag_part = complex_times(real_part, imag_part, inner_real, -inner_imag)
    real_part, imag_part = apply_matrix(
        "bkjm,nj->bknm", real_part, imag_part, mid_real / mid_radix, -mid_imag / mid_radix
    )
    real_part, imag_part = complex_times(real_part, imag_part, twist_real, -twist_imag)
    matrix_real = outer_real[:half_first] / first_radix
    matrix_imag = -outer_imag[:half_first] / first_radix
    out_real, out_imag = apply_matrix(
        "bknm,ak->banm", real_part, imag_part, matrix_real, matrix_imag
    )
    return (out_real.reshape(batch_rows, -1), out_imag.reshape(batch_rows, -1))


def spectrum(decay_rows, residue_rows, radix_sizes, seq_length):
    first_radix, mid_radix, last_radix = radix_sizes
    length_all = first_radix * mid_radix * last_radix
    poles = decay_rows.shape[1]
    shape_all = (first_radix, mid_radix, last_radix)
    frequency = (
        lax.broadcasted_iota(jnp.int32, shape_all, 0)
        + first_radix * lax.broadcasted_iota(jnp.int32, shape_all, 1)
        + first_radix * mid_radix * lax.broadcasted_iota(jnp.int32, shape_all, 2)
    )
    half_angle = frequency.astype(jnp.float32) * (math.pi / length_all)
    sin_half = jnp.sin(half_angle)
    sin_full = jnp.sin(2.0 * half_angle)
    parity_sign = (1 - 2 * (frequency % 2)).astype(jnp.float32)

    def add_pole(pole_index, running):
        run_real, run_imag = running
        rate_col = lax.dynamic_slice_in_dim(decay_rows, pole_index, 1, 1).reshape(-1, 1, 1, 1)
        weight = lax.dynamic_slice_in_dim(residue_rows, pole_index, 1, 1).reshape(
            -1, 1, 1, 1
        ) * jnp.sqrt(2.0 * rate_col / poles)
        retained = jnp.exp(-rate_col)
        den_real = -jnp.expm1(-rate_col) + 2.0 * retained * sin_half * sin_half
        den_imag = retained * sin_full
        pole_scale = (
            weight
            * (1.0 - jnp.exp(-rate_col * seq_length) * parity_sign)
            / (den_real * den_real + den_imag * den_imag)
        )
        return (run_real + pole_scale * den_real, run_imag - pole_scale * den_imag)

    zeros_all = jnp.zeros((decay_rows.shape[0],) + shape_all, jnp.float32)
    return lax.fori_loop(0, poles, add_pole, (zeros_all, zeros_all))


def general(x_gate, x_post, values, decay, residue, w_out):
    tok_rows, block_width = x_gate.shape
    ctx_count = lax.axis_size("ctx")
    tp_count = lax.axis_size("tp")
    chan_group = block_width // ctx_count
    seq_length = tok_rows * ctx_count
    radix_sizes = radices(2 * seq_length)
    table_set = tables(radix_sizes)
    first_row = lax.axis_index("ctx") * chan_group
    own_rate = lax.dynamic_slice_in_dim(decay, first_row, chan_group, 1)
    own_residue = lax.dynamic_slice_in_dim(residue, first_row, chan_group, 1)
    own_spec = [
        spectrum(own_rate[filter_index], own_residue[filter_index], radix_sizes, seq_length)
        for filter_index in range(2)
    ]
    forward_rows = [x_gate, values] + [x_post]
    row_count = len(forward_rows)
    base_rows = jnp.stack(forward_rows)
    copied = base_rows
    for bit_index in range(tp_count.bit_length() - 1):
        copied = partner(copied, "tp", bit_index)
    sent_rows = jnp.concatenate([base_rows, copied[:, :, ::-1]], axis=0)
    received = lax.all_to_all(
        jnp.swapaxes(sent_rows, 1, 2), "ctx", split_axis=1, concat_axis=2, tiled=True
    )
    gate_fwd = received[0].astype(jnp.float32)
    value_fwd = received[1].astype(jnp.float32)
    mirrored = received[row_count:, :, ::-1].astype(jnp.float32)
    spec_real, spec_imag = forward(value_fwd, mirrored[1], table_set, radix_sizes)
    spec_real, spec_imag = complex_times(spec_real, spec_imag, own_spec[0][0], own_spec[0][1])
    along_fwd, along_rev = inverse(spec_real, spec_imag, table_set, radix_sizes)
    spec_real, spec_imag = forward(
        gate_fwd * along_fwd, mirrored[0] * along_rev, table_set, radix_sizes
    )
    spec_real, spec_imag = complex_times(spec_real, spec_imag, own_spec[1][0], own_spec[1][1])
    sum_fwd, sum_rev = inverse(spec_real, spec_imag, table_set, radix_sizes)
    sum_fwd = received[2].astype(jnp.float32) * sum_fwd
    sum_rev = mirrored[2] * sum_rev
    results = jnp.stack([sum_fwd, sum_rev[:, ::-1]])
    returned = lax.all_to_all(
        results.astype(jnp.bfloat16), "ctx", split_axis=2, concat_axis=1, tiled=True
    ).astype(results.dtype)
    flipped = returned[1, ::-1, :]
    for bit_index in range(tp_count.bit_length() - 1):
        flipped = partner(flipped.astype(jnp.bfloat16), "tp", bit_index).astype(flipped.dtype)
    total_rows = returned[0] + flipped
    total_rows = total_rows.T
    mixed_rows = total_rows.astype(jnp.bfloat16)
    whole_rows = lax.all_gather(mixed_rows, "tp", axis=1, tiled=True)
    projected = lax.dot_general(
        whole_rows,
        lax.all_gather(w_out, "ctx", axis=0, tiled=True),
        (((1,), (1,)), ((), ())),
        preferred_element_type=jnp.float32,
    )
    return projected.astype(jnp.bfloat16)


def cycle(row_factor, col_factor, modulus):
    quarter = modulus // 4
    turned = row_factor * col_factor + quarter // 2
    quadrant = turned // quarter % 4
    angle = (turned % quarter - quarter // 2).astype(jnp.float32) * (2.0 * math.pi / modulus)
    square = angle * angle

    def series(first):
        total = jnp.zeros_like(square)
        for power in range(first + 10, first, -2):
            total = (total + (-1.0) ** ((power - first) // 2) / math.factorial(power)) * square
        return total

    cos = 1.0 + series(0)
    sin = angle + angle * series(1)
    odd = quadrant % 2 == 1
    cos, sin = jnp.where(odd, sin, cos), jnp.where(odd, cos, sin)
    return jnp.where((quadrant == 1) | (quadrant == 2), -cos, cos), jnp.where(quadrant >= 2, -sin, sin)


def put_tables(table_ref, back_ref):
    block = back_ref.shape[1]
    modulus = 4 * block
    coarse = 16
    rows = lax.broadcasted_iota(jnp.int32, (coarse, block), 0)
    cols = lax.broadcasted_iota(jnp.int32, (coarse, block), 1)

    def parts(big, small):
        for place in range(block // coarse):
            big_cos, big_sin = (part[place : place + 1] for part in big)
            cos = halves(big_cos * small[0] - big_sin * small[1])
            sin = halves(-(big_sin * small[0] + big_cos * small[1]))
            yield place * coarse, cos, sin

    def put(ref, first, columns, value):
        ref[first : first + coarse, columns] = value[0]
        low = first + ref.shape[0] // 2
        ref[low : low + coarse, columns] = value[1]

    frequency = 2 * cols + 1
    for first, cos, sin in parts(cycle(coarse * rows, frequency, modulus), cycle(rows, frequency, modulus)):
        put(table_ref, first, slice(0, block), cos)
        put(table_ref, first, slice(block, 2 * block), sin)
    for first, cos, sin in parts(cycle(2 * coarse * rows, cols, modulus), cycle(2 * rows + 1, cols, modulus)):
        put(back_ref, first, slice(0, block), cos)
        put(back_ref, block + first, slice(0, block), sin)


def halves(value):
    high = value.astype(jnp.bfloat16)
    return high, (value - high.astype(jnp.float32)).astype(jnp.bfloat16)


def mul(left, right):
    return jnp.dot(left, right, preferred_element_type=jnp.float32)


def mul3(high, low, table_ref):
    left = jnp.concatenate([high, high, low], axis=1)
    return mul(left, jnp.concatenate([table_ref[...], table_ref[: table_ref.shape[0] // 2]], axis=0))


def mul2(value, table_ref):
    return mul(jnp.concatenate([value, value], axis=1), table_ref[...])


def pack_kernel(
    gate_hbm, value_hbm, post_hbm, decay_hbm, residue_hbm,
    out_hbm, own_hbm, sent_hbm, held_ref, cut_ref, ready_ref, sems, out_sems,
):
    ctx_count, _, group, tok = out_hbm.shape
    width = gate_hbm.shape[1]
    half = decay_hbm.shape[0]
    position = lax.axis_index("ctx")
    pairs = []
    for place, index in enumerate((position, ctx_count - 1 - position)):
        columns = pl.ds(pl.multiple_of(index * group // tok * tok, tok), tok)
        pairs += [(decay_hbm.at[:, columns], cut_ref.at[place, :half]), (residue_hbm.at[:, columns], cut_ref.at[place, half:])]
    pairs += [(source, held_ref.at[place]) for place, source in enumerate((value_hbm, gate_hbm, post_hbm))]
    copies = [pltpu.make_async_copy(*pair, sems.at[place]) for place, pair in enumerate(pairs)]
    for copy in copies:
        copy.start()
    sends = []
    for place, target in enumerate((own_hbm, sent_hbm)):
        copies[2 * place].wait()
        copies[2 * place + 1].wait()
        sends.append(pltpu.make_async_copy(cut_ref.at[place], target, out_sems.at[3 + place]))
        sends[-1].start()
    for place, copy in enumerate(copies[4:]):
        copy.wait()
        for first in range(0, width, tok):
            turned = held_ref[place, :, first : first + tok].T
            for part in range(tok // group):
                ready_ref[first // group + part, place] = turned[part * group : (part + 1) * group]
        sends.append(pltpu.make_async_copy(ready_ref.at[:, place], out_hbm.at[:, place], out_sems.at[place]))
        sends[-1].start()
    for send in sends:
        send.wait()


def mirror_rows(value):
    row = lax.broadcasted_iota(jnp.int32, (8, value.shape[1]), 0)
    result = []
    for first in range(value.shape[0] - 8, -1, -8):
        part = value[first : first + 8]
        for shift in (1, 2, 4):
            part = jnp.where(row & shift == 0, pltpu.roll(part, 8 - shift, 0), pltpu.roll(part, shift, 0))
        result.append(part)
    return jnp.concatenate(result, axis=0)


def put_filter(poles, index, turned, time_ref):
    lanes = 128
    rows_all, block = time_ref.shape
    group = turned.shape[0]
    ramp = lax.broadcasted_iota(jnp.int32, (8, lanes), 1).astype(jnp.float32)
    for row in range(0, group, 8):
        rows = slice(row, row + 8)
        rate = turned[rows, index * poles : (index + 1) * poles]
        scale = turned[rows, (2 + index) * poles : (3 + index) * poles] * (jnp.sqrt(rate * (2.0 / poles)) / block)
        slope = rate * -math.log2(math.e)
        sums = [None] * (rows_all // group * block // lanes)
        for pole in range(poles):
            level = jnp.broadcast_to(slope[:, pole : pole + 1], (8, lanes))
            term = scale[:, pole : pole + 1] * jnp.exp2(level * ramp)
            step = jnp.exp2(level * lanes)
            for place in range(len(sums)):
                sums[place] = term if pole == 0 else sums[place] + term
                if place + 1 < len(sums):
                    term = term * step
        for place, total in enumerate(sums):
            lag, lane = divmod(place * lanes, block)
            time_ref[lag * group + row : lag * group + row + 8, lane : lane + lanes] = total


def put_spectra(spec, out_ref):
    blocks, group, twice = out_ref.shape
    block = twice // 2
    sign = (1 - 2 * (lax.broadcasted_iota(jnp.int32, (group, block), 1) % 2)).astype(jnp.float32)
    for lag in range(blocks):
        real = spec[lag * group : (lag + 1) * group, :block]
        imag = spec[lag * group : (lag + 1) * group, block:]
        if lag > 0:
            real = real - sign * spec[(lag - 1) * group : lag * group, block:]
            imag = imag + sign * spec[(lag - 1) * group : lag * group, :block]
        out_ref[lag, :, :block] = real
        out_ref[lag, :, block:] = imag


def filter_kernel(poles, par_ref, out_ref, table_ref, back_ref, time_ref, turned_ref):
    group = out_ref.shape[2]
    put_tables(table_ref, back_ref)
    turned_ref[...] = par_ref[...].T
    turned = turned_ref[pl.ds(pl.multiple_of(lax.axis_index("ctx") * group % turned_ref.shape[0], group), group)]
    put_filter(poles, 0, turned, time_ref.at[0])
    spec = mul3(*halves(time_ref[0]), table_ref)
    put_filter(poles, 1, turned, time_ref.at[1])
    put_spectra(spec, out_ref.at[0])
    put_spectra(mul3(*halves(time_ref[1]), table_ref), out_ref.at[1])


def conv_kernel(
    poles, x_ref, own_ref, par_ref, table_ref, back_ref, out_hbm,
    paired_ref, time_ref, turned_ref, spec_ref, high_ref, low_ref, ready_ref, sems,
):
    turned_ref[...] = par_ref[...].T
    blocks, group, twice = own_ref.shape[1:]
    block = twice // 2
    rows_all = blocks * group
    tall, wide = 16, 128
    pieces = x_ref.shape[0] // blocks
    first = (x_ref.shape[0] - 1 - lax.axis_index("ctx")) * group % turned_ref.shape[0]
    turned = mirror_rows(turned_ref[pl.ds(pl.multiple_of(first, group), group)])

    def rows_of(position):
        return jnp.concatenate(
            [
                jnp.concatenate([x_ref[m * pieces + s, position] for s in range(pieces)], axis=1)
                for m in range(blocks)
            ],
            axis=0,
        )

    def times(index, side, source, row, lane):
        data = []
        for m in range(blocks):
            rows = slice(source + m * group + row, source + m * group + row + tall)
            data.append((spec_ref[rows, lane : lane + wide], spec_ref[rows, block + lane : block + lane + wide]))
        sums = [None] * blocks
        for lag in range(blocks):
            h_ref = (own_ref, paired_ref)[side]
            f_re = h_ref[index, lag, row : row + tall, lane : lane + wide]
            f_im = h_ref[index, lag, row : row + tall, block + lane : block + lane + wide]
            for m in range(blocks - lag):
                target, (d_re, d_im) = (m + lag, data[m]) if side == 0 else (m, data[m + lag])
                if side == 0:
                    real, imag = f_re * d_re - f_im * d_im, f_re * d_im + f_im * d_re
                else:
                    real, imag = f_re * d_re + f_im * d_im, f_re * d_im - f_im * d_re
                if sums[target] is not None:
                    real, imag = sums[target][0] + real, sums[target][1] + imag
                sums[target] = (real, imag)
        return sums

    def keep(target, row, lane, sums):
        for m in range(blocks):
            rows = slice(target + m * group + row, target + m * group + row + tall)
            for part in range(2):
                cols = slice(part * block + lane, part * block + lane + wide)
                high_ref[rows, cols], low_ref[rows, cols] = halves(sums[m][part])

    chunks = [(row, lane) for row in range(0, group, tall) for lane in range(0, block, wide)]

    value = rows_of(0)
    gate = rows_of(1).astype(jnp.float32)
    spec_ref[:rows_all] = mul2(value, table_ref)
    sides = [slice(side * rows_all, (side + 1) * rows_all) for side in range(2)]
    put_filter(poles, 0, turned, time_ref.at[0])
    spec = mul3(*halves(time_ref[0]), table_ref)
    for row, lane in chunks:
        keep(0, row, lane, times(0, 0, 0, row, lane))
    put_spectra(spec, paired_ref.at[0])
    gated = [gate * mul3(high_ref[sides[0]], low_ref[sides[0]], back_ref)]
    put_filter(poles, 1, turned, time_ref.at[1])
    for row, lane in chunks:
        keep(rows_all, row, lane, times(0, 1, 0, row, lane))
    gated.append(gate * mul3(high_ref[sides[1]], low_ref[sides[1]], back_ref))
    spec = mul3(*halves(time_ref[1]), table_ref)
    for side in range(2):
        spec_ref[sides[side]] = mul3(*halves(gated[side]), table_ref)
    put_spectra(spec, paired_ref.at[1])
    for row, lane in chunks:
        ahead, back = times(1, 0, 0, row, lane), times(1, 1, rows_all, row, lane)
        keep(0, row, lane, [(a[0] + b[0], a[1] + b[1]) for a, b in zip(ahead, back)])
    post = rows_of(2)
    tok = block // pieces
    sends = []
    for part in range(2):
        rows = slice(part * rows_all // 2, (part + 1) * rows_all // 2)
        summed = mul3(high_ref[rows], low_ref[rows], back_ref)
        mixed = (post[rows].astype(jnp.float32) * summed).astype(jnp.bfloat16)
        first = part * blocks // 2 * pieces
        for m in range(blocks // 2):
            for s in range(pieces):
                ready_ref[first + m * pieces + s] = mixed[m * group : (m + 1) * group, s * tok : (s + 1) * tok]
        span = pl.ds(first, blocks // 2 * pieces)
        for copy in range(out_hbm.shape[1]):
            sends.append(pltpu.make_async_copy(ready_ref.at[span], out_hbm.at[span, copy], sems.at[part, copy]))
            sends[-1].start()
    for send in sends:
        send.wait()


def project_kernel(mixed_ref, *refs):
    w_refs, (out_hbm, held_ref, ready_ref, sems) = refs[:-4], refs[-4:]
    rows = w_refs[0].shape[0]
    tile = 2 * rows
    position = lax.axis_index("ctx")
    parity = position % 2
    even = pl.multiple_of(parity * rows, rows)
    odd = pl.multiple_of((1 - parity) * rows, rows)
    masks = (0, 2 - parity, 1 + parity, 3)
    ctx_count, tp_count = mixed_ref.shape[:2]
    mixed = jnp.concatenate([mixed_ref[i, z] for z in range(tp_count) for i in range(ctx_count)], axis=0)
    sends = []
    for half in range(2):
        total = mul(jnp.concatenate([w_ref[...] for w_ref in w_refs[4 * half : 4 * half + 4]], axis=0), mixed)
        for pair in range(2):
            place = 2 * half + pair
            held_ref[place, pl.ds(even, rows)] = total[pair * tile : pair * tile + rows]
            held_ref[place, pl.ds(odd, rows)] = total[pair * tile + rows : (pair + 1) * tile]
            ready_ref[place] = held_ref[place].T.astype(jnp.bfloat16)
            columns = pl.ds(pl.multiple_of((position // 2 ^ masks[place]) * tile, tile), tile)
            sends.append(pltpu.make_async_copy(ready_ref.at[place], out_hbm.at[:, columns], sems.at[place]))
            sends[-1].start()
    for send in sends:
        send.wait()


def whole_call(kernel, out_shape, scratch, flops, nbytes, *operands, in_hbm=0, out_hbm=()):
    results = pl.pallas_call(
        kernel,
        out_shape=out_shape,
        in_specs=[
            pl.BlockSpec(memory_space=pltpu.HBM if place < in_hbm else pltpu.VMEM) for place in range(len(operands))
        ],
        out_specs=[
            pl.BlockSpec(memory_space=pltpu.HBM if place in out_hbm else pltpu.VMEM) for place in range(len(out_shape))
        ],
        scratch_shapes=scratch,
        cost_estimate=pl.CostEstimate(flops=flops, bytes_accessed=nbytes, transcendentals=0),
        compiler_params=pltpu.CompilerParams(vmem_limit_bytes=None if in_hbm else 32 * 2**20),
    )(*operands)
    return results if len(out_shape) > 1 else results[0]


def blocked(x_gate, x_post, values, decay, residue, w_out):
    tok, width = x_gate.shape
    ctx_count = lax.axis_size("ctx")
    tp_count = lax.axis_size("tp")
    group = width // ctx_count
    poles = decay.shape[2]
    block = 2 * tok
    blocks = tok * ctx_count // block
    rows, channels = w_out.shape
    half = 2 * poles

    packed, own, mirrored = whole_call(
        pack_kernel,
        (
            jax.ShapeDtypeStruct((ctx_count, 3, group, tok), jnp.bfloat16),
            jax.ShapeDtypeStruct((2 * half, tok), jnp.float32),
            jax.ShapeDtypeStruct((2 * half, tok), jnp.float32),
        ),
        [
            pltpu.VMEM((3, tok, width), jnp.bfloat16),
            pltpu.VMEM((2, 2 * half, tok), jnp.float32),
            pltpu.VMEM((ctx_count, 3, group, tok), jnp.bfloat16),
            pltpu.SemaphoreType.DMA((7,)),
            pltpu.SemaphoreType.DMA((5,)),
        ],
        0,
        6 * tok * width * 2,
        x_gate,
        values,
        x_post,
        jnp.swapaxes(decay, 1, 2).reshape(half, width),
        jnp.swapaxes(residue, 1, 2).reshape(half, width),
        in_hbm=5,
        out_hbm=(0, 1, 2),
    )
    paired = lax.ppermute(mirrored, "tp", [(z, tp_count - 1 - z) for z in range(tp_count)])
    received = lax.all_to_all(packed, "ctx", split_axis=0, concat_axis=0, tiled=True)

    w_late, mirrored = lax.optimization_barrier((w_out, mirrored))

    def cross(block, even_mask, odd_mask):
        return lax.ppermute(block, "ctx", [(i, i ^ (odd_mask if i % 2 else even_mask)) for i in range(ctx_count)])

    w_first = cross(w_late, 4, 2)
    own_spectra, table, back_table = whole_call(
        functools.partial(filter_kernel, poles),
        (
            jax.ShapeDtypeStruct((2, blocks, group, 2 * block), jnp.float32),
            jax.ShapeDtypeStruct((2 * block, 2 * block), jnp.bfloat16),
            jax.ShapeDtypeStruct((4 * block, block), jnp.bfloat16),
        ),
        [
            pltpu.VMEM((2, blocks * group, block), jnp.float32),
            pltpu.VMEM((tok, 2 * half), jnp.float32),
        ],
        2 * 2 * blocks * group * block * 2 * block * 3,
        2 * blocks * group * 2 * block * 4,
        own,
    )
    mixed = whole_call(
        functools.partial(conv_kernel, poles),
        (jax.ShapeDtypeStruct((ctx_count, tp_count, group, tok), jnp.bfloat16),),
        [
            pltpu.VMEM((2, blocks, group, 2 * block), jnp.float32),
            pltpu.VMEM((2, blocks * group, block), jnp.float32),
            pltpu.VMEM((tok, 2 * half), jnp.float32),
            pltpu.VMEM((2 * blocks * group, 2 * block), jnp.float32),
            pltpu.VMEM((2 * blocks * group, 2 * block), jnp.bfloat16),
            pltpu.VMEM((2 * blocks * group, 2 * block), jnp.bfloat16),
            pltpu.VMEM((ctx_count, group, tok), jnp.bfloat16),
            pltpu.SemaphoreType.DMA((2, tp_count)),
        ],
        2 * 8 * blocks * group * block * 2 * block * 3,
        4 * blocks * group * 2 * block * 4,
        received,
        own_spectra,
        paired,
        table,
        back_table,
        out_hbm=(0,),
    )
    mixed, w_first, w_own = lax.optimization_barrier((mixed, w_first, w_out))
    w_third = cross(w_first, 2, 4)
    w_second = cross(w_own, 2, 4)
    w_other = [partner(block, "ctx", 0) for block in (w_own, w_first, w_second, w_third)]
    w_blocks = [w_own, w_other[0], w_first, w_other[2], w_second, w_other[1], w_third, w_other[3]]
    every = lax.all_to_all(
        mixed.reshape(ctx_count * tp_count, group, tok), ("ctx", "tp"), split_axis=0, concat_axis=0, tiled=True
    ).reshape(ctx_count, tp_count, group, tok)
    return whole_call(
        project_kernel,
        (jax.ShapeDtypeStruct((tok, rows * ctx_count), jnp.bfloat16),),
        [
            pltpu.VMEM((ctx_count // 2, 2 * rows, tok), jnp.float32),
            pltpu.VMEM((ctx_count // 2, tok, 2 * rows), jnp.bfloat16),
            pltpu.SemaphoreType.DMA((ctx_count // 2,)),
        ],
        2 * tok * rows * ctx_count * channels,
        2 * rows * ctx_count * channels,
        every,
        *w_blocks,
        out_hbm=(0,),
    )


def local(x_gate, x_post, values, decay, residue, w_out):
    tok, width = x_gate.shape
    ctx_count = lax.axis_size("ctx")
    if tok == 128 and width == 512 and ctx_count == 8 and w_out.shape[0] == 64 and lax.axis_size("tp") == 4:
        return blocked(x_gate, x_post, values, decay, residue, w_out)
    return general(x_gate, x_post, values, decay, residue, w_out)


def solution(mesh):
    in_specs = (
        P("ctx", "tp"),
        P("ctx", "tp"),
        P("ctx", "tp"),
        P(None, "tp", None),
        P(None, "tp", None),
        P(("tp", "ctx"), None),
    )
    out_specs = P("ctx", "tp")
    return jax.shard_map(local, mesh=mesh, in_specs=in_specs, out_specs=out_specs, check_vma=False)
```
